32 devices in a mesh: section: 2 (over core), ctx: 4 (over y, x), fsdp: 4 (over z).
Axes of the slice: x: 2, y: 2, z: 4, core: 2. Of those that a mesh axis runs over, the one named last changes fastest.
Arguments:
- inputs: bfloat16 [2, 4, 1024, 896], P(None, 'fsdp', 'ctx'), may hold values from -6 to 6
- attend_gain: bfloat16 [2, 896], P('section', 'fsdp'), may hold values from 0.5 to 1.5
- projections: bfloat16 [2, 896, 1152], P('section', 'fsdp'), may hold values from -0.1875 to 0.1875
- biases: bfloat16 [2, 1152], P('section', 'fsdp'), may hold values from -3 to 3
- output_weight: bfloat16 [2, 896, 896], P('section', 'fsdp'), may hold values from -6 to 6
- mixer_gain: bfloat16 [2, 896], P('section', 'fsdp'), may hold values from 0.5 to 1.5
- expand_weight: bfloat16 [2, 896, 9728], P('section', 'fsdp'), may hold values from -0.1875 to 0.1875
- down_weight: bfloat16 [2, 4864, 896], P('section', 'fsdp'), may hold values from -0.078125 to 0.078125
- positions: int32 [2, 4, 1024], P(None, 'fsdp'), may hold values from 0 to 1023, as said below
- cotangent: bfloat16 [2, 4, 1024, 896], P(None, 'fsdp', 'ctx'), may hold values from -6 to 6
Outputs:
- activations: bfloat16 [2, 2, 4, 1024, 896], P('section', None, 'fsdp', 'ctx')
- input_grads: float32 [2, 2, 4, 1024, 896], P('section', None, 'fsdp', 'ctx')
- grad_attend: float32 [2, 896], P('section', 'fsdp')
- grad_projections: float32 [2, 896, 1152], P('section', 'fsdp')
- grad_biases: float32 [2, 1024], P('section', 'fsdp')
- grad_value_bias: float32 [2, 128], P('section', 'fsdp')
- grad_output: float32 [2, 896, 896], P('section', 'fsdp')
- grad_mixer: float32 [2, 896], P('section', 'fsdp')
- grad_expand: float32 [2, 896, 9728], P('section', 'fsdp')
- grad_down: float32 [2, 4864, 896], P('section', 'fsdp')
The draws below stay inside these ranges and needn't reach their ends.
Inputs may be any that keep to these rules, and one draw needn't show every extreme that they name: For each sequence, positions is a permutation of 0 to 1023 made of runs of 128 consecutive numbers, each run starting at a multiple of 128 and stored in an aligned group of 128 rows.
All inputs are finite; a program needn't handle non-finite values.
Results may differ from the reference program's by a relative error of at most 0.017.
Values may be sent and summed in bfloat16 or wider, within the bound.
A program may use at most 384 MiB of HBM per device.

```python
import jax
import jax.numpy as jnp
from jax import lax

D = 896
HEADS = 14
KV_HEADS = 2
HEAD_DIM = 64
FF = 4864
SEQ = 1024
MICRO = 2
SEQS = 4
PIECE = 128
KV_WIDTH = 128
N_SECTION = 2


def draw_positions(key, part):
    key = jax.random.fold_in(key, 7)
    run_count = SEQ // PIECE
    seq_keys = jax.random.split(key, MICRO * SEQS)

    def one_order(seq_key):
        return jax.random.permutation(seq_key, run_count)
    orders = jax.vmap(one_order)(seq_keys).astype(jnp.int32)
    spots = orders[:, :, None] * PIECE + jnp.arange(PIECE, dtype=jnp.int32)[None, None, :]
    return spots.reshape(MICRO, SEQS, SEQ).astype(jnp.int32)


def level_of(rng, shape, cuts, least, largest):
    loudness, own = 1.0, jax.random.fold_in(rng, 6)
    for position, parts in cuts:
        steps = jnp.exp(jax.random.uniform(jax.random.fold_in(own, position), (parts,), jnp.float32, least / len(cuts), largest / len(cuts)))
        loudness = loudness * jnp.repeat(steps, shape[position] // parts).reshape([-1 if axis == position else 1 for axis in range(len(shape))])
    return loudness


def normal_values(stream_key, shape, spread, reach, cuts=(), held_as=jnp.bfloat16):
    values = jax.random.normal(stream_key, shape, jnp.float32) * spread
    if len(cuts) > 0:
        values = level_of(stream_key, shape, cuts, -0.22, 0.18) * values
    return jnp.clip(values, min=-reach, max=reach).astype(held_as)


def setup_inputs(seed: int = 0) -> dict:
    key_list = jax.random.split(jax.random.key(seed), 11)
    return {
        "inputs": normal_values(key_list[0], (MICRO, SEQS, SEQ, D), 1.0, 6.0, ((1, 4), (2, 4))),
        "attend_gain": jnp.clip(1.0 + 0.1 * jax.random.normal(key_list[1], (N_SECTION, D), jnp.float32), 0.5, 1.5).astype(jnp.bfloat16),
        "projections": normal_values(key_list[2], (N_SECTION, D, D + 2 * KV_WIDTH), D ** -0.5, 0.1875, ((0, 2), (1, 4))),
        "biases": normal_values(key_list[3], (N_SECTION, D + 2 * KV_WIDTH), 0.5, 3.0, ((0, 2), (1, 4))),
        "output_weight": normal_values(key_list[4], (N_SECTION, D, D), (max(1, 2 * D // SEQ)) ** -0.5, 6.0, ((0, 2), (1, 4))),
        "mixer_gain": jnp.clip(1.0 + 0.1 * jax.random.normal(key_list[5], (N_SECTION, D), jnp.float32), 0.5, 1.5).astype(jnp.bfloat16),
        "expand_weight": normal_values(key_list[6], (N_SECTION, D, 2 * FF), D ** -0.5, 0.1875, ((0, 2), (1, 4))),
        "down_weight": normal_values(key_list[7], (N_SECTION, FF, D), FF ** -0.5, 0.078125, ((0, 2), (1, 4))),
        "positions": draw_positions(jax.random.fold_in(key_list[10], 71), 0),
        "cotangent": normal_values(key_list[9], (MICRO, SEQS, SEQ, D), 1.0, 6.0, ((1, 4), (2, 4))),
    }


epsilon = 1e-06
theta_base = 1000000.0
masked_value = -1e+30

@jax.custom_vjp
def low(v):
    return lax.optimization_barrier(v.astype(jnp.bfloat16)).astype(jnp.float32)

@jax.custom_vjp
def low_back(v):
    return v

def low_keep(v):
    return (low(v), None)

def low_pass(kept, grad):
    return (grad,)

def back_keep(v):
    return (v, None)

def back_low(kept, grad):
    return (low(grad),)
low.defvjp(low_keep, low_pass)
low_back.defvjp(back_keep, back_low)

def matmul(left, right):
    return jnp.dot(left, right, precision=lax.Precision.HIGHEST)

def normalize(values, gain_row):
    return values * lax.rsqrt(lax.optimization_barrier(jnp.mean(values * values, axis=-1, keepdims=True)) + epsilon) * gain_row

def tables(positions_row):
    half_dim = HEAD_DIM // 2
    frequency = theta_base ** (-(jnp.arange(half_dim, dtype=jnp.float32) * 2.0) / HEAD_DIM)
    angles = positions_row.astype(jnp.float32)[:, None] * frequency[None, :]
    angles = jnp.concatenate([angles, angles], axis=-1)
    return (jnp.cos(angles)[:, None, :], jnp.sin(angles)[:, None, :])

def turned(values):
    half_dim = values.shape[-1] // 2
    return jnp.concatenate([-values[..., half_dim:], values[..., :half_dim]], axis=-1)

def rotary(values, cosine, sine):
    return values * cosine + turned(values) * sine

def attention(queries, keyset, valueset, positions_row):
    group_size = HEADS // KV_HEADS
    key_heads = jnp.repeat(keyset, group_size, axis=1)
    value_heads = jnp.repeat(valueset, group_size, axis=1)
    block_rows = min(512, SEQ)
    query_blocks = queries.reshape(SEQ // block_rows, block_rows, HEADS, HEAD_DIM)
    position_blocks = positions_row.reshape(SEQ // block_rows, block_rows)

    def one_block(block_pair):
        query_block, position_block = block_pair
        scores = jnp.einsum('qhd,khd->hqk', query_block, key_heads, precision=lax.Precision.HIGHEST) * HEAD_DIM ** (-0.5)
        scores = low_back(scores)
        allowed = positions_row[None, None, :] <= position_block[None, :, None]
        scores = jnp.where(allowed, scores, masked_value)
        weights_low = low(jax.nn.softmax(scores, axis=-1))
        return jnp.einsum('hqk,khd->qhd', weights_low, value_heads, precision=lax.Precision.HIGHEST)
    blocks = lax.map(jax.checkpoint(one_block), (query_blocks, position_blocks))
    return blocks.reshape(SEQ, HEADS * HEAD_DIM)

def layer_apply(weights, hidden, cosine, sine, positions_row):
    first_gain, project, offset, out_weight, second_gain, expand, shrink = weights
    normed = low(normalize(hidden, first_gain))
    combined = matmul(normed, project) + offset
    query_part = low_back(combined[:, :D])
    key_part = low_back(combined[:, D:D + KV_WIDTH])
    value_part = low(low_back(combined[:, D + KV_WIDTH:]))
    queries = low(rotary(query_part.reshape(SEQ, HEADS, HEAD_DIM), cosine, sine))
    keyset = low(rotary(key_part.reshape(SEQ, KV_HEADS, HEAD_DIM), cosine, sine))
    context = attention(queries, keyset, value_part.reshape(SEQ, KV_HEADS, HEAD_DIM), positions_row)
    context = low(low_back(context))
    middle = hidden + low_back(matmul(context, out_weight))
    second_normed = low(normalize(middle, second_gain))
    widened = low_back(matmul(second_normed, expand))
    activated = low(jax.nn.silu(widened[:, :FF]) * widened[:, FF:])
    return middle + low_back(matmul(activated, shrink))

def reference(inputs, attend_gain, projections, biases, output_weight, mixer_gain, expand_weight, down_weight, positions, cotangent):
    params = (attend_gain.astype(jnp.float32), projections.astype(jnp.float32), biases.astype(jnp.float32), output_weight.astype(jnp.float32), mixer_gain.astype(jnp.float32), expand_weight.astype(jnp.float32), down_weight.astype(jnp.float32))
    seq_count = MICRO * SEQS
    sources = inputs.reshape(seq_count, SEQ, D)
    orders = positions.reshape(seq_count, SEQ)
    upstreams = cotangent.reshape(seq_count, SEQ, D)

    def per_sequence(totals, sequence_item):
        source, positions_row, upstream = sequence_item
        cosine, sine = tables(positions_row)

        def whole_net(weights, start_rows, bridge):
            first_layer = tuple((weight[0] for weight in weights))
            second_layer = tuple((weight[1] for weight in weights))
            layer_one = low_back(low(layer_apply(first_layer, start_rows, cosine, sine, positions_row)) + bridge)
            return (layer_apply(second_layer, layer_one, cosine, sine, positions_row), layer_one)
        final_out, pullback, layer_one = jax.vjp(whole_net, params, source.astype(jnp.float32), jnp.zeros((SEQ, D), jnp.float32), has_aux=True)
        weight_grads, start_grad, bridge_grad = pullback(upstream.astype(jnp.float32))
        totals = jax.tree.map(lambda former, latter: former + latter, totals, weight_grads)
        return (totals, (layer_one.astype(jnp.bfloat16), final_out.astype(jnp.bfloat16), start_grad, bridge_grad))
    initial = jax.tree.map(jnp.zeros_like, params)
    totals, (first_acts, finals, start_grads, bridge_grads) = lax.scan(per_sequence, initial, (sources, orders, upstreams))
    activations = jnp.stack([first_acts, finals]).reshape(N_SECTION, MICRO, SEQS, SEQ, D)
    input_grads = jnp.stack([start_grads, bridge_grads]).reshape(N_SECTION, MICRO, SEQS, SEQ, D)
    bias_total = totals[2]
    return (activations, input_grads, totals[0], totals[1], bias_total[:, :D + KV_WIDTH], bias_total[:, D + KV_WIDTH:], totals[3], totals[4], totals[5], totals[6])
```

```python
import jax
import jax.numpy as jnp
from jax import lax
from jax.sharding import PartitionSpec as P

HEAD_DIM = 64
SECTION, CTX, FSDP = "section", "ctx", "fsdp"

epsilon = 1e-06
theta_base = 1000000.0
masked_value = -1e30

bf16 = jnp.bfloat16
f32 = jnp.float32


def swap_sections(block):
    return lax.ppermute(block, SECTION, [(0, 1), (1, 0)])


def from_peer(block, distance):
    count = lax.axis_size(CTX)
    return lax.ppermute(block, CTX, [(i, i ^ distance) for i in range(count)])


def normalize_rows(values, gain_row):
    norm_scale = lax.rsqrt(jnp.mean(values * values, axis=-1, keepdims=True) + epsilon)
    return (values * norm_scale * gain_row, norm_scale)


def norm_back(upstream, values, norm_scale, gain_row):
    scaled = upstream * gain_row
    gain_grad = jnp.sum(upstream * values * norm_scale, axis=0)
    scale_cubed = norm_scale * norm_scale * norm_scale
    values_grad = norm_scale * scaled - values * scale_cubed * jnp.mean(
        scaled * values, axis=-1, keepdims=True
    )
    return (values_grad, gain_grad)


def tables(positions_row):
    half_dim = HEAD_DIM // 2
    frequency = theta_base ** (-(jnp.arange(half_dim, dtype=f32) * 2.0) / HEAD_DIM)
    angles = positions_row.astype(f32)[:, None] * frequency[None, :]
    angles = jnp.concatenate([angles, angles], axis=-1)
    return (jnp.cos(angles)[:, None, :], jnp.sin(angles)[:, None, :])


def turned(values):
    half_dim = values.shape[-1] // 2
    return jnp.concatenate([-values[..., half_dim:], values[..., :half_dim]], axis=-1)


def rotate(values, cosine, sine):
    return values * cosine + turned(values) * sine


def unrotate(grads, cosine, sine):
    return grads * cosine - turned(grads * sine)


def dot(left, right):
    return jnp.dot(left, right, preferred_element_type=f32)


def pick(index, options):
    chosen = options[0]
    for position in range(1, len(options)):
        chosen = jnp.where(index == position, options[position], chosen)
    return chosen


def head_scores(queries, every_kv, head_index, group_size, key_positions, query_positions):
    grouped = queries[:, head_index * group_size : (head_index + 1) * group_size, :]
    key_block = every_kv[:, head_index * HEAD_DIM : (head_index + 1) * HEAD_DIM]
    scores = jnp.einsum(
        "qgd,kd->gqk", grouped, key_block, preferred_element_type=f32
    ) * HEAD_DIM ** (-0.5)
    allowed = key_positions[None, None, :] <= query_positions[None, :, None]
    return (jnp.where(allowed, scores, masked_value), grouped, key_block)


def attend(layer, hidden, place):
    first_gain, bias, second_gain, weights = layer[:4]
    cosine, sine, key_positions, query_positions = place
    row_count, model_width = hidden.shape
    pair_width = (bias.shape[0] - model_width) // 2
    head_count = model_width // HEAD_DIM
    kv_count = pair_width // HEAD_DIM
    group_size = head_count // kv_count
    wide = model_width + 2 * pair_width
    normed, first_scale = normalize_rows(hidden, first_gain)
    normed = normed.astype(bf16)
    combined = dot(normed, weights[:, :wide]) + bias
    queries = rotate(
        combined[:, :model_width].reshape(row_count, head_count, HEAD_DIM), cosine, sine
    ).astype(bf16)
    key_rows = rotate(
        combined[:, model_width : model_width + pair_width].reshape(row_count, kv_count, HEAD_DIM),
        cosine,
        sine,
    )
    local_kv = jnp.concatenate(
        [key_rows.reshape(row_count, pair_width), combined[:, model_width + pair_width :]], axis=1
    ).astype(bf16)
    every_kv = lax.all_gather(local_kv, CTX, axis=0, tiled=True)
    contexts = []
    row_maxes = []
    row_totals = []
    for head_index in range(kv_count):
        masked, grouped, key_block = head_scores(
            queries, every_kv, head_index, group_size, key_positions, query_positions
        )
        row_max = jnp.max(masked, axis=-1, keepdims=True)
        exponent = jnp.exp(masked - row_max)
        row_total = jnp.sum(exponent, axis=-1, keepdims=True)
        attention_low = (exponent / row_total).astype(bf16)
        value_block = every_kv[
            :, pair_width + head_index * HEAD_DIM : pair_width + (head_index + 1) * HEAD_DIM
        ]
        contexts.append(
            jnp.einsum("gqk,kd->qgd", attention_low, value_block, preferred_element_type=f32)
        )
        row_maxes.append(row_max)
        row_totals.append(row_total)
    context = jnp.concatenate(contexts, axis=1).reshape(row_count, model_width).astype(bf16)
    middle = hidden + dot(context, weights[:, wide:])
    second_normed, second_scale = normalize_rows(middle, second_gain)
    kept = (hidden, first_scale, normed, queries, every_kv, row_maxes, row_totals, context)
    return middle, second_normed.astype(bf16), second_scale, kept


def attend_back(layer, kept, middle_grad, place):
    first_gain, bias, second_gain, weights = layer[:4]
    cosine, sine, key_positions, query_positions = place
    hidden, first_scale, normed, queries, every_kv, row_maxes, row_totals, context = kept
    row_count, model_width = hidden.shape
    pair_width = every_kv.shape[1] // 2
    head_count = model_width // HEAD_DIM
    kv_count = pair_width // HEAD_DIM
    group_size = head_count // kv_count
    wide = model_width + 2 * pair_width
    middle_low = middle_grad.astype(bf16)
    output_grad = jnp.einsum("rd,re->de", context, middle_low, preferred_element_type=f32)
    context_grad = jnp.einsum(
        "re,de->rd", middle_low, weights[:, wide:], preferred_element_type=f32
    )
    context_grad = context_grad.astype(bf16).reshape(row_count, head_count, HEAD_DIM)
    query_grads = []
    key_grads = []
    value_grads = []
    for head_index in range(kv_count):
        masked, grouped, key_block = head_scores(
            queries, every_kv, head_index, group_size, key_positions, query_positions
        )
        attention_full = jnp.exp(masked - row_maxes[head_index]) / row_totals[head_index]
        attention_low = attention_full.astype(bf16)
        value_block = every_kv[
            :, pair_width + head_index * HEAD_DIM : pair_width + (head_index + 1) * HEAD_DIM
        ]
        context_block = context_grad[:, head_index * group_size : (head_index + 1) * group_size, :]
        probs_grad = jnp.einsum(
            "qgd,kd->gqk", context_block, value_block, preferred_element_type=f32
        )
        row_delta = jnp.sum(attention_full * probs_grad, axis=-1, keepdims=True)
        scores_grad = (attention_full * (probs_grad - row_delta)).astype(bf16)
        query_grads.append(
            jnp.einsum("gqk,kd->qgd", scores_grad, key_block, preferred_element_type=f32)
            * HEAD_DIM ** (-0.5)
        )
        key_grads.append(
            jnp.einsum("gqk,qgd->kd", scores_grad, grouped, preferred_element_type=f32)
            * HEAD_DIM ** (-0.5)
        )
        value_grads.append(
            jnp.einsum("gqk,qgd->kd", attention_low, context_block, preferred_element_type=f32)
        )
    every_grad = jnp.concatenate(key_grads + value_grads, axis=1)
    own_grad = lax.psum_scatter(
        every_grad.astype(bf16), CTX, scatter_dimension=0, tiled=True
    ).astype(f32)
    query_turned = unrotate(jnp.concatenate(query_grads, axis=1), cosine, sine).reshape(
        row_count, model_width
    )
    key_turned = unrotate(
        own_grad[:, :pair_width].reshape(row_count, kv_count, HEAD_DIM), cosine, sine
    ).reshape(row_count, pair_width)
    combined_grad = jnp.concatenate(
        [query_turned, key_turned, own_grad[:, pair_width:]], axis=1
    ).astype(bf16)
    project_grad = jnp.einsum("rd,rf->df", normed, combined_grad, preferred_element_type=f32)
    offset_grad = jnp.sum(combined_grad.astype(f32), axis=0)
    normed_grad = jnp.einsum(
        "rf,df->rd", combined_grad, weights[:, :wide], preferred_element_type=f32
    )
    hidden_part, first_grad = norm_back(normed_grad, hidden, first_scale, first_gain)
    attn_grad = jnp.concatenate([project_grad, output_grad], axis=1).astype(bf16)
    return middle_grad + hidden_part, first_grad, offset_grad, attn_grad


def feed(layer, second_normed):
    gate_w, up_w, down_w = layer[4:]
    count = lax.axis_size(CTX)
    blocks = [second_normed] + [from_peer(second_normed, k) for k in range(1, count)]
    gates, ups, acts = [], [], []
    total = None
    for k, block in enumerate(blocks):
        gate = dot(block, gate_w)
        up = dot(block, up_w)
        act = (jax.nn.silu(gate) * up).astype(bf16)
        part = dot(act, down_w)
        gates.append(gate)
        ups.append(up)
        acts.append(act)
        if k:
            part = from_peer(part.astype(bf16), k).astype(f32)
        total = part if total is None else total + part
    return total, (blocks, gates, ups, acts)


def feed_back(layer, kept, grad_out):
    gate_w, up_w, down_w = layer[4:]
    blocks, gates, ups, acts = kept
    count = lax.axis_size(CTX)
    grads = [grad_out] + [from_peer(grad_out, k) for k in range(1, count)]
    total = None
    gate_grads, up_grads = [], []
    for k in range(count):
        spread = jnp.einsum("rd,fd->rf", grads[k], down_w, preferred_element_type=f32)
        gate, up = gates[k], ups[k]
        sig = jax.nn.sigmoid(gate)
        gate_grad = (spread * up * sig * (1.0 + gate * (1.0 - sig))).astype(bf16)
        up_grad = (spread * (gate * sig)).astype(bf16)
        part = jnp.einsum("rf,df->rd", gate_grad, gate_w, preferred_element_type=f32) + jnp.einsum(
            "rf,df->rd", up_grad, up_w, preferred_element_type=f32
        )
        gate_grads.append(gate_grad)
        up_grads.append(up_grad)
        if k:
            part = from_peer(part.astype(bf16), k).astype(f32)
        total = part if total is None else total + part
    rows = jnp.concatenate(blocks, axis=0)
    down_grad = jnp.einsum(
        "rf,rd->fd",
        jnp.concatenate(acts, axis=0),
        jnp.concatenate(grads, axis=0),
        preferred_element_type=f32,
    ).astype(bf16)
    gate_w_grad = jnp.einsum(
        "rd,rf->df", rows, jnp.concatenate(gate_grads, axis=0), preferred_element_type=f32
    ).astype(bf16)
    up_w_grad = jnp.einsum(
        "rd,rf->df", rows, jnp.concatenate(up_grads, axis=0), preferred_element_type=f32
    ).astype(bf16)
    return total, down_grad, jnp.concatenate([gate_w_grad, up_w_grad], axis=1)


def per_device(
    inputs,
    attend_gain,
    projections,
    biases,
    output_weight,
    mixer_gain,
    expand_weight,
    down_weight,
    positions,
    cotangent,
):
    row_count, model_width = inputs.shape[2:]
    section = lax.axis_index(SECTION)
    is_first = section == 0
    ctx = lax.axis_index(CTX)
    fsdp = lax.axis_index(FSDP)
    ctx_count = lax.axis_size(CTX)
    fsdp_count = lax.axis_size(FSDP)
    shard_rows = projections.shape[1]
    half = shard_rows // 2
    wide = projections.shape[2]
    ff_width = expand_weight.shape[2] // 2
    shard_units = down_weight.shape[1]
    units = shard_units // ctx_count
    both = (FSDP, SECTION)

    def mine(array):
        return lax.dynamic_index_in_dim(array, section, 0, keepdims=False)

    source = mine(inputs)[0].astype(f32)
    upstream = mine(cotangent)[0]
    key_positions = mine(positions)[0]
    query_positions = lax.dynamic_slice_in_dim(key_positions, ctx * row_count, row_count)
    cosine, sine = tables(query_positions)
    place = (cosine, sine, key_positions, query_positions)

    small = jnp.concatenate([attend_gain, biases, mixer_gain], axis=1)
    small = lax.all_gather(small, (SECTION, FSDP), axis=0, tiled=True).astype(f32)
    small = small.reshape(2, fsdp_count, -1)
    bias_part = biases.shape[1]

    def small_of(layer):
        rows = small[layer]
        return (
            rows[:, :shard_rows].reshape(-1),
            rows[:, shard_rows : shard_rows + bias_part].reshape(-1),
            rows[:, shard_rows + bias_part :].reshape(-1),
        )

    attn_shard = jnp.concatenate([projections[0], output_weight[0]], axis=1)

    def unit_columns(side):
        pieces = []
        for shard in range(fsdp_count):
            start = side * ff_width + shard * shard_units
            pieces.append(
                pick(
                    ctx,
                    [
                        expand_weight[0, :, start + k * units : start + (k + 1) * units]
                        for k in range(ctx_count)
                    ],
                )
            )
        return jnp.concatenate(pieces, axis=1)

    gate_shard = unit_columns(0)
    up_shard = unit_columns(1)
    down_shard = lax.dynamic_slice_in_dim(down_weight[0], ctx * units, units)

    def halves(array):
        size = array.shape[0] // 2
        low, high = array[:size], array[size:]
        own = jnp.where(is_first, low, high)
        other = swap_sections(jnp.where(is_first, high, low))
        return jnp.where(is_first, own, other), jnp.where(is_first, other, own)

    attn_pair = halves(attn_shard)
    gate_pair = halves(gate_shard)
    up_pair = halves(up_shard)
    down_pair = halves(down_shard)

    def gather(piece):
        return lax.all_gather(piece, both, axis=0, tiled=True)

    layers = []
    for layer in range(2):
        layers.append(
            small_of(layer)
            + (
                gather(attn_pair[layer]),
                gather(gate_pair[layer]),
                gather(up_pair[layer]),
                gather(down_pair[layer]),
            )
        )

    hidden = source
    stored = []
    sent = []
    for layer in range(2):
        middle, second_normed, second_scale, kept = attend(layers[layer], hidden, place)
        total, fed = feed(layers[layer], second_normed)
        low = (middle + total).astype(bf16)
        sent.append(low)
        hidden = low.astype(f32)
        stored.append((middle, second_scale, kept, fed))

    grad = upstream
    hidden_grads = [None, None]
    small_grads = [None, None]
    weight_grads = [None, None]
    for layer in (1, 0):
        middle, second_scale, kept, fed = stored[layer]
        total, down_grad, expand_grad = feed_back(layers[layer], fed, grad)
        middle_part, second_grad = norm_back(total, middle, second_scale, layers[layer][2])
        middle_grad = grad.astype(f32) + middle_part
        hidden_grad, first_grad, offset_grad, attn_grad = attend_back(
            layers[layer], kept, middle_grad, place
        )
        attn_part = lax.psum_scatter(
            attn_grad.reshape(model_width, ctx_count, -1).swapaxes(0, 1).reshape(ctx_count * model_width, -1),
            CTX,
            scatter_dimension=0,
            tiled=True,
        )
        row_grad = jnp.concatenate([expand_grad, attn_part], axis=1)
        weight_grads[layer] = (
            lax.psum_scatter(row_grad, both, scatter_dimension=0, tiled=True),
            lax.psum_scatter(down_grad, both, scatter_dimension=0, tiled=True),
        )
        small_grads[layer] = jnp.concatenate([first_grad, offset_grad, second_grad])
        hidden_grads[layer] = hidden_grad
        grad = hidden_grad.astype(bf16)

    def to_layer(pair):
        own = jnp.where(is_first, pair[0], pair[1])
        other = swap_sections(jnp.where(is_first, pair[1], pair[0]))
        return jnp.where(is_first, own, other), jnp.where(is_first, other, own)

    def finish(pair):
        low, high = to_layer(pair)
        return lax.all_gather(jnp.concatenate([low, high], axis=0), CTX, axis=0).astype(f32)

    row_all = finish((weight_grads[0][0], weight_grads[1][0]))
    down_all = finish((weight_grads[0][1], weight_grads[1][1]))
    grad_down = down_all.reshape(1, shard_units, model_width)
    columns = []
    for side in range(2):
        for shard in range(fsdp_count):
            start = side * fsdp_count * units + shard * units
            for k in range(ctx_count):
                columns.append(row_all[k, :, start : start + units])
    grad_expand = jnp.concatenate(columns, axis=1)[None]
    attn_all = jnp.concatenate(
        [row_all[k, :, 2 * fsdp_count * units :] for k in range(ctx_count)], axis=1
    )
    grad_projections = attn_all[:, :wide][None]
    grad_output = attn_all[:, wide:][None]

    small_all = lax.psum(jnp.stack(small_grads), (CTX, FSDP, SECTION))
    small_own = mine(small_all)
    first_all, offset_all, second_all = (
        small_own[:model_width],
        small_own[model_width : model_width + wide],
        small_own[model_width + wide :],
    )
    pair_width = (wide - model_width) // 2

    def part(vector):
        size = vector.shape[0] // fsdp_count
        return lax.dynamic_slice_in_dim(vector, fsdp * size, size)[None]

    def from_both(pair):
        own = jnp.where(is_first, pair[0], pair[1])
        other = swap_sections(jnp.where(is_first, pair[1], pair[0]))
        return jnp.stack(
            [jnp.where(is_first, own, other), jnp.where(is_first, other, own)]
        )[None, :, None]

    activations = from_both(sent)
    input_grads = from_both([hidden_grads[0], hidden_grads[1].astype(bf16).astype(f32)])
    return (
        activations,
        input_grads,
        part(first_all),
        grad_projections,
        part(offset_all[: model_width + pair_width]),
        part(offset_all[model_width + pair_width :]),
        grad_output,
        part(second_all),
        grad_expand,
        grad_down,
    )


def solution(mesh):
    return jax.shard_map(
        per_device,
        mesh=mesh,
        in_specs=(
            P(None, FSDP, CTX, None),
            P(SECTION, FSDP),
            P(SECTION, FSDP, None),
            P(SECTION, FSDP),
            P(SECTION, FSDP, None),
            P(SECTION, FSDP),
            P(SECTION, FSDP, None),
            P(SECTION, FSDP, None),
            P(None, FSDP, None),
            P(None, FSDP, CTX, None),
        ),
        out_specs=(
            P(SECTION, None, FSDP, CTX, None),
            P(SECTION, None, FSDP, CTX, None),
            P(SECTION, FSDP),
            P(SECTION, FSDP, None),
            P(SECTION, FSDP),
            P(SECTION, FSDP),
            P(SECTION, FSDP, None),
            P(SECTION, FSDP),
            P(SECTION, FSDP, None),
            P(SECTION, FSDP, None),
        ),
        check_vma=False,
    )
```

```python
import functools

import jax
import jax.numpy as jnp
from jax import lax
from jax.experimental import pallas as pl
from jax.experimental.pallas import tpu as pltpu
from jax.sharding import PartitionSpec as P

HEAD_DIM = 64
SECTION, CTX, FSDP = "section", "ctx", "fsdp"

epsilon = 1e-06
theta_base = 1000000.0
masked_value = -1e30

bf16 = jnp.bfloat16
f32 = jnp.float32


def swap_sections(block):
    return lax.ppermute(block, SECTION, [(0, 1), (1, 0)])


def tables(positions_row):
    half_dim = HEAD_DIM // 2
    frequency = theta_base ** (-(jnp.arange(half_dim, dtype=f32) * 2.0) / HEAD_DIM)
    angles = positions_row.astype(f32)[:, None] * frequency[None, :]
    cosine, sine = jnp.cos(angles), jnp.sin(angles)
    return (
        jnp.concatenate([cosine] * 4, axis=-1),
        jnp.concatenate([-sine, sine, -sine, sine], axis=-1),
    )


def from_peer(block, distance):
    count = lax.axis_size(CTX)
    return lax.ppermute(block, CTX, [(i, i ^ distance) for i in range(count)])


def pick(index, options):
    chosen = options[0]
    for position in range(1, len(options)):
        chosen = jnp.where(index == position, options[position], chosen)
    return chosen


MESH = pl.DeviceIdType.MESH
VMEM = pltpu.VMEM
LIMIT = 56 * 1024 * 1024


def flip(index, distance):
    place = 1
    while place <= distance:
        if (distance // place) % 2:
            index = index + place - 2 * place * ((index // place) % 2)
        place *= 2
    return index


def peer_of(distance):
    return (
        lax.axis_index(SECTION),
        flip(lax.axis_index(CTX), distance),
        lax.axis_index(FSDP),
    )


def greet(count):
    barrier = pltpu.get_barrier_semaphore()
    for k in range(1, count):
        pl.semaphore_signal(barrier, inc=1, device_id=peer_of(k), device_id_type=MESH)
    pl.semaphore_wait(barrier, count - 1)


def remote(source, target, send_sem, recv_sem, k):
    return pltpu.make_async_remote_copy(
        src_ref=source,
        dst_ref=target,
        send_sem=send_sem.at[k],
        recv_sem=recv_sem.at[k],
        device_id=peer_of(k),
        device_id_type=MESH,
    )


def matmul(left, right):
    return lax.dot_general(left, right, (((1,), (0,)), ((), ())), preferred_element_type=f32)


def matmul_nt(left, right):
    return lax.dot_general(left, right, (((1,), (1,)), ((), ())), preferred_element_type=f32)


def matmul_tn(left, right):
    return lax.dot_general(left, right, (((0,), (0,)), ((), ())), preferred_element_type=f32)


def tiles(size, step):
    return [(start, min(step, size - start)) for start in range(0, size, step)]


def row_scale(values):
    return lax.rsqrt(jnp.mean(values * values, axis=-1, keepdims=True) + epsilon)


def call(kernel, outs, scratch, cid, *args):
    return pl.pallas_call(
        kernel,
        out_shape=[jax.ShapeDtypeStruct(shape, kind) for shape, kind in outs],
        in_specs=[pl.BlockSpec(memory_space=VMEM)] * len(args),
        out_specs=[pl.BlockSpec(memory_space=VMEM)] * len(outs),
        scratch_shapes=scratch,
        compiler_params=pltpu.CompilerParams(
            collective_id=cid, has_side_effects=True, vmem_limit_bytes=LIMIT
        ),
    )(*args)


def turn_tile(values):
    lane = lax.broadcasted_iota(jnp.int32, values.shape, 1)
    width = values.shape[1]
    half = HEAD_DIM // 2
    ahead = pltpu.roll(values, width - half, 1)
    behind = pltpu.roll(values, half, 1)
    return jnp.where(lane % HEAD_DIM < half, ahead, behind)


def head_in_group(tile, head, group):
    lane = lax.broadcasted_iota(jnp.int32, tile.shape, 1)
    values = tile.astype(f32)
    moved = jnp.where(head % 2 == group, values, pltpu.roll(values, HEAD_DIM, 1))
    return jnp.where(lane // HEAD_DIM == group, moved, 0.0).astype(bf16)


def attend_kernel(
    count, x_ref, g1_ref, bias_ref, g2_ref, w_ref, cos_ref, sin_ref, kpos_ref, qpos_ref,
    normed_ref, q_ref, kv_ref, lse_ref, ctx_ref, mid_ref, low2_ref,
    mask_ref, s_ref, p_ref, vt_ref, ctxf_ref, send_sem, recv_sem,
):
    rows, width = x_ref.shape
    pair = kv_ref.shape[2] // 2
    wide = width + 2 * pair
    heads = width // HEAD_DIM
    group_size = heads // (pair // HEAD_DIM)
    greet(count)
    x = x_ref[...].astype(f32)
    normed = (x * row_scale(x) * g1_ref[...]).astype(bf16)
    normed_ref[...] = normed
    cos, sin = cos_ref[...], sin_ref[...]
    kv = matmul(normed, w_ref[:, width:wide]) + bias_ref[:, width:wide]
    keys = kv[:, :pair]
    kv_ref[0, :, :pair] = (keys * cos + turn_tile(keys) * sin).astype(bf16)
    kv_ref[0, :, pair:] = kv[:, pair:].astype(bf16)
    for k in range(1, count):
        remote(kv_ref.at[0], kv_ref.at[k], send_sem, recv_sem, k).start()
    merged = matmul(normed, w_ref[:, :width]) + bias_ref[:, :width]
    for start, size in tiles(width, 2 * HEAD_DIM):
        part = merged[:, start : start + size]
        turned_part = (part * cos + turn_tile(part) * sin) * HEAD_DIM ** (-0.5)
        q_ref[:, start : start + size] = turned_part.astype(bf16)
    for k in range(count):
        allowed = kpos_ref[k * rows : (k + 1) * rows, :] <= qpos_ref[...]
        mask_ref[k] = jnp.where(allowed, 0.0, masked_value)
    for k in range(count):
        if k:
            remote(kv_ref.at[0], kv_ref.at[k], send_sem, recv_sem, k).wait_recv()
        vt_ref[:, k * rows : (k + 1) * rows] = kv_ref[k, :, pair:].astype(f32).T.astype(bf16)

    def one_head(head, carry):
        group = head // group_size
        start = pl.multiple_of((head // 2) * (2 * HEAD_DIM), 2 * HEAD_DIM)
        tile = q_ref[:, pl.ds(start, 2 * HEAD_DIM)]
        query = head_in_group(tile, head, group)
        top = None
        for k in range(count):
            scores = matmul_nt(kv_ref[k, :, :pair], query) + mask_ref[k]
            s_ref[k] = scores
            here = jnp.max(scores, axis=0, keepdims=True)
            top = here if top is None else jnp.maximum(top, here)
        total = None
        for k in range(count):
            weight = jnp.exp(s_ref[k] - top)
            here = jnp.sum(weight, axis=0, keepdims=True)
            total = here if total is None else total + here
            p_ref[k * rows : (k + 1) * rows, :] = weight.astype(bf16)
        value_rows = vt_ref[pl.ds(pl.multiple_of(group * HEAD_DIM, HEAD_DIM), HEAD_DIM), :]
        context = matmul(value_rows, p_ref[...]) * (1.0 / total)
        place = pl.ds(pl.multiple_of(head * HEAD_DIM, HEAD_DIM), HEAD_DIM)
        ctxf_ref[place, :] = context
        lse_ref[pl.ds(head, 1), :] = top + jnp.log(total)
        return carry

    lax.fori_loop(0, heads, one_head, 0)
    context = ctxf_ref[...]
    ctx_ref[...] = context.astype(bf16)
    middle = x + matmul(context.T.astype(bf16), w_ref[:, wide:])
    mid_ref[...] = middle
    low2_ref[...] = (middle * row_scale(middle) * g2_ref[...]).astype(bf16)
    for k in range(1, count):
        remote(kv_ref.at[0], kv_ref.at[k], send_sem, recv_sem, k).wait_send()


def attend(layer, hidden, place):
    first_gain, bias, second_gain, weights = layer[:4]
    cosine, sine, key_positions, query_positions = place
    rows, width = hidden.shape
    count = lax.axis_size(CTX)
    wide = bias.shape[1]
    pair = (wide - width) // 2
    keys = count * rows
    heads = width // HEAD_DIM
    return call(
        functools.partial(attend_kernel, count),
        [
            ((rows, width), bf16),
            ((rows, width), bf16),
            ((count, rows, 2 * pair), bf16),
            ((-(-heads // 8) * 8, rows), f32),
            ((width, rows), bf16),
            ((rows, width), f32),
            ((rows, width), bf16),
        ],
        [
            VMEM((count, rows, rows), f32),
            VMEM((count, rows, rows), f32),
            VMEM((keys, rows), bf16),
            VMEM((pair, keys), bf16),
            VMEM((width, rows), f32),
            pltpu.SemaphoreType.DMA((count,)),
            pltpu.SemaphoreType.DMA((count,)),
        ],
        1,
        hidden, first_gain, bias, second_gain, weights, cosine, sine, key_positions, query_positions,
    )


def attend_back_kernel(
    count, dmid_ref, x_ref, g1_ref, w_ref, cos_ref, sin_ref, kpos_ref, qpos_ref,
    q_ref, kv_ref, lse_ref,
    dh_ref, merged_ref, gain_ref, bias_ref, low_ref,
    mask_ref, p_ref, dp_ref, ds_ref, kt_ref, dctx_ref, dq_ref, dkv_ref, out_ref, in_ref,
    send_sem, recv_sem,
):
    rows, width = x_ref.shape
    pair = kv_ref.shape[2] // 2
    wide = width + 2 * pair
    heads = width // HEAD_DIM
    group_size = heads // (pair // HEAD_DIM)
    greet(count)
    low = dmid_ref[...].astype(bf16)
    low_ref[...] = low
    dctx = matmul_nt(low, w_ref[:, wide:]).astype(bf16)
    dctx_ref[...] = dctx
    for k in range(count):
        allowed = kpos_ref[k * rows : (k + 1) * rows, :] <= qpos_ref[...]
        mask_ref[k] = jnp.where(allowed, 0.0, masked_value)
        kt_ref[:, k * rows : (k + 1) * rows] = kv_ref[k, :, :pair].astype(f32).T.astype(bf16)
    dkv_ref[...] = jnp.zeros_like(dkv_ref)

    def one_head(head, carry):
        group = head // group_size
        start = pl.multiple_of((head // 2) * (2 * HEAD_DIM), 2 * HEAD_DIM)
        query = head_in_group(q_ref[:, pl.ds(start, 2 * HEAD_DIM)], head, group)
        upstream = head_in_group(dctx_ref[:, pl.ds(start, 2 * HEAD_DIM)], head, group)
        lse = lse_ref[pl.ds(head, 1), :]
        delta = None
        for k in range(count):
            scores = matmul_nt(kv_ref[k, :, :pair], query) + mask_ref[k]
            weight = jnp.exp(scores - lse)
            weight_grad = matmul_nt(kv_ref[k, :, pair:], upstream)
            p_ref[k] = weight
            dp_ref[k] = weight_grad
            dkv_ref[k, :, pair:] += matmul(weight.astype(bf16), upstream)
            here = jnp.sum(weight * weight_grad, axis=0, keepdims=True)
            delta = here if delta is None else delta + here
        for k in range(count):
            score_grad = (p_ref[k] * (dp_ref[k] - delta)).astype(bf16)
            ds_ref[k * rows : (k + 1) * rows, :] = score_grad
            dkv_ref[k, :, :pair] += matmul(score_grad, query)
        key_rows = kt_ref[pl.ds(pl.multiple_of(group * HEAD_DIM, HEAD_DIM), HEAD_DIM), :]
        place = pl.ds(pl.multiple_of(head * HEAD_DIM, HEAD_DIM), HEAD_DIM)
        dq_ref[place, :] = matmul(key_rows, ds_ref[...]) * HEAD_DIM ** (-0.5)
        return carry

    lax.fori_loop(0, heads, one_head, 0)
    for k in range(1, count):
        out_ref[k] = dkv_ref[k].astype(bf16)
        remote(out_ref.at[k], in_ref.at[k], send_sem, recv_sem, k).start()
    cos, sin = cos_ref[...], sin_ref[...]
    dq = dq_ref[...].T

    def unturn(part):
        return (part * cos - turn_tile(part) * sin).astype(bf16)

    for start, size in tiles(width, 2 * HEAD_DIM):
        merged_ref[:, start : start + size] = unturn(dq[:, start : start + size])
    total = dkv_ref[0]
    for k in range(1, count):
        remote(out_ref.at[k], in_ref.at[k], send_sem, recv_sem, k).wait_recv()
        total = total + in_ref[k].astype(f32)
    merged_ref[:, width : width + pair] = unturn(total[:, :pair])
    merged_ref[:, width + pair :] = total[:, pair:].astype(bf16)
    merged = merged_ref[...]
    bias_ref[...] = jnp.sum(merged.astype(f32), axis=0, keepdims=True)
    normed_grad = matmul_nt(merged, w_ref[:, :wide])
    x = x_ref[...].astype(f32)
    scale = row_scale(x)
    gain_ref[...] = jnp.sum(normed_grad * x * scale, axis=0, keepdims=True)
    scaled = normed_grad * g1_ref[...]
    mean = jnp.mean(scaled * x, axis=-1, keepdims=True)
    dh_ref[...] = dmid_ref[...] + scale * scaled - x * (scale * scale * scale * mean)
    for k in range(1, count):
        remote(out_ref.at[k], in_ref.at[k], send_sem, recv_sem, k).wait_send()


def attend_back(layer, kept, middle_grad, place):
    first_gain, bias, second_gain, weights = layer[:4]
    cosine, sine, key_positions, query_positions = place
    hidden, normed, queries, every_kv, lse = kept
    rows, width = hidden.shape
    count = lax.axis_size(CTX)
    wide = bias.shape[1]
    pair = (wide - width) // 2
    keys = count * rows
    return call(
        functools.partial(attend_back_kernel, count),
        [
            ((rows, width), f32),
            ((rows, wide), bf16),
            ((1, width), f32),
            ((1, wide), f32),
            ((rows, width), bf16),
        ],
        [
            VMEM((count, rows, rows), f32),
            VMEM((count, rows, rows), f32),
            VMEM((count, rows, rows), f32),
            VMEM((keys, rows), bf16),
            VMEM((pair, keys), bf16),
            VMEM((rows, width), bf16),
            VMEM((width, rows), f32),
            VMEM((count, rows, 2 * pair), f32),
            VMEM((count, rows, 2 * pair), bf16),
            VMEM((count, rows, 2 * pair), bf16),
            pltpu.SemaphoreType.DMA((count,)),
            pltpu.SemaphoreType.DMA((count,)),
        ],
        2,
        middle_grad, hidden, first_gain, weights, cosine, sine, key_positions, query_positions,
        queries, every_kv, lse,
    )


def unit_chunks(units):
    main = units // 128 * 128
    chunks = [(start, main + start, start, size) for start, size in tiles(main, 512)]
    if units > main:
        chunks.append((2 * main, main + units, main, units - main))
    return chunks


def pack_units(gate, up):
    main = gate.shape[1] // 128 * 128
    return jnp.concatenate([gate[:, :main], up[:, :main], gate[:, main:], up[:, main:]], axis=1)


def unpack_units(packed):
    units = packed.shape[-1] // 2
    main = units // 128 * 128
    gate = jnp.concatenate([packed[..., :main], packed[..., 2 * main : main + units]], axis=-1)
    up = jnp.concatenate([packed[..., main : 2 * main], packed[..., main + units :]], axis=-1)
    return gate, up


def gate_and_up(block, expand_ref, gate_start, up_start, size):
    if size % 128:
        both = matmul(block, expand_ref[:, gate_start : up_start + size])
        return both[:, :size], both[:, size:]
    gate = matmul(block, expand_ref[:, gate_start : gate_start + size])
    return gate, matmul(block, expand_ref[:, up_start : up_start + size])


def feed_kernel(
    count, low_ref, mid_ref, expand_ref, down_ref,
    out_ref, blocks_ref, kept_gate_ref, kept_up_ref,
    act_ref, part_ref, sent_ref, got_ref, send_sem, recv_sem, send_sem2, recv_sem2,
):
    units = down_ref.shape[0]
    greet(count)
    for k in range(1, count):
        remote(low_ref, blocks_ref.at[k], send_sem, recv_sem, k).start()
    blocks_ref[0] = low_ref[...]
    for k in range(count):
        if k:
            remote(low_ref, blocks_ref.at[k], send_sem, recv_sem, k).wait_recv()
        block = blocks_ref[k]
        for gate_start, up_start, start, size in unit_chunks(units):
            gate, up = gate_and_up(block, expand_ref, gate_start, up_start, size)
            kept_gate_ref[k, :, start : start + size] = gate.astype(bf16)
            kept_up_ref[k, :, start : start + size] = up.astype(bf16)
            act_ref[:, start : start + size] = (gate / (1.0 + jnp.exp(-gate)) * up).astype(bf16)
        part = matmul(act_ref[...], down_ref[...])
        if k:
            sent_ref[k] = part.astype(bf16)
            remote(sent_ref.at[k], got_ref.at[k], send_sem2, recv_sem2, k).start()
        else:
            part_ref[...] = part
    total = mid_ref[...] + part_ref[...]
    for k in range(1, count):
        remote(sent_ref.at[k], got_ref.at[k], send_sem2, recv_sem2, k).wait_recv()
        total = total + got_ref[k].astype(f32)
    out_ref[...] = total.astype(bf16)
    for k in range(1, count):
        remote(low_ref, blocks_ref.at[k], send_sem, recv_sem, k).wait_send()
        remote(sent_ref.at[k], got_ref.at[k], send_sem2, recv_sem2, k).wait_send()


def feed(layer, second_normed, middle):
    expand_w, down_w = layer[4:]
    count = lax.axis_size(CTX)
    rows, width = second_normed.shape
    units = down_w.shape[0]
    sems = [pltpu.SemaphoreType.DMA((count,))] * 4
    return call(
        functools.partial(feed_kernel, count),
        [
            ((rows, width), bf16),
            ((count, rows, width), bf16),
            ((count, rows, units), bf16),
            ((count, rows, units), bf16),
        ],
        [
            VMEM((rows, units), bf16),
            VMEM((rows, width), f32),
            VMEM((count, rows, width), bf16),
            VMEM((count, rows, width), bf16),
        ]
        + sems,
        3,
        second_normed, middle, expand_w, down_w,
    )


def feed_back_kernel(
    count, grad_ref, mid_ref, g2_ref, blocks_ref, kept_gate_ref, kept_up_ref, expand_ref, down_ref,
    dmid_ref, gain_ref, dexpand_ref, ddown_ref,
    grads_ref, act_ref, dwide_ref, part_ref, sent_ref, got_ref,
    send_sem, recv_sem, send_sem2, recv_sem2,
):
    rows, width = grad_ref.shape
    units = down_ref.shape[0]
    greet(count)
    for k in range(1, count):
        remote(grad_ref, grads_ref.at[k], send_sem, recv_sem, k).start()
    grads_ref[0] = grad_ref[...]
    for k in range(count):
        if k:
            remote(grad_ref, grads_ref.at[k], send_sem, recv_sem, k).wait_recv()
        block = grads_ref[k]
        for gate_start, up_start, start, size in unit_chunks(units):
            cut = slice(start, start + size)
            spread = matmul_nt(block, down_ref[cut, :])
            gate = kept_gate_ref[k, :, cut].astype(f32)
            up = kept_up_ref[k, :, cut].astype(f32)
            sig = 1.0 / (1.0 + jnp.exp(-gate))
            silu = gate * sig
            act_ref[k, :, cut] = (silu * up).astype(bf16)
            dgate = (spread * up * sig * (1.0 + gate * (1.0 - sig))).astype(bf16)
            dup = (spread * silu).astype(bf16)
            if size % 128:
                dwide_ref[k, :, gate_start : up_start + size] = jnp.concatenate([dgate, dup], axis=1)
            else:
                dwide_ref[k, :, gate_start : gate_start + size] = dgate
                dwide_ref[k, :, up_start : up_start + size] = dup
        part = matmul_nt(dwide_ref[k], expand_ref[...])
        if k:
            sent_ref[k] = part.astype(bf16)
            remote(sent_ref.at[k], got_ref.at[k], send_sem2, recv_sem2, k).start()
        else:
            part_ref[...] = part
    tall = count * rows
    grads = grads_ref[...].reshape(tall, width)
    for start, size in tiles(units // 128 * 128, 384) + [(units // 128 * 128, units % 128)] * (units % 128 > 0):
        act = act_ref[:, :, start : start + size].reshape(tall, size)
        ddown_ref[start : start + size, :] = matmul_tn(act, grads).astype(bf16)
    blocks = blocks_ref[...].reshape(tall, width)
    for start, size in tiles(2 * units, 512):
        dwide = dwide_ref[:, :, start : start + size].reshape(tall, size)
        dexpand_ref[:, start : start + size] = matmul_tn(blocks, dwide).astype(bf16)
    total = part_ref[...]
    for k in range(1, count):
        remote(sent_ref.at[k], got_ref.at[k], send_sem2, recv_sem2, k).wait_recv()
        total = total + got_ref[k].astype(f32)
    middle = mid_ref[...]
    scale = row_scale(middle)
    gain_ref[...] = jnp.sum(total * middle * scale, axis=0, keepdims=True)
    scaled = total * g2_ref[...]
    mean = jnp.mean(scaled * middle, axis=-1, keepdims=True)
    dmid_ref[...] = (
        grad_ref[...].astype(f32) + scale * scaled - middle * (scale * scale * scale * mean)
    )
    for k in range(1, count):
        remote(grad_ref, grads_ref.at[k], send_sem, recv_sem, k).wait_send()
        remote(sent_ref.at[k], got_ref.at[k], send_sem2, recv_sem2, k).wait_send()


def feed_back(layer, middle, blocks, kept_gate, kept_up, grad_out):
    second_gain = layer[2]
    expand_w, down_w = layer[4:]
    count = lax.axis_size(CTX)
    rows, width = grad_out.shape
    units = down_w.shape[0]
    sems = [pltpu.SemaphoreType.DMA((count,))] * 4
    return call(
        functools.partial(feed_back_kernel, count),
        [
            ((rows, width), f32),
            ((1, width), f32),
            ((width, 2 * units), bf16),
            ((units, width), bf16),
        ],
        [
            VMEM((count, rows, width), bf16),
            VMEM((count, rows, units), bf16),
            VMEM((count, rows, 2 * units), bf16),
            VMEM((rows, width), f32),
            VMEM((count, rows, width), bf16),
            VMEM((count, rows, width), bf16),
        ]
        + sems,
        4,
        grad_out, middle, second_gain, blocks, kept_gate, kept_up, expand_w, down_w,
    )


def per_device(
    inputs,
    attend_gain,
    projections,
    biases,
    output_weight,
    mixer_gain,
    expand_weight,
    down_weight,
    positions,
    cotangent,
):
    row_count, model_width = inputs.shape[2:]
    section = lax.axis_index(SECTION)
    is_first = section == 0
    ctx = lax.axis_index(CTX)
    fsdp = lax.axis_index(FSDP)
    ctx_count = lax.axis_size(CTX)
    fsdp_count = lax.axis_size(FSDP)
    shard_rows = projections.shape[1]
    half = shard_rows // 2
    wide = projections.shape[2]
    ff_width = expand_weight.shape[2] // 2
    shard_units = down_weight.shape[1]
    units = shard_units // ctx_count
    both = (FSDP, SECTION)

    def mine(array):
        return lax.dynamic_index_in_dim(array, section, 0, keepdims=False)

    source = mine(inputs)[0]
    upstream = mine(cotangent)[0]
    key_positions = mine(positions)[0]
    query_positions = lax.dynamic_slice_in_dim(key_positions, ctx * row_count, row_count)
    cosine, sine = tables(query_positions)
    by_distance = jnp.concatenate(
        [
            lax.dynamic_slice_in_dim(key_positions, (ctx ^ k) * row_count, row_count)
            for k in range(ctx_count)
        ]
    )
    place = (cosine, sine, by_distance[:, None], query_positions[None])

    small = jnp.concatenate([attend_gain, biases, mixer_gain], axis=1)
    small = lax.all_gather(small, (SECTION, FSDP), axis=0, tiled=True).astype(f32)
    small = small.reshape(2, fsdp_count, -1)
    bias_part = biases.shape[1]

    def small_of(layer):
        rows = small[layer]
        return (
            rows[:, :shard_rows].reshape(1, -1),
            rows[:, shard_rows : shard_rows + bias_part].reshape(1, -1),
            rows[:, shard_rows + bias_part :].reshape(1, -1),
        )

    attn_shard = jnp.concatenate([projections[0], output_weight[0]], axis=1)

    def unit_columns(side):
        pieces = []
        for shard in range(fsdp_count):
            start = side * ff_width + shard * shard_units
            pieces.append(
                pick(
                    ctx,
                    [
                        expand_weight[0, :, start + k * units : start + (k + 1) * units]
                        for k in range(ctx_count)
                    ],
                )
            )
        return jnp.concatenate(pieces, axis=1)

    expand_shard = pack_units(unit_columns(0), unit_columns(1))
    down_shard = lax.dynamic_slice_in_dim(down_weight[0], ctx * units, units)

    def halves(array):
        size = array.shape[0] // 2
        low, high = array[:size], array[size:]
        own = jnp.where(is_first, low, high)
        other = swap_sections(jnp.where(is_first, high, low))
        return jnp.where(is_first, own, other), jnp.where(is_first, other, own)

    attn_pair = halves(attn_shard)
    expand_pair = halves(expand_shard)
    down_pair = halves(down_shard)

    def gather(piece):
        return lax.all_gather(piece, both, axis=0, tiled=True)

    layers = []
    for layer in range(2):
        layers.append(
            small_of(layer)
            + (
                gather(attn_pair[layer]),
                gather(expand_pair[layer]),
                gather(down_pair[layer]),
            )
        )

    hidden = source
    stored = []
    sent = []
    for layer in range(2):
        normed, queries, every_kv, lse, context, middle, second_normed = attend(
            layers[layer], hidden, place
        )
        kept = (hidden, normed, queries, every_kv, lse, context)
        hidden, blocks, kept_gate, kept_up = feed(layers[layer], second_normed, middle)
        sent.append(hidden)
        stored.append((middle, kept, blocks, kept_gate, kept_up))

    chain = []

    def scatter(array):
        if chain:
            array = lax.optimization_barrier((array, chain[-1]))[0]
        chain.append(lax.psum_scatter(array, both, scatter_dimension=0, tiled=True))
        return chain[-1]

    def from_peers(array):
        return [array] + [from_peer(array, k) for k in range(1, ctx_count)]

    def ctx_sum(array):
        size = array.shape[1] // ctx_count
        total = None
        for k in range(ctx_count):
            cut = lax.dynamic_slice_in_dim(array, (ctx ^ k) * size, size, axis=1)
            cut = (from_peer(cut, k) if k else cut).astype(f32)
            total = cut if total is None else total + cut
        return total.astype(bf16)

    grad = upstream
    hidden_grads = [None, None]
    small_grads = [None, None]
    down_parts = [None, None]
    expand_parts = [None, None]
    attn_parts = [None, None]
    waiting = None
    for layer in (1, 0):
        middle, kept, blocks, kept_gate, kept_up = stored[layer]
        middle_grad, second_grad, expand_grad, down_grad = feed_back(
            layers[layer], middle, blocks, kept_gate, kept_up, grad
        )
        down_parts[layer] = from_peers(scatter(down_grad))
        if waiting is not None:
            expand_grad = jnp.concatenate([expand_grad, waiting], axis=1)
        part = scatter(expand_grad)
        if waiting is not None:
            attn_parts[1] = from_peers(part[:, 2 * units * fsdp_count :])
            part = part[:, : 2 * units * fsdp_count]
        expand_parts[layer] = from_peers(part)
        hidden_grad, merged_grad, first_grad, offset_grad, middle_low = attend_back(
            layers[layer], kept[:5], middle_grad, place
        )
        attn_grad = jnp.concatenate(
            [
                jnp.einsum("rd,rf->df", kept[1], merged_grad, preferred_element_type=f32),
                jnp.dot(kept[5], middle_low, preferred_element_type=f32),
            ],
            axis=1,
        ).astype(bf16)
        waiting = ctx_sum(attn_grad)
        small_grads[layer] = jnp.concatenate([first_grad, offset_grad, second_grad], axis=1)[0]
        hidden_grads[layer] = hidden_grad
        grad = hidden_grad.astype(bf16)
    attn_parts[0] = from_peers(scatter(waiting))

    def finish(parts):
        own = [jnp.where(is_first, low, high) for low, high in zip(*parts)]
        other = [swap_sections(jnp.where(is_first, high, low)) for low, high in zip(*parts)]
        whole = [
            jnp.concatenate(
                [jnp.where(is_first, one, two), jnp.where(is_first, two, one)], axis=0
            )
            for one, two in zip(own, other)
        ]
        return [pick(ctx ^ k, whole) for k in range(ctx_count)]

    down_all = finish(down_parts)
    expand_all = [unpack_units(array) for array in finish(expand_parts)]
    attn_all = jnp.concatenate(finish(attn_parts), axis=1).astype(f32)
    grad_down = jnp.concatenate(down_all, axis=0).astype(f32)[None]
    columns = [
        expand_all[k][side][:, shard * units : (shard + 1) * units]
        for side in range(2)
        for shard in range(fsdp_count)
        for k in range(ctx_count)
    ]
    grad_expand = jnp.concatenate(columns, axis=1).astype(f32)[None]
    grad_projections = attn_all[:, :wide][None]
    grad_output = attn_all[:, wide:][None]

    small_all = lax.psum(jnp.stack(small_grads), (CTX, FSDP, SECTION))
    small_own = mine(small_all)
    first_all, offset_all, second_all = (
        small_own[:model_width],
        small_own[model_width : model_width + wide],
        small_own[model_width + wide :],
    )
    pair_width = (wide - model_width) // 2

    def part(vector):
        size = vector.shape[0] // fsdp_count
        return lax.dynamic_slice_in_dim(vector, fsdp * size, size)[None]

    def from_both(pair):
        own = jnp.where(is_first, pair[0], pair[1])
        other = swap_sections(jnp.where(is_first, pair[1], pair[0]))
        return jnp.stack(
            [jnp.where(is_first, own, other), jnp.where(is_first, other, own)]
        )[None, :, None]

    activations = from_both(sent)
    input_grads = from_both([hidden_grads[0], hidden_grads[1].astype(bf16).astype(f32)])
    return (
        activations,
        input_grads,
        part(first_all),
        grad_projections,
        part(offset_all[: model_width + pair_width]),
        part(offset_all[model_width + pair_width :]),
        grad_output,
        part(second_all),
        grad_expand,
        grad_down,
    )


def solution(mesh):
    return jax.shard_map(
        per_device,
        mesh=mesh,
        in_specs=(
            P(None, FSDP, CTX, None),
            P(SECTION, FSDP),
            P(SECTION, FSDP, None),
            P(SECTION, FSDP),
            P(SECTION, FSDP, None),
            P(SECTION, FSDP),
            P(SECTION, FSDP, None),
            P(SECTION, FSDP, None),
            P(None, FSDP, None),
            P(None, FSDP, CTX, None),
        ),
        out_specs=(
            P(SECTION, None, FSDP, CTX, None),
            P(SECTION, None, FSDP, CTX, None),
            P(SECTION, FSDP),
            P(SECTION, FSDP, None),
            P(SECTION, FSDP),
            P(SECTION, FSDP),
            P(SECTION, FSDP, None),
            P(SECTION, FSDP),
            P(SECTION, FSDP, None),
            P(SECTION, FSDP, None),
        ),
        check_vma=False,
    )
```

```python
import functools

import jax
import jax.numpy as jnp
from jax import lax
from jax.experimental import pallas as pl
from jax.experimental.pallas import tpu as pltpu
from jax.sharding import PartitionSpec as P

HEAD_DIM = 64
SECTION, CTX, FSDP = "section", "ctx", "fsdp"

epsilon = 1e-06
theta_base = 1000000.0
masked_value = -1e30

bf16 = jnp.bfloat16
f32 = jnp.float32


def swap_sections(block):
    return lax.ppermute(block, SECTION, [(0, 1), (1, 0)])


def tables(positions_row):
    half_dim = HEAD_DIM // 2
    frequency = theta_base ** (-(jnp.arange(half_dim, dtype=f32) * 2.0) / HEAD_DIM)
    angles = positions_row.astype(f32)[:, None] * frequency[None, :]
    cosine, sine = jnp.cos(angles), jnp.sin(angles)
    return (
        jnp.concatenate([cosine] * 4, axis=-1),
        jnp.concatenate([-sine, sine, -sine, sine], axis=-1),
    )


def pick(index, options):
    chosen = options[0]
    for position in range(1, len(options)):
        chosen = jnp.where(index == position, options[position], chosen)
    return chosen


MESH = pl.DeviceIdType.MESH
VMEM = pltpu.VMEM
LIMIT = 56 * 1024 * 1024


def flip(index, distance):
    place = 1
    while place <= distance:
        if (distance // place) % 2:
            index = index + place - 2 * place * ((index // place) % 2)
        place *= 2
    return index


def place_of():
    return lax.axis_index(SECTION), lax.axis_index(CTX), lax.axis_index(FSDP)


def peer_of(distance):
    section, ctx, fsdp = place_of()
    return (section, flip(ctx, distance), fsdp)


def greet_all(devices):
    barrier = pltpu.get_barrier_semaphore()
    for device in devices:
        pl.semaphore_signal(barrier, inc=1, device_id=device, device_id_type=MESH)
    pl.semaphore_wait(barrier, len(devices))


def greet(count):
    greet_all([peer_of(k) for k in range(1, count)])


def send(source, target, send_sem, recv_sem, device):
    return pltpu.make_async_remote_copy(
        src_ref=source,
        dst_ref=target,
        send_sem=send_sem,
        recv_sem=recv_sem,
        device_id=device,
        device_id_type=MESH,
    )


def remote(source, target, send_sem, recv_sem, k):
    return send(source, target, send_sem.at[k], recv_sem.at[k], peer_of(k))


def matmul(left, right):
    return lax.dot_general(left, right, (((1,), (0,)), ((), ())), preferred_element_type=f32)


def matmul_nt(left, right):
    return lax.dot_general(left, right, (((1,), (1,)), ((), ())), preferred_element_type=f32)


def matmul_tn(left, right):
    return lax.dot_general(left, right, (((0,), (0,)), ((), ())), preferred_element_type=f32)


def tiles(size, step):
    return [(start, min(step, size - start)) for start in range(0, size, step)]


def row_scale(values):
    return lax.rsqrt(jnp.mean(values * values, axis=-1, keepdims=True) + epsilon)


def call(kernel, outs, scratch, cid, *args, far=(), far_outs=()):
    def spec(position, away):
        return pl.BlockSpec(memory_space=pl.ANY if position in away else VMEM)

    return pl.pallas_call(
        kernel,
        out_shape=[jax.ShapeDtypeStruct(shape, kind) for shape, kind in outs],
        in_specs=[spec(position, far) for position in range(len(args))],
        out_specs=[spec(position, far_outs) for position in range(len(outs))],
        scratch_shapes=scratch,
        compiler_params=pltpu.CompilerParams(
            collective_id=cid, has_side_effects=True, vmem_limit_bytes=LIMIT
        ),
    )(*args)


def dma(*shape):
    return pltpu.SemaphoreType.DMA(shape)


class Collect:
    def __init__(self, ctx_count, fsdp_count, shard_ref, w_ref, sems):
        self.shard_ref, self.w_ref = shard_ref, w_ref
        self.z_send, self.z_recv, self.y_send, self.y_recv, self.v_send, self.v_recv, self.own_sem = sems
        self.shards = range(1, fsdp_count)
        self.places = range(1, ctx_count)
        self.fsdp_count = fsdp_count
        self.section, self.ctx, self.fsdp = place_of()
        self.sister = (1 - self.section, self.ctx, self.fsdp)
        self.rows, width = shard_ref.shape
        self.piece = width // (2 * ctx_count)
        self.mine = pl.ds(pl.multiple_of(self.fsdp * self.rows, self.rows), self.rows)
        self.friends = (
            [self.ahead(d) for d in self.shards] + [peer_of(k) for k in self.places] + [self.sister]
        )

    def ahead(self, d):
        return (self.section, self.ctx, lax.rem(self.fsdp + d, self.fsdp_count))

    def behind(self, d):
        return lax.rem(self.fsdp + self.fsdp_count - d, self.fsdp_count)

    def columns(self, where, core):
        return pl.ds(pl.multiple_of((where * 2 + core) * self.piece, self.piece), self.piece)

    def block(self, d, where, core):
        start = pl.multiple_of(self.behind(d) * self.rows, self.rows)
        return self.w_ref.at[pl.ds(start, self.rows), self.columns(where, core)]

    def own(self, d):
        cols = self.columns(self.ctx, self.section)
        source, target = self.shard_ref.at[:, cols], self.w_ref.at[self.mine, cols]
        return send(source, target, self.z_send.at[d], self.z_recv.at[d], self.ahead(d))

    def kept(self):
        return pltpu.make_async_copy(self.shard_ref, self.w_ref.at[self.mine], self.own_sem.at[0])

    def spread(self, d, k):
        source = self.block(d, self.ctx, self.section)
        device = peer_of(k) if k else self.sister
        return send(source, source, self.y_send.at[d, k], self.y_recv.at[d, k], device)

    def passed(self, d, k):
        source = self.block(d, flip(self.ctx, k), self.section)
        return send(source, source, self.v_send.at[d, k], self.v_recv.at[d, k], self.sister)

    def begin(self):
        for d in self.shards:
            self.own(d).start()
        self.kept().start()

    def relay(self):
        for d in self.shards:
            came = self.block(d, self.ctx, self.section)
            send(came, came, self.z_send.at[d], self.z_recv.at[d], self.sister).wait_recv()
            for k in (*self.places, 0):
                self.spread(d, k).start()

    def hand(self):
        for d in self.shards:
            for k in self.places:
                came = self.block(d, flip(self.ctx, k), self.section)
                send(came, came, self.y_send.at[d, k], self.y_recv.at[d, k], self.sister).wait_recv()
                self.passed(d, k).start()

    def finish(self):
        for d in self.shards:
            for k in (0, *self.places):
                came = self.block(d, flip(self.ctx, k), 1 - self.section)
                recv = (self.v_recv if k else self.y_recv).at[d, k]
                send(came, came, self.v_send.at[d, k], recv, self.sister).wait_recv()
        for d in self.shards:
            self.own(d).wait_send()
            self.spread(d, 0).wait_send()
            for k in self.places:
                self.spread(d, k).wait_send()
                self.passed(d, k).wait_send()
        self.kept().wait()


def collect_sems(ctx_count, fsdp_count):
    table = dma(fsdp_count, ctx_count)
    return [dma(fsdp_count), dma(fsdp_count), table, table, table, table, dma(1)]


def collect_kernel(
    ctx_count, fsdp_count, shard_ref, small_ref, w_ref, smalls_ref, s_send, s_recv, *sems
):
    steps = Collect(ctx_count, fsdp_count, shard_ref, w_ref, sems)

    def small(d):
        target = smalls_ref.at[steps.fsdp]
        return send(small_ref, target, s_send.at[d], s_recv.at[d], steps.ahead(d))

    greet_all(steps.friends)
    steps.begin()
    for d in steps.shards:
        small(d).start()
    smalls_ref[steps.fsdp] = small_ref[...]
    steps.relay()
    steps.hand()
    steps.finish()
    for d in steps.shards:
        came = smalls_ref.at[steps.behind(d)]
        send(came, came, s_send.at[d], s_recv.at[d], steps.sister).wait_recv()
    for d in steps.shards:
        small(d).wait_send()


def collect(shard, small):
    ctx_count, fsdp_count = lax.axis_size(CTX), lax.axis_size(FSDP)
    rows, width = shard.shape
    return call(
        functools.partial(collect_kernel, ctx_count, fsdp_count),
        [((fsdp_count * rows, width), bf16), ((fsdp_count,) + small.shape, bf16)],
        [dma(fsdp_count), dma(fsdp_count)] + collect_sems(ctx_count, fsdp_count),
        5,
        shard, small, far_outs=(0,),
    )


class SquareSum:
    def __init__(self, ctx_count, grad_ref, a_ref, b_out, b_in, sems):
        self.grad_ref, self.a_ref, self.b_out, self.b_in = grad_ref, a_ref, b_out, b_in
        self.a_send, self.a_recv, self.b_send, self.b_recv = sems
        self.places = range(1, ctx_count)
        self.section, self.ctx, fsdp = place_of()
        self.sister = (1 - self.section, self.ctx, fsdp)
        self.piece = grad_ref.shape[1] // (2 * ctx_count)

    def columns(self, k, core):
        start = (flip(self.ctx, k) * 2 + core) * self.piece
        return pl.ds(pl.multiple_of(start, self.piece), self.piece)

    def chip(self, k):
        source = self.grad_ref.at[:, self.columns(k, 1 - self.section)]
        return send(source, self.a_ref.at[k], self.a_send.at[k], self.a_recv.at[k], self.sister)

    def square(self, k):
        return remote(self.b_out.at[k], self.b_in.at[k], self.b_send, self.b_recv, k)

    def begin(self):
        for k in (*self.places, 0):
            self.chip(k).start()

    def middle(self):
        for k in (*self.places, 0):
            self.chip(k).wait_recv()
            own = self.grad_ref[:, self.columns(k, self.section)].astype(f32)
            self.b_out[k] = (own + self.a_ref[k].astype(f32)).astype(bf16)
            if k:
                self.square(k).start()

    def end(self):
        total = self.b_out[0].astype(f32)
        for k in self.places:
            self.square(k).wait_recv()
            total = total + self.b_in[k].astype(f32)
        return total.astype(bf16)

    def sent(self):
        self.chip(0).wait_send()
        for k in self.places:
            self.chip(k).wait_send()
            self.square(k).wait_send()


def square_scratch(ctx_count, grad):
    width, both = grad.shape
    piece = VMEM((ctx_count, width, both // (2 * ctx_count)), bf16)
    return [piece, piece, piece, dma(ctx_count), dma(ctx_count), dma(ctx_count), dma(ctx_count)]


def every_owner(ctx_count, layer, start_or_wait, sources, targets, send_sem, recv_sem):
    section, ctx, fsdp = place_of()
    for k in range(ctx_count):
        device = (layer, flip(ctx, k), fsdp)

        def go():
            for i, (source, target) in enumerate(zip(sources, targets)):
                copy = send(
                    source,
                    target.at[ctx, section],
                    send_sem.at[i, k],
                    recv_sem.at[i, section, k],
                    device,
                )
                copy.start() if start_or_wait == "start" else copy.wait_send()

        pl.when(section != layer)(go) if k == 0 else go()


def from_owners(ctx_count, layer, targets, send_sem, recv_sem):
    section, ctx, fsdp = place_of()
    for core in range(2):
        for k in range(ctx_count):
            if core == layer and k == 0:
                continue

            def go():
                for i, target in enumerate(targets):
                    came = target.at[flip(ctx, k), core]
                    send(
                        came, came, send_sem.at[i, k], recv_sem.at[i, core, k], (1 - section, ctx, fsdp)
                    ).wait_recv()

            pl.when(section == layer)(go)


def chip_square(ctx_count):
    section, ctx, fsdp = place_of()
    return [
        (section if same else 1 - section, flip(ctx, k), fsdp)
        for k in range(ctx_count)
        for same in (True, False)
        if k or not same
    ]


def turn_tile(values):
    lane = lax.broadcasted_iota(jnp.int32, values.shape, 1)
    width = values.shape[1]
    half = HEAD_DIM // 2
    ahead = pltpu.roll(values, width - half, 1)
    behind = pltpu.roll(values, half, 1)
    return jnp.where(lane % HEAD_DIM < half, ahead, behind)


def head_in_group(tile, head, group):
    lane = lax.broadcasted_iota(jnp.int32, tile.shape, 1)
    values = tile.astype(f32)
    moved = values if head % 2 == group else pltpu.roll(values, HEAD_DIM, 1)
    return jnp.where(lane // HEAD_DIM == group, moved, 0.0).astype(bf16)


def attend_kernel(count, fsdp_count, fetch, *refs):
    x_ref, g1_ref, bias_ref, g2_ref, w_ref, cos_ref, sin_ref, kpos_ref, qpos_ref = refs[:9]
    refs = refs[9:]
    shard_ref, refs = (refs[0], refs[1:]) if fetch else (None, refs)
    normed_ref, q_ref, kv_ref, lse_ref, ctx_ref, mid_ref, low2_ref = refs[:7]
    refs = refs[7:]
    next_ref, refs = (refs[0], refs[1:]) if fetch else (None, refs)
    mask_ref, s_ref, p_ref, vt_ref, ctxf_ref, send_sem, recv_sem, *sems = refs
    rows, width = x_ref.shape
    pair = kv_ref.shape[2] // 2
    wide = width + 2 * pair
    heads = width // HEAD_DIM
    group_size = heads // (pair // HEAD_DIM)
    if fetch:
        steps = Collect(count, fsdp_count, shard_ref, next_ref, sems)
        greet_all(steps.friends)
        steps.begin()
    else:
        greet(count)
    x = x_ref[...].astype(f32)
    normed = (x * row_scale(x) * g1_ref[...]).astype(bf16)
    normed_ref[...] = normed
    cos, sin = cos_ref[...], sin_ref[...]
    kv = matmul(normed, w_ref[:, width:wide]) + bias_ref[:, width:wide]
    keys = kv[:, :pair]
    kv_ref[0, :, :pair] = (keys * cos + turn_tile(keys) * sin).astype(bf16)
    kv_ref[0, :, pair:] = kv[:, pair:].astype(bf16)
    for k in range(1, count):
        remote(kv_ref.at[0], kv_ref.at[k], send_sem, recv_sem, k).start()
    merged = matmul(normed, w_ref[:, :width]) + bias_ref[:, :width]
    for start, size in tiles(width, 2 * HEAD_DIM):
        part = merged[:, start : start + size]
        turned_part = (part * cos + turn_tile(part) * sin) * HEAD_DIM ** (-0.5)
        q_ref[:, start : start + size] = turned_part.astype(bf16)
    for k in range(count):
        allowed = kpos_ref[k * rows : (k + 1) * rows, :] <= qpos_ref[...]
        mask_ref[k] = jnp.where(allowed, 0.0, masked_value)
    if fetch:
        steps.relay()
    for k in range(count):
        if k:
            remote(kv_ref.at[0], kv_ref.at[k], send_sem, recv_sem, k).wait_recv()
        vt_ref[:, k * rows : (k + 1) * rows] = kv_ref[k, :, pair:].astype(f32).T.astype(bf16)

    for head in range(heads):
        group = head // group_size
        start = head // 2 * (2 * HEAD_DIM)
        query = head_in_group(q_ref[:, start : start + 2 * HEAD_DIM], head, group)
        top = None
        for k in range(count):
            scores = matmul_nt(kv_ref[k, :, :pair], query) + mask_ref[k]
            s_ref[k] = scores
            here = jnp.max(scores, axis=0, keepdims=True)
            top = here if top is None else jnp.maximum(top, here)
        total = None
        for k in range(count):
            weight = jnp.exp(s_ref[k] - top)
            here = jnp.sum(weight, axis=0, keepdims=True)
            total = here if total is None else total + here
            p_ref[k * rows : (k + 1) * rows, :] = weight.astype(bf16)
        value_rows = vt_ref[group * HEAD_DIM : (group + 1) * HEAD_DIM, :]
        context = matmul(value_rows, p_ref[...]) * (1.0 / total)
        ctxf_ref[head * HEAD_DIM : (head + 1) * HEAD_DIM, :] = context
        lse_ref[head : head + 1, :] = top + jnp.log(total)
        if fetch and head == heads // 2:
            steps.hand()
    context = ctxf_ref[...]
    ctx_ref[...] = context.astype(bf16)
    middle = x + matmul(context.T.astype(bf16), w_ref[:, wide:])
    mid_ref[...] = middle
    low2_ref[...] = (middle * row_scale(middle) * g2_ref[...]).astype(bf16)
    for k in range(1, count):
        remote(kv_ref.at[0], kv_ref.at[k], send_sem, recv_sem, k).wait_send()
    if fetch:
        steps.finish()


def attend(layer, hidden, place, shard=None):
    first_gain, bias, second_gain, weights = layer[:4]
    cosine, sine, key_positions, query_positions = place
    rows, width = hidden.shape
    count = lax.axis_size(CTX)
    wide = bias.shape[1]
    pair = (wide - width) // 2
    keys = count * rows
    heads = width // HEAD_DIM
    fetch = shard is not None
    fsdp_count = lax.axis_size(FSDP)
    args = (
        hidden, first_gain, bias, second_gain, weights, cosine, sine, key_positions, query_positions,
    )
    return call(
        functools.partial(attend_kernel, count, fsdp_count, fetch),
        [
            ((rows, width), bf16),
            ((rows, width), bf16),
            ((count, rows, 2 * pair), bf16),
            ((-(-heads // 8) * 8, rows), f32),
            ((width, rows), bf16),
            ((rows, width), f32),
            ((rows, width), bf16),
        ]
        + [(weights.shape, bf16)] * fetch,
        [
            VMEM((count, rows, rows), f32),
            VMEM((count, rows, rows), f32),
            VMEM((keys, rows), bf16),
            VMEM((pair, keys), bf16),
            VMEM((width, rows), f32),
            dma(count),
            dma(count),
        ]
        + (collect_sems(count, fsdp_count) if fetch else []),
        10 if fetch else 1,
        *args, *([shard] if fetch else []),
        far_outs=(7,) if fetch else (),
    )


def attend_back_kernel(count, carried, *refs):
    (
        dmid_ref, x_ref, g1_ref, w_ref, cos_ref, sin_ref, kpos_ref, qpos_ref,
        normed_ref, q_ref, kv_ref, lse_ref, ctx_ref,
    ) = refs[:13]
    refs = refs[13:]
    load_ref, refs = (refs[0], refs[1:]) if carried else (None, refs)
    dh_ref, gain_ref, bias_ref, grad_ref = refs[:4]
    refs = refs[4:]
    summed_ref, refs = (refs[0], refs[1:]) if carried else (None, refs)
    (
        mask_ref, p_ref, dp_ref, ds_ref, kt_ref, dctx_ref, dq_ref, dkv_ref, out_ref, in_ref,
        merged_ref, low_ref, send_sem, recv_sem, *scratch,
    ) = refs
    rows, width = x_ref.shape
    pair = kv_ref.shape[2] // 2
    wide = width + 2 * pair
    heads = width // HEAD_DIM
    group_size = heads // (pair // HEAD_DIM)
    if carried:
        steps = SquareSum(count, load_ref, *scratch[:3], scratch[3:])
        greet_all([peer_of(k) for k in range(1, count)] + [steps.sister])
        steps.begin()
    else:
        greet(count)
    low = dmid_ref[...].astype(bf16)
    low_ref[...] = low
    dctx = matmul_nt(low, w_ref[:, wide:]).astype(bf16)
    dctx_ref[...] = dctx
    for k in range(count):
        allowed = kpos_ref[k * rows : (k + 1) * rows, :] <= qpos_ref[...]
        mask_ref[k] = jnp.where(allowed, 0.0, masked_value)
        kt_ref[:, k * rows : (k + 1) * rows] = kv_ref[k, :, :pair].astype(f32).T.astype(bf16)
    dkv_ref[...] = jnp.zeros_like(dkv_ref)

    for head in range(heads):
        group = head // group_size
        start = head // 2 * (2 * HEAD_DIM)
        query = head_in_group(q_ref[:, start : start + 2 * HEAD_DIM], head, group)
        upstream = head_in_group(dctx_ref[:, start : start + 2 * HEAD_DIM], head, group)
        lse = lse_ref[head : head + 1, :]
        delta = None
        for k in range(count):
            scores = matmul_nt(kv_ref[k, :, :pair], query) + mask_ref[k]
            weight = jnp.exp(scores - lse)
            weight_grad = matmul_nt(kv_ref[k, :, pair:], upstream)
            p_ref[k] = weight
            dp_ref[k] = weight_grad
            dkv_ref[k, :, pair:] += matmul(weight.astype(bf16), upstream)
            here = jnp.sum(weight * weight_grad, axis=0, keepdims=True)
            delta = here if delta is None else delta + here
        for k in range(count):
            score_grad = (p_ref[k] * (dp_ref[k] - delta)).astype(bf16)
            ds_ref[k * rows : (k + 1) * rows, :] = score_grad
            dkv_ref[k, :, :pair] += matmul(score_grad, query)
        key_rows = kt_ref[group * HEAD_DIM : (group + 1) * HEAD_DIM, :]
        dq_ref[head * HEAD_DIM : (head + 1) * HEAD_DIM, :] = (
            matmul(key_rows, ds_ref[...]) * HEAD_DIM ** (-0.5)
        )
        if carried and head == heads // 3:
            steps.middle()
    for k in range(1, count):
        out_ref[k] = dkv_ref[k].astype(bf16)
        remote(out_ref.at[k], in_ref.at[k], send_sem, recv_sem, k).start()
    cos, sin = cos_ref[...], sin_ref[...]
    dq = dq_ref[...].T

    def unturn(part):
        return (part * cos - turn_tile(part) * sin).astype(bf16)

    for start, size in tiles(width, 2 * HEAD_DIM):
        merged_ref[:, start : start + size] = unturn(dq[:, start : start + size])
    grad_ref[:, wide:] = matmul(ctx_ref[...], low_ref[...]).astype(bf16)
    normed = normed_ref[...]

    def project_grad(first, last):
        for start, size in tiles(last - first, 512):
            cut = slice(first + start, first + start + size)
            grad_ref[:, cut] = matmul_tn(normed, merged_ref[:, cut]).astype(bf16)

    project_grad(0, width)
    normed_grad = matmul_nt(merged_ref[:, :width], w_ref[:, :width])
    total = dkv_ref[0]
    for k in range(1, count):
        remote(out_ref.at[k], in_ref.at[k], send_sem, recv_sem, k).wait_recv()
        total = total + in_ref[k].astype(f32)
    merged_ref[:, width : width + pair] = unturn(total[:, :pair])
    merged_ref[:, width + pair :] = total[:, pair:].astype(bf16)
    project_grad(width, wide)
    normed_grad = normed_grad + matmul_nt(merged_ref[:, width:], w_ref[:, width:wide])
    bias_ref[...] = jnp.sum(merged_ref[...].astype(f32), axis=0, keepdims=True)
    x = x_ref[...].astype(f32)
    scale = row_scale(x)
    gain_ref[...] = jnp.sum(normed_grad * x * scale, axis=0, keepdims=True)
    scaled = normed_grad * g1_ref[...]
    mean = jnp.mean(scaled * x, axis=-1, keepdims=True)
    dh_ref[...] = dmid_ref[...] + scale * scaled - x * (scale * scale * scale * mean)
    for k in range(1, count):
        remote(out_ref.at[k], in_ref.at[k], send_sem, recv_sem, k).wait_send()
    if carried:
        summed_ref[...] = steps.end()
        steps.sent()


def attend_back(layer, kept, middle_grad, place, load=None):
    first_gain, bias, second_gain, weights = layer[:4]
    cosine, sine, key_positions, query_positions = place
    hidden, normed, queries, every_kv, lse, context = kept
    rows, width = hidden.shape
    count = lax.axis_size(CTX)
    wide = bias.shape[1]
    pair = (wide - width) // 2
    keys = count * rows
    carried = load is not None
    args = (
        middle_grad, hidden, first_gain, weights, cosine, sine, key_positions, query_positions,
        normed, queries, every_kv, lse, context,
    )
    return call(
        functools.partial(attend_back_kernel, count, carried),
        [
            ((rows, width), f32),
            ((1, width), f32),
            ((1, wide), f32),
            ((width, wide + width), bf16),
        ]
        + [((width, (wide + width) // (2 * count)), bf16)] * carried,
        [
            VMEM((count, rows, rows), f32),
            VMEM((count, rows, rows), f32),
            VMEM((count, rows, rows), f32),
            VMEM((keys, rows), bf16),
            VMEM((pair, keys), bf16),
            VMEM((rows, width), bf16),
            VMEM((width, rows), f32),
            VMEM((count, rows, 2 * pair), f32),
            VMEM((count, rows, 2 * pair), bf16),
            VMEM((count, rows, 2 * pair), bf16),
            VMEM((rows, wide), bf16),
            VMEM((rows, width), bf16),
            dma(count),
            dma(count),
        ]
        + (square_scratch(count, load) if carried else []),
        6 if carried else 2,
        *args, *([load] if carried else []),
    )


def unit_chunks(units):
    main = units // 128 * 128
    chunks = [(start, main + start, start, size) for start, size in tiles(main, 512)]
    if units > main:
        chunks.append((2 * main, main + units, main, units - main))
    return chunks


def pack_units(gate, up):
    main = gate.shape[1] // 128 * 128
    return jnp.concatenate([gate[:, :main], up[:, :main], gate[:, main:], up[:, main:]], axis=1)


def unpack_units(packed):
    units = packed.shape[-1] // 2
    main = units // 128 * 128
    gate = jnp.concatenate([packed[..., :main], packed[..., 2 * main : main + units]], axis=-1)
    up = jnp.concatenate([packed[..., main : 2 * main], packed[..., main + units :]], axis=-1)
    return gate, up


def gate_and_up(block, expand_ref, gate_start, up_start, size):
    if size % 128:
        both = matmul(block, expand_ref[:, gate_start : up_start + size])
        return both[:, :size], both[:, size:]
    gate = matmul(block, expand_ref[:, gate_start : gate_start + size])
    return gate, matmul(block, expand_ref[:, up_start : up_start + size])


def feed_kernel(
    count, turns, low_ref, mid_ref, expand_ref, down_ref,
    out_ref, blocks_ref, kept_gate_ref, kept_up_ref,
    act_ref, part_ref, sent_ref, got_ref, send_sem, recv_sem, send_sem2, recv_sem2, turn_sem,
):
    units = down_ref.shape[0]
    if turns:
        section, ctx, fsdp = place_of()
        greet_all([peer_of(k) for k in range(1, count)] + [(1 - section, ctx, fsdp)])

        @pl.when(section == 1)
        def _():
            pl.semaphore_wait(turn_sem, 1)
    else:
        greet(count)
    for k in range(1, count):
        remote(low_ref, blocks_ref.at[k], send_sem, recv_sem, k).start()
    if turns:

        @pl.when(section == 0)
        def _():
            for k in range(1, count):
                remote(low_ref, blocks_ref.at[k], send_sem, recv_sem, k).wait_send()
            pl.semaphore_signal(
                turn_sem, inc=1, device_id=(1 - section, ctx, fsdp), device_id_type=MESH
            )
    blocks_ref[0] = low_ref[...]
    for k in range(count):
        if k:
            remote(low_ref, blocks_ref.at[k], send_sem, recv_sem, k).wait_recv()
        block = blocks_ref[k]
        for gate_start, up_start, start, size in unit_chunks(units):
            gate, up = gate_and_up(block, expand_ref, gate_start, up_start, size)
            kept_gate_ref[k, :, start : start + size] = gate.astype(bf16)
            kept_up_ref[k, :, start : start + size] = up.astype(bf16)
            act_ref[:, start : start + size] = (gate / (1.0 + jnp.exp(-gate)) * up).astype(bf16)
        part = matmul(act_ref[...], down_ref[...])
        if k:
            sent_ref[k] = part.astype(bf16)
            remote(sent_ref.at[k], got_ref.at[k], send_sem2, recv_sem2, k).start()
        else:
            part_ref[...] = part
    total = mid_ref[...] + part_ref[...]
    for k in range(1, count):
        remote(sent_ref.at[k], got_ref.at[k], send_sem2, recv_sem2, k).wait_recv()
        total = total + got_ref[k].astype(f32)
    out_ref[...] = total.astype(bf16)
    for k in range(1, count):
        remote(sent_ref.at[k], got_ref.at[k], send_sem2, recv_sem2, k).wait_send()
    if turns:

        @pl.when(section == 1)
        def _():
            for k in range(1, count):
                remote(low_ref, blocks_ref.at[k], send_sem, recv_sem, k).wait_send()
    else:
        for k in range(1, count):
            remote(low_ref, blocks_ref.at[k], send_sem, recv_sem, k).wait_send()


def feed(layer, second_normed, middle, turns):
    expand_w, down_w = layer[4:]
    count = lax.axis_size(CTX)
    rows, width = second_normed.shape
    units = down_w.shape[0]
    sems = [pltpu.SemaphoreType.DMA((count,))] * 4
    return call(
        functools.partial(feed_kernel, count, turns),
        [
            ((rows, width), bf16),
            ((count, rows, width), bf16),
            ((count, rows, units), bf16),
            ((count, rows, units), bf16),
        ],
        [
            VMEM((rows, units), bf16),
            VMEM((rows, width), f32),
            VMEM((count, rows, width), bf16),
            VMEM((count, rows, width), bf16),
        ]
        + sems
        + [pltpu.SemaphoreType.REGULAR],
        3 if turns else 9,
        second_normed, middle, expand_w, down_w,
    )


def feed_back_kernel(
    count, grad_ref, mid_ref, g2_ref, blocks_ref, kept_gate_ref, kept_up_ref, expand_ref, down_ref,
    dmid_ref, gain_ref, dexpand_ref, ddown_ref,
    grads_ref, act_ref, dwide_ref, part_ref, sent_ref, got_ref,
    send_sem, recv_sem, send_sem2, recv_sem2,
):
    rows, width = grad_ref.shape
    units = down_ref.shape[0]
    greet(count)
    for k in range(1, count):
        remote(grad_ref, grads_ref.at[k], send_sem, recv_sem, k).start()
    grads_ref[0] = grad_ref[...]
    for k in range(count):
        if k:
            remote(grad_ref, grads_ref.at[k], send_sem, recv_sem, k).wait_recv()
        block = grads_ref[k]
        for gate_start, up_start, start, size in unit_chunks(units):
            cut = slice(start, start + size)
            spread = matmul_nt(block, down_ref[cut, :])
            gate = kept_gate_ref[k, :, cut].astype(f32)
            up = kept_up_ref[k, :, cut].astype(f32)
            sig = 1.0 / (1.0 + jnp.exp(-gate))
            silu = gate * sig
            act_ref[k, :, cut] = (silu * up).astype(bf16)
            dgate = (spread * up * sig * (1.0 + gate * (1.0 - sig))).astype(bf16)
            dup = (spread * silu).astype(bf16)
            if size % 128:
                dwide_ref[k, :, gate_start : up_start + size] = jnp.concatenate([dgate, dup], axis=1)
            else:
                dwide_ref[k, :, gate_start : gate_start + size] = dgate
                dwide_ref[k, :, up_start : up_start + size] = dup
        part = matmul_nt(dwide_ref[k], expand_ref[...])
        if k:
            sent_ref[k] = part.astype(bf16)
            remote(sent_ref.at[k], got_ref.at[k], send_sem2, recv_sem2, k).start()
        else:
            part_ref[...] = part
    tall = count * rows
    grads = grads_ref[...].reshape(tall, width)
    for start, size in tiles(units // 128 * 128, 384) + [(units // 128 * 128, units % 128)] * (units % 128 > 0):
        act = act_ref[:, :, start : start + size].reshape(tall, size)
        ddown_ref[start : start + size, :] = matmul_tn(act, grads).astype(bf16)
    blocks = blocks_ref[...].reshape(tall, width)
    for start, size in tiles(2 * units, 512):
        dwide = dwide_ref[:, :, start : start + size].reshape(tall, size)
        dexpand_ref[:, start : start + size] = matmul_tn(blocks, dwide).astype(bf16)
    total = part_ref[...]
    for k in range(1, count):
        remote(sent_ref.at[k], got_ref.at[k], send_sem2, recv_sem2, k).wait_recv()
        total = total + got_ref[k].astype(f32)
    middle = mid_ref[...]
    scale = row_scale(middle)
    gain_ref[...] = jnp.sum(total * middle * scale, axis=0, keepdims=True)
    scaled = total * g2_ref[...]
    mean = jnp.mean(scaled * middle, axis=-1, keepdims=True)
    dmid_ref[...] = (
        grad_ref[...].astype(f32) + scale * scaled - middle * (scale * scale * scale * mean)
    )
    for k in range(1, count):
        remote(grad_ref, grads_ref.at[k], send_sem, recv_sem, k).wait_send()
        remote(sent_ref.at[k], got_ref.at[k], send_sem2, recv_sem2, k).wait_send()


def feed_back(layer, middle, blocks, kept_gate, kept_up, grad_out):
    second_gain = layer[2]
    expand_w, down_w = layer[4:]
    count = lax.axis_size(CTX)
    rows, width = grad_out.shape
    units = down_w.shape[0]
    sems = [pltpu.SemaphoreType.DMA((count,))] * 4
    return call(
        functools.partial(feed_back_kernel, count),
        [
            ((rows, width), f32),
            ((1, width), f32),
            ((width, 2 * units), bf16),
            ((units, width), bf16),
        ],
        [
            VMEM((count, rows, width), bf16),
            VMEM((count, rows, units), bf16),
            VMEM((count, rows, 2 * units), bf16),
            VMEM((rows, width), f32),
            VMEM((count, rows, width), bf16),
            VMEM((count, rows, width), bf16),
        ]
        + sems,
        4,
        grad_out, middle, second_gain, blocks, kept_gate, kept_up, expand_w, down_w,
    )


def attn_sum_kernel(
    ctx_count, fsdp_count, wide, low_ref, high_ref, small_ref, expand_ref, down_ref,
    projections_ref, output_ref, total_ref, expand_all_ref, down_all_ref,
    c_out, c_in, d_out, whole_ref, s_out, s_in,
    c_send, c_recv, d_send, d_recv, s_send, s_recv, e_send, e_recv, e_own, *square_refs,
):
    section, ctx, fsdp = place_of()
    sister = (1 - section, ctx, fsdp)
    width, piece = high_ref.shape
    rows = width // fsdp_count
    places = range(1, ctx_count)
    shards = range(1, fsdp_count)
    steps = SquareSum(ctx_count, low_ref, *square_refs[:3], square_refs[3:])
    sources, targets = (expand_ref, down_ref), (expand_all_ref, down_all_ref)
    kept = [
        pltpu.make_async_copy(source, target.at[ctx, section], e_own.at[i])
        for i, (source, target) in enumerate(zip(sources, targets))
    ]

    def ahead(d):
        return (section, ctx, lax.rem(fsdp + d, fsdp_count))

    def c_copy(layer, d):
        target = lax.rem(fsdp + d, fsdp_count)
        source = c_out.at[layer, pl.ds(pl.multiple_of(target * rows, rows), rows)]
        return send(source, c_in.at[layer, d], c_send.at[layer, d], c_recv.at[layer, d], ahead(d))

    def s_copy(step, source, device):
        return send(s_out.at[source], s_in.at[step], s_send.at[step], s_recv.at[step], device)

    def line_sum(layer):
        total = c_out[layer, pl.ds(pl.multiple_of(fsdp * rows, rows), rows)].astype(f32)
        for d in shards:
            c_copy(layer, d).wait_recv()
            total = total + c_in[layer, d].astype(f32)
        d_out[layer] = total.astype(bf16)
        every_owner(
            ctx_count, layer, "start", [d_out.at[layer]], [whole_ref], d_send.at[layer], d_recv
        )

        @pl.when(section == layer)
        def _():
            whole_ref[ctx, section] = d_out[layer]

    hops = [(0, 0, sister)]
    hops += [(k, 1, peer_of(k)) for k in places]
    hops += [(ctx_count - 1 + d, 2, ahead(d)) for d in shards]

    greet_all(chip_square(ctx_count) + [ahead(d) for d in shards])
    steps.begin()
    s_out[0] = small_ref[...]
    s_copy(*hops[0]).start()
    c_out[1] = high_ref[...]
    for d in shards:
        c_copy(1, d).start()

    @pl.when(section == 1)
    def _():
        for copy in kept:
            copy.start()

    steps.middle()
    s_copy(*hops[0]).wait_recv()
    s_out[1] = s_out[0] + s_in[0]
    for k in places:
        s_copy(*hops[k]).start()
    line_sum(1)
    c_out[0] = steps.end()
    for d in shards:
        c_copy(0, d).start()
    every_owner(ctx_count, 1, "start", sources, targets, e_send, e_recv)
    part = s_out[1]
    for k in places:
        s_copy(*hops[k]).wait_recv()
        part = part + s_in[k]
    s_out[2] = part
    for d in shards:
        s_copy(*hops[ctx_count - 1 + d]).start()
    line_sum(0)
    part = s_out[2]
    for d in shards:
        s_copy(*hops[ctx_count - 1 + d]).wait_recv()
        part = part + s_in[ctx_count - 1 + d]
    total_ref[...] = part
    for layer in (1, 0):
        from_owners(ctx_count, layer, [whole_ref], d_send.at[layer], d_recv)
    for where in range(ctx_count):
        for core in range(2):
            start = (where * 2 + core) * piece
            block = whole_ref[where, core].astype(f32)
            size = max(min(wide - start, piece), 0)
            if size:
                projections_ref[:, start : start + size] = block[:, :size]
            if size < piece:
                first = start + size - wide
                output_ref[:, first : first + piece - size] = block[:, size:]
    from_owners(ctx_count, 1, targets, e_send, e_recv)
    steps.sent()
    for layer in (1, 0):
        for d in shards:
            c_copy(layer, d).wait_send()
        every_owner(
            ctx_count, layer, "wait", [d_out.at[layer]], [whole_ref], d_send.at[layer], d_recv
        )
    every_owner(ctx_count, 1, "wait", sources, targets, e_send, e_recv)
    for hop in hops:
        s_copy(*hop).wait_send()

    @pl.when(section == 1)
    def _():
        for copy in kept:
            copy.wait()


def attn_sum(low, high, small, expand_part, down_part, wide):
    ctx_count, fsdp_count = lax.axis_size(CTX), lax.axis_size(FSDP)
    width, both = low.shape
    rows = width // fsdp_count
    piece = both // (2 * ctx_count)
    hops = ctx_count + fsdp_count - 1
    return call(
        functools.partial(attn_sum_kernel, ctx_count, fsdp_count, wide),
        [
            ((rows, wide), f32),
            ((rows, both - wide), f32),
            (small.shape, f32),
            ((ctx_count, 2) + expand_part.shape, bf16),
            ((ctx_count, 2) + down_part.shape, bf16),
        ],
        [
            VMEM((2, width, piece), bf16),
            VMEM((2, fsdp_count, rows, piece), bf16),
            VMEM((2, rows, piece), bf16),
            VMEM((ctx_count, 2, rows, piece), bf16),
            VMEM((3,) + small.shape, f32),
            VMEM((hops,) + small.shape, f32),
            dma(2, fsdp_count), dma(2, fsdp_count),
            dma(2, 1, ctx_count), dma(1, 2, ctx_count),
            dma(hops), dma(hops),
            dma(2, ctx_count), dma(2, 2, ctx_count), dma(2),
        ]
        + square_scratch(ctx_count, low),
        7,
        low, high, small, expand_part, down_part, far_outs=(3, 4),
    )


def settle_kernel(
    ctx_count, expand_ref, down_ref, expand_all_ref, down_all_ref,
    expand_out, down_out, send_sem, recv_sem, own_sem,
):
    section, ctx, _ = place_of()
    greet_all(chip_square(ctx_count))
    sources, targets = (expand_ref, down_ref), (expand_out, down_out)
    every_owner(ctx_count, 0, "start", sources, targets, send_sem, recv_sem)
    kept = [
        pltpu.make_async_copy(source, target.at[ctx, section], own_sem.at[i])
        for i, (source, target) in enumerate(zip(sources, targets))
    ]
    loads = [
        pltpu.make_async_copy(source, target, own_sem.at[2 + i])
        for i, (source, target) in enumerate(zip((expand_all_ref, down_all_ref), targets))
    ]

    @pl.when(section == 0)
    def _():
        for copy in kept:
            copy.start()
        for copy in kept:
            copy.wait()

    @pl.when(section == 1)
    def _():
        for copy in loads:
            copy.start()
        for copy in loads:
            copy.wait()

    from_owners(ctx_count, 0, targets, send_sem, recv_sem)
    every_owner(ctx_count, 0, "wait", sources, targets, send_sem, recv_sem)


def spread_kernel(chunk, shards, side_width, block_ref, out_ref):
    count = block_ref.shape[0]
    for where in range(count):
        sides = unpack_units(block_ref[where].astype(f32))
        for side, values in enumerate(sides):
            for shard in range(shards):
                start = side * side_width + (shard * count + where) * chunk
                out_ref[:, start : start + chunk] = values[:, shard * chunk : (shard + 1) * chunk]


def finish(expand_part, down_part, expand_all, down_all, ff_width):
    ctx_count, fsdp_count = lax.axis_size(CTX), lax.axis_size(FSDP)
    half, packed = expand_part.shape
    half_units, width = down_part.shape
    expand_all, down_all = call(
        functools.partial(settle_kernel, ctx_count),
        [(expand_all.shape, bf16), (down_all.shape, bf16)],
        [dma(2, ctx_count), dma(2, 2, ctx_count), dma(4)],
        8,
        expand_part, down_part, expand_all, down_all,
        far=(2, 3),
    )
    rows = 2 * half
    step = 32 if rows % 32 == 0 else 16
    grad_expand = pl.pallas_call(
        functools.partial(spread_kernel, packed // 2 // fsdp_count, fsdp_count, ff_width),
        grid=(rows // step,),
        out_shape=jax.ShapeDtypeStruct((rows, 2 * ff_width), f32),
        in_specs=[pl.BlockSpec((ctx_count, step, packed), lambda i: (0, i, 0))],
        out_specs=pl.BlockSpec((step, 2 * ff_width), lambda i: (i, 0)),
        compiler_params=pltpu.CompilerParams(vmem_limit_bytes=LIMIT),
    )(expand_all.reshape(ctx_count, rows, packed))
    grad_down = down_all.astype(f32).reshape(2 * ctx_count * half_units, width)
    return grad_expand, grad_down


def per_device(
    inputs,
    attend_gain,
    projections,
    biases,
    output_weight,
    mixer_gain,
    expand_weight,
    down_weight,
    positions,
    cotangent,
):
    row_count, model_width = inputs.shape[2:]
    section = lax.axis_index(SECTION)
    is_first = section == 0
    ctx = lax.axis_index(CTX)
    fsdp = lax.axis_index(FSDP)
    ctx_count = lax.axis_size(CTX)
    fsdp_count = lax.axis_size(FSDP)
    shard_rows = projections.shape[1]
    wide = projections.shape[2]
    ff_width = expand_weight.shape[2] // 2
    shard_units = down_weight.shape[1]
    units = shard_units // ctx_count
    both = (FSDP, SECTION)

    def mine(array):
        return lax.dynamic_index_in_dim(array, section, 0, keepdims=False)

    source = mine(inputs)[0]
    upstream = mine(cotangent)[0]
    key_positions = mine(positions)[0]
    query_positions = lax.dynamic_slice_in_dim(key_positions, ctx * row_count, row_count)
    cosine, sine = tables(query_positions)
    by_distance = jnp.concatenate(
        [
            lax.dynamic_slice_in_dim(key_positions, (ctx ^ k) * row_count, row_count)
            for k in range(ctx_count)
        ]
    )
    place = (cosine, sine, by_distance[:, None], query_positions[None])

    bias_part = biases.shape[1]
    small_width = -(-bias_part // 128) * 128

    def padded(row):
        return jnp.pad(row, ((0, 0), (0, small_width - row.shape[1])))

    small_shard = jnp.concatenate(
        [padded(attend_gain), padded(biases), padded(mixer_gain), jnp.zeros((13, small_width), bf16)]
    )
    attn_shard = jnp.concatenate([projections[0], output_weight[0]], axis=1)

    def in_order(array):
        other = swap_sections(array)
        return jnp.where(is_first, array, other), jnp.where(is_first, other, array)

    def unit_columns(side):
        pieces = []
        for shard in range(fsdp_count):
            start = side * ff_width + shard * shard_units
            pieces.append(
                pick(
                    ctx,
                    [
                        expand_weight[0, :, start + k * units : start + (k + 1) * units]
                        for k in range(ctx_count)
                    ],
                )
            )
        return jnp.concatenate(pieces, axis=1)

    expand_shard = pack_units(unit_columns(0), unit_columns(1))
    down_shard = lax.dynamic_slice_in_dim(down_weight[0], ctx * units, units)

    def halves(array):
        size = array.shape[0] // 2
        low, high = array[:size], array[size:]
        own = jnp.where(is_first, low, high)
        other = swap_sections(jnp.where(is_first, high, low))
        return jnp.where(is_first, own, other), jnp.where(is_first, other, own)

    expand_pair = halves(expand_shard)
    down_pair = halves(down_shard)
    first_shard, second_shard = in_order(attn_shard)
    small_pair = jnp.concatenate(in_order(small_shard))

    def gather(piece):
        return lax.all_gather(piece, both, axis=0, tiled=True)

    expands, downs = [None, None], [None, None]
    expands[0], downs[0] = gather(expand_pair[0]), gather(down_pair[0])
    first_shard, small_pair = lax.optimization_barrier(
        (first_shard, small_pair, expand_pair[0], down_pair[0])
    )[:2]
    weights, smalls = collect(first_shard, small_pair)
    smalls = smalls.astype(f32)
    weights = [weights, None]
    expands[1], downs[1] = gather(expand_pair[1]), gather(down_pair[1])

    def layer_of(layer):
        first = 16 * layer
        return (
            smalls[:, first, :shard_rows].reshape(1, -1),
            smalls[:, first + 1, :bias_part].reshape(1, -1),
            smalls[:, first + 2, :shard_rows].reshape(1, -1),
            weights[layer],
            expands[layer],
            downs[layer],
        )

    layers = []
    hidden = source
    stored = []
    sent = []
    for layer in range(2):
        layers.append(layer_of(layer))
        normed, queries, every_kv, lse, context, middle, second_normed, *fetched = attend(
            layers[layer], hidden, place, None if layer else second_shard
        )
        if fetched:
            weights[1] = fetched[0]
        kept = (hidden, normed, queries, every_kv, lse, context)
        hidden, blocks, kept_gate, kept_up = feed(layers[layer], second_normed, middle, False)
        sent.append(hidden)
        stored.append((middle, kept, blocks, kept_gate, kept_up))

    def scatter(array):
        return lax.psum_scatter(array, both, scatter_dimension=0, tiled=True)

    grad = upstream
    hidden_grads = [None, None]
    small_grads = [None, None]
    attn_grads = [None, None]
    scattered = ()
    summed = ()
    for layer in (1, 0):
        middle, kept, blocks, kept_gate, kept_up = stored[layer]
        middle_grad, second_grad, expand_grad, down_grad = feed_back(
            layers[layer], middle, blocks, kept_gate, kept_up, grad
        )
        if scattered:
            expand_grad, down_grad, *scattered = lax.optimization_barrier(
                (expand_grad, down_grad, *scattered)
            )
        hidden_grad, first_grad, offset_grad, attn_grads[layer], *summed = attend_back(
            layers[layer], kept, middle_grad, place, attn_grads[1]
        )
        earlier, scattered = scattered, (scatter(expand_grad), scatter(down_grad))
        small_grads[layer] = jnp.concatenate([first_grad, offset_grad, second_grad], axis=1)[0]
        hidden_grads[layer] = hidden_grad
        grad = hidden_grad.astype(bf16)

    spare = -small_grads[0].shape[0] % model_width
    small_rows = [jnp.pad(vector, (0, spare)).reshape(-1, model_width) for vector in small_grads]
    small_count = small_rows[0].shape[0]
    rows_left = -2 * small_count % 8
    small_stack = jnp.pad(jnp.concatenate(small_rows), ((0, rows_left), (0, 0)))
    grad_projections, grad_output, small_all, *gathered = attn_sum(
        attn_grads[0], *summed, small_stack, *earlier, wide
    )
    grad_expand, grad_down = finish(*scattered, *gathered, ff_width)
    small_own = jnp.where(
        is_first, small_all[:small_count], small_all[small_count : 2 * small_count]
    ).reshape(-1)
    first_all, offset_all, second_all = (
        small_own[:model_width],
        small_own[model_width : model_width + wide],
        small_own[model_width + wide : 2 * model_width + wide],
    )
    pair_width = (wide - model_width) // 2

    def part(vector):
        size = vector.shape[0] // fsdp_count
        return lax.dynamic_slice_in_dim(vector, fsdp * size, size)[None]

    def from_both(pair):
        own = jnp.where(is_first, pair[0], pair[1])
        other = swap_sections(jnp.where(is_first, pair[1], pair[0]))
        return jnp.stack(
            [jnp.where(is_first, own, other), jnp.where(is_first, other, own)]
        )[None, :, None]

    activations = from_both(sent)
    input_grads = from_both([hidden_grads[0], hidden_grads[1].astype(bf16).astype(f32)])
    return (
        activations,
        input_grads,
        part(first_all),
        grad_projections[None],
        part(offset_all[: model_width + pair_width]),
        part(offset_all[model_width + pair_width :]),
        grad_output[None],
        part(second_all),
        grad_expand[None],
        grad_down[None],
    )


def solution(mesh):
    return jax.shard_map(
        per_device,
        mesh=mesh,
        in_specs=(
            P(None, FSDP, CTX, None),
            P(SECTION, FSDP),
            P(SECTION, FSDP, None),
            P(SECTION, FSDP),
            P(SECTION, FSDP, None),
            P(SECTION, FSDP),
            P(SECTION, FSDP, None),
            P(SECTION, FSDP, None),
            P(None, FSDP, None),
            P(None, FSDP, CTX, None),
        ),
        out_specs=(
            P(SECTION, None, FSDP, CTX, None),
            P(SECTION, None, FSDP, CTX, None),
            P(SECTION, FSDP),
            P(SECTION, FSDP, None),
            P(SECTION, FSDP),
            P(SECTION, FSDP),
            P(SECTION, FSDP, None),
            P(SECTION, FSDP),
            P(SECTION, FSDP, None),
            P(SECTION, FSDP, None),
        ),
        check_vma=False,
    )
```

```python
import functools

import jax
import jax.numpy as jnp
from jax import lax
from jax.experimental import pallas as pl
from jax.experimental.pallas import tpu as pltpu
from jax.sharding import PartitionSpec as P

HEAD_DIM = 64
SECTION, CTX, FSDP = "section", "ctx", "fsdp"

epsilon = 1e-06
theta_base = 1000000.0
masked_value = -1e30

bf16 = jnp.bfloat16
f32 = jnp.float32


def swap_sections(block):
    return lax.ppermute(block, SECTION, [(0, 1), (1, 0)])


def tables(positions_row):
    half_dim = HEAD_DIM // 2
    frequency = theta_base ** (-(jnp.arange(half_dim, dtype=f32) * 2.0) / HEAD_DIM)
    angles = positions_row.astype(f32)[:, None] * frequency[None, :]
    cosine, sine = jnp.cos(angles), jnp.sin(angles)
    return (
        jnp.concatenate([cosine] * 4, axis=-1),
        jnp.concatenate([-sine, sine, -sine, sine], axis=-1),
    )


def pick(index, options):
    chosen = options[0]
    for position in range(1, len(options)):
        chosen = jnp.where(index == position, options[position], chosen)
    return chosen


MESH = pl.DeviceIdType.MESH
VMEM = pltpu.VMEM
LIMIT = 56 * 1024 * 1024


def flip(index, distance):
    place = 1
    while place <= distance:
        if (distance // place) % 2:
            index = index + place - 2 * place * ((index // place) % 2)
        place *= 2
    return index


def place_of():
    return lax.axis_index(SECTION), lax.axis_index(CTX), lax.axis_index(FSDP)


def peer_of(distance):
    section, ctx, fsdp = place_of()
    return (section, flip(ctx, distance), fsdp)


def greet_all(devices):
    barrier = pltpu.get_barrier_semaphore()
    for device in devices:
        pl.semaphore_signal(barrier, inc=1, device_id=device, device_id_type=MESH)
    pl.semaphore_wait(barrier, len(devices))


def greet(count):
    greet_all([peer_of(k) for k in range(1, count)])


def send(source, target, send_sem, recv_sem, device):
    return pltpu.make_async_remote_copy(
        src_ref=source,
        dst_ref=target,
        send_sem=send_sem,
        recv_sem=recv_sem,
        device_id=device,
        device_id_type=MESH,
    )


def remote(source, target, send_sem, recv_sem, k):
    return send(source, target, send_sem.at[k], recv_sem.at[k], peer_of(k))


def matmul(left, right):
    return lax.dot_general(left, right, (((1,), (0,)), ((), ())), preferred_element_type=f32)


def matmul_nt(left, right):
    return lax.dot_general(left, right, (((1,), (1,)), ((), ())), preferred_element_type=f32)


def matmul_tn(left, right):
    return lax.dot_general(left, right, (((0,), (0,)), ((), ())), preferred_element_type=f32)


def tiles(size, step):
    return [(start, min(step, size - start)) for start in range(0, size, step)]


def row_scale(values):
    return lax.rsqrt(jnp.mean(values * values, axis=-1, keepdims=True) + epsilon)


def call(kernel, outs, scratch, cid, *args, far=(), far_outs=()):
    def spec(position, away):
        return pl.BlockSpec(memory_space=pl.ANY if position in away else VMEM)

    return pl.pallas_call(
        kernel,
        out_shape=[jax.ShapeDtypeStruct(shape, kind) for shape, kind in outs],
        in_specs=[spec(position, far) for position in range(len(args))],
        out_specs=[spec(position, far_outs) for position in range(len(outs))],
        scratch_shapes=scratch,
        compiler_params=pltpu.CompilerParams(
            collective_id=cid, has_side_effects=True, vmem_limit_bytes=LIMIT
        ),
    )(*args)


def dma(*shape):
    return pltpu.SemaphoreType.DMA(shape)


class Collect:
    def __init__(self, ctx_count, fsdp_count, shard_ref, w_ref, sems):
        self.shard_ref, self.w_ref = shard_ref, w_ref
        self.z_send, self.z_recv, self.y_send, self.y_recv, self.v_send, self.v_recv, self.own_sem = sems
        self.shards = range(1, fsdp_count)
        self.places = range(1, ctx_count)
        self.fsdp_count = fsdp_count
        self.section, self.ctx, self.fsdp = place_of()
        self.sister = (1 - self.section, self.ctx, self.fsdp)
        self.rows, width = shard_ref.shape
        self.piece = width // (2 * ctx_count)
        self.mine = pl.ds(pl.multiple_of(self.fsdp * self.rows, self.rows), self.rows)
        self.friends = (
            [self.ahead(d) for d in self.shards] + [peer_of(k) for k in self.places] + [self.sister]
        )

    def ahead(self, d):
        return (self.section, self.ctx, lax.rem(self.fsdp + d, self.fsdp_count))

    def behind(self, d):
        return lax.rem(self.fsdp + self.fsdp_count - d, self.fsdp_count)

    def columns(self, where, core):
        return pl.ds(pl.multiple_of((where * 2 + core) * self.piece, self.piece), self.piece)

    def block(self, d, where, core):
        start = pl.multiple_of(self.behind(d) * self.rows, self.rows)
        return self.w_ref.at[pl.ds(start, self.rows), self.columns(where, core)]

    def own(self, d):
        cols = self.columns(self.ctx, self.section)
        source, target = self.shard_ref.at[:, cols], self.w_ref.at[self.mine, cols]
        return send(source, target, self.z_send.at[d], self.z_recv.at[d], self.ahead(d))

    def kept(self):
        return pltpu.make_async_copy(self.shard_ref, self.w_ref.at[self.mine], self.own_sem.at[0])

    def spread(self, d, k):
        source = self.block(d, self.ctx, self.section)
        device = peer_of(k) if k else self.sister
        return send(source, source, self.y_send.at[d, k], self.y_recv.at[d, k], device)

    def passed(self, d, k):
        source = self.block(d, flip(self.ctx, k), self.section)
        return send(source, source, self.v_send.at[d, k], self.v_recv.at[d, k], self.sister)

    def begin(self):
        for d in self.shards:
            self.own(d).start()
        self.kept().start()

    def relay(self):
        for d in self.shards:
            came = self.block(d, self.ctx, self.section)
            send(came, came, self.z_send.at[d], self.z_recv.at[d], self.sister).wait_recv()
            for k in (*self.places, 0):
                self.spread(d, k).start()

    def hand(self):
        for d in self.shards:
            for k in self.places:
                came = self.block(d, flip(self.ctx, k), self.section)
                send(came, came, self.y_send.at[d, k], self.y_recv.at[d, k], self.sister).wait_recv()
                self.passed(d, k).start()

    def finish(self):
        for d in self.shards:
            for k in (0, *self.places):
                came = self.block(d, flip(self.ctx, k), 1 - self.section)
                recv = (self.v_recv if k else self.y_recv).at[d, k]
                send(came, came, self.v_send.at[d, k], recv, self.sister).wait_recv()
        for d in self.shards:
            self.own(d).wait_send()
            self.spread(d, 0).wait_send()
            for k in self.places:
                self.spread(d, k).wait_send()
                self.passed(d, k).wait_send()
        self.kept().wait()


def collect_sems(ctx_count, fsdp_count):
    table = dma(fsdp_count, ctx_count)
    return [dma(fsdp_count), dma(fsdp_count), table, table, table, table, dma(1)]


def collect_kernel(
    ctx_count, fsdp_count, shard_ref, small_ref, w_ref, smalls_ref, s_send, s_recv, *sems
):
    steps = Collect(ctx_count, fsdp_count, shard_ref, w_ref, sems)

    def small(d):
        target = smalls_ref.at[steps.fsdp]
        return send(small_ref, target, s_send.at[d], s_recv.at[d], steps.ahead(d))

    greet_all(steps.friends)
    steps.begin()
    for d in steps.shards:
        small(d).start()
    smalls_ref[steps.fsdp] = small_ref[...]
    steps.relay()
    steps.hand()
    steps.finish()
    for d in steps.shards:
        came = smalls_ref.at[steps.behind(d)]
        send(came, came, s_send.at[d], s_recv.at[d], steps.sister).wait_recv()
    for d in steps.shards:
        small(d).wait_send()


def collect(shard, small):
    ctx_count, fsdp_count = lax.axis_size(CTX), lax.axis_size(FSDP)
    rows, width = shard.shape
    return call(
        functools.partial(collect_kernel, ctx_count, fsdp_count),
        [((fsdp_count * rows, width), bf16), ((fsdp_count,) + small.shape, bf16)],
        [dma(fsdp_count), dma(fsdp_count)] + collect_sems(ctx_count, fsdp_count),
        5,
        shard, small, far_outs=(0,),
    )


class SquareSum:
    def __init__(self, ctx_count, grad_ref, a_ref, b_out, b_in, sems):
        self.grad_ref, self.a_ref, self.b_out = grad_ref, a_ref, b_out
        self.a_send, self.a_recv, b_send, b_recv = sems
        self.parts = Parts(ctx_count, b_out, b_in, b_send, b_recv)
        self.order = (*range(ctx_count - 1, 0, -1), 0)
        self.section, self.ctx, fsdp = place_of()
        self.sister = (1 - self.section, self.ctx, fsdp)
        self.piece = grad_ref.shape[1] // (2 * ctx_count)

    def columns(self, k, core):
        start = (flip(self.ctx, k) * 2 + core) * self.piece
        return pl.ds(pl.multiple_of(start, self.piece), self.piece)

    def chip(self, k):
        source = self.grad_ref.at[:, self.columns(k, 1 - self.section)]
        return send(source, self.a_ref.at[k], self.a_send.at[k], self.a_recv.at[k], self.sister)

    def begin(self):
        for k in self.order:
            self.chip(k).start()

    def middle(self):
        for k in self.order:
            self.chip(k).wait_recv()
            own = self.grad_ref[:, self.columns(k, self.section)].astype(f32)
            total = own + self.a_ref[k].astype(f32)
            if k:
                self.parts.put(k, total)
            else:
                self.b_out[0] = total.astype(bf16)

    def merge(self):
        self.parts.merge()

    def end(self):
        return self.parts.total(self.b_out[0].astype(f32)).astype(bf16)

    def sent(self):
        for k in self.order:
            self.chip(k).wait_send()
        self.parts.sent()


def square_scratch(ctx_count, grad):
    width, both = grad.shape
    piece = VMEM((ctx_count, width, both // (2 * ctx_count)), bf16)
    sems = [dma(ctx_count), dma(ctx_count), dma(ctx_count, 2), dma(ctx_count, 2)]
    return [piece, piece, piece] + sems


def every_owner(ctx_count, layer, start_or_wait, sources, targets, send_sem, recv_sem):
    section, ctx, fsdp = place_of()
    for k in range(ctx_count):
        device = (layer, flip(ctx, k), fsdp)

        def go():
            for i, (source, target) in enumerate(zip(sources, targets)):
                copy = send(
                    source,
                    target.at[ctx, section],
                    send_sem.at[i, k],
                    recv_sem.at[i, section, k],
                    device,
                )
                copy.start() if start_or_wait == "start" else copy.wait_send()

        pl.when(section != layer)(go) if k == 0 else go()


def from_owners(ctx_count, layer, targets, send_sem, recv_sem):
    section, ctx, fsdp = place_of()
    for core in range(2):
        for k in range(ctx_count):
            if core == layer and k == 0:
                continue

            def go():
                for i, target in enumerate(targets):
                    came = target.at[flip(ctx, k), core]
                    send(
                        came, came, send_sem.at[i, k], recv_sem.at[i, core, k], (1 - section, ctx, fsdp)
                    ).wait_recv()

            pl.when(section == layer)(go)


class Owners:
    def __init__(self, ctx_count, layer, sources, targets, send_sem, recv_sem, onward_sem):
        self.layer, self.targets = layer, targets
        self.send_sem, self.recv_sem, self.onward_sem = send_sem, recv_sem, onward_sem
        self.section, self.ctx, self.fsdp = place_of()
        self.count, self.square = ctx_count, ctx_count == 4
        rows = sources[0].shape[0]
        cut = rows * 5 // 7 // 16 * 16
        self.square = self.square and 0 < cut < rows and rows % 16 == 0
        if self.square:
            low, high = pl.ds(0, cut), pl.ds(cut, rows - cut)
            self.pieces = [(sources[0].at[low], 0, low), (sources[0].at[high], 0, high)]
            self.pieces.append((sources[1], 1, None))
        else:
            self.pieces = [(source, i, None) for i, source in enumerate(sources)]
        self.keeper = self.section == layer

    def spot(self, i, k, core):
        _, which, rows = self.pieces[i]
        spot = self.targets[which].at[flip(self.ctx, k), core]
        return spot if rows is None else spot.at[rows]

    def peer(self, k):
        return (self.layer, flip(self.ctx, k), self.fsdp)

    def own(self, i, k):
        return send(
            self.pieces[i][0],
            self.spot(i, 0, self.section),
            self.send_sem.at[i, k],
            self.recv_sem.at[i, self.section, k],
            self.peer(k),
        )

    def onward(self, i, core):
        came = 2 if i == 0 else 1
        spot = self.spot(i, came, core)
        return send(
            spot, spot, self.onward_sem.at[i, core], self.recv_sem.at[i, core, 3], self.peer(3 - came)
        )

    def outgoing(self):
        if self.square:
            return [(1, 1), (2, 1), (0, 2), (0, 1), (1, 2), (2, 2)]
        return [(i, k) for k in range(1, self.count) for i in range(len(self.pieces))]

    def begin(self):
        for i, k in self.outgoing():
            self.own(i, k).start()

        @pl.when(jnp.logical_not(self.keeper))
        def _():
            for i in range(len(self.pieces)):
                self.own(i, 0).start()

    def arrival(self, i, core, k):
        spot = self.spot(i, k, core)
        recv = self.recv_sem.at[i, core, k]
        send(spot, spot, self.send_sem.at[i, k], recv, (1 - self.section, self.ctx, self.fsdp)).wait_recv()

    def relay(self):
        if self.square:

            @pl.when(self.keeper)
            def _():
                for i, k in ((1, 1), (2, 1), (0, 2)):
                    for core in range(2):
                        self.arrival(i, core, k)
                        self.onward(i, core).start()

    def end(self):
        early = ((1, 1), (2, 1), (0, 2)) if self.square else ()

        @pl.when(self.keeper)
        def _():
            for k in range(self.count):
                for core in range(2):
                    for i in range(len(self.pieces)):
                        if (i, k) not in early and (k or core != self.layer):
                            self.arrival(i, core, k)
            if self.square:
                for i in range(3):
                    for core in range(2):
                        self.onward(i, core).wait_send()

        @pl.when(jnp.logical_not(self.keeper))
        def _():
            for i in range(len(self.pieces)):
                self.own(i, 0).wait_send()

        for i, k in self.outgoing():
            self.own(i, k).wait_send()


def owner_sems(ctx_count):
    return [dma(3, ctx_count), dma(3, 2, ctx_count), dma(3, 2)]


def chip_square(ctx_count):
    section, ctx, fsdp = place_of()
    return [
        (section if same else 1 - section, flip(ctx, k), fsdp)
        for k in range(ctx_count)
        for same in (True, False)
        if k or not same
    ]


def turn_tile(values):
    lane = lax.broadcasted_iota(jnp.int32, values.shape, 1)
    width = values.shape[1]
    half = HEAD_DIM // 2
    ahead = pltpu.roll(values, width - half, 1)
    behind = pltpu.roll(values, half, 1)
    return jnp.where(lane % HEAD_DIM < half, ahead, behind)


def head_in_group(tile, head, group):
    lane = lax.broadcasted_iota(jnp.int32, tile.shape, 1)
    values = tile.astype(f32)
    moved = values if head % 2 == group else pltpu.roll(values, HEAD_DIM, 1)
    return jnp.where(lane // HEAD_DIM == group, moved, 0.0).astype(bf16)


def attend_kernel(count, fsdp_count, fetch, *refs):
    x_ref, g1_ref, bias_ref, g2_ref, w_ref, cos_ref, sin_ref, kpos_ref, qpos_ref = refs[:9]
    refs = refs[9:]
    shard_ref, refs = (refs[0], refs[1:]) if fetch else (None, refs)
    normed_ref, q_ref, kv_ref, lse_ref, ctx_ref, mid_ref, low2_ref = refs[:7]
    refs = refs[7:]
    next_ref, refs = (refs[0], refs[1:]) if fetch else (None, refs)
    mask_ref, s_ref, p_ref, vt_ref, ctxf_ref, send_sem, recv_sem, *sems = refs
    rows, width = x_ref.shape
    pair = kv_ref.shape[2] // 2
    wide = width + 2 * pair
    heads = width // HEAD_DIM
    group_size = heads // (pair // HEAD_DIM)
    if fetch:
        steps = Collect(count, fsdp_count, shard_ref, next_ref, sems)
        greet_all(steps.friends)
        steps.begin()
    else:
        greet(count)
    x = x_ref[...].astype(f32)
    normed = (x * row_scale(x) * g1_ref[...]).astype(bf16)
    normed_ref[...] = normed
    cos, sin = cos_ref[...], sin_ref[...]
    kv = matmul(normed, w_ref[:, width:wide]) + bias_ref[:, width:wide]
    keys = kv[:, :pair]
    kv_ref[0, :, :pair] = (keys * cos + turn_tile(keys) * sin).astype(bf16)
    kv_ref[0, :, pair:] = kv[:, pair:].astype(bf16)
    for k in range(1, count):
        remote(kv_ref.at[0], kv_ref.at[k], send_sem, recv_sem, k).start()
    merged = matmul(normed, w_ref[:, :width]) + bias_ref[:, :width]
    for start, size in tiles(width, 2 * HEAD_DIM):
        part = merged[:, start : start + size]
        turned_part = (part * cos + turn_tile(part) * sin) * HEAD_DIM ** (-0.5)
        q_ref[:, start : start + size] = turned_part.astype(bf16)
    for k in range(count):
        allowed = kpos_ref[k * rows : (k + 1) * rows, :] <= qpos_ref[...]
        mask_ref[k] = jnp.where(allowed, 0.0, masked_value)
    if fetch:
        steps.relay()
    for k in range(count):
        if k:
            remote(kv_ref.at[0], kv_ref.at[k], send_sem, recv_sem, k).wait_recv()
        vt_ref[:, k * rows : (k + 1) * rows] = kv_ref[k, :, pair:].astype(f32).T.astype(bf16)

    for head in range(heads):
        group = head // group_size
        start = head // 2 * (2 * HEAD_DIM)
        query = head_in_group(q_ref[:, start : start + 2 * HEAD_DIM], head, group)
        top = None
        for k in range(count):
            scores = matmul_nt(kv_ref[k, :, :pair], query) + mask_ref[k]
            s_ref[k] = scores
            here = jnp.max(scores, axis=0, keepdims=True)
            top = here if top is None else jnp.maximum(top, here)
        total = None
        for k in range(count):
            weight = jnp.exp(s_ref[k] - top)
            here = jnp.sum(weight, axis=0, keepdims=True)
            total = here if total is None else total + here
            p_ref[k * rows : (k + 1) * rows, :] = weight.astype(bf16)
        value_rows = vt_ref[group * HEAD_DIM : (group + 1) * HEAD_DIM, :]
        context = matmul(value_rows, p_ref[...]) * (1.0 / total)
        ctxf_ref[head * HEAD_DIM : (head + 1) * HEAD_DIM, :] = context
        lse_ref[head : head + 1, :] = top + jnp.log(total)
        if fetch and head == heads // 2:
            steps.hand()
    context = ctxf_ref[...]
    ctx_ref[...] = context.astype(bf16)
    middle = x + matmul(context.T.astype(bf16), w_ref[:, wide:])
    mid_ref[...] = middle
    low2_ref[...] = (middle * row_scale(middle) * g2_ref[...]).astype(bf16)
    for k in range(1, count):
        remote(kv_ref.at[0], kv_ref.at[k], send_sem, recv_sem, k).wait_send()
    if fetch:
        steps.finish()


def attend(layer, hidden, place, shard=None):
    first_gain, bias, second_gain, weights = layer[:4]
    cosine, sine, key_positions, query_positions = place
    rows, width = hidden.shape
    count = lax.axis_size(CTX)
    wide = bias.shape[1]
    pair = (wide - width) // 2
    keys = count * rows
    heads = width // HEAD_DIM
    fetch = shard is not None
    fsdp_count = lax.axis_size(FSDP)
    args = (
        hidden, first_gain, bias, second_gain, weights, cosine, sine, key_positions, query_positions,
    )
    return call(
        functools.partial(attend_kernel, count, fsdp_count, fetch),
        [
            ((rows, width), bf16),
            ((rows, width), bf16),
            ((count, rows, 2 * pair), bf16),
            ((-(-heads // 8) * 8, rows), f32),
            ((width, rows), bf16),
            ((rows, width), f32),
            ((rows, width), bf16),
        ]
        + [(weights.shape, bf16)] * fetch,
        [
            VMEM((count, rows, rows), f32),
            VMEM((count, rows, rows), f32),
            VMEM((keys, rows), bf16),
            VMEM((pair, keys), bf16),
            VMEM((width, rows), f32),
            dma(count),
            dma(count),
        ]
        + (collect_sems(count, fsdp_count) if fetch else []),
        10 if fetch else 1,
        *args, *([shard] if fetch else []),
        far_outs=(7,) if fetch else (),
    )


def attend_back_kernel(count, carried, *refs):
    (
        dmid_ref, x_ref, g1_ref, w_ref, cos_ref, sin_ref, kpos_ref, qpos_ref,
        normed_ref, q_ref, kv_ref, lse_ref, ctx_ref,
    ) = refs[:13]
    refs = refs[13:]
    load_ref, refs = (refs[0], refs[1:]) if carried else (None, refs)
    dh_ref, gain_ref, bias_ref, grad_ref = refs[:4]
    refs = refs[4:]
    summed_ref, refs = (refs[0], refs[1:]) if carried else (None, refs)
    (
        mask_ref, p_ref, dp_ref, ds_ref, kt_ref, dctx_ref, dq_ref, dkv_ref, out_ref, in_ref,
        merged_ref, low_ref, send_sem, recv_sem, *scratch,
    ) = refs
    rows, width = x_ref.shape
    pair = kv_ref.shape[2] // 2
    wide = width + 2 * pair
    heads = width // HEAD_DIM
    group_size = heads // (pair // HEAD_DIM)
    if carried:
        steps = SquareSum(count, load_ref, *scratch[:3], scratch[3:])
        greet_all([peer_of(k) for k in range(1, count)] + [steps.sister])
        steps.begin()
    else:
        greet(count)
    low = dmid_ref[...].astype(bf16)
    low_ref[...] = low
    dctx = matmul_nt(low, w_ref[:, wide:]).astype(bf16)
    dctx_ref[...] = dctx
    for k in range(count):
        allowed = kpos_ref[k * rows : (k + 1) * rows, :] <= qpos_ref[...]
        mask_ref[k] = jnp.where(allowed, 0.0, masked_value)
        kt_ref[:, k * rows : (k + 1) * rows] = kv_ref[k, :, :pair].astype(f32).T.astype(bf16)
    dkv_ref[...] = jnp.zeros_like(dkv_ref)

    for head in range(heads):
        group = head // group_size
        start = head // 2 * (2 * HEAD_DIM)
        query = head_in_group(q_ref[:, start : start + 2 * HEAD_DIM], head, group)
        upstream = head_in_group(dctx_ref[:, start : start + 2 * HEAD_DIM], head, group)
        lse = lse_ref[head : head + 1, :]
        delta = None
        for k in range(count):
            scores = matmul_nt(kv_ref[k, :, :pair], query) + mask_ref[k]
            weight = jnp.exp(scores - lse)
            weight_grad = matmul_nt(kv_ref[k, :, pair:], upstream)
            p_ref[k] = weight
            dp_ref[k] = weight_grad
            dkv_ref[k, :, pair:] += matmul(weight.astype(bf16), upstream)
            here = jnp.sum(weight * weight_grad, axis=0, keepdims=True)
            delta = here if delta is None else delta + here
        for k in range(count):
            score_grad = (p_ref[k] * (dp_ref[k] - delta)).astype(bf16)
            ds_ref[k * rows : (k + 1) * rows, :] = score_grad
            dkv_ref[k, :, :pair] += matmul(score_grad, query)
        key_rows = kt_ref[group * HEAD_DIM : (group + 1) * HEAD_DIM, :]
        dq_ref[head * HEAD_DIM : (head + 1) * HEAD_DIM, :] = (
            matmul(key_rows, ds_ref[...]) * HEAD_DIM ** (-0.5)
        )
        if carried and head == 1:
            steps.middle()
        if carried and head == heads // 2:
            steps.merge()
    for k in range(1, count):
        out_ref[k] = dkv_ref[k].astype(bf16)
        remote(out_ref.at[k], in_ref.at[k], send_sem, recv_sem, k).start()
    cos, sin = cos_ref[...], sin_ref[...]
    dq = dq_ref[...].T

    def unturn(part):
        return (part * cos - turn_tile(part) * sin).astype(bf16)

    for start, size in tiles(width, 2 * HEAD_DIM):
        merged_ref[:, start : start + size] = unturn(dq[:, start : start + size])
    grad_ref[:, wide:] = matmul(ctx_ref[...], low_ref[...]).astype(bf16)
    normed = normed_ref[...]

    def project_grad(first, last):
        for start, size in tiles(last - first, 512):
            cut = slice(first + start, first + start + size)
            grad_ref[:, cut] = matmul_tn(normed, merged_ref[:, cut]).astype(bf16)

    project_grad(0, width)
    normed_grad = matmul_nt(merged_ref[:, :width], w_ref[:, :width])
    total = dkv_ref[0]
    for k in range(1, count):
        remote(out_ref.at[k], in_ref.at[k], send_sem, recv_sem, k).wait_recv()
        total = total + in_ref[k].astype(f32)
    merged_ref[:, width : width + pair] = unturn(total[:, :pair])
    merged_ref[:, width + pair :] = total[:, pair:].astype(bf16)
    project_grad(width, wide)
    normed_grad = normed_grad + matmul_nt(merged_ref[:, width:], w_ref[:, width:wide])
    bias_ref[...] = jnp.sum(merged_ref[...].astype(f32), axis=0, keepdims=True)
    x = x_ref[...].astype(f32)
    scale = row_scale(x)
    gain_ref[...] = jnp.sum(normed_grad * x * scale, axis=0, keepdims=True)
    scaled = normed_grad * g1_ref[...]
    mean = jnp.mean(scaled * x, axis=-1, keepdims=True)
    dh_ref[...] = dmid_ref[...] + scale * scaled - x * (scale * scale * scale * mean)
    for k in range(1, count):
        remote(out_ref.at[k], in_ref.at[k], send_sem, recv_sem, k).wait_send()
    if carried:
        summed_ref[...] = steps.end()
        steps.sent()


def attend_back(layer, kept, middle_grad, place, load=None):
    first_gain, bias, second_gain, weights = layer[:4]
    cosine, sine, key_positions, query_positions = place
    hidden, normed, queries, every_kv, lse, context = kept
    rows, width = hidden.shape
    count = lax.axis_size(CTX)
    wide = bias.shape[1]
    pair = (wide - width) // 2
    keys = count * rows
    carried = load is not None
    args = (
        middle_grad, hidden, first_gain, weights, cosine, sine, key_positions, query_positions,
        normed, queries, every_kv, lse, context,
    )
    return call(
        functools.partial(attend_back_kernel, count, carried),
        [
            ((rows, width), f32),
            ((1, width), f32),
            ((1, wide), f32),
            ((width, wide + width), bf16),
        ]
        + [((width, (wide + width) // (2 * count)), bf16)] * carried,
        [
            VMEM((count, rows, rows), f32),
            VMEM((count, rows, rows), f32),
            VMEM((count, rows, rows), f32),
            VMEM((keys, rows), bf16),
            VMEM((pair, keys), bf16),
            VMEM((rows, width), bf16),
            VMEM((width, rows), f32),
            VMEM((count, rows, 2 * pair), f32),
            VMEM((count, rows, 2 * pair), bf16),
            VMEM((count, rows, 2 * pair), bf16),
            VMEM((rows, wide), bf16),
            VMEM((rows, width), bf16),
            dma(count),
            dma(count),
        ]
        + (square_scratch(count, load) if carried else []),
        6 if carried else 2,
        *args, *([load] if carried else []),
    )


def unit_chunks(units):
    main = units // 128 * 128
    chunks = [(start, main + start, start, size) for start, size in tiles(main, 512)]
    if units > main:
        chunks.append((2 * main, main + units, main, units - main))
    return chunks


def pack_units(gate, up):
    main = gate.shape[1] // 128 * 128
    return jnp.concatenate([gate[:, :main], up[:, :main], gate[:, main:], up[:, main:]], axis=1)


def unpack_units(packed):
    units = packed.shape[-1] // 2
    main = units // 128 * 128
    gate = jnp.concatenate([packed[..., :main], packed[..., 2 * main : main + units]], axis=-1)
    up = jnp.concatenate([packed[..., main : 2 * main], packed[..., main + units :]], axis=-1)
    return gate, up


class Rows:
    def __init__(self, count, own_ref, slots_ref, send_sem, recv_sem):
        self.own_ref, self.slots_ref = own_ref, slots_ref
        self.send_sem, self.recv_sem = send_sem, recv_sem
        self.count, self.square = count, count == 4
        self.half = own_ref.shape[0] // 2

    def rows(self, h):
        return pl.ds(h * self.half, self.half)

    def copy(self, source, k, h, peer):
        target = self.slots_ref.at[k, self.rows(h)]
        return send(source, target, self.send_sem.at[k, h], self.recv_sem.at[k, h], peer_of(peer))

    def own(self, k, h):
        return self.copy(self.own_ref.at[self.rows(h)], k, h, k)

    def onward(self, h):
        came = 1 if h else 2
        return self.copy(self.slots_ref.at[came, self.rows(h)], 3, h, 3 - came)

    def order(self):
        if self.square:
            return [(1, 1), (2, 0), (1, 0), (2, 1)]
        return [(k, h) for k in range(1, self.count) for h in range(2)]

    def begin(self):
        for k, h in self.order():
            self.own(k, h).start()

    def relay(self):
        if self.square:
            for k, h in ((1, 1), (2, 0)):
                self.own(k, h).wait_recv()
                self.onward(h).start()

    def take(self, k):
        for h in range(2):
            if not (self.square and (k, h) in ((1, 1), (2, 0))):
                self.copy(self.own_ref.at[self.rows(h)], k, h, k).wait_recv()

    def sent(self):
        for k, h in self.order():
            self.own(k, h).wait_send()
        if self.square:
            for h in range(2):
                self.onward(h).wait_send()


class Parts:
    def __init__(self, count, parts_ref, got_ref, send_sem, recv_sem):
        self.parts_ref, self.got_ref = parts_ref, got_ref
        self.send_sem, self.recv_sem = send_sem, recv_sem
        self.count, self.square = count, count == 4
        self.half = parts_ref.shape[1] // 2

    def rows(self, h):
        return pl.ds(h * self.half, self.half)

    def copy(self, k, h):
        peer = 1 + h if self.square and k == 3 else k
        source, target = self.parts_ref.at[k, self.rows(h)], self.got_ref.at[k, self.rows(h)]
        return send(source, target, self.send_sem.at[k, h], self.recv_sem.at[k, h], peer_of(peer))

    def put(self, k, part):
        self.parts_ref[k] = part.astype(bf16)
        for h in range(2):
            if not (self.square and (k, h) in ((1, 1), (2, 0))):
                self.copy(k, h).start()

    def merge(self):
        if self.square:
            for k, h in ((2, 0), (1, 1)):
                self.copy(3, h).wait_recv()
                rows = slice(h * self.half, (h + 1) * self.half)
                total = self.parts_ref[k, rows].astype(f32) + self.got_ref[3, rows].astype(f32)
                self.parts_ref[k, rows] = total.astype(bf16)
                self.copy(k, h).start()

    def total(self, own):
        for k in range(1, 3 if self.square else self.count):
            for h in range(2):
                self.copy(k, h).wait_recv()
            own = own + self.got_ref[k].astype(f32)
        return own

    def sent(self):
        for k in range(1, self.count):
            for h in range(2):
                self.copy(k, h).wait_send()


class Loads:
    def __init__(self, sources, targets, sem):
        self.copies = [
            pltpu.make_async_copy(source, target, sem.at[i])
            for i, (source, target) in enumerate(zip(sources, targets))
        ]
        for copy in self.copies:
            copy.start()

    def take(self, *which):
        for i in which:
            self.copies[i].wait()


def gate_and_up(block, expand_ref, gate_start, up_start, size):
    if size % 128:
        both = matmul(block, expand_ref[:, gate_start : up_start + size])
        return both[:, :size], both[:, size:]
    gate = matmul(block, expand_ref[:, gate_start : gate_start + size])
    return gate, matmul(block, expand_ref[:, up_start : up_start + size])


def feed_kernel(
    count, low_ref, mid_ref, expand_any, down_any,
    out_ref, blocks_ref, kept_gate_ref, kept_up_ref,
    expand_ref, down_ref, act_ref, part_ref, sent_ref, got_ref,
    send_sem, recv_sem, send_sem2, recv_sem2, load_sem,
):
    units = down_ref.shape[0]
    loads = Loads((expand_any, down_any), (expand_ref, down_ref), load_sem)
    rows = Rows(count, low_ref, blocks_ref, send_sem, recv_sem)
    parts = Parts(count, sent_ref, got_ref, send_sem2, recv_sem2)
    greet(count)
    rows.begin()
    blocks_ref[0] = low_ref[...]
    loads.take(0, 1)
    for k in range(count):
        if k:
            rows.take(k)
        block = blocks_ref[k]
        for gate_start, up_start, start, size in unit_chunks(units):
            gate, up = gate_and_up(block, expand_ref, gate_start, up_start, size)
            kept_gate_ref[k, :, start : start + size] = gate.astype(bf16)
            kept_up_ref[k, :, start : start + size] = up.astype(bf16)
            act_ref[:, start : start + size] = (gate / (1.0 + jnp.exp(-gate)) * up).astype(bf16)
        part = matmul(act_ref[...], down_ref[...])
        if k:
            parts.put(k, part)
        else:
            part_ref[...] = part + mid_ref[...]
            rows.relay()
    parts.merge()
    out_ref[...] = parts.total(part_ref[...]).astype(bf16)
    rows.sent()
    parts.sent()


def feed(layer, second_normed, middle):
    expand_w, down_w = layer[4:]
    count = lax.axis_size(CTX)
    rows, width = second_normed.shape
    units = down_w.shape[0]
    return call(
        functools.partial(feed_kernel, count),
        [
            ((rows, width), bf16),
            ((count, rows, width), bf16),
            ((count, rows, units), bf16),
            ((count, rows, units), bf16),
        ],
        [
            VMEM(expand_w.shape, bf16),
            VMEM(down_w.shape, bf16),
            VMEM((rows, units), bf16),
            VMEM((rows, width), f32),
            VMEM((count, rows, width), bf16),
            VMEM((count, rows, width), bf16),
        ]
        + [dma(count, 2)] * 4
        + [dma(2)],
        3,
        second_normed, middle, expand_w, down_w, far=(2, 3),
    )


def feed_back_kernel(
    count, grad_ref, mid_ref, g2_ref, blocks_any, kept_gate_any, kept_up_any, expand_any, down_any,
    dmid_ref, gain_ref, dexpand_ref, ddown_ref,
    blocks_ref, kept_gate_ref, kept_up_ref, expand_ref, down_ref,
    grads_ref, act_ref, dwide_ref, part_ref, sent_ref, got_ref,
    send_sem, recv_sem, send_sem2, recv_sem2, load_sem,
):
    rows, width = grad_ref.shape
    units = down_ref.shape[0]
    loads = Loads(
        (down_any, kept_gate_any, kept_up_any, expand_any, blocks_any),
        (down_ref, kept_gate_ref, kept_up_ref, expand_ref, blocks_ref),
        load_sem,
    )
    gather = Rows(count, grad_ref, grads_ref, send_sem, recv_sem)
    parts = Parts(count, sent_ref, got_ref, send_sem2, recv_sem2)
    greet(count)
    gather.begin()
    grads_ref[0] = grad_ref[...]
    loads.take(0, 1, 2)
    for k in range(count):
        if k:
            gather.take(k)
        block = grads_ref[k]
        for gate_start, up_start, start, size in unit_chunks(units):
            cut = slice(start, start + size)
            spread = matmul_nt(block, down_ref[cut, :])
            gate = kept_gate_ref[k, :, cut].astype(f32)
            up = kept_up_ref[k, :, cut].astype(f32)
            sig = 1.0 / (1.0 + jnp.exp(-gate))
            silu = gate * sig
            act_ref[k, :, cut] = (silu * up).astype(bf16)
            dgate = (spread * up * sig * (1.0 + gate * (1.0 - sig))).astype(bf16)
            dup = (spread * silu).astype(bf16)
            if size % 128:
                dwide_ref[k, :, gate_start : up_start + size] = jnp.concatenate([dgate, dup], axis=1)
            else:
                dwide_ref[k, :, gate_start : gate_start + size] = dgate
                dwide_ref[k, :, up_start : up_start + size] = dup
        if not k:
            loads.take(3)
        part = matmul_nt(dwide_ref[k], expand_ref[...])
        if k:
            parts.put(k, part)
        else:
            part_ref[...] = part
            gather.relay()
    loads.take(4)
    tall = count * rows
    grads = grads_ref[...].reshape(tall, width)
    main = units // 128 * 128
    for start, size in tiles(main, 384) + [(main, units - main)] * (units > main):
        act = act_ref[:, :, start : start + size].reshape(tall, size)
        ddown_ref[start : start + size, :] = matmul_tn(act, grads).astype(bf16)
    parts.merge()
    blocks = blocks_ref[...].reshape(tall, width)
    for start, size in tiles(2 * units, 512):
        dwide = dwide_ref[:, :, start : start + size].reshape(tall, size)
        dexpand_ref[:, start : start + size] = matmul_tn(blocks, dwide).astype(bf16)
    total = parts.total(part_ref[...])
    middle = mid_ref[...]
    scale = row_scale(middle)
    gain_ref[...] = jnp.sum(total * middle * scale, axis=0, keepdims=True)
    scaled = total * g2_ref[...]
    mean = jnp.mean(scaled * middle, axis=-1, keepdims=True)
    dmid_ref[...] = (
        grad_ref[...].astype(f32) + scale * scaled - middle * (scale * scale * scale * mean)
    )
    gather.sent()
    parts.sent()


def feed_back(layer, middle, blocks, kept_gate, kept_up, grad_out):
    second_gain = layer[2]
    expand_w, down_w = layer[4:]
    count = lax.axis_size(CTX)
    rows, width = grad_out.shape
    units = down_w.shape[0]
    brought = (blocks, kept_gate, kept_up, expand_w, down_w)
    return call(
        functools.partial(feed_back_kernel, count),
        [
            ((rows, width), f32),
            ((1, width), f32),
            ((width, 2 * units), bf16),
            ((units, width), bf16),
        ],
        [VMEM(array.shape, bf16) for array in brought]
        + [
            VMEM((count, rows, width), bf16),
            VMEM((count, rows, units), bf16),
            VMEM((count, rows, 2 * units), bf16),
            VMEM((rows, width), f32),
            VMEM((count, rows, width), bf16),
            VMEM((count, rows, width), bf16),
        ]
        + [dma(count, 2)] * 4
        + [dma(5)],
        4,
        grad_out, middle, second_gain, *brought, far=(3, 4, 5, 6, 7),
    )


def attn_sum_kernel(
    ctx_count, fsdp_count, wide, low_ref, high_ref, small_ref, expand_ref, down_ref,
    projections_ref, output_ref, total_ref, expand_all_ref, down_all_ref,
    c_out, c_in, d_out, whole_ref, s_out, s_in,
    c_send, c_recv, d_send, d_recv, s_send, s_recv, e_send, e_recv, e_onward, e_own, *square_refs,
):
    section, ctx, fsdp = place_of()
    sister = (1 - section, ctx, fsdp)
    width, piece = high_ref.shape
    rows = width // fsdp_count
    places = range(1, ctx_count)
    shards = range(1, fsdp_count)
    steps = SquareSum(ctx_count, low_ref, *square_refs[:3], square_refs[3:])
    sources, targets = (expand_ref, down_ref), (expand_all_ref, down_all_ref)
    kept = [
        pltpu.make_async_copy(source, target.at[ctx, section], e_own.at[i])
        for i, (source, target) in enumerate(zip(sources, targets))
    ]

    owners = Owners(ctx_count, 1, sources, targets, e_send, e_recv, e_onward)

    def ahead(d):
        return (section, ctx, lax.rem(fsdp + d, fsdp_count))

    def c_copy(layer, d):
        target = lax.rem(fsdp + d, fsdp_count)
        source = c_out.at[layer, pl.ds(pl.multiple_of(target * rows, rows), rows)]
        return send(source, c_in.at[layer, d], c_send.at[layer, d], c_recv.at[layer, d], ahead(d))

    def s_copy(step, source, device):
        return send(s_out.at[source], s_in.at[step], s_send.at[step], s_recv.at[step], device)

    def line_sum(layer):
        total = c_out[layer, pl.ds(pl.multiple_of(fsdp * rows, rows), rows)].astype(f32)
        for d in shards:
            c_copy(layer, d).wait_recv()
            total = total + c_in[layer, d].astype(f32)
        d_out[layer] = total.astype(bf16)
        every_owner(
            ctx_count, layer, "start", [d_out.at[layer]], [whole_ref], d_send.at[layer], d_recv
        )

        @pl.when(section == layer)
        def _():
            whole_ref[ctx, section] = d_out[layer]

    hops = [(0, 0, sister)]
    hops += [(k, 1, peer_of(k)) for k in places]
    hops += [(ctx_count - 1 + d, 2, ahead(d)) for d in shards]

    greet_all(chip_square(ctx_count) + [ahead(d) for d in shards])
    steps.begin()
    s_out[0] = small_ref[...]
    s_copy(*hops[0]).start()
    c_out[1] = high_ref[...]
    for d in shards:
        c_copy(1, d).start()

    @pl.when(section == 1)
    def _():
        for copy in kept:
            copy.start()

    steps.middle()
    s_copy(*hops[0]).wait_recv()
    s_out[1] = s_out[0] + s_in[0]
    for k in places:
        s_copy(*hops[k]).start()
    owners.begin()
    line_sum(1)
    steps.merge()
    c_out[0] = steps.end()
    for d in shards:
        c_copy(0, d).start()
    owners.relay()
    part = s_out[1]
    for k in places:
        s_copy(*hops[k]).wait_recv()
        part = part + s_in[k]
    s_out[2] = part
    for d in shards:
        s_copy(*hops[ctx_count - 1 + d]).start()
    line_sum(0)
    part = s_out[2]
    for d in shards:
        s_copy(*hops[ctx_count - 1 + d]).wait_recv()
        part = part + s_in[ctx_count - 1 + d]
    total_ref[...] = part
    for layer in (1, 0):
        from_owners(ctx_count, layer, [whole_ref], d_send.at[layer], d_recv)
    for where in range(ctx_count):
        for core in range(2):
            start = (where * 2 + core) * piece
            block = whole_ref[where, core].astype(f32)
            size = max(min(wide - start, piece), 0)
            if size:
                projections_ref[:, start : start + size] = block[:, :size]
            if size < piece:
                first = start + size - wide
                output_ref[:, first : first + piece - size] = block[:, size:]
    owners.end()
    steps.sent()
    for layer in (1, 0):
        for d in shards:
            c_copy(layer, d).wait_send()
        every_owner(
            ctx_count, layer, "wait", [d_out.at[layer]], [whole_ref], d_send.at[layer], d_recv
        )
    for hop in hops:
        s_copy(*hop).wait_send()

    @pl.when(section == 1)
    def _():
        for copy in kept:
            copy.wait()


def attn_sum(low, high, small, expand_part, down_part, wide):
    ctx_count, fsdp_count = lax.axis_size(CTX), lax.axis_size(FSDP)
    width, both = low.shape
    rows = width // fsdp_count
    piece = both // (2 * ctx_count)
    hops = ctx_count + fsdp_count - 1
    return call(
        functools.partial(attn_sum_kernel, ctx_count, fsdp_count, wide),
        [
            ((rows, wide), f32),
            ((rows, both - wide), f32),
            (small.shape, f32),
            ((ctx_count, 2) + expand_part.shape, bf16),
            ((ctx_count, 2) + down_part.shape, bf16),
        ],
        [
            VMEM((2, width, piece), bf16),
            VMEM((2, fsdp_count, rows, piece), bf16),
            VMEM((2, rows, piece), bf16),
            VMEM((ctx_count, 2, rows, piece), bf16),
            VMEM((3,) + small.shape, f32),
            VMEM((hops,) + small.shape, f32),
            dma(2, fsdp_count), dma(2, fsdp_count),
            dma(2, 1, ctx_count), dma(1, 2, ctx_count),
            dma(hops), dma(hops),
        ]
        + owner_sems(ctx_count)
        + [dma(2)]
        + square_scratch(ctx_count, low),
        7,
        low, high, small, expand_part, down_part, far_outs=(3, 4),
    )


def settle_kernel(
    ctx_count, expand_ref, down_ref, expand_all_ref, down_all_ref,
    expand_out, down_out, send_sem, recv_sem, onward_sem, own_sem,
):
    section, ctx, _ = place_of()
    greet_all(chip_square(ctx_count))
    sources, targets = (expand_ref, down_ref), (expand_out, down_out)
    owners = Owners(ctx_count, 0, sources, targets, send_sem, recv_sem, onward_sem)
    owners.begin()
    kept = [
        pltpu.make_async_copy(source, target.at[ctx, section], own_sem.at[i])
        for i, (source, target) in enumerate(zip(sources, targets))
    ]
    loads = [
        pltpu.make_async_copy(source, target, own_sem.at[2 + i])
        for i, (source, target) in enumerate(zip((expand_all_ref, down_all_ref), targets))
    ]

    @pl.when(section == 0)
    def _():
        for copy in kept:
            copy.start()
        for copy in kept:
            copy.wait()

    @pl.when(section == 1)
    def _():
        for copy in loads:
            copy.start()
        for copy in loads:
            copy.wait()

    owners.relay()
    owners.end()


def spread_kernel(chunk, shards, side_width, block_ref, out_ref):
    count = block_ref.shape[0]
    for where in range(count):
        sides = unpack_units(block_ref[where].astype(f32))
        for side, values in enumerate(sides):
            for shard in range(shards):
                start = side * side_width + (shard * count + where) * chunk
                out_ref[:, start : start + chunk] = values[:, shard * chunk : (shard + 1) * chunk]


def finish(expand_part, down_part, expand_all, down_all, ff_width):
    ctx_count, fsdp_count = lax.axis_size(CTX), lax.axis_size(FSDP)
    half, packed = expand_part.shape
    half_units, width = down_part.shape
    expand_all, down_all = call(
        functools.partial(settle_kernel, ctx_count),
        [(expand_all.shape, bf16), (down_all.shape, bf16)],
        owner_sems(ctx_count) + [dma(4)],
        8,
        expand_part, down_part, expand_all, down_all,
        far=(2, 3),
    )
    rows = 2 * half
    step = 32 if rows % 32 == 0 else 16
    grad_expand = pl.pallas_call(
        functools.partial(spread_kernel, packed // 2 // fsdp_count, fsdp_count, ff_width),
        grid=(rows // step,),
        out_shape=jax.ShapeDtypeStruct((rows, 2 * ff_width), f32),
        in_specs=[pl.BlockSpec((ctx_count, step, packed), lambda i: (0, i, 0))],
        out_specs=pl.BlockSpec((step, 2 * ff_width), lambda i: (i, 0)),
        compiler_params=pltpu.CompilerParams(vmem_limit_bytes=LIMIT),
    )(expand_all.reshape(ctx_count, rows, packed))
    grad_down = down_all.astype(f32).reshape(2 * ctx_count * half_units, width)
    return grad_expand, grad_down


def per_device(
    inputs,
    attend_gain,
    projections,
    biases,
    output_weight,
    mixer_gain,
    expand_weight,
    down_weight,
    positions,
    cotangent,
):
    row_count, model_width = inputs.shape[2:]
    section = lax.axis_index(SECTION)
    is_first = section == 0
    ctx = lax.axis_index(CTX)
    fsdp = lax.axis_index(FSDP)
    ctx_count = lax.axis_size(CTX)
    fsdp_count = lax.axis_size(FSDP)
    shard_rows = projections.shape[1]
    wide = projections.shape[2]
    ff_width = expand_weight.shape[2] // 2
    shard_units = down_weight.shape[1]
    units = shard_units // ctx_count
    both = (FSDP, SECTION)

    def mine(array):
        return lax.dynamic_index_in_dim(array, section, 0, keepdims=False)

    source = mine(inputs)[0]
    upstream = mine(cotangent)[0]
    key_positions = mine(positions)[0]
    query_positions = lax.dynamic_slice_in_dim(key_positions, ctx * row_count, row_count)
    cosine, sine = tables(query_positions)
    by_distance = jnp.concatenate(
        [
            lax.dynamic_slice_in_dim(key_positions, (ctx ^ k) * row_count, row_count)
            for k in range(ctx_count)
        ]
    )
    place = (cosine, sine, by_distance[:, None], query_positions[None])

    bias_part = biases.shape[1]
    small_width = -(-bias_part // 128) * 128

    def padded(row):
        return jnp.pad(row, ((0, 0), (0, small_width - row.shape[1])))

    small_shard = jnp.concatenate(
        [padded(attend_gain), padded(biases), padded(mixer_gain), jnp.zeros((13, small_width), bf16)]
    )
    attn_shard = jnp.concatenate([projections[0], output_weight[0]], axis=1)

    def in_order(array):
        other = swap_sections(array)
        return jnp.where(is_first, array, other), jnp.where(is_first, other, array)

    def unit_columns(side):
        pieces = []
        for shard in range(fsdp_count):
            start = side * ff_width + shard * shard_units
            pieces.append(
                pick(
                    ctx,
                    [
                        expand_weight[0, :, start + k * units : start + (k + 1) * units]
                        for k in range(ctx_count)
                    ],
                )
            )
        return jnp.concatenate(pieces, axis=1)

    expand_shard = pack_units(unit_columns(0), unit_columns(1))
    down_shard = lax.dynamic_slice_in_dim(down_weight[0], ctx * units, units)

    def halves(array):
        size = array.shape[0] // 2
        low, high = array[:size], array[size:]
        own = jnp.where(is_first, low, high)
        other = swap_sections(jnp.where(is_first, high, low))
        return jnp.where(is_first, own, other), jnp.where(is_first, other, own)

    expand_pair = halves(expand_shard)
    down_pair = halves(down_shard)
    first_shard, second_shard = in_order(attn_shard)
    small_pair = jnp.concatenate(in_order(small_shard))

    def gather(piece):
        return lax.all_gather(piece, both, axis=0, tiled=True)

    expands, downs = [None, None], [None, None]
    expands[0], downs[0] = gather(expand_pair[0]), gather(down_pair[0])
    first_shard, small_pair = lax.optimization_barrier(
        (first_shard, small_pair, expand_pair[0], down_pair[0])
    )[:2]
    weights, smalls = collect(first_shard, small_pair)
    smalls = smalls.astype(f32)
    weights = [weights, None]
    expands[1], downs[1] = gather(expand_pair[1]), gather(down_pair[1])

    def layer_of(layer):
        first = 16 * layer
        return (
            smalls[:, first, :shard_rows].reshape(1, -1),
            smalls[:, first + 1, :bias_part].reshape(1, -1),
            smalls[:, first + 2, :shard_rows].reshape(1, -1),
            weights[layer],
            expands[layer],
            downs[layer],
        )

    layers = []
    hidden = source
    stored = []
    sent = []
    for layer in range(2):
        layers.append(layer_of(layer))
        normed, queries, every_kv, lse, context, middle, second_normed, *fetched = attend(
            layers[layer], hidden, place, None if layer else second_shard
        )
        if fetched:
            weights[1] = fetched[0]
        kept = (hidden, normed, queries, every_kv, lse, context)
        hidden, blocks, kept_gate, kept_up = feed(layers[layer], second_normed, middle)
        sent.append(hidden)
        stored.append((middle, kept, blocks, kept_gate, kept_up))

    def scatter(array):
        return lax.psum_scatter(array, both, scatter_dimension=0, tiled=True)

    grad = upstream
    hidden_grads = [None, None]
    small_grads = [None, None]
    attn_grads = [None, None]
    scattered = ()
    summed = ()
    for layer in (1, 0):
        middle, kept, blocks, kept_gate, kept_up = stored[layer]
        middle_grad, second_grad, expand_grad, down_grad = feed_back(
            layers[layer], middle, blocks, kept_gate, kept_up, grad
        )
        hidden_grad, first_grad, offset_grad, attn_grads[layer], *summed = attend_back(
            layers[layer], kept, middle_grad, place, attn_grads[1]
        )
        earlier = scattered
        if earlier:
            down_grad, _ = lax.optimization_barrier((down_grad, earlier[1]))
            expand_grad, _ = lax.optimization_barrier((expand_grad, (earlier[0], attn_grads[0])))
        down_part = scatter(down_grad)
        scattered = (scatter(expand_grad), down_part)
        small_grads[layer] = jnp.concatenate([first_grad, offset_grad, second_grad], axis=1)[0]
        hidden_grads[layer] = hidden_grad
        grad = hidden_grad.astype(bf16)

    spare = -small_grads[0].shape[0] % model_width
    small_rows = [jnp.pad(vector, (0, spare)).reshape(-1, model_width) for vector in small_grads]
    small_count = small_rows[0].shape[0]
    rows_left = -2 * small_count % 8
    small_stack = jnp.pad(jnp.concatenate(small_rows), ((0, rows_left), (0, 0)))
    grad_projections, grad_output, small_all, *gathered = attn_sum(
        attn_grads[0], *summed, small_stack, *earlier, wide
    )
    grad_expand, grad_down = finish(*scattered, *gathered, ff_width)
    small_own = jnp.where(
        is_first, small_all[:small_count], small_all[small_count : 2 * small_count]
    ).reshape(-1)
    first_all, offset_all, second_all = (
        small_own[:model_width],
        small_own[model_width : model_width + wide],
        small_own[model_width + wide : 2 * model_width + wide],
    )
    pair_width = (wide - model_width) // 2

    def part(vector):
        size = vector.shape[0] // fsdp_count
        return lax.dynamic_slice_in_dim(vector, fsdp * size, size)[None]

    def from_both(pair):
        own = jnp.where(is_first, pair[0], pair[1])
        other = swap_sections(jnp.where(is_first, pair[1], pair[0]))
        return jnp.stack(
            [jnp.where(is_first, own, other), jnp.where(is_first, other, own)]
        )[None, :, None]

    activations = from_both(sent)
    input_grads = from_both([hidden_grads[0], hidden_grads[1].astype(bf16).astype(f32)])
    return (
        activations,
        input_grads,
        part(first_all),
        grad_projections[None],
        part(offset_all[: model_width + pair_width]),
        part(offset_all[model_width + pair_width :]),
        grad_output[None],
        part(second_all),
        grad_expand[None],
        grad_down[None],
    )


def solution(mesh):
    return jax.shard_map(
        per_device,
        mesh=mesh,
        in_specs=(
            P(None, FSDP, CTX, None),
            P(SECTION, FSDP),
            P(SECTION, FSDP, None),
            P(SECTION, FSDP),
            P(SECTION, FSDP, None),
            P(SECTION, FSDP),
            P(SECTION, FSDP, None),
            P(SECTION, FSDP, None),
            P(None, FSDP, None),
            P(None, FSDP, CTX, None),
        ),
        out_specs=(
            P(SECTION, None, FSDP, CTX, None),
            P(SECTION, None, FSDP, CTX, None),
            P(SECTION, FSDP),
            P(SECTION, FSDP, None),
            P(SECTION, FSDP),
            P(SECTION, FSDP),
            P(SECTION, FSDP, None),
            P(SECTION, FSDP),
            P(SECTION, FSDP, None),
            P(SECTION, FSDP, None),
        ),
        check_vma=False,
    )
```

```python
import functools

import jax
import jax.numpy as jnp
from jax import lax
from jax.experimental import pallas as pl
from jax.experimental.pallas import tpu as pltpu
from jax.sharding import PartitionSpec as P

HEAD_DIM = 64
SECTION, CTX, FSDP = "section", "ctx", "fsdp"

epsilon = 1e-06
theta_base = 1000000.0
masked_value = -1e30

bf16 = jnp.bfloat16
f32 = jnp.float32


def swap_sections(block):
    return lax.ppermute(block, SECTION, [(0, 1), (1, 0)])


def tables(positions_row):
    half_dim = HEAD_DIM // 2
    frequency = theta_base ** (-(jnp.arange(half_dim, dtype=f32) * 2.0) / HEAD_DIM)
    angles = positions_row.astype(f32)[:, None] * frequency[None, :]
    cosine, sine = jnp.cos(angles), jnp.sin(angles)
    return (
        jnp.concatenate([cosine] * 4, axis=-1),
        jnp.concatenate([-sine, sine, -sine, sine], axis=-1),
    )


def pick(index, options):
    chosen = options[0]
    for position in range(1, len(options)):
        chosen = jnp.where(index == position, options[position], chosen)
    return chosen


MESH = pl.DeviceIdType.MESH
VMEM = pltpu.VMEM
LIMIT = 56 * 1024 * 1024


def flip(index, distance):
    place = 1
    while place <= distance:
        if (distance // place) % 2:
            index = index + place - 2 * place * ((index // place) % 2)
        place *= 2
    return index


def place_of():
    return lax.axis_index(SECTION), lax.axis_index(CTX), lax.axis_index(FSDP)


def peer_of(distance):
    section, ctx, fsdp = place_of()
    return (section, flip(ctx, distance), fsdp)


def greet_all(devices):
    barrier = pltpu.get_barrier_semaphore()
    for device in devices:
        pl.semaphore_signal(barrier, inc=1, device_id=device, device_id_type=MESH)
    pl.semaphore_wait(barrier, len(devices))


def greet(count):
    greet_all([peer_of(k) for k in range(1, count)])


def send(source, target, send_sem, recv_sem, device):
    return pltpu.make_async_remote_copy(
        src_ref=source,
        dst_ref=target,
        send_sem=send_sem,
        recv_sem=recv_sem,
        device_id=device,
        device_id_type=MESH,
    )


def remote(source, target, send_sem, recv_sem, k):
    return send(source, target, send_sem.at[k], recv_sem.at[k], peer_of(k))


def matmul(left, right):
    return lax.dot_general(left, right, (((1,), (0,)), ((), ())), preferred_element_type=f32)


def matmul_nt(left, right):
    return lax.dot_general(left, right, (((1,), (1,)), ((), ())), preferred_element_type=f32)


def matmul_tn(left, right):
    return lax.dot_general(left, right, (((0,), (0,)), ((), ())), preferred_element_type=f32)


def tiles(size, step):
    return [(start, min(step, size - start)) for start in range(0, size, step)]


def row_scale(values):
    return lax.rsqrt(jnp.mean(values * values, axis=-1, keepdims=True) + epsilon)


def call(kernel, outs, scratch, cid, *args, far=(), far_outs=()):
    def spec(position, away):
        return pl.BlockSpec(memory_space=pl.ANY if position in away else VMEM)

    return pl.pallas_call(
        kernel,
        out_shape=[jax.ShapeDtypeStruct(shape, kind) for shape, kind in outs],
        in_specs=[spec(position, far) for position in range(len(args))],
        out_specs=[spec(position, far_outs) for position in range(len(outs))],
        scratch_shapes=scratch,
        compiler_params=pltpu.CompilerParams(
            collective_id=cid, has_side_effects=True, vmem_limit_bytes=LIMIT
        ),
    )(*args)


def dma(*shape):
    return pltpu.SemaphoreType.DMA(shape)


class Collect:
    def __init__(self, ctx_count, fsdp_count, shard_ref, w_ref, sems):
        self.shard_ref, self.w_ref = shard_ref, w_ref
        self.z_send, self.z_recv, self.y_send, self.y_recv, self.v_send, self.v_recv, self.own_sem = sems
        self.shards = range(1, fsdp_count)
        self.places = range(1, ctx_count)
        self.fsdp_count = fsdp_count
        self.section, self.ctx, self.fsdp = place_of()
        self.sister = (1 - self.section, self.ctx, self.fsdp)
        self.rows, width = shard_ref.shape
        self.piece = width // (2 * ctx_count)
        self.mine = pl.ds(pl.multiple_of(self.fsdp * self.rows, self.rows), self.rows)
        self.friends = (
            [self.ahead(d) for d in self.shards] + [peer_of(k) for k in self.places] + [self.sister]
        )

    def ahead(self, d):
        return (self.section, self.ctx, lax.rem(self.fsdp + d, self.fsdp_count))

    def behind(self, d):
        return lax.rem(self.fsdp + self.fsdp_count - d, self.fsdp_count)

    def columns(self, where, core):
        return pl.ds(pl.multiple_of((where * 2 + core) * self.piece, self.piece), self.piece)

    def block(self, d, where, core):
        start = pl.multiple_of(self.behind(d) * self.rows, self.rows)
        return self.w_ref.at[pl.ds(start, self.rows), self.columns(where, core)]

    def own(self, d):
        cols = self.columns(self.ctx, self.section)
        source, target = self.shard_ref.at[:, cols], self.w_ref.at[self.mine, cols]
        return send(source, target, self.z_send.at[d], self.z_recv.at[d], self.ahead(d))

    def kept(self):
        return pltpu.make_async_copy(self.shard_ref, self.w_ref.at[self.mine], self.own_sem.at[0])

    def spread(self, d, k):
        source = self.block(d, self.ctx, self.section)
        device = peer_of(k) if k else self.sister
        return send(source, source, self.y_send.at[d, k], self.y_recv.at[d, k], device)

    def passed(self, d, k):
        source = self.block(d, flip(self.ctx, k), self.section)
        return send(source, source, self.v_send.at[d, k], self.v_recv.at[d, k], self.sister)

    def begin(self):
        for d in self.shards:
            self.own(d).start()
        self.kept().start()

    def relay(self):
        for d in self.shards:
            came = self.block(d, self.ctx, self.section)
            send(came, came, self.z_send.at[d], self.z_recv.at[d], self.sister).wait_recv()
            for k in (*self.places, 0):
                self.spread(d, k).start()

    def hand(self):
        for d in self.shards:
            for k in self.places:
                came = self.block(d, flip(self.ctx, k), self.section)
                send(came, came, self.y_send.at[d, k], self.y_recv.at[d, k], self.sister).wait_recv()
                self.passed(d, k).start()

    def finish(self):
        for d in self.shards:
            for k in (0, *self.places):
                came = self.block(d, flip(self.ctx, k), 1 - self.section)
                recv = (self.v_recv if k else self.y_recv).at[d, k]
                send(came, came, self.v_send.at[d, k], recv, self.sister).wait_recv()
        for d in self.shards:
            self.own(d).wait_send()
            self.spread(d, 0).wait_send()
            for k in self.places:
                self.spread(d, k).wait_send()
                self.passed(d, k).wait_send()
        self.kept().wait()


def collect_sems(ctx_count, fsdp_count):
    table = dma(fsdp_count, ctx_count)
    return [dma(fsdp_count), dma(fsdp_count), table, table, table, table, dma(1)]


def collect_kernel(
    ctx_count, fsdp_count, sizes, shard_ref, small_ref, w_ref, vectors_ref, smalls_ref, s_send, s_recv,
    *sems
):
    steps = Collect(ctx_count, fsdp_count, shard_ref, w_ref, sems)

    def small(d):
        target = smalls_ref.at[steps.fsdp]
        return send(small_ref, target, s_send.at[d], s_recv.at[d], steps.ahead(d))

    greet_all(steps.friends)
    steps.begin()
    for d in steps.shards:
        small(d).start()
    smalls_ref[steps.fsdp] = small_ref[...]
    steps.relay()
    steps.hand()
    steps.finish()
    for d in steps.shards:
        came = smalls_ref.at[steps.behind(d)]
        send(came, came, s_send.at[d], s_recv.at[d], steps.sister).wait_recv()
    for shard in range(fsdp_count):
        rows = smalls_ref[shard].astype(f32)
        for layer in range(2):
            for i, size in enumerate(sizes):
                row = 4 * layer + i
                vectors_ref[row : row + 1, shard * size : (shard + 1) * size] = rows[
                    16 * layer + i : 16 * layer + i + 1, :size
                ]
    for d in steps.shards:
        small(d).wait_send()


def collect(shard, small, sizes):
    ctx_count, fsdp_count = lax.axis_size(CTX), lax.axis_size(FSDP)
    rows, width = shard.shape
    return call(
        functools.partial(collect_kernel, ctx_count, fsdp_count, sizes),
        [((fsdp_count * rows, width), bf16), ((8, fsdp_count * max(sizes)), f32)],
        [VMEM((fsdp_count,) + small.shape, bf16), dma(fsdp_count), dma(fsdp_count)]
        + collect_sems(ctx_count, fsdp_count),
        5,
        shard, small, far_outs=(0,),
    )


class SquareSum:
    def __init__(self, ctx_count, grad_ref, a_ref, b_out, b_in, sems):
        self.grad_ref, self.a_ref, self.b_out = grad_ref, a_ref, b_out
        self.a_send, self.a_recv, b_send, b_recv = sems
        self.parts = Parts(ctx_count, b_out, b_in, b_send, b_recv)
        self.order = (*range(ctx_count - 1, 0, -1), 0)
        self.section, self.ctx, fsdp = place_of()
        self.sister = (1 - self.section, self.ctx, fsdp)
        self.piece = grad_ref.shape[1] // (2 * ctx_count)

    def columns(self, k, core):
        start = (flip(self.ctx, k) * 2 + core) * self.piece
        return pl.ds(pl.multiple_of(start, self.piece), self.piece)

    def chip(self, k):
        source = self.grad_ref.at[:, self.columns(k, 1 - self.section)]
        return send(source, self.a_ref.at[k], self.a_send.at[k], self.a_recv.at[k], self.sister)

    def begin(self):
        for k in self.order:
            self.chip(k).start()

    def middle(self):
        for k in self.order:
            self.chip(k).wait_recv()
            own = self.grad_ref[:, self.columns(k, self.section)].astype(f32)
            total = own + self.a_ref[k].astype(f32)
            if k:
                self.parts.put(k, total)
            else:
                self.b_out[0] = total.astype(bf16)

    def merge(self):
        self.parts.merge()

    def end(self):
        return self.parts.total(self.b_out[0].astype(f32)).astype(bf16)

    def sent(self):
        for k in self.order:
            self.chip(k).wait_send()
        self.parts.sent()


def square_scratch(ctx_count, grad):
    width, both = grad.shape
    piece = VMEM((ctx_count, width, both // (2 * ctx_count)), bf16)
    sems = [dma(ctx_count), dma(ctx_count), dma(ctx_count, 2), dma(ctx_count, 2)]
    return [piece, piece, piece] + sems


def every_owner(ctx_count, layer, start_or_wait, sources, targets, send_sem, recv_sem):
    section, ctx, fsdp = place_of()
    for k in range(ctx_count):
        device = (layer, flip(ctx, k), fsdp)

        def go():
            for i, (source, target) in enumerate(zip(sources, targets)):
                copy = send(
                    source,
                    target.at[ctx, section],
                    send_sem.at[i, k],
                    recv_sem.at[i, section, k],
                    device,
                )
                copy.start() if start_or_wait == "start" else copy.wait_send()

        pl.when(section != layer)(go) if k == 0 else go()


def from_owners(ctx_count, layer, targets, send_sem, recv_sem):
    section, ctx, fsdp = place_of()
    for core in range(2):
        for k in range(ctx_count):
            if core == layer and k == 0:
                continue

            def go():
                for i, target in enumerate(targets):
                    came = target.at[flip(ctx, k), core]
                    send(
                        came, came, send_sem.at[i, k], recv_sem.at[i, core, k], (1 - section, ctx, fsdp)
                    ).wait_recv()

            pl.when(section == layer)(go)


class Owners:
    def __init__(self, ctx_count, layer, sources, targets, cuts, sems):
        self.layer, self.targets = layer, targets
        self.send_sem, self.recv_sem, self.onward_sem = sems
        self.section, self.ctx, self.fsdp = place_of()
        self.count, self.square = ctx_count, ctx_count == 4
        self.pieces = []
        for i, source in enumerate(sources):
            for h in range(2) if self.square else (0,):
                cut = cuts[i][h] if self.square else None
                self.pieces.append((source.at[cut] if self.square else source, i, cut, h))
        self.all = range(len(self.pieces))
        self.early = [(i, 2 - self.pieces[i][3]) for i in self.all if self.square]
        self.keeper = self.section == layer

    def spot(self, i, k, core):
        _, which, cut, _ = self.pieces[i]
        spot = self.targets[which].at[flip(self.ctx, k), core]
        return spot if cut is None else spot.at[cut]

    def peer(self, k):
        return (self.layer, flip(self.ctx, k), self.fsdp)

    def own(self, i, k):
        return send(
            self.pieces[i][0],
            self.spot(i, 0, self.section),
            self.send_sem.at[i, k],
            self.recv_sem.at[i, self.section, k],
            self.peer(k),
        )

    def onward(self, i, core):
        came = 2 - self.pieces[i][3]
        spot = self.spot(i, came, core)
        return send(
            spot, spot, self.onward_sem.at[i, core], self.recv_sem.at[i, core, 3], self.peer(3 - came)
        )

    def outgoing(self):
        if self.square:
            late = [(i, 3 - k) for i, k in self.early]
            return self.early + late
        return [(i, k) for k in range(1, self.count) for i in self.all]

    def begin(self):
        for i, k in self.outgoing():
            self.own(i, k).start()

        @pl.when(jnp.logical_not(self.keeper))
        def _():
            for i in self.all:
                self.own(i, 0).start()

    def arrival(self, i, core, k):
        spot = self.spot(i, k, core)
        recv = self.recv_sem.at[i, core, k]
        sister = (1 - self.section, self.ctx, self.fsdp)
        send(spot, spot, self.send_sem.at[i, k], recv, sister).wait_recv()

    def relay(self):
        if self.square:

            @pl.when(self.keeper)
            def _():
                for i, k in self.early:
                    for core in range(2):
                        self.arrival(i, core, k)
                        self.onward(i, core).start()

    def end(self):
        @pl.when(self.keeper)
        def _():
            for k in range(self.count):
                for core in range(2):
                    for i in self.all:
                        if (i, k) not in self.early and (k or core != self.layer):
                            self.arrival(i, core, k)
            if self.square:
                for i in self.all:
                    for core in range(2):
                        self.onward(i, core).wait_send()

        @pl.when(jnp.logical_not(self.keeper))
        def _():
            for i in self.all:
                self.own(i, 0).wait_send()

        for i, k in self.outgoing():
            self.own(i, k).wait_send()


def row_halves(rows):
    cut = rows // 2 // 16 * 16
    return (pl.ds(0, cut), pl.ds(cut, rows - cut))


def column_halves(width):
    cut = -(-width // 256) * 128
    return ((slice(None), pl.ds(0, cut)), (slice(None), pl.ds(cut, width - cut)))


def owner_sems(ctx_count):
    return [dma(4, ctx_count), dma(4, 2, ctx_count), dma(4, 2)]


class LineSum:
    def __init__(self, fsdp_count, grad_ref, done_ref, refs):
        self.own_ref, self.a_ref, self.sum_ref, self.in_ref, self.a_sem, self.z_send, self.z_recv = refs
        self.grad_ref, self.done_ref = grad_ref, done_ref
        self.section, self.ctx, self.fsdp = place_of()
        self.fsdp_count = fsdp_count
        self.group = fsdp_count // 2
        self.units = grad_ref.shape[0] // fsdp_count
        self.sister = (1 - self.section, self.ctx, self.fsdp)
        self.holds = self.fsdp // self.group == self.section

    def part(self, core):
        size = self.group * self.units
        return self.grad_ref.at[pl.ds(pl.multiple_of(core * size, size), size)]

    def load(self):
        return pltpu.make_async_copy(self.part(self.section), self.own_ref, self.a_sem.at[2])

    def chip(self):
        source = self.part(1 - self.section)
        return send(source, self.a_ref, self.a_sem.at[0], self.a_sem.at[1], self.sister)

    def line(self, j):
        device = (self.section, self.ctx, self.section * self.group + j)
        source = self.sum_ref.at[pl.ds(j * self.units, self.units)]
        return send(source, self.in_ref.at[self.fsdp], self.z_send.at[j], self.z_recv.at[self.fsdp], device)

    def elsewhere(self, j):
        return pl.when(self.section * self.group + j != self.fsdp)

    def begin(self):
        self.chip().start()
        self.load().start()

    def middle(self):
        self.load().wait()
        self.chip().wait_recv()
        self.sum_ref[...] = (self.own_ref[...].astype(f32) + self.a_ref[...].astype(f32)).astype(bf16)
        for j in range(self.group):

            @self.elsewhere(j)
            def _():
                self.line(j).start()

    def end(self):
        @pl.when(self.holds)
        def _():
            start = lax.rem(self.fsdp, self.group) * self.units
            total = self.sum_ref[pl.ds(pl.multiple_of(start, self.units), self.units)].astype(f32)
            for d in range(1, self.fsdp_count):
                came = lax.rem(self.fsdp + d, self.fsdp_count)
                spot = self.in_ref.at[came]
                send(spot, spot, self.z_send.at[0], self.z_recv.at[came], self.sister).wait_recv()
                total = total + self.in_ref[came].astype(f32)
            self.done_ref[...] = total.astype(bf16)

    def sent(self):
        self.chip().wait_send()
        for j in range(self.group):

            @self.elsewhere(j)
            def _():
                self.line(j).wait_send()


def line_scratch(fsdp_count, grad):
    units, width = grad.shape
    half = VMEM((units // 2, width), bf16)
    shards = VMEM((fsdp_count, units // fsdp_count, width), bf16)
    return [half, half, half, shards, dma(3), dma(fsdp_count), dma(fsdp_count)]


class Handout:
    def __init__(self, ctx_count, fsdp_count, layer, done_ref, all_ref, refs):
        self.own_sem, self.o_send, self.o_recv, self.n_send = refs
        self.layer, self.done_ref, self.all_ref = layer, done_ref, all_ref
        self.section, self.ctx, self.fsdp = place_of()
        self.count, self.square = ctx_count, ctx_count == 4
        self.halves = column_halves(done_ref.shape[1])
        self.holder = self.fsdp // (fsdp_count // 2)
        self.holds = self.section == self.holder
        self.keeps = self.section == layer
        self.away = jnp.logical_and(self.holds, jnp.logical_not(self.keeps))
        self.at_home = jnp.logical_and(self.holds, self.keeps)
        self.early = ((1, 1), (2, 0)) if self.square else ()
        late = ((1, 0), (2, 1)) if self.square else ()
        pairs = [(k, h) for k in range(1, ctx_count) for h in range(2)]
        self.sends = (*self.early, *late) if self.square else pairs

    def spot(self, k, h):
        return self.all_ref.at[flip(self.ctx, k)].at[self.halves[h]]

    def peer(self, k):
        return (self.layer, flip(self.ctx, k), self.fsdp)

    def out(self, k, h):
        source = self.done_ref.at[self.halves[h]]
        return send(source, self.spot(0, h), self.o_send.at[k, h], self.o_recv.at[k, h], self.peer(k))

    def onward(self, h):
        came = 1 if h else 2
        spot = self.spot(came, h)
        return send(spot, spot, self.n_send.at[h], self.o_recv.at[3, h], self.peer(3 - came))

    def arrival(self, k, h):
        spot = self.spot(k, h)
        sister = (1 - self.section, self.ctx, self.fsdp)
        send(spot, spot, self.o_send.at[k, h], self.o_recv.at[k, h], sister).wait_recv()

    def kept(self):
        return pltpu.make_async_copy(self.done_ref, self.all_ref.at[self.ctx], self.own_sem.at[0])

    def begin(self):
        @pl.when(self.holds)
        def _():
            for k, h in self.sends:
                self.out(k, h).start()

        @pl.when(self.away)
        def _():
            for h in range(2):
                self.out(0, h).start()

        @pl.when(self.at_home)
        def _():
            self.kept().start()

    def relay(self):
        @pl.when(self.keeps)
        def _():
            for k, h in self.early:
                self.arrival(k, h)
                self.onward(h).start()

    def end(self):
        @pl.when(self.keeps)
        def _():
            for k in range(1, self.count):
                for h in range(2):
                    if (k, h) not in self.early:
                        self.arrival(k, h)
            for _, h in self.early:
                self.onward(h).wait_send()

        @pl.when(jnp.logical_and(self.keeps, jnp.logical_not(self.holds)))
        def _():
            for h in range(2):
                self.arrival(0, h)

        @pl.when(self.holds)
        def _():
            for k, h in self.sends:
                self.out(k, h).wait_send()

        @pl.when(self.away)
        def _():
            for h in range(2):
                self.out(0, h).wait_send()

        @pl.when(self.at_home)
        def _():
            self.kept().wait()


def handout_sems(ctx_count):
    return [dma(1), dma(ctx_count, 2), dma(ctx_count, 2), dma(2)]


def chip_square(ctx_count):
    section, ctx, fsdp = place_of()
    return [
        (section if same else 1 - section, flip(ctx, k), fsdp)
        for k in range(ctx_count)
        for same in (True, False)
        if k or not same
    ]


def turn_tile(values):
    lane = lax.broadcasted_iota(jnp.int32, values.shape, 1)
    width = values.shape[1]
    half = HEAD_DIM // 2
    ahead = pltpu.roll(values, width - half, 1)
    behind = pltpu.roll(values, half, 1)
    return jnp.where(lane % HEAD_DIM < half, ahead, behind)


def head_in_group(tile, head, group):
    lane = lax.broadcasted_iota(jnp.int32, tile.shape, 1)
    values = tile.astype(f32)
    moved = values if head % 2 == group else pltpu.roll(values, HEAD_DIM, 1)
    return jnp.where(lane // HEAD_DIM == group, moved, 0.0).astype(bf16)


def attend_kernel(count, fsdp_count, layer, fetch, *refs):
    x_ref, vectors_ref, w_ref, cos_ref, sin_ref, kpos_ref, qpos_ref = refs[:7]
    refs = refs[7:]
    shard_ref, refs = (refs[0], refs[1:]) if fetch else (None, refs)
    normed_ref, q_ref, kv_ref, lse_ref, ctx_ref, mid_ref, low2_ref = refs[:7]
    refs = refs[7:]
    next_ref, refs = (refs[0], refs[1:]) if fetch else (None, refs)
    mask_ref, s_ref, p_ref, vt_ref, ctxf_ref, send_sem, recv_sem, *sems = refs
    rows, width = x_ref.shape
    pair = kv_ref.shape[2] // 2
    wide = width + 2 * pair
    heads = width // HEAD_DIM
    group_size = heads // (pair // HEAD_DIM)
    if fetch:
        steps = Collect(count, fsdp_count, shard_ref, next_ref, sems)
        greet_all(steps.friends)
        steps.begin()
    else:
        greet(count)
    x = x_ref[...].astype(f32)
    gain1, bias, gain2 = (vectors_ref[4 * layer + i : 4 * layer + i + 1, :] for i in range(3))
    normed = (x * row_scale(x) * gain1[:, :width]).astype(bf16)
    normed_ref[...] = normed
    cos, sin = cos_ref[...], sin_ref[...]
    kv = matmul(normed, w_ref[:, width:wide]) + bias[:, width:wide]
    keys = kv[:, :pair]
    kv_ref[0, :, :pair] = (keys * cos + turn_tile(keys) * sin).astype(bf16)
    kv_ref[0, :, pair:] = kv[:, pair:].astype(bf16)
    for k in range(1, count):
        remote(kv_ref.at[0], kv_ref.at[k], send_sem, recv_sem, k).start()
    merged = matmul(normed, w_ref[:, :width]) + bias[:, :width]
    for start, size in tiles(width, 2 * HEAD_DIM):
        part = merged[:, start : start + size]
        turned_part = (part * cos + turn_tile(part) * sin) * HEAD_DIM ** (-0.5)
        q_ref[:, start : start + size] = turned_part.astype(bf16)
    for k in range(count):
        allowed = kpos_ref[k * rows : (k + 1) * rows, :] <= qpos_ref[...]
        mask_ref[k] = jnp.where(allowed, 0.0, masked_value)
    if fetch:
        steps.relay()
    for k in range(count):
        if k:
            remote(kv_ref.at[0], kv_ref.at[k], send_sem, recv_sem, k).wait_recv()
        vt_ref[:, k * rows : (k + 1) * rows] = kv_ref[k, :, pair:].astype(f32).T.astype(bf16)

    for head in range(heads):
        group = head // group_size
        start = head // 2 * (2 * HEAD_DIM)
        query = head_in_group(q_ref[:, start : start + 2 * HEAD_DIM], head, group)
        top = None
        for k in range(count):
            scores = matmul_nt(kv_ref[k, :, :pair], query) + mask_ref[k]
            s_ref[k] = scores
            here = jnp.max(scores, axis=0, keepdims=True)
            top = here if top is None else jnp.maximum(top, here)
        total = None
        for k in range(count):
            weight = jnp.exp(s_ref[k] - top)
            here = jnp.sum(weight, axis=0, keepdims=True)
            total = here if total is None else total + here
            p_ref[k * rows : (k + 1) * rows, :] = weight.astype(bf16)
        value_rows = vt_ref[group * HEAD_DIM : (group + 1) * HEAD_DIM, :]
        context = matmul(value_rows, p_ref[...]) * (1.0 / total)
        ctxf_ref[head * HEAD_DIM : (head + 1) * HEAD_DIM, :] = context
        lse_ref[head : head + 1, :] = top + jnp.log(total)
        if fetch and head == heads // 2:
            steps.hand()
    context = ctxf_ref[...]
    ctx_ref[...] = context.astype(bf16)
    middle = x + matmul(context.T.astype(bf16), w_ref[:, wide:])
    mid_ref[...] = middle
    low2_ref[...] = (middle * row_scale(middle) * gain2[:, :width]).astype(bf16)
    for k in range(1, count):
        remote(kv_ref.at[0], kv_ref.at[k], send_sem, recv_sem, k).wait_send()
    if fetch:
        steps.finish()


def attend(layer, hidden, place, shard=None):
    index, vectors, weights = layer[:3]
    cosine, sine, key_positions, query_positions = place
    rows, width = hidden.shape
    count = lax.axis_size(CTX)
    wide = weights.shape[1] - width
    pair = (wide - width) // 2
    keys = count * rows
    heads = width // HEAD_DIM
    fetch = shard is not None
    fsdp_count = lax.axis_size(FSDP)
    args = (hidden, vectors, weights, cosine, sine, key_positions, query_positions)
    return call(
        functools.partial(attend_kernel, count, fsdp_count, index, fetch),
        [
            ((rows, width), bf16),
            ((rows, width), bf16),
            ((count, rows, 2 * pair), bf16),
            ((-(-heads // 8) * 8, rows), f32),
            ((width, rows), bf16),
            ((rows, width), f32),
            ((rows, width), bf16),
        ]
        + [(weights.shape, bf16)] * fetch,
        [
            VMEM((count, rows, rows), f32),
            VMEM((count, rows, rows), f32),
            VMEM((keys, rows), bf16),
            VMEM((pair, keys), bf16),
            VMEM((width, rows), f32),
            dma(count),
            dma(count),
        ]
        + (collect_sems(count, fsdp_count) if fetch else []),
        10 if fetch else 1,
        *args, *([shard] if fetch else []),
        far_outs=(7,) if fetch else (),
    )


def attend_back_kernel(count, layer, carried, *refs):
    (
        dmid_ref, x_ref, vectors_ref, w_ref, cos_ref, sin_ref, kpos_ref, qpos_ref,
        normed_ref, q_ref, kv_ref, lse_ref, ctx_ref,
    ) = refs[:13]
    refs = refs[13:]
    (load_ref, expand_ref), refs = (refs[:2], refs[2:]) if carried else ((None, None), refs)
    dh_ref, gain_ref, bias_ref, grad_ref = refs[:4]
    refs = refs[4:]
    (summed_ref, expand_all_ref), refs = (refs[:2], refs[2:]) if carried else ((None, None), refs)
    (
        mask_ref, p_ref, dp_ref, ds_ref, kt_ref, dctx_ref, dq_ref, dkv_ref, out_ref, in_ref,
        merged_ref, low_ref, send_sem, recv_sem, *scratch,
    ) = refs
    rows, width = x_ref.shape
    pair = kv_ref.shape[2] // 2
    wide = width + 2 * pair
    heads = width // HEAD_DIM
    group_size = heads // (pair // HEAD_DIM)
    if carried:
        section, ctx, _ = place_of()
        steps = SquareSum(count, load_ref, *scratch[:3], scratch[3:7])
        halves = [row_halves(expand_ref.shape[0])]
        owners = Owners(count, 1, [expand_ref], [expand_all_ref], halves, scratch[7:10])
        kept = pltpu.make_async_copy(expand_ref, expand_all_ref.at[ctx, section], scratch[10].at[0])
        greet_all(chip_square(count))
        steps.begin()
        owners.begin()

        @pl.when(owners.keeper)
        def _():
            kept.start()

    else:
        greet(count)
    low = dmid_ref[...].astype(bf16)
    low_ref[...] = low
    dctx = matmul_nt(low, w_ref[:, wide:]).astype(bf16)
    dctx_ref[...] = dctx
    for k in range(count):
        allowed = kpos_ref[k * rows : (k + 1) * rows, :] <= qpos_ref[...]
        mask_ref[k] = jnp.where(allowed, 0.0, masked_value)
        kt_ref[:, k * rows : (k + 1) * rows] = kv_ref[k, :, :pair].astype(f32).T.astype(bf16)
    dkv_ref[...] = jnp.zeros_like(dkv_ref)

    for head in range(heads):
        group = head // group_size
        start = head // 2 * (2 * HEAD_DIM)
        query = head_in_group(q_ref[:, start : start + 2 * HEAD_DIM], head, group)
        upstream = head_in_group(dctx_ref[:, start : start + 2 * HEAD_DIM], head, group)
        lse = lse_ref[head : head + 1, :]
        delta = None
        for k in range(count):
            scores = matmul_nt(kv_ref[k, :, :pair], query) + mask_ref[k]
            weight = jnp.exp(scores - lse)
            weight_grad = matmul_nt(kv_ref[k, :, pair:], upstream)
            p_ref[k] = weight
            dp_ref[k] = weight_grad
            dkv_ref[k, :, pair:] += matmul(weight.astype(bf16), upstream)
            here = jnp.sum(weight * weight_grad, axis=0, keepdims=True)
            delta = here if delta is None else delta + here
        for k in range(count):
            score_grad = (p_ref[k] * (dp_ref[k] - delta)).astype(bf16)
            ds_ref[k * rows : (k + 1) * rows, :] = score_grad
            dkv_ref[k, :, :pair] += matmul(score_grad, query)
        key_rows = kt_ref[group * HEAD_DIM : (group + 1) * HEAD_DIM, :]
        dq_ref[head * HEAD_DIM : (head + 1) * HEAD_DIM, :] = (
            matmul(key_rows, ds_ref[...]) * HEAD_DIM ** (-0.5)
        )
        if carried and head == heads // 5:
            steps.middle()
        if carried and head == heads // 3:
            owners.relay()
        if carried and head == heads * 2 // 3:
            steps.merge()
    for k in range(1, count):
        out_ref[k] = dkv_ref[k].astype(bf16)
        remote(out_ref.at[k], in_ref.at[k], send_sem, recv_sem, k).start()
    cos, sin = cos_ref[...], sin_ref[...]
    dq = dq_ref[...].T

    def unturn(part):
        return (part * cos - turn_tile(part) * sin).astype(bf16)

    for start, size in tiles(width, 2 * HEAD_DIM):
        merged_ref[:, start : start + size] = unturn(dq[:, start : start + size])
    grad_ref[:, wide:] = matmul(ctx_ref[...], low_ref[...]).astype(bf16)
    normed = normed_ref[...]

    def project_grad(first, last):
        for start, size in tiles(last - first, 512):
            cut = slice(first + start, first + start + size)
            grad_ref[:, cut] = matmul_tn(normed, merged_ref[:, cut]).astype(bf16)

    project_grad(0, width)
    normed_grad = matmul_nt(merged_ref[:, :width], w_ref[:, :width])
    total = dkv_ref[0]
    for k in range(1, count):
        remote(out_ref.at[k], in_ref.at[k], send_sem, recv_sem, k).wait_recv()
        total = total + in_ref[k].astype(f32)
    merged_ref[:, width : width + pair] = unturn(total[:, :pair])
    merged_ref[:, width + pair :] = total[:, pair:].astype(bf16)
    project_grad(width, wide)
    normed_grad = normed_grad + matmul_nt(merged_ref[:, width:], w_ref[:, width:wide])
    bias_ref[...] = jnp.sum(merged_ref[...].astype(f32), axis=0, keepdims=True)
    x = x_ref[...].astype(f32)
    scale = row_scale(x)
    gain_ref[...] = jnp.sum(normed_grad * x * scale, axis=0, keepdims=True)
    scaled = normed_grad * vectors_ref[4 * layer : 4 * layer + 1, :width]
    mean = jnp.mean(scaled * x, axis=-1, keepdims=True)
    hidden_grad = dmid_ref[...] + scale * scaled - x * (scale * scale * scale * mean)
    dh_ref[...] = hidden_grad.astype(dh_ref.dtype)
    for k in range(1, count):
        remote(out_ref.at[k], in_ref.at[k], send_sem, recv_sem, k).wait_send()
    if carried:
        summed_ref[...] = steps.end()
        steps.sent()
        owners.end()

        @pl.when(owners.keeper)
        def _():
            kept.wait()


def attend_back(layer, kept, middle_grad, place, load=()):
    index, vectors, weights = layer[:3]
    cosine, sine, key_positions, query_positions = place
    hidden, normed, queries, every_kv, lse, context = kept
    rows, width = hidden.shape
    count = lax.axis_size(CTX)
    wide = weights.shape[1] - width
    pair = (wide - width) // 2
    keys = count * rows
    carried = bool(load)
    args = (
        middle_grad, hidden, vectors, weights, cosine, sine, key_positions, query_positions,
        normed, queries, every_kv, lse, context,
    )
    return call(
        functools.partial(attend_back_kernel, count, index, carried),
        [
            ((rows, width), bf16 if index else f32),
            ((1, width), f32),
            ((1, wide), f32),
            ((width, wide + width), bf16),
        ]
        + (
            [((width, (wide + width) // (2 * count)), bf16), ((count, 2) + load[1].shape, bf16)]
            if carried
            else []
        ),
        [
            VMEM((count, rows, rows), f32),
            VMEM((count, rows, rows), f32),
            VMEM((count, rows, rows), f32),
            VMEM((keys, rows), bf16),
            VMEM((pair, keys), bf16),
            VMEM((rows, width), bf16),
            VMEM((width, rows), f32),
            VMEM((count, rows, 2 * pair), f32),
            VMEM((count, rows, 2 * pair), bf16),
            VMEM((count, rows, 2 * pair), bf16),
            VMEM((rows, wide), bf16),
            VMEM((rows, width), bf16),
            dma(count),
            dma(count),
        ]
        + (square_scratch(count, load[0]) + owner_sems(count) + [dma(1)] if carried else []),
        6 if carried else 2,
        *args, *load,
        far_outs=(5,) if carried else (),
    )


def unit_chunks(units):
    main = units // 128 * 128
    chunks = [(start, main + start, start, size) for start, size in tiles(main, 512)]
    if units > main:
        chunks.append((2 * main, main + units, main, units - main))
    return chunks


def pack_units(gate, up):
    main = gate.shape[1] // 128 * 128
    return jnp.concatenate([gate[:, :main], up[:, :main], gate[:, main:], up[:, main:]], axis=1)


def unpack_units(packed):
    units = packed.shape[-1] // 2
    main = units // 128 * 128
    if units == main:
        return packed[..., :main], packed[..., main:]
    gate = jnp.concatenate([packed[..., :main], packed[..., 2 * main : main + units]], axis=-1)
    up = jnp.concatenate([packed[..., main : 2 * main], packed[..., main + units :]], axis=-1)
    return gate, up


class Rows:
    def __init__(self, count, own_ref, slots_ref, send_sem, recv_sem):
        self.own_ref, self.slots_ref = own_ref, slots_ref
        self.send_sem, self.recv_sem = send_sem, recv_sem
        self.count, self.square = count, count == 4
        self.half = own_ref.shape[0] // 2

    def rows(self, h):
        return pl.ds(h * self.half, self.half)

    def copy(self, source, k, h, peer):
        target = self.slots_ref.at[k, self.rows(h)]
        return send(source, target, self.send_sem.at[k, h], self.recv_sem.at[k, h], peer_of(peer))

    def own(self, k, h):
        return self.copy(self.own_ref.at[self.rows(h)], k, h, k)

    def onward(self, h):
        came = 1 if h else 2
        return self.copy(self.slots_ref.at[came, self.rows(h)], 3, h, 3 - came)

    def order(self):
        if self.square:
            return [(1, 1), (2, 0), (1, 0), (2, 1)]
        return [(k, h) for k in range(1, self.count) for h in range(2)]

    def begin(self):
        for k, h in self.order():
            self.own(k, h).start()

    def relay(self):
        if self.square:
            for k, h in ((1, 1), (2, 0)):
                self.own(k, h).wait_recv()
                self.onward(h).start()

    def take(self, k):
        for h in range(2):
            if not (self.square and (k, h) in ((1, 1), (2, 0))):
                self.copy(self.own_ref.at[self.rows(h)], k, h, k).wait_recv()

    def sent(self):
        for k, h in self.order():
            self.own(k, h).wait_send()
        if self.square:
            for h in range(2):
                self.onward(h).wait_send()


class Parts:
    def __init__(self, count, parts_ref, got_ref, send_sem, recv_sem):
        self.parts_ref, self.got_ref = parts_ref, got_ref
        self.send_sem, self.recv_sem = send_sem, recv_sem
        self.count, self.square = count, count == 4
        self.half = parts_ref.shape[1] // 2

    def rows(self, h):
        return pl.ds(h * self.half, self.half)

    def copy(self, k, h):
        peer = 1 + h if self.square and k == 3 else k
        source, target = self.parts_ref.at[k, self.rows(h)], self.got_ref.at[k, self.rows(h)]
        return send(source, target, self.send_sem.at[k, h], self.recv_sem.at[k, h], peer_of(peer))

    def put(self, k, part):
        self.parts_ref[k] = part.astype(bf16)
        for h in range(2):
            if not (self.square and (k, h) in ((1, 1), (2, 0))):
                self.copy(k, h).start()

    def merge(self):
        if self.square:
            for k, h in ((2, 0), (1, 1)):
                self.copy(3, h).wait_recv()
                rows = slice(h * self.half, (h + 1) * self.half)
                total = self.parts_ref[k, rows].astype(f32) + self.got_ref[3, rows].astype(f32)
                self.parts_ref[k, rows] = total.astype(bf16)
                self.copy(k, h).start()

    def total(self, own):
        for k in range(1, 3 if self.square else self.count):
            for h in range(2):
                self.copy(k, h).wait_recv()
            own = own + self.got_ref[k].astype(f32)
        return own

    def sent(self):
        for k in range(1, self.count):
            for h in range(2):
                self.copy(k, h).wait_send()


class Loads:
    def __init__(self, sources, targets, sem):
        self.copies = [
            pltpu.make_async_copy(source, target, sem.at[i])
            for i, (source, target) in enumerate(zip(sources, targets))
        ]
        for copy in self.copies:
            copy.start()

    def take(self, *which):
        for i in which:
            self.copies[i].wait()


def gate_and_up(block, expand_ref, gate_start, up_start, size):
    if size % 128:
        both = matmul(block, expand_ref[:, gate_start : up_start + size])
        return both[:, :size], both[:, size:]
    gate = matmul(block, expand_ref[:, gate_start : gate_start + size])
    return gate, matmul(block, expand_ref[:, up_start : up_start + size])


def feed_kernel(
    count, low_ref, mid_ref, expand_any, down_any,
    out_ref, blocks_ref, kept_gate_ref, kept_up_ref,
    expand_ref, down_ref, act_ref, part_ref, sent_ref, got_ref,
    send_sem, recv_sem, send_sem2, recv_sem2, load_sem,
):
    units = down_ref.shape[0]
    loads = Loads((expand_any, down_any), (expand_ref, down_ref), load_sem)
    rows = Rows(count, low_ref, blocks_ref, send_sem, recv_sem)
    parts = Parts(count, sent_ref, got_ref, send_sem2, recv_sem2)
    greet(count)
    rows.begin()
    blocks_ref[0] = low_ref[...]
    loads.take(0, 1)
    for k in range(count):
        if k:
            rows.take(k)
        block = blocks_ref[k]
        for gate_start, up_start, start, size in unit_chunks(units):
            gate, up = gate_and_up(block, expand_ref, gate_start, up_start, size)
            kept_gate_ref[k, :, start : start + size] = gate.astype(bf16)
            kept_up_ref[k, :, start : start + size] = up.astype(bf16)
            act_ref[:, start : start + size] = (gate / (1.0 + jnp.exp(-gate)) * up).astype(bf16)
        part = matmul(act_ref[...], down_ref[...])
        if k:
            parts.put(k, part)
        else:
            part_ref[...] = part + mid_ref[...]
            rows.relay()
    parts.merge()
    out_ref[...] = parts.total(part_ref[...]).astype(bf16)
    rows.sent()
    parts.sent()


def feed(layer, second_normed, middle):
    expand_w, down_w = layer[3:]
    count = lax.axis_size(CTX)
    rows, width = second_normed.shape
    units = down_w.shape[0]
    return call(
        functools.partial(feed_kernel, count),
        [
            ((rows, width), bf16),
            ((count, rows, width), bf16),
            ((count, rows, units), bf16),
            ((count, rows, units), bf16),
        ],
        [
            VMEM(expand_w.shape, bf16),
            VMEM(down_w.shape, bf16),
            VMEM((rows, units), bf16),
            VMEM((rows, width), f32),
            VMEM((count, rows, width), bf16),
            VMEM((count, rows, width), bf16),
        ]
        + [dma(count, 2)] * 4
        + [dma(2)],
        3,
        second_normed, middle, expand_w, down_w, far=(2, 3),
    )


def feed_back_kernel(count, fsdp_count, layer, carried, *refs):
    (
        grad_ref, mid_ref, vectors_ref,
        blocks_any, kept_gate_any, kept_up_any, expand_any, down_any,
    ) = refs[:8]
    refs = refs[8:]
    line_ref, refs = (refs[0], refs[1:]) if carried else (None, refs)
    dmid_ref, gain_ref, dexpand_ref, ddown_ref = refs[:4]
    refs = refs[4:]
    done_ref, refs = (refs[0], refs[1:]) if carried else (None, refs)
    (
        blocks_ref, kept_gate_ref, kept_up_ref, expand_ref, down_ref,
        grads_ref, act_ref, dwide_ref, part_ref, sent_ref, got_ref,
        send_sem, recv_sem, send_sem2, recv_sem2, load_sem, *scratch,
    ) = refs
    rows, width = grad_ref.shape
    units = down_ref.shape[0]
    loads = Loads(
        (down_any, kept_gate_any, kept_up_any, expand_any, blocks_any),
        (down_ref, kept_gate_ref, kept_up_ref, expand_ref, blocks_ref),
        load_sem,
    )
    gather = Rows(count, grad_ref, grads_ref, send_sem, recv_sem)
    parts = Parts(count, sent_ref, got_ref, send_sem2, recv_sem2)
    if carried:
        line = LineSum(fsdp_count, line_ref, done_ref, scratch)
        section, ctx, fsdp = place_of()
        greet_all(
            [peer_of(k) for k in range(1, count)]
            + [line.sister]
            + [(section, ctx, lax.rem(fsdp + d, fsdp_count)) for d in range(1, fsdp_count)]
        )
        line.begin()
    else:
        greet(count)
    gather.begin()
    grads_ref[0] = grad_ref[...]
    loads.take(0, 1, 2)
    for k in range(count):
        if k:
            gather.take(k)
        block = grads_ref[k]
        for gate_start, up_start, start, size in unit_chunks(units):
            cut = slice(start, start + size)
            spread = matmul_nt(block, down_ref[cut, :])
            gate = kept_gate_ref[k, :, cut].astype(f32)
            up = kept_up_ref[k, :, cut].astype(f32)
            sig = 1.0 / (1.0 + jnp.exp(-gate))
            silu = gate * sig
            act_ref[k, :, cut] = (silu * up).astype(bf16)
            dgate = (spread * up * sig * (1.0 + gate * (1.0 - sig))).astype(bf16)
            dup = (spread * silu).astype(bf16)
            if size % 128:
                dwide_ref[k, :, gate_start : up_start + size] = jnp.concatenate([dgate, dup], axis=1)
            else:
                dwide_ref[k, :, gate_start : gate_start + size] = dgate
                dwide_ref[k, :, up_start : up_start + size] = dup
        if not k:
            loads.take(3)
        part = matmul_nt(dwide_ref[k], expand_ref[...])
        if k:
            parts.put(k, part)
        else:
            part_ref[...] = part
            gather.relay()
            if carried:
                line.middle()
    loads.take(4)
    tall = count * rows
    grads = grads_ref[...].reshape(tall, width)
    main = units // 128 * 128
    for start, size in tiles(main, 384) + [(main, units - main)] * (units > main):
        act = act_ref[:, :, start : start + size].reshape(tall, size)
        ddown_ref[start : start + size, :] = matmul_tn(act, grads).astype(bf16)
    parts.merge()
    blocks = blocks_ref[...].reshape(tall, width)
    for start, size in tiles(2 * units, 512):
        dwide = dwide_ref[:, :, start : start + size].reshape(tall, size)
        dexpand_ref[:, start : start + size] = matmul_tn(blocks, dwide).astype(bf16)
    if carried:
        line.end()
    total = parts.total(part_ref[...])
    middle = mid_ref[...]
    scale = row_scale(middle)
    gain_ref[...] = jnp.sum(total * middle * scale, axis=0, keepdims=True)
    scaled = total * vectors_ref[4 * layer + 2 : 4 * layer + 3, :width]
    mean = jnp.mean(scaled * middle, axis=-1, keepdims=True)
    dmid_ref[...] = (
        grad_ref[...].astype(f32) + scale * scaled - middle * (scale * scale * scale * mean)
    )
    gather.sent()
    parts.sent()
    if carried:
        line.sent()


def feed_back(layer, middle, blocks, kept_gate, kept_up, grad_out, load=()):
    index, vectors = layer[:2]
    expand_w, down_w = layer[3:]
    count = lax.axis_size(CTX)
    rows, width = grad_out.shape
    units = down_w.shape[0]
    fsdp_count = lax.axis_size(FSDP)
    brought = (blocks, kept_gate, kept_up, expand_w, down_w)
    return call(
        functools.partial(feed_back_kernel, count, fsdp_count, index, bool(load)),
        [
            ((rows, width), f32),
            ((1, width), f32),
            ((width, 2 * units), bf16),
            ((units, width), bf16),
        ]
        + [((units // fsdp_count, width), bf16)] * len(load),
        [VMEM(array.shape, bf16) for array in brought]
        + [
            VMEM((count, rows, width), bf16),
            VMEM((count, rows, units), bf16),
            VMEM((count, rows, 2 * units), bf16),
            VMEM((rows, width), f32),
            VMEM((count, rows, width), bf16),
            VMEM((count, rows, width), bf16),
        ]
        + [dma(count, 2)] * 4
        + [dma(5)]
        + (line_scratch(fsdp_count, load[0]) if load else []),
        4 + 7 * index,
        grad_out, middle, vectors, *brought, *load, far=(3, 4, 5, 6, 7, 8),
    )


def attn_sum_kernel(
    ctx_count, fsdp_count, wide, low_ref, high_ref, small_ref, down_ref,
    act_zero_ref, act_one_ref, grad_zero_ref, grad_one_ref, down_grad_ref, expand_ref, expand_all_ref,
    projections_ref, output_ref, total_ref, down_all_ref, act_ref, grad_ref, expand_out,
    wide_ref, done_ref,
    c_out, c_in, d_out, whole_ref, s_out, s_in,
    c_send, c_recv, d_send, d_recv, s_send, s_recv, *more,
):
    section, ctx, fsdp = place_of()
    sister = (1 - section, ctx, fsdp)
    width, piece = high_ref.shape
    rows = width // fsdp_count
    places = range(1, ctx_count)
    shards = range(1, fsdp_count)
    steps = SquareSum(ctx_count, low_ref, *more[:3], more[3:7])
    halves = [row_halves(expand_ref.shape[0])]
    owners = Owners(ctx_count, 0, [expand_ref], [expand_out], halves, more[7:10])
    own_sem, swap_send, swap_recv = more[10:13]
    kept = pltpu.make_async_copy(expand_ref, expand_out.at[ctx, section], own_sem.at[0])
    load = pltpu.make_async_copy(expand_all_ref, expand_out, own_sem.at[1])
    down = LineSum(fsdp_count, down_grad_ref, done_ref, more[13:20])
    handouts = [
        Handout(ctx_count, fsdp_count, 1, down_ref, down_all_ref, more[20:24]),
        Handout(ctx_count, fsdp_count, 0, done_ref, down_all_ref, more[24:28]),
    ]
    layers = ((act_zero_ref, grad_zero_ref), (act_one_ref, wide_ref))

    def swap(i, layer):
        target = (act_ref, grad_ref)[i].at[section]
        return send(layers[layer][i], target, swap_send.at[i], swap_recv.at[i], sister)

    def ahead(d):
        return (section, ctx, lax.rem(fsdp + d, fsdp_count))

    def c_copy(layer, d):
        target = lax.rem(fsdp + d, fsdp_count)
        source = c_out.at[layer, pl.ds(pl.multiple_of(target * rows, rows), rows)]
        return send(source, c_in.at[layer, d], c_send.at[layer, d], c_recv.at[layer, d], ahead(d))

    def s_copy(step, source, device):
        return send(s_out.at[source], s_in.at[step], s_send.at[step], s_recv.at[step], device)

    def line_sum(layer):
        total = c_out[layer, pl.ds(pl.multiple_of(fsdp * rows, rows), rows)].astype(f32)
        for d in shards:
            c_copy(layer, d).wait_recv()
            total = total + c_in[layer, d].astype(f32)
        d_out[layer] = total.astype(bf16)
        every_owner(
            ctx_count, layer, "start", [d_out.at[layer]], [whole_ref], d_send.at[layer], d_recv
        )

        @pl.when(section == layer)
        def _():
            whole_ref[ctx, section] = d_out[layer]

    hops = [(0, 0, sister)]
    hops += [(k, 1, peer_of(k)) for k in places]
    hops += [(ctx_count - 1 + d, 2, ahead(d)) for d in shards]

    greet_all(chip_square(ctx_count) + [ahead(d) for d in shards])
    steps.begin()
    down.begin()
    owners.begin()

    @pl.when(section == 0)
    def _():
        kept.start()

    @pl.when(section == 1)
    def _():
        load.start()

    wide_ref[...] = grad_one_ref[...].astype(f32)
    for layer in range(2):

        @pl.when(section != layer)
        def _():
            for i in range(2):
                swap(i, layer).start()

        @pl.when(section == layer)
        def _():
            for i, target in enumerate((act_ref, grad_ref)):
                target[section] = layers[layer][i][...]

    s_out[0] = small_ref[...]
    s_copy(*hops[0]).start()
    c_out[1] = high_ref[...]
    for d in shards:
        c_copy(1, d).start()

    steps.middle()
    down.middle()
    handouts[0].begin()
    owners.relay()
    s_copy(*hops[0]).wait_recv()
    s_out[1] = s_out[0] + s_in[0]
    for k in places:
        s_copy(*hops[k]).start()
    line_sum(1)
    steps.merge()
    c_out[0] = steps.end()
    for d in shards:
        c_copy(0, d).start()
    handouts[0].relay()
    down.end()
    handouts[1].begin()
    part = s_out[1]
    for k in places:
        s_copy(*hops[k]).wait_recv()
        part = part + s_in[k]
    s_out[2] = part
    for d in shards:
        s_copy(*hops[ctx_count - 1 + d]).start()
    line_sum(0)
    part = s_out[2]
    for d in shards:
        s_copy(*hops[ctx_count - 1 + d]).wait_recv()
        part = part + s_in[ctx_count - 1 + d]
    total_ref[...] = part
    for layer in (1, 0):
        from_owners(ctx_count, layer, [whole_ref], d_send.at[layer], d_recv)
    for where in range(ctx_count):
        for core in range(2):
            start = (where * 2 + core) * piece
            block = whole_ref[where, core].astype(f32)
            size = max(min(wide - start, piece), 0)
            if size:
                projections_ref[:, start : start + size] = block[:, :size]
            if size < piece:
                first = start + size - wide
                output_ref[:, first : first + piece - size] = block[:, size:]
    owners.end()
    handouts[1].relay()
    for handout in handouts:
        handout.end()
    down.sent()

    @pl.when(section == 0)
    def _():
        kept.wait()

    @pl.when(section == 1)
    def _():
        load.wait()

    for i in range(2):
        swap(i, 0).wait()
    steps.sent()
    for layer in (1, 0):
        for d in shards:
            c_copy(layer, d).wait_send()
        every_owner(
            ctx_count, layer, "wait", [d_out.at[layer]], [whole_ref], d_send.at[layer], d_recv
        )
    for hop in hops:
        s_copy(*hop).wait_send()


def attn_sum(low, high, small, down_one, acts, grads, down_grad, expand_part, expand_all, wide):
    ctx_count, fsdp_count = lax.axis_size(CTX), lax.axis_size(FSDP)
    width, both = low.shape
    rows = width // fsdp_count
    piece = both // (2 * ctx_count)
    hops = ctx_count + fsdp_count - 1
    return call(
        functools.partial(attn_sum_kernel, ctx_count, fsdp_count, wide),
        [
            ((rows, wide), f32),
            ((rows, both - wide), f32),
            (small.shape, f32),
            ((ctx_count,) + down_one.shape, bf16),
            ((2,) + acts[0].shape, bf16),
            ((2,) + grads[0].shape, f32),
            (expand_all.shape, bf16),
        ],
        [
            VMEM(grads[0].shape, f32),
            VMEM(down_one.shape, bf16),
            VMEM((2, width, piece), bf16),
            VMEM((2, fsdp_count, rows, piece), bf16),
            VMEM((2, rows, piece), bf16),
            VMEM((ctx_count, 2, rows, piece), bf16),
            VMEM((3,) + small.shape, f32),
            VMEM((hops,) + small.shape, f32),
            dma(2, fsdp_count), dma(2, fsdp_count),
            dma(2, 1, ctx_count), dma(1, 2, ctx_count),
            dma(hops), dma(hops),
        ]
        + square_scratch(ctx_count, low)
        + owner_sems(ctx_count)
        + [dma(2), dma(2), dma(2)]
        + line_scratch(fsdp_count, down_grad)
        + handout_sems(ctx_count) * 2,
        7,
        low, high, small, down_one, *acts, *grads, down_grad, expand_part, expand_all,
        far=(8, 10), far_outs=(3,),
    )


def spread_kernel(chunk, stride, shards, side_width, block_ref, out_ref):
    count = block_ref.shape[0]
    for where in range(count):
        sides = unpack_units(block_ref[where].astype(f32))
        for side, values in enumerate(sides):
            for shard in range(shards):
                start = side * side_width + (shard * count + where) * chunk
                out_ref[:, start : start + chunk] = values[:, shard * stride : shard * stride + chunk]


def finish(expand_all, ff_width, units):
    ctx_count, fsdp_count = lax.axis_size(CTX), lax.axis_size(FSDP)
    half, packed = expand_all.shape[2:]
    rows = 2 * half
    step = 32 if rows % 32 == 0 else 16
    stride = packed // 2 // fsdp_count
    return pl.pallas_call(
        functools.partial(spread_kernel, units, stride, fsdp_count, ff_width),
        grid=(rows // step,),
        out_shape=jax.ShapeDtypeStruct((rows, 2 * ff_width), f32),
        in_specs=[pl.BlockSpec((ctx_count, step, packed), lambda i: (0, i, 0))],
        out_specs=pl.BlockSpec((step, 2 * ff_width), lambda i: (i, 0)),
        compiler_params=pltpu.CompilerParams(vmem_limit_bytes=LIMIT),
    )(expand_all.reshape(ctx_count, rows, packed))


def per_device(
    inputs,
    attend_gain,
    projections,
    biases,
    output_weight,
    mixer_gain,
    expand_weight,
    down_weight,
    positions,
    cotangent,
):
    row_count, model_width = inputs.shape[2:]
    section = lax.axis_index(SECTION)
    is_first = section == 0
    ctx = lax.axis_index(CTX)
    fsdp = lax.axis_index(FSDP)
    ctx_count = lax.axis_size(CTX)
    fsdp_count = lax.axis_size(FSDP)
    shard_rows = projections.shape[1]
    wide = projections.shape[2]
    ff_width = expand_weight.shape[2] // 2
    shard_units = down_weight.shape[1]
    units = shard_units // ctx_count
    spare_units = -units % 16
    both = (FSDP, SECTION)

    def mine(array):
        return lax.dynamic_index_in_dim(array, section, 0, keepdims=False)

    source = mine(inputs)[0]
    upstream = mine(cotangent)[0]
    key_positions = mine(positions)[0]
    query_positions = lax.dynamic_slice_in_dim(key_positions, ctx * row_count, row_count)
    cosine, sine = tables(query_positions)
    by_distance = jnp.concatenate(
        [
            lax.dynamic_slice_in_dim(key_positions, (ctx ^ k) * row_count, row_count)
            for k in range(ctx_count)
        ]
    )
    place = (cosine, sine, by_distance[:, None], query_positions[None])

    bias_part = biases.shape[1]
    small_width = -(-bias_part // 128) * 128

    def padded(row):
        return jnp.pad(row, ((0, 0), (0, small_width - row.shape[1])))

    small_shard = jnp.concatenate(
        [padded(attend_gain), padded(biases), padded(mixer_gain), jnp.zeros((13, small_width), bf16)]
    )
    attn_shard = jnp.concatenate([projections[0], output_weight[0]], axis=1)

    def in_order(array):
        other = swap_sections(array)
        return jnp.where(is_first, array, other), jnp.where(is_first, other, array)

    def unit_columns(side):
        pieces = []
        for shard in range(fsdp_count):
            start = side * ff_width + shard * shard_units
            pieces.append(
                pick(
                    ctx,
                    [
                        expand_weight[0, :, start + k * units : start + (k + 1) * units]
                        for k in range(ctx_count)
                    ],
                )
            )
            if spare_units:
                pieces.append(jnp.zeros((shard_rows, spare_units), bf16))
        return jnp.concatenate(pieces, axis=1)

    expand_shard = pack_units(unit_columns(0), unit_columns(1))
    down_shard = lax.dynamic_slice_in_dim(down_weight[0], ctx * units, units)
    down_shard = jnp.pad(down_shard, ((0, spare_units), (0, 0)))

    def halves(array):
        size = array.shape[0] // 2
        low, high = array[:size], array[size:]
        own = jnp.where(is_first, low, high)
        other = swap_sections(jnp.where(is_first, high, low))
        return jnp.where(is_first, own, other), jnp.where(is_first, other, own)

    expand_pair = halves(expand_shard)
    down_pair = halves(down_shard)
    first_shard, second_shard = in_order(attn_shard)
    small_pair = jnp.concatenate(in_order(small_shard))

    def gather(piece):
        return lax.all_gather(piece, both, axis=0, tiled=True)

    expands, downs = [None, None], [None, None]
    expands[0], downs[0] = gather(expand_pair[0]), gather(down_pair[0])
    first_shard, small_pair = lax.optimization_barrier(
        (first_shard, small_pair, expand_pair[0], down_pair[0])
    )[:2]
    weights, vectors = collect(first_shard, small_pair, (shard_rows, bias_part, shard_rows))
    weights = [weights, None]
    expands[1], downs[1] = gather(expand_pair[1]), gather(down_pair[1])

    def layer_of(layer):
        return (layer, vectors, weights[layer], expands[layer], downs[layer])

    layers = []
    hidden = source
    stored = []
    sent = []
    for layer in range(2):
        layers.append(layer_of(layer))
        normed, queries, every_kv, lse, context, middle, second_normed, *fetched = attend(
            layers[layer], hidden, place, None if layer else second_shard
        )
        if fetched:
            weights[1] = fetched[0]
        kept = (hidden, normed, queries, every_kv, lse, context)
        hidden, blocks, kept_gate, kept_up = feed(layers[layer], second_normed, middle)
        sent.append(hidden)
        stored.append((middle, kept, blocks, kept_gate, kept_up))

    def scatter(array):
        return lax.psum_scatter(array, both, scatter_dimension=0, tiled=True)

    grad = upstream
    hidden_grads = [None, None]
    small_grads = [None, None]
    attn_grads = [None, None]
    for layer in (1, 0):
        middle, kept, blocks, kept_gate, kept_up = stored[layer]
        load = () if layer else (down_grad,)
        middle_grad, second_grad, expand_grad, down_grad, *summed = feed_back(
            layers[layer], middle, blocks, kept_gate, kept_up, grad, load
        )
        if layer:
            expand_one = scatter(expand_grad)
            load = ()
        else:
            expand_grad, expand_one = lax.optimization_barrier((expand_grad, expand_one))
            expand_zero = scatter(expand_grad)
            (down_one,) = summed
            load = (attn_grads[1], expand_one)
        hidden_grad, first_grad, offset_grad, attn_grads[layer], *summed = attend_back(
            layers[layer], kept, middle_grad, place, load
        )
        small_grads[layer] = jnp.concatenate([first_grad, offset_grad, second_grad], axis=1)[0]
        hidden_grads[layer] = hidden_grad
        grad = hidden_grad

    spare = -small_grads[0].shape[0] % model_width
    small_rows = [jnp.pad(vector, (0, spare)).reshape(-1, model_width) for vector in small_grads]
    small_count = small_rows[0].shape[0]
    rows_left = -2 * small_count % 8
    small_stack = jnp.pad(jnp.concatenate(small_rows), ((0, rows_left), (0, 0)))
    attn_one, expand_one = summed
    (
        grad_projections, grad_output, small_all, down_all, activations, input_grads, expand_all,
    ) = attn_sum(
        attn_grads[0], attn_one, small_stack, down_one, sent, hidden_grads,
        down_grad, expand_zero, expand_one, wide,
    )
    grad_expand = finish(expand_all, ff_width, units)
    grad_down = down_all[:, :units].astype(f32).reshape(shard_units, model_width)
    small_own = jnp.where(
        is_first, small_all[:small_count], small_all[small_count : 2 * small_count]
    ).reshape(-1)
    first_all, offset_all, second_all = (
        small_own[:model_width],
        small_own[model_width : model_width + wide],
        small_own[model_width + wide : 2 * model_width + wide],
    )
    pair_width = (wide - model_width) // 2

    def part(vector):
        size = vector.shape[0] // fsdp_count
        return lax.dynamic_slice_in_dim(vector, fsdp * size, size)[None]

    return (
        activations[None, :, None],
        input_grads[None, :, None],
        part(first_all),
        grad_projections[None],
        part(offset_all[: model_width + pair_width]),
        part(offset_all[model_width + pair_width :]),
        grad_output[None],
        part(second_all),
        grad_expand[None],
        grad_down[None],
    )


def solution(mesh):
    return jax.shard_map(
        per_device,
        mesh=mesh,
        in_specs=(
            P(None, FSDP, CTX, None),
            P(SECTION, FSDP),
            P(SECTION, FSDP, None),
            P(SECTION, FSDP),
            P(SECTION, FSDP, None),
            P(SECTION, FSDP),
            P(SECTION, FSDP, None),
            P(SECTION, FSDP, None),
            P(None, FSDP, None),
            P(None, FSDP, CTX, None),
        ),
        out_specs=(
            P(SECTION, None, FSDP, CTX, None),
            P(SECTION, None, FSDP, CTX, None),
            P(SECTION, FSDP),
            P(SECTION, FSDP, None),
            P(SECTION, FSDP),
            P(SECTION, FSDP),
            P(SECTION, FSDP, None),
            P(SECTION, FSDP),
            P(SECTION, FSDP, None),
            P(SECTION, FSDP, None),
        ),
        check_vma=False,
    )
```

```python
import functools

import jax
import jax.numpy as jnp
from jax import lax
from jax.experimental import pallas as pl
from jax.experimental.pallas import tpu as pltpu
from jax.sharding import PartitionSpec as P

HEAD_DIM = 64
SECTION, CTX, FSDP = "section", "ctx", "fsdp"

epsilon = 1e-06
theta_base = 1000000.0
masked_value = -1e30

bf16 = jnp.bfloat16
f32 = jnp.float32


def swap_sections(block):
    return lax.ppermute(block, SECTION, [(0, 1), (1, 0)])


def tables(positions_row):
    half_dim = HEAD_DIM // 2
    frequency = theta_base ** (-(jnp.arange(half_dim, dtype=f32) * 2.0) / HEAD_DIM)
    angles = positions_row.astype(f32)[:, None] * frequency[None, :]
    cosine, sine = jnp.cos(angles), jnp.sin(angles)
    return (
        jnp.concatenate([cosine] * 4, axis=-1),
        jnp.concatenate([-sine, sine, -sine, sine], axis=-1),
    )


def pick(index, options):
    chosen = options[0]
    for position in range(1, len(options)):
        chosen = jnp.where(index == position, options[position], chosen)
    return chosen


MESH = pl.DeviceIdType.MESH
VMEM = pltpu.VMEM
LIMIT = 56 * 1024 * 1024


def flip(index, distance):
    place = 1
    while place <= distance:
        if (distance // place) % 2:
            index = index + place - 2 * place * ((index // place) % 2)
        place *= 2
    return index


def place_of():
    return lax.axis_index(SECTION), lax.axis_index(CTX), lax.axis_index(FSDP)


def peer_of(distance):
    section, ctx, fsdp = place_of()
    return (section, flip(ctx, distance), fsdp)


def greet_all(devices):
    barrier = pltpu.get_barrier_semaphore()
    for device in devices:
        pl.semaphore_signal(barrier, inc=1, device_id=device, device_id_type=MESH)
    pl.semaphore_wait(barrier, len(devices))


def greet(count):
    greet_all([peer_of(k) for k in range(1, count)])


def send(source, target, send_sem, recv_sem, device):
    return pltpu.make_async_remote_copy(
        src_ref=source,
        dst_ref=target,
        send_sem=send_sem,
        recv_sem=recv_sem,
        device_id=device,
        device_id_type=MESH,
    )


def remote(source, target, send_sem, recv_sem, k):
    return send(source, target, send_sem.at[k], recv_sem.at[k], peer_of(k))


def matmul(left, right):
    return lax.dot_general(left, right, (((1,), (0,)), ((), ())), preferred_element_type=f32)


def matmul_nt(left, right):
    return lax.dot_general(left, right, (((1,), (1,)), ((), ())), preferred_element_type=f32)


def matmul_tn(left, right):
    return lax.dot_general(left, right, (((0,), (0,)), ((), ())), preferred_element_type=f32)


def tiles(size, step):
    return [(start, min(step, size - start)) for start in range(0, size, step)]


def row_scale(values):
    return lax.rsqrt(jnp.mean(values * values, axis=-1, keepdims=True) + epsilon)


def call(kernel, outs, scratch, cid, *args, far=(), far_outs=()):
    def spec(position, away):
        return pl.BlockSpec(memory_space=pl.ANY if position in away else VMEM)

    return pl.pallas_call(
        kernel,
        out_shape=[jax.ShapeDtypeStruct(shape, kind) for shape, kind in outs],
        in_specs=[spec(position, far) for position in range(len(args))],
        out_specs=[spec(position, far_outs) for position in range(len(outs))],
        scratch_shapes=scratch,
        compiler_params=pltpu.CompilerParams(
            collective_id=cid, has_side_effects=True, vmem_limit_bytes=LIMIT
        ),
    )(*args)


def dma(*shape):
    return pltpu.SemaphoreType.DMA(shape)


class Relay:
    def __init__(self, fsdp_count, source, spot, z_send, z_recv):
        self.count, self.source, self.spot = fsdp_count, source, spot
        self.z_send, self.z_recv = z_send, z_recv
        self.section, self.ctx, self.fsdp = place_of()
        self.hops = [(side, e) for e in range(1, fsdp_count) for side in (1, 0)]

    def device(self, side):
        step = 1 if side else self.count - 1
        return (self.section, self.ctx, lax.rem(self.fsdp + step, self.count))

    def goes_on(self, side):
        return self.fsdp < self.count - 1 if side else self.fsdp > 0

    def came(self, side, e):
        return self.fsdp >= e if side else self.fsdp < self.count - e

    def origin(self, side, e):
        return lax.rem(self.fsdp + (self.count - e if side else e), self.count)

    def copy(self, side, e):
        spot = self.spot(self.origin(side, e))
        source = spot if e else self.source
        return send(source, spot, self.z_send.at[side, e], self.z_recv.at[side, e + 1], self.device(side))

    def begin(self):
        for side in range(2):

            @pl.when(self.goes_on(side))
            def _():
                self.copy(side, 0).start()

    def each(self, step):
        for side, e in self.hops:
            pl.when(self.came(side, e))(functools.partial(step, side, e))

    def steps(self):
        return range(1, self.count)

    def take(self, side, e):
        spot = self.spot(self.origin(side, e))
        sems = self.z_send.at[side, e], self.z_recv.at[side, e]
        send(spot, spot, *sems, self.device(side)).wait_recv()
        if e < self.count - 1:

            @pl.when(self.goes_on(side))
            def _():
                self.copy(side, e).start()

    def sent(self):
        for side, e in [(0, 0), (1, 0)] + self.hops:
            if e < self.count - 1:

                @pl.when(jnp.logical_and(self.came(side, e), self.goes_on(side)))
                def _():
                    self.copy(side, e).wait_send()


class Collect:
    def __init__(self, ctx_count, fsdp_count, shard_ref, w_ref, sems):
        self.shard_ref, self.w_ref = shard_ref, w_ref
        z_send, z_recv, self.y_send, self.y_recv, self.v_send, self.v_recv, self.own_sem = sems
        self.places = range(1, ctx_count)
        self.fsdp_count = fsdp_count
        self.section, self.ctx, self.fsdp = place_of()
        self.sister = (1 - self.section, self.ctx, self.fsdp)
        self.rows, width = shard_ref.shape
        self.piece = width // (2 * ctx_count)
        self.mine = pl.ds(pl.multiple_of(self.fsdp * self.rows, self.rows), self.rows)
        own = shard_ref.at[:, self.columns(self.ctx, self.section)]
        self.line = Relay(
            fsdp_count, own, lambda shard: self.spot(shard, self.ctx, self.section), z_send, z_recv
        )
        self.ahead = [
            (self.section, self.ctx, lax.rem(self.fsdp + d, fsdp_count)) for d in range(1, fsdp_count)
        ]
        self.friends = self.ahead + [peer_of(k) for k in self.places] + [self.sister]

    def columns(self, where, core):
        return pl.ds(pl.multiple_of((where * 2 + core) * self.piece, self.piece), self.piece)

    def spot(self, shard, where, core):
        rows = pl.ds(pl.multiple_of(shard * self.rows, self.rows), self.rows)
        return self.w_ref.at[rows, self.columns(where, core)]

    def block(self, side, e, where, core):
        return self.spot(self.line.origin(side, e), where, core)

    def kept(self):
        return pltpu.make_async_copy(self.shard_ref, self.w_ref.at[self.mine], self.own_sem.at[0])

    def spread(self, side, e, k):
        source = self.block(side, e, self.ctx, self.section)
        device = peer_of(k) if k else self.sister
        i = side * self.fsdp_count + e
        return send(source, source, self.y_send.at[i, k], self.y_recv.at[i, k], device)

    def passed(self, side, e, k):
        source = self.block(side, e, flip(self.ctx, k), self.section)
        i = side * self.fsdp_count + e
        return send(source, source, self.v_send.at[i, k], self.v_recv.at[i, k], self.sister)

    def begin(self):
        self.line.begin()
        self.kept().start()

    def relay(self, which):
        def step(side, e):
            if e == which:
                self.line.take(side, e)
                for k in (*self.places, 0):
                    self.spread(side, e, k).start()

        self.line.each(step)

    def hand(self):
        def step(side, e):
            i = side * self.fsdp_count + e
            for k in self.places:
                came = self.block(side, e, flip(self.ctx, k), self.section)
                send(came, came, self.y_send.at[i, k], self.y_recv.at[i, k], self.sister).wait_recv()
                self.passed(side, e, k).start()

        self.line.each(step)

    def finish(self):
        def arrivals(side, e):
            i = side * self.fsdp_count + e
            for k in (0, *self.places):
                came = self.block(side, e, flip(self.ctx, k), 1 - self.section)
                recv = (self.v_recv if k else self.y_recv).at[i, k]
                send(came, came, self.v_send.at[i, k], recv, self.sister).wait_recv()

        def sent(side, e):
            self.spread(side, e, 0).wait_send()
            for k in self.places:
                self.spread(side, e, k).wait_send()
                self.passed(side, e, k).wait_send()

        self.line.each(arrivals)
        self.line.each(sent)
        self.line.sent()
        self.kept().wait()


def collect_sems(ctx_count, fsdp_count):
    line = dma(2, fsdp_count)
    table = dma(2 * fsdp_count, ctx_count)
    return [line, line, table, table, table, table, dma(1)]


class Line:
    def __init__(self, fsdp_count, piece_ref, out_ref, sems):
        self.piece_ref, self.out_ref = piece_ref, out_ref
        z_send, z_recv, self.v_send, self.v_recv, self.own_sem = sems
        self.section, self.ctx, self.fsdp = place_of()
        self.count = fsdp_count
        self.rows = piece_ref.shape[0]
        cut = -(-self.rows // 32) * 16
        self.parts = ((0, cut), (cut, self.rows - cut))
        self.sister = (1 - self.section, self.ctx, self.fsdp)
        self.lines = [
            Relay(
                fsdp_count,
                piece_ref.at[pl.ds(start, size)],
                functools.partial(self.spot, core),
                z_send,
                z_recv,
            )
            for core, (start, size) in enumerate(self.parts)
        ]
        self.ahead = [
            (self.section, self.ctx, lax.rem(self.fsdp + d, fsdp_count)) for d in range(1, fsdp_count)
        ]

    def spot(self, core, shard):
        start, size = self.parts[core]
        return self.out_ref.at[pl.ds(pl.multiple_of(shard * self.rows + start, 16), size)]

    def passed(self, core, side, e):
        spot = self.spot(core, self.lines[core].origin(side, e))
        i = side * self.count + e
        return send(spot, spot, self.v_send.at[i], self.v_recv.at[i], self.sister)

    def kept(self):
        start = pl.multiple_of(self.fsdp * self.rows, 16)
        return pltpu.make_async_copy(
            self.piece_ref, self.out_ref.at[pl.ds(start, self.rows)], self.own_sem.at[0]
        )

    def each_core(self, step):
        for core in range(2):
            pl.when(self.section == core)(functools.partial(step, core))

    def begin(self):
        self.each_core(lambda core: self.lines[core].begin())
        self.kept().start()

    def relay(self, which):
        def step(core):
            def take(side, e):
                if e == which:
                    self.lines[core].take(side, e)
                    self.passed(core, side, e).start()

            self.lines[core].each(take)

        self.each_core(step)

    def end(self):
        def step(core):
            line = self.lines[core]
            line.each(lambda side, e: self.passed(1 - core, side, e).wait_recv())
            line.each(lambda side, e: self.passed(core, side, e).wait_send())
            line.sent()

        self.each_core(step)
        self.kept().wait()


def line_sems(fsdp_count):
    hops = dma(2 * fsdp_count)
    return [dma(2, fsdp_count), dma(2, fsdp_count), hops, hops, dma(1)]


def collect_kernel(
    ctx_count, fsdp_count, sizes, low_ref, high_ref, small_ref, low_w_ref, high_w_ref, vectors_ref,
    smalls_ref, s_send, s_recv, *sems
):
    half = len(sems) // 2
    steps = Collect(ctx_count, fsdp_count, low_ref, low_w_ref, sems[:half])
    later = Collect(ctx_count, fsdp_count, high_ref, high_w_ref, sems[half:])

    shards = range(1, fsdp_count)

    def small(d):
        target = smalls_ref.at[steps.fsdp]
        return send(small_ref, target, s_send.at[d], s_recv.at[d], steps.ahead[d - 1])

    greet_all(steps.friends)
    steps.begin()
    later.begin()
    for d in shards:
        small(d).start()
    smalls_ref[steps.fsdp] = small_ref[...]
    for e in steps.line.steps():
        steps.relay(e)
        later.relay(e)
    steps.hand()
    later.hand()
    steps.finish()
    later.finish()
    for d in shards:
        came = smalls_ref.at[lax.rem(steps.fsdp + fsdp_count - d, fsdp_count)]
        send(came, came, s_send.at[d], s_recv.at[d], steps.sister).wait_recv()
    for shard in range(fsdp_count):
        rows = smalls_ref[shard].astype(f32)
        for layer in range(2):
            for i, size in enumerate(sizes):
                row = 4 * layer + i
                vectors_ref[row : row + 1, shard * size : (shard + 1) * size] = rows[
                    16 * layer + i : 16 * layer + i + 1, :size
                ]
    for d in shards:
        small(d).wait_send()


def collect(low, high, small, sizes):
    ctx_count, fsdp_count = lax.axis_size(CTX), lax.axis_size(FSDP)
    rows, width = low.shape
    whole = ((fsdp_count * rows, width), bf16)
    return call(
        functools.partial(collect_kernel, ctx_count, fsdp_count, sizes),
        [whole, whole, ((8, fsdp_count * max(sizes)), f32)],
        [VMEM((fsdp_count,) + small.shape, bf16), dma(fsdp_count), dma(fsdp_count)]
        + collect_sems(ctx_count, fsdp_count) * 2,
        5,
        low, high, small, far_outs=(0, 1),
    )


class SquareSum:
    def __init__(self, ctx_count, grad_ref, a_ref, b_out, b_in, sems):
        self.grad_ref, self.a_ref, self.b_out = grad_ref, a_ref, b_out
        self.a_send, self.a_recv, b_send, b_recv = sems
        self.parts = Parts(ctx_count, b_out, b_in, b_send, b_recv)
        self.order = (*range(ctx_count - 1, 0, -1), 0)
        self.section, self.ctx, fsdp = place_of()
        self.sister = (1 - self.section, self.ctx, fsdp)
        self.piece = grad_ref.shape[1] // (2 * ctx_count)

    def columns(self, k, core):
        start = (flip(self.ctx, k) * 2 + core) * self.piece
        return pl.ds(pl.multiple_of(start, self.piece), self.piece)

    def chip(self, k):
        source = self.grad_ref.at[:, self.columns(k, 1 - self.section)]
        return send(source, self.a_ref.at[k], self.a_send.at[k], self.a_recv.at[k], self.sister)

    def begin(self):
        for k in self.order:
            self.chip(k).start()

    def middle(self):
        for k in self.order:
            self.chip(k).wait_recv()
            own = self.grad_ref[:, self.columns(k, self.section)].astype(f32)
            total = own + self.a_ref[k].astype(f32)
            if k:
                self.parts.put(k, total)
            else:
                self.b_out[0] = total.astype(bf16)

    def merge(self):
        self.parts.merge()

    def end(self):
        return self.parts.total(self.b_out[0].astype(f32)).astype(bf16)

    def sent(self):
        for k in self.order:
            self.chip(k).wait_send()
        self.parts.sent()


def square_scratch(ctx_count, grad):
    width, both = grad.shape
    piece = VMEM((ctx_count, width, both // (2 * ctx_count)), bf16)
    sems = [dma(ctx_count), dma(ctx_count), dma(ctx_count, 2), dma(ctx_count, 2)]
    return [piece, piece, piece] + sems


def every_owner(ctx_count, layer, start_or_wait, sources, targets, send_sem, recv_sem):
    section, ctx, fsdp = place_of()
    for k in range(ctx_count):
        device = (layer, flip(ctx, k), fsdp)

        def go():
            for i, (source, target) in enumerate(zip(sources, targets)):
                copy = send(
                    source,
                    target.at[ctx, section],
                    send_sem.at[i, k],
                    recv_sem.at[i, section, k],
                    device,
                )
                copy.start() if start_or_wait == "start" else copy.wait_send()

        pl.when(section != layer)(go) if k == 0 else go()


def from_owners(ctx_count, layer, targets, send_sem, recv_sem):
    section, ctx, fsdp = place_of()
    for core in range(2):
        for k in range(ctx_count):
            if core == layer and k == 0:
                continue

            def go():
                for i, target in enumerate(targets):
                    came = target.at[flip(ctx, k), core]
                    send(
                        came, came, send_sem.at[i, k], recv_sem.at[i, core, k], (1 - section, ctx, fsdp)
                    ).wait_recv()

            pl.when(section == layer)(go)


class Owners:
    def __init__(self, ctx_count, layer, sources, targets, cuts, sems):
        self.layer, self.targets = layer, targets
        self.send_sem, self.recv_sem, self.onward_sem = sems
        self.section, self.ctx, self.fsdp = place_of()
        self.count, self.square = ctx_count, ctx_count == 4
        self.pieces = []
        for i, source in enumerate(sources):
            for h in range(2) if self.square else (0,):
                cut = cuts[i][h] if self.square else None
                self.pieces.append((source.at[cut] if self.square else source, i, cut, h))
        self.all = range(len(self.pieces))
        self.early = [(i, 2 - self.pieces[i][3]) for i in self.all if self.square]
        self.keeper = self.section == layer

    def spot(self, i, k, core):
        _, which, cut, _ = self.pieces[i]
        spot = self.targets[which].at[flip(self.ctx, k), core]
        return spot if cut is None else spot.at[cut]

    def peer(self, k):
        return (self.layer, flip(self.ctx, k), self.fsdp)

    def own(self, i, k):
        return send(
            self.pieces[i][0],
            self.spot(i, 0, self.section),
            self.send_sem.at[i, k],
            self.recv_sem.at[i, self.section, k],
            self.peer(k),
        )

    def onward(self, i, core):
        came = 2 - self.pieces[i][3]
        spot = self.spot(i, came, core)
        return send(
            spot, spot, self.onward_sem.at[i, core], self.recv_sem.at[i, core, 3], self.peer(3 - came)
        )

    def outgoing(self):
        if self.square:
            late = [(i, 3 - k) for i, k in self.early]
            return self.early + late
        return [(i, k) for k in range(1, self.count) for i in self.all]

    def begin(self):
        for i, k in self.outgoing():
            self.own(i, k).start()

        @pl.when(jnp.logical_not(self.keeper))
        def _():
            for i in self.all:
                self.own(i, 0).start()

    def arrival(self, i, core, k):
        spot = self.spot(i, k, core)
        recv = self.recv_sem.at[i, core, k]
        sister = (1 - self.section, self.ctx, self.fsdp)
        send(spot, spot, self.send_sem.at[i, k], recv, sister).wait_recv()

    def relay(self):
        if self.square:

            @pl.when(self.keeper)
            def _():
                for i, k in self.early:
                    for core in range(2):
                        self.arrival(i, core, k)
                        self.onward(i, core).start()

    def end(self):
        @pl.when(self.keeper)
        def _():
            for k in range(self.count):
                for core in range(2):
                    for i in self.all:
                        if (i, k) not in self.early and (k or core != self.layer):
                            self.arrival(i, core, k)
            if self.square:
                for i in self.all:
                    for core in range(2):
                        self.onward(i, core).wait_send()

        @pl.when(jnp.logical_not(self.keeper))
        def _():
            for i in self.all:
                self.own(i, 0).wait_send()

        for i, k in self.outgoing():
            self.own(i, k).wait_send()


def row_halves(rows):
    cut = rows // 2 // 16 * 16
    return (pl.ds(0, cut), pl.ds(cut, rows - cut))


def column_halves(width):
    cut = -(-width // 256) * 128
    return ((slice(None), pl.ds(0, cut)), (slice(None), pl.ds(cut, width - cut)))


def owner_sems(ctx_count):
    return [dma(4, ctx_count), dma(4, 2, ctx_count), dma(4, 2)]


class LineSum:
    def __init__(self, fsdp_count, grad_ref, done_ref, refs):
        self.own_ref, self.a_ref, self.sum_ref, self.in_ref, self.a_sem, self.z_send, self.z_recv = refs
        self.grad_ref, self.done_ref = grad_ref, done_ref
        self.section, self.ctx, self.fsdp = place_of()
        self.fsdp_count = fsdp_count
        self.group = fsdp_count // 2
        self.units = grad_ref.shape[0] // fsdp_count
        self.sister = (1 - self.section, self.ctx, self.fsdp)
        self.holds = self.fsdp // self.group == self.section

    def part(self, core):
        size = self.group * self.units
        return self.grad_ref.at[pl.ds(pl.multiple_of(core * size, size), size)]

    def load(self):
        return pltpu.make_async_copy(self.part(self.section), self.own_ref, self.a_sem.at[2])

    def chip(self):
        source = self.part(1 - self.section)
        return send(source, self.a_ref, self.a_sem.at[0], self.a_sem.at[1], self.sister)

    def line(self, j):
        device = (self.section, self.ctx, self.section * self.group + j)
        source = self.sum_ref.at[pl.ds(j * self.units, self.units)]
        return send(source, self.in_ref.at[self.fsdp], self.z_send.at[j], self.z_recv.at[self.fsdp], device)

    def elsewhere(self, j):
        return pl.when(self.section * self.group + j != self.fsdp)

    def begin(self):
        self.chip().start()
        self.load().start()

    def middle(self):
        self.load().wait()
        self.chip().wait_recv()
        self.sum_ref[...] = (self.own_ref[...].astype(f32) + self.a_ref[...].astype(f32)).astype(bf16)
        for j in range(self.group):

            @self.elsewhere(j)
            def _():
                self.line(j).start()

    def end(self):
        @pl.when(self.holds)
        def _():
            start = lax.rem(self.fsdp, self.group) * self.units
            total = self.sum_ref[pl.ds(pl.multiple_of(start, self.units), self.units)].astype(f32)
            for d in range(1, self.fsdp_count):
                came = lax.rem(self.fsdp + d, self.fsdp_count)
                spot = self.in_ref.at[came]
                send(spot, spot, self.z_send.at[0], self.z_recv.at[came], self.sister).wait_recv()
                total = total + self.in_ref[came].astype(f32)
            self.done_ref[...] = total.astype(bf16)

    def sent(self):
        self.chip().wait_send()
        for j in range(self.group):

            @self.elsewhere(j)
            def _():
                self.line(j).wait_send()


def line_scratch(fsdp_count, grad):
    units, width = grad.shape
    half = VMEM((units // 2, width), bf16)
    shards = VMEM((fsdp_count, units // fsdp_count, width), bf16)
    return [half, half, half, shards, dma(3), dma(fsdp_count), dma(fsdp_count)]


class Handout:
    def __init__(self, ctx_count, fsdp_count, layer, done_ref, all_ref, refs):
        self.own_sem, self.o_send, self.o_recv, self.n_send = refs
        self.layer, self.done_ref, self.all_ref = layer, done_ref, all_ref
        self.section, self.ctx, self.fsdp = place_of()
        self.count, self.square = ctx_count, ctx_count == 4
        self.halves = column_halves(done_ref.shape[1])
        self.holder = self.fsdp // (fsdp_count // 2)
        self.holds = self.section == self.holder
        self.keeps = self.section == layer
        self.away = jnp.logical_and(self.holds, jnp.logical_not(self.keeps))
        self.at_home = jnp.logical_and(self.holds, self.keeps)
        self.early = ((1, 1), (2, 0)) if self.square else ()
        late = ((1, 0), (2, 1)) if self.square else ()
        pairs = [(k, h) for k in range(1, ctx_count) for h in range(2)]
        self.sends = (*self.early, *late) if self.square else pairs

    def spot(self, k, h):
        return self.all_ref.at[flip(self.ctx, k)].at[self.halves[h]]

    def peer(self, k):
        return (self.layer, flip(self.ctx, k), self.fsdp)

    def out(self, k, h):
        source = self.done_ref.at[self.halves[h]]
        return send(source, self.spot(0, h), self.o_send.at[k, h], self.o_recv.at[k, h], self.peer(k))

    def onward(self, h):
        came = 1 if h else 2
        spot = self.spot(came, h)
        return send(spot, spot, self.n_send.at[h], self.o_recv.at[3, h], self.peer(3 - came))

    def arrival(self, k, h):
        spot = self.spot(k, h)
        sister = (1 - self.section, self.ctx, self.fsdp)
        send(spot, spot, self.o_send.at[k, h], self.o_recv.at[k, h], sister).wait_recv()

    def kept(self):
        return pltpu.make_async_copy(self.done_ref, self.all_ref.at[self.ctx], self.own_sem.at[0])

    def begin(self):
        @pl.when(self.holds)
        def _():
            for k, h in self.sends:
                self.out(k, h).start()

        @pl.when(self.away)
        def _():
            for h in range(2):
                self.out(0, h).start()

        @pl.when(self.at_home)
        def _():
            self.kept().start()

    def relay(self):
        @pl.when(self.keeps)
        def _():
            for k, h in self.early:
                self.arrival(k, h)
                self.onward(h).start()

    def end(self):
        @pl.when(self.keeps)
        def _():
            for k in range(1, self.count):
                for h in range(2):
                    if (k, h) not in self.early:
                        self.arrival(k, h)
            for _, h in self.early:
                self.onward(h).wait_send()

        @pl.when(jnp.logical_and(self.keeps, jnp.logical_not(self.holds)))
        def _():
            for h in range(2):
                self.arrival(0, h)

        @pl.when(self.holds)
        def _():
            for k, h in self.sends:
                self.out(k, h).wait_send()

        @pl.when(self.away)
        def _():
            for h in range(2):
                self.out(0, h).wait_send()

        @pl.when(self.at_home)
        def _():
            self.kept().wait()


def handout_sems(ctx_count):
    return [dma(1), dma(ctx_count, 2), dma(ctx_count, 2), dma(2)]


def chip_square(ctx_count):
    section, ctx, fsdp = place_of()
    return [
        (section if same else 1 - section, flip(ctx, k), fsdp)
        for k in range(ctx_count)
        for same in (True, False)
        if k or not same
    ]


def turn_tile(values):
    lane = lax.broadcasted_iota(jnp.int32, values.shape, 1)
    width = values.shape[1]
    half = HEAD_DIM // 2
    ahead = pltpu.roll(values, width - half, 1)
    behind = pltpu.roll(values, half, 1)
    return jnp.where(lane % HEAD_DIM < half, ahead, behind)


def head_in_group(tile, head, group):
    lane = lax.broadcasted_iota(jnp.int32, tile.shape, 1)
    values = tile.astype(f32)
    moved = values if head % 2 == group else pltpu.roll(values, HEAD_DIM, 1)
    return jnp.where(lane // HEAD_DIM == group, moved, 0.0).astype(bf16)


def attend_kernel(count, fsdp_count, layer, *refs):
    x_ref, vectors_ref, w_ref, cos_ref, sin_ref, kpos_ref, qpos_ref = refs[:7]
    refs = refs[7:]
    if layer:
        shard_ref, *refs = refs
    normed_ref, q_ref, kv_ref, lse_ref, ctx_ref, mid_ref, low2_ref = refs[:7]
    refs = refs[7:]
    if layer:
        next_ref, *refs = refs
    mask_ref, s_ref, p_ref, vt_ref, ctxf_ref, send_sem, recv_sem, *sems = refs
    rows, width = x_ref.shape
    pair = kv_ref.shape[2] // 2
    wide = width + 2 * pair
    heads = width // HEAD_DIM
    group_size = heads // (pair // HEAD_DIM)
    if layer:
        line = Line(fsdp_count, shard_ref, next_ref, sems)
        greet_all([peer_of(k) for k in range(1, count)] + [line.sister] + line.ahead)
        line.begin()
    else:
        greet(count)
    x = x_ref[...].astype(f32)
    gain1, bias, gain2 = (vectors_ref[4 * layer + i : 4 * layer + i + 1, :] for i in range(3))
    normed = (x * row_scale(x) * gain1[:, :width]).astype(bf16)
    normed_ref[...] = normed
    cos, sin = cos_ref[...], sin_ref[...]
    kv = matmul(normed, w_ref[:, width:wide]) + bias[:, width:wide]
    keys = kv[:, :pair]
    kv_ref[0, :, :pair] = (keys * cos + turn_tile(keys) * sin).astype(bf16)
    kv_ref[0, :, pair:] = kv[:, pair:].astype(bf16)
    for k in range(1, count):
        remote(kv_ref.at[0], kv_ref.at[k], send_sem, recv_sem, k).start()
    merged = matmul(normed, w_ref[:, :width]) + bias[:, :width]
    for start, size in tiles(width, 2 * HEAD_DIM):
        part = merged[:, start : start + size]
        turned_part = (part * cos + turn_tile(part) * sin) * HEAD_DIM ** (-0.5)
        q_ref[:, start : start + size] = turned_part.astype(bf16)
    for k in range(count):
        allowed = kpos_ref[k * rows : (k + 1) * rows, :] <= qpos_ref[...]
        mask_ref[k] = jnp.where(allowed, 0.0, masked_value)
    for k in range(count):
        if k:
            remote(kv_ref.at[0], kv_ref.at[k], send_sem, recv_sem, k).wait_recv()
        vt_ref[:, k * rows : (k + 1) * rows] = kv_ref[k, :, pair:].astype(f32).T.astype(bf16)

    for head in range(heads):
        group = head // group_size
        start = head // 2 * (2 * HEAD_DIM)
        query = head_in_group(q_ref[:, start : start + 2 * HEAD_DIM], head, group)
        top = None
        for k in range(count):
            scores = matmul_nt(kv_ref[k, :, :pair], query) + mask_ref[k]
            s_ref[k] = scores
            here = jnp.max(scores, axis=0, keepdims=True)
            top = here if top is None else jnp.maximum(top, here)
        total = None
        for k in range(count):
            weight = jnp.exp(s_ref[k] - top)
            here = jnp.sum(weight, axis=0, keepdims=True)
            total = here if total is None else total + here
            p_ref[k * rows : (k + 1) * rows, :] = weight.astype(bf16)
        value_rows = vt_ref[group * HEAD_DIM : (group + 1) * HEAD_DIM, :]
        context = matmul(value_rows, p_ref[...]) * (1.0 / total)
        ctxf_ref[head * HEAD_DIM : (head + 1) * HEAD_DIM, :] = context
        lse_ref[head : head + 1, :] = top + jnp.log(total)
        for e in range(1, fsdp_count - 1) if layer else ():
            if head == e * heads // fsdp_count + 1:
                line.relay(e)
    context = ctxf_ref[...]
    ctx_ref[...] = context.astype(bf16)
    middle = x + matmul(context.T.astype(bf16), w_ref[:, wide:])
    mid_ref[...] = middle
    low2_ref[...] = (middle * row_scale(middle) * gain2[:, :width]).astype(bf16)
    for k in range(1, count):
        remote(kv_ref.at[0], kv_ref.at[k], send_sem, recv_sem, k).wait_send()
    if layer:
        line.relay(fsdp_count - 1)
        line.end()


def attend(layer, hidden, place, piece=()):
    index, vectors, weights = layer[:3]
    cosine, sine, key_positions, query_positions = place
    rows, width = hidden.shape
    count = lax.axis_size(CTX)
    wide = weights.shape[1] - width
    pair = (wide - width) // 2
    keys = count * rows
    heads = width // HEAD_DIM
    fsdp_count = lax.axis_size(FSDP)
    args = (hidden, vectors, weights, cosine, sine, key_positions, query_positions)
    return call(
        functools.partial(attend_kernel, count, fsdp_count, index),
        [
            ((rows, width), bf16),
            ((rows, width), bf16),
            ((count, rows, 2 * pair), bf16),
            ((-(-heads // 8) * 8, rows), f32),
            ((width, rows), bf16),
            ((rows, width), f32),
            ((rows, width), bf16),
        ]
        + [((fsdp_count * array.shape[0], width), bf16) for array in piece],
        [
            VMEM((count, rows, rows), f32),
            VMEM((count, rows, rows), f32),
            VMEM((keys, rows), bf16),
            VMEM((pair, keys), bf16),
            VMEM((width, rows), f32),
            dma(count),
            dma(count),
        ]
        + line_sems(fsdp_count) * len(piece),
        1 if index else 10,
        *args, *piece,
        far_outs=(7,) * len(piece),
    )


def attend_back_kernel(count, layer, carried, *refs):
    (
        dmid_ref, x_ref, vectors_ref, w_ref, cos_ref, sin_ref, kpos_ref, qpos_ref,
        normed_ref, q_ref, kv_ref, lse_ref, ctx_ref,
    ) = refs[:13]
    refs = refs[13:]
    (load_ref, expand_ref), refs = (refs[:2], refs[2:]) if carried else ((None, None), refs)
    dh_ref, gain_ref, bias_ref, grad_ref = refs[:4]
    refs = refs[4:]
    (summed_ref, expand_all_ref), refs = (refs[:2], refs[2:]) if carried else ((None, None), refs)
    (
        mask_ref, p_ref, dp_ref, ds_ref, kt_ref, dctx_ref, dq_ref, dkv_ref, out_ref, in_ref,
        merged_ref, low_ref, send_sem, recv_sem, *scratch,
    ) = refs
    rows, width = x_ref.shape
    pair = kv_ref.shape[2] // 2
    wide = width + 2 * pair
    heads = width // HEAD_DIM
    group_size = heads // (pair // HEAD_DIM)
    if carried:
        section, ctx, _ = place_of()
        steps = SquareSum(count, load_ref, *scratch[:3], scratch[3:7])
        halves = [row_halves(expand_ref.shape[0])]
        owners = Owners(count, 1, [expand_ref], [expand_all_ref], halves, scratch[7:10])
        kept = pltpu.make_async_copy(expand_ref, expand_all_ref.at[ctx, section], scratch[10].at[0])
        greet_all(chip_square(count))
        steps.begin()
        owners.begin()

        @pl.when(owners.keeper)
        def _():
            kept.start()

    else:
        greet(count)
    low = dmid_ref[...].astype(bf16)
    low_ref[...] = low
    dctx = matmul_nt(low, w_ref[:, wide:]).astype(bf16)
    dctx_ref[...] = dctx
    for k in range(count):
        allowed = kpos_ref[k * rows : (k + 1) * rows, :] <= qpos_ref[...]
        mask_ref[k] = jnp.where(allowed, 0.0, masked_value)
        kt_ref[:, k * rows : (k + 1) * rows] = kv_ref[k, :, :pair].astype(f32).T.astype(bf16)
    dkv_ref[...] = jnp.zeros_like(dkv_ref)

    for head in range(heads):
        group = head // group_size
        start = head // 2 * (2 * HEAD_DIM)
        query = head_in_group(q_ref[:, start : start + 2 * HEAD_DIM], head, group)
        upstream = head_in_group(dctx_ref[:, start : start + 2 * HEAD_DIM], head, group)
        lse = lse_ref[head : head + 1, :]
        delta = None
        for k in range(count):
            scores = matmul_nt(kv_ref[k, :, :pair], query) + mask_ref[k]
            weight = jnp.exp(scores - lse)
            weight_grad = matmul_nt(kv_ref[k, :, pair:], upstream)
            p_ref[k] = weight
            dp_ref[k] = weight_grad
            dkv_ref[k, :, pair:] += matmul(weight.astype(bf16), upstream)
            here = jnp.sum(weight * weight_grad, axis=0, keepdims=True)
            delta = here if delta is None else delta + here
        for k in range(count):
            score_grad = (p_ref[k] * (dp_ref[k] - delta)).astype(bf16)
            ds_ref[k * rows : (k + 1) * rows, :] = score_grad
            dkv_ref[k, :, :pair] += matmul(score_grad, query)
        key_rows = kt_ref[group * HEAD_DIM : (group + 1) * HEAD_DIM, :]
        dq_ref[head * HEAD_DIM : (head + 1) * HEAD_DIM, :] = (
            matmul(key_rows, ds_ref[...]) * HEAD_DIM ** (-0.5)
        )
        if carried and head == heads // 5:
            steps.middle()
        if carried and head == heads // 3:
            owners.relay()
        if carried and head == heads * 2 // 3:
            steps.merge()
    for k in range(1, count):
        out_ref[k] = dkv_ref[k].astype(bf16)
        remote(out_ref.at[k], in_ref.at[k], send_sem, recv_sem, k).start()
    cos, sin = cos_ref[...], sin_ref[...]
    dq = dq_ref[...].T

    def unturn(part):
        return (part * cos - turn_tile(part) * sin).astype(bf16)

    for start, size in tiles(width, 2 * HEAD_DIM):
        merged_ref[:, start : start + size] = unturn(dq[:, start : start + size])
    grad_ref[:, wide:] = matmul(ctx_ref[...], low_ref[...]).astype(bf16)
    normed = normed_ref[...]

    def project_grad(first, last):
        for start, size in tiles(last - first, 512):
            cut = slice(first + start, first + start + size)
            grad_ref[:, cut] = matmul_tn(normed, merged_ref[:, cut]).astype(bf16)

    project_grad(0, width)
    normed_grad = matmul_nt(merged_ref[:, :width], w_ref[:, :width])
    total = dkv_ref[0]
    for k in range(1, count):
        remote(out_ref.at[k], in_ref.at[k], send_sem, recv_sem, k).wait_recv()
        total = total + in_ref[k].astype(f32)
    merged_ref[:, width : width + pair] = unturn(total[:, :pair])
    merged_ref[:, width + pair :] = total[:, pair:].astype(bf16)
    project_grad(width, wide)
    normed_grad = normed_grad + matmul_nt(merged_ref[:, width:], w_ref[:, width:wide])
    bias_ref[...] = jnp.sum(merged_ref[...].astype(f32), axis=0, keepdims=True)
    x = x_ref[...].astype(f32)
    scale = row_scale(x)
    gain_ref[...] = jnp.sum(normed_grad * x * scale, axis=0, keepdims=True)
    scaled = normed_grad * vectors_ref[4 * layer : 4 * layer + 1, :width]
    mean = jnp.mean(scaled * x, axis=-1, keepdims=True)
    hidden_grad = dmid_ref[...] + scale * scaled - x * (scale * scale * scale * mean)
    dh_ref[...] = hidden_grad.astype(dh_ref.dtype)
    for k in range(1, count):
        remote(out_ref.at[k], in_ref.at[k], send_sem, recv_sem, k).wait_send()
    if carried:
        summed_ref[...] = steps.end()
        steps.sent()
        owners.end()

        @pl.when(owners.keeper)
        def _():
            kept.wait()


def attend_back(layer, kept, middle_grad, place, load=()):
    index, vectors, weights = layer[:3]
    cosine, sine, key_positions, query_positions = place
    hidden, normed, queries, every_kv, lse, context = kept
    rows, width = hidden.shape
    count = lax.axis_size(CTX)
    wide = weights.shape[1] - width
    pair = (wide - width) // 2
    keys = count * rows
    carried = bool(load)
    args = (
        middle_grad, hidden, vectors, weights, cosine, sine, key_positions, query_positions,
        normed, queries, every_kv, lse, context,
    )
    return call(
        functools.partial(attend_back_kernel, count, index, carried),
        [
            ((rows, width), bf16 if index else f32),
            ((1, width), f32),
            ((1, wide), f32),
            ((width, wide + width), bf16),
        ]
        + (
            [((width, (wide + width) // (2 * count)), bf16), ((count, 2) + load[1].shape, bf16)]
            if carried
            else []
        ),
        [
            VMEM((count, rows, rows), f32),
            VMEM((count, rows, rows), f32),
            VMEM((count, rows, rows), f32),
            VMEM((keys, rows), bf16),
            VMEM((pair, keys), bf16),
            VMEM((rows, width), bf16),
            VMEM((width, rows), f32),
            VMEM((count, rows, 2 * pair), f32),
            VMEM((count, rows, 2 * pair), bf16),
            VMEM((count, rows, 2 * pair), bf16),
            VMEM((rows, wide), bf16),
            VMEM((rows, width), bf16),
            dma(count),
            dma(count),
        ]
        + (square_scratch(count, load[0]) + owner_sems(count) + [dma(1)] if carried else []),
        6 if carried else 2,
        *args, *load,
        far_outs=(5,) if carried else (),
    )


def unit_chunks(units):
    main = units // 128 * 128
    chunks = [(start, main + start, start, size) for start, size in tiles(main, 512)]
    if units > main:
        chunks.append((2 * main, main + units, main, units - main))
    return chunks


def pack_units(gate, up):
    main = gate.shape[1] // 128 * 128
    return jnp.concatenate([gate[:, :main], up[:, :main], gate[:, main:], up[:, main:]], axis=1)


def unpack_units(packed):
    units = packed.shape[-1] // 2
    main = units // 128 * 128
    if units == main:
        return packed[..., :main], packed[..., main:]
    gate = jnp.concatenate([packed[..., :main], packed[..., 2 * main : main + units]], axis=-1)
    up = jnp.concatenate([packed[..., main : 2 * main], packed[..., main + units :]], axis=-1)
    return gate, up


class Rows:
    def __init__(self, count, own_ref, slots_ref, send_sem, recv_sem):
        self.own_ref, self.slots_ref = own_ref, slots_ref
        self.send_sem, self.recv_sem = send_sem, recv_sem
        self.count, self.square = count, count == 4
        self.half = own_ref.shape[0] // 2

    def rows(self, h):
        return pl.ds(h * self.half, self.half)

    def copy(self, source, k, h, peer):
        target = self.slots_ref.at[k, self.rows(h)]
        return send(source, target, self.send_sem.at[k, h], self.recv_sem.at[k, h], peer_of(peer))

    def own(self, k, h):
        return self.copy(self.own_ref.at[self.rows(h)], k, h, k)

    def onward(self, h):
        came = 1 if h else 2
        return self.copy(self.slots_ref.at[came, self.rows(h)], 3, h, 3 - came)

    def order(self):
        if self.square:
            return [(1, 1), (2, 0), (1, 0), (2, 1)]
        return [(k, h) for k in range(1, self.count) for h in range(2)]

    def begin(self):
        for k, h in self.order():
            self.own(k, h).start()

    def relay(self):
        if self.square:
            for k, h in ((1, 1), (2, 0)):
                self.own(k, h).wait_recv()
                self.onward(h).start()

    def take(self, k):
        for h in range(2):
            if not (self.square and (k, h) in ((1, 1), (2, 0))):
                self.copy(self.own_ref.at[self.rows(h)], k, h, k).wait_recv()

    def sent(self):
        for k, h in self.order():
            self.own(k, h).wait_send()
        if self.square:
            for h in range(2):
                self.onward(h).wait_send()


class Parts:
    def __init__(self, count, parts_ref, got_ref, send_sem, recv_sem):
        self.parts_ref, self.got_ref = parts_ref, got_ref
        self.send_sem, self.recv_sem = send_sem, recv_sem
        self.count, self.square = count, count == 4
        self.half = parts_ref.shape[1] // 2

    def rows(self, h):
        return pl.ds(h * self.half, self.half)

    def copy(self, k, h):
        peer = 1 + h if self.square and k == 3 else k
        source, target = self.parts_ref.at[k, self.rows(h)], self.got_ref.at[k, self.rows(h)]
        return send(source, target, self.send_sem.at[k, h], self.recv_sem.at[k, h], peer_of(peer))

    def put(self, k, part):
        self.parts_ref[k] = part.astype(bf16)
        for h in range(2):
            if not (self.square and (k, h) in ((1, 1), (2, 0))):
                self.copy(k, h).start()

    def merge(self):
        if self.square:
            for k, h in ((2, 0), (1, 1)):
                self.copy(3, h).wait_recv()
                rows = slice(h * self.half, (h + 1) * self.half)
                total = self.parts_ref[k, rows].astype(f32) + self.got_ref[3, rows].astype(f32)
                self.parts_ref[k, rows] = total.astype(bf16)
                self.copy(k, h).start()

    def total(self, own):
        for k in range(1, 3 if self.square else self.count):
            for h in range(2):
                self.copy(k, h).wait_recv()
            own = own + self.got_ref[k].astype(f32)
        return own

    def sent(self):
        for k in range(1, self.count):
            for h in range(2):
                self.copy(k, h).wait_send()


class Loads:
    def __init__(self, sources, targets, sem):
        self.copies = [
            pltpu.make_async_copy(source, target, sem.at[i])
            for i, (source, target) in enumerate(zip(sources, targets))
        ]
        for copy in self.copies:
            copy.start()

    def take(self, *which):
        for i in which:
            self.copies[i].wait()


def gate_and_up(block, expand_ref, gate_start, up_start, size):
    if size % 128:
        both = matmul(block, expand_ref[:, gate_start : up_start + size])
        return both[:, :size], both[:, size:]
    gate = matmul(block, expand_ref[:, gate_start : gate_start + size])
    return gate, matmul(block, expand_ref[:, up_start : up_start + size])


def feed_kernel(
    count, low_ref, mid_ref, expand_any, down_any,
    out_ref, blocks_ref, kept_gate_ref, kept_up_ref,
    expand_ref, down_ref, act_ref, part_ref, sent_ref, got_ref,
    send_sem, recv_sem, send_sem2, recv_sem2, load_sem,
):
    units = down_ref.shape[0]
    loads = Loads((expand_any, down_any), (expand_ref, down_ref), load_sem)
    rows = Rows(count, low_ref, blocks_ref, send_sem, recv_sem)
    parts = Parts(count, sent_ref, got_ref, send_sem2, recv_sem2)
    greet(count)
    rows.begin()
    blocks_ref[0] = low_ref[...]
    loads.take(0, 1)
    for k in range(count):
        if k:
            rows.take(k)
        block = blocks_ref[k]
        for gate_start, up_start, start, size in unit_chunks(units):
            gate, up = gate_and_up(block, expand_ref, gate_start, up_start, size)
            kept_gate_ref[k, :, start : start + size] = gate.astype(bf16)
            kept_up_ref[k, :, start : start + size] = up.astype(bf16)
            act_ref[:, start : start + size] = (gate / (1.0 + jnp.exp(-gate)) * up).astype(bf16)
        part = matmul(act_ref[...], down_ref[...])
        if k:
            parts.put(k, part)
        else:
            part_ref[...] = part + mid_ref[...]
            rows.relay()
    parts.merge()
    out_ref[...] = parts.total(part_ref[...]).astype(bf16)
    rows.sent()
    parts.sent()


def feed(layer, second_normed, middle):
    expand_w, down_w = layer[3:]
    count = lax.axis_size(CTX)
    rows, width = second_normed.shape
    units = down_w.shape[0]
    return call(
        functools.partial(feed_kernel, count),
        [
            ((rows, width), bf16),
            ((count, rows, width), bf16),
            ((count, rows, units), bf16),
            ((count, rows, units), bf16),
        ],
        [
            VMEM(expand_w.shape, bf16),
            VMEM(down_w.shape, bf16),
            VMEM((rows, units), bf16),
            VMEM((rows, width), f32),
            VMEM((count, rows, width), bf16),
            VMEM((count, rows, width), bf16),
        ]
        + [dma(count, 2)] * 4
        + [dma(2)],
        3,
        second_normed, middle, expand_w, down_w, far=(2, 3),
    )


def feed_back_kernel(count, fsdp_count, layer, carried, *refs):
    (
        grad_ref, mid_ref, vectors_ref,
        blocks_any, kept_gate_any, kept_up_any, expand_any, down_any,
    ) = refs[:8]
    refs = refs[8:]
    line_ref, refs = (refs[0], refs[1:]) if carried else (None, refs)
    dmid_ref, gain_ref, dexpand_ref, ddown_ref = refs[:4]
    refs = refs[4:]
    done_ref, refs = (refs[0], refs[1:]) if carried else (None, refs)
    (
        blocks_ref, kept_gate_ref, kept_up_ref, expand_ref, down_ref,
        grads_ref, act_ref, dwide_ref, part_ref, sent_ref, got_ref,
        send_sem, recv_sem, send_sem2, recv_sem2, load_sem, *scratch,
    ) = refs
    rows, width = grad_ref.shape
    units = down_ref.shape[0]
    loads = Loads(
        (down_any, kept_gate_any, kept_up_any, expand_any, blocks_any),
        (down_ref, kept_gate_ref, kept_up_ref, expand_ref, blocks_ref),
        load_sem,
    )
    gather = Rows(count, grad_ref, grads_ref, send_sem, recv_sem)
    parts = Parts(count, sent_ref, got_ref, send_sem2, recv_sem2)
    if carried:
        line = LineSum(fsdp_count, line_ref, done_ref, scratch)
        section, ctx, fsdp = place_of()
        greet_all(
            [peer_of(k) for k in range(1, count)]
            + [line.sister]
            + [(section, ctx, lax.rem(fsdp + d, fsdp_count)) for d in range(1, fsdp_count)]
        )
        line.begin()
    else:
        greet(count)
    gather.begin()
    grads_ref[0] = grad_ref[...]
    loads.take(0, 1, 2)
    for k in range(count):
        if k:
            gather.take(k)
        block = grads_ref[k]
        for gate_start, up_start, start, size in unit_chunks(units):
            cut = slice(start, start + size)
            spread = matmul_nt(block, down_ref[cut, :])
            gate = kept_gate_ref[k, :, cut].astype(f32)
            up = kept_up_ref[k, :, cut].astype(f32)
            sig = 1.0 / (1.0 + jnp.exp(-gate))
            silu = gate * sig
            act_ref[k, :, cut] = (silu * up).astype(bf16)
            dgate = (spread * up * sig * (1.0 + gate * (1.0 - sig))).astype(bf16)
            dup = (spread * silu).astype(bf16)
            if size % 128:
                dwide_ref[k, :, gate_start : up_start + size] = jnp.concatenate([dgate, dup], axis=1)
            else:
                dwide_ref[k, :, gate_start : gate_start + size] = dgate
                dwide_ref[k, :, up_start : up_start + size] = dup
        if not k:
            loads.take(3)
        part = matmul_nt(dwide_ref[k], expand_ref[...])
        if k:
            parts.put(k, part)
        else:
            part_ref[...] = part
            gather.relay()
            if carried:
                line.middle()
    loads.take(4)
    tall = count * rows
    grads = grads_ref[...].reshape(tall, width)
    main = units // 128 * 128
    for start, size in tiles(main, 384) + [(main, units - main)] * (units > main):
        act = act_ref[:, :, start : start + size].reshape(tall, size)
        ddown_ref[start : start + size, :] = matmul_tn(act, grads).astype(bf16)
    parts.merge()
    blocks = blocks_ref[...].reshape(tall, width)
    for start, size in tiles(2 * units, 512):
        dwide = dwide_ref[:, :, start : start + size].reshape(tall, size)
        dexpand_ref[:, start : start + size] = matmul_tn(blocks, dwide).astype(bf16)
    if carried:
        line.end()
    total = parts.total(part_ref[...])
    middle = mid_ref[...]
    scale = row_scale(middle)
    gain_ref[...] = jnp.sum(total * middle * scale, axis=0, keepdims=True)
    scaled = total * vectors_ref[4 * layer + 2 : 4 * layer + 3, :width]
    mean = jnp.mean(scaled * middle, axis=-1, keepdims=True)
    dmid_ref[...] = (
        grad_ref[...].astype(f32) + scale * scaled - middle * (scale * scale * scale * mean)
    )
    gather.sent()
    parts.sent()
    if carried:
        line.sent()


def feed_back(layer, middle, blocks, kept_gate, kept_up, grad_out, load=()):
    index, vectors = layer[:2]
    expand_w, down_w = layer[3:]
    count = lax.axis_size(CTX)
    rows, width = grad_out.shape
    units = down_w.shape[0]
    fsdp_count = lax.axis_size(FSDP)
    brought = (blocks, kept_gate, kept_up, expand_w, down_w)
    return call(
        functools.partial(feed_back_kernel, count, fsdp_count, index, bool(load)),
        [
            ((rows, width), f32),
            ((1, width), f32),
            ((width, 2 * units), bf16),
            ((units, width), bf16),
        ]
        + [((units // fsdp_count, width), bf16)] * len(load),
        [VMEM(array.shape, bf16) for array in brought]
        + [
            VMEM((count, rows, width), bf16),
            VMEM((count, rows, units), bf16),
            VMEM((count, rows, 2 * units), bf16),
            VMEM((rows, width), f32),
            VMEM((count, rows, width), bf16),
            VMEM((count, rows, width), bf16),
        ]
        + [dma(count, 2)] * 4
        + [dma(5)]
        + (line_scratch(fsdp_count, load[0]) if load else []),
        4 + 7 * index,
        grad_out, middle, vectors, *brought, *load, far=(3, 4, 5, 6, 7, 8),
    )


def attn_sum_kernel(
    ctx_count, fsdp_count, wide, low_ref, high_ref, small_ref, down_ref,
    act_zero_ref, act_one_ref, grad_zero_ref, grad_one_ref, down_grad_ref, expand_ref, expand_all_ref,
    projections_ref, output_ref, total_ref, down_all_ref, act_ref, grad_ref, expand_out,
    wide_ref, done_ref,
    c_out, c_in, d_out, whole_ref, s_out, s_in,
    c_send, c_recv, d_send, d_recv, s_send, s_recv, *more,
):
    section, ctx, fsdp = place_of()
    sister = (1 - section, ctx, fsdp)
    width, piece = high_ref.shape
    rows = width // fsdp_count
    places = range(1, ctx_count)
    shards = range(1, fsdp_count)
    steps = SquareSum(ctx_count, low_ref, *more[:3], more[3:7])
    halves = [row_halves(expand_ref.shape[0])]
    owners = Owners(ctx_count, 0, [expand_ref], [expand_out], halves, more[7:10])
    own_sem, swap_send, swap_recv = more[10:13]
    kept = pltpu.make_async_copy(expand_ref, expand_out.at[ctx, section], own_sem.at[0])
    load = pltpu.make_async_copy(expand_all_ref, expand_out, own_sem.at[1])
    down = LineSum(fsdp_count, down_grad_ref, done_ref, more[13:20])
    handouts = [
        Handout(ctx_count, fsdp_count, 1, down_ref, down_all_ref, more[20:24]),
        Handout(ctx_count, fsdp_count, 0, done_ref, down_all_ref, more[24:28]),
    ]
    layers = ((act_zero_ref, grad_zero_ref), (act_one_ref, wide_ref))

    def swap(i, layer):
        target = (act_ref, grad_ref)[i].at[section]
        return send(layers[layer][i], target, swap_send.at[i], swap_recv.at[i], sister)

    def ahead(d):
        return (section, ctx, lax.rem(fsdp + d, fsdp_count))

    def c_copy(layer, d):
        target = lax.rem(fsdp + d, fsdp_count)
        source = c_out.at[layer, pl.ds(pl.multiple_of(target * rows, rows), rows)]
        return send(source, c_in.at[layer, d], c_send.at[layer, d], c_recv.at[layer, d], ahead(d))

    def s_copy(step, source, device):
        return send(s_out.at[source], s_in.at[step], s_send.at[step], s_recv.at[step], device)

    def line_sum(layer):
        total = c_out[layer, pl.ds(pl.multiple_of(fsdp * rows, rows), rows)].astype(f32)
        for d in shards:
            c_copy(layer, d).wait_recv()
            total = total + c_in[layer, d].astype(f32)
        d_out[layer] = total.astype(bf16)
        every_owner(
            ctx_count, layer, "start", [d_out.at[layer]], [whole_ref], d_send.at[layer], d_recv
        )

        @pl.when(section == layer)
        def _():
            whole_ref[ctx, section] = d_out[layer]

    hops = [(0, 0, sister)]
    hops += [(k, 1, peer_of(k)) for k in places]
    hops += [(ctx_count - 1 + d, 2, ahead(d)) for d in shards]

    greet_all(chip_square(ctx_count) + [ahead(d) for d in shards])
    steps.begin()
    down.begin()
    owners.begin()

    @pl.when(section == 0)
    def _():
        kept.start()

    @pl.when(section == 1)
    def _():
        load.start()

    wide_ref[...] = grad_one_ref[...].astype(f32)
    for layer in range(2):

        @pl.when(section != layer)
        def _():
            for i in range(2):
                swap(i, layer).start()

        @pl.when(section == layer)
        def _():
            for i, target in enumerate((act_ref, grad_ref)):
                target[section] = layers[layer][i][...]

    s_out[0] = small_ref[...]
    s_copy(*hops[0]).start()
    c_out[1] = high_ref[...]
    for d in shards:
        c_copy(1, d).start()

    steps.middle()
    down.middle()
    handouts[0].begin()
    owners.relay()
    s_copy(*hops[0]).wait_recv()
    s_out[1] = s_out[0] + s_in[0]
    for k in places:
        s_copy(*hops[k]).start()
    line_sum(1)
    steps.merge()
    c_out[0] = steps.end()
    for d in shards:
        c_copy(0, d).start()
    handouts[0].relay()
    down.end()
    handouts[1].begin()
    part = s_out[1]
    for k in places:
        s_copy(*hops[k]).wait_recv()
        part = part + s_in[k]
    s_out[2] = part
    for d in shards:
        s_copy(*hops[ctx_count - 1 + d]).start()
    line_sum(0)
    part = s_out[2]
    for d in shards:
        s_copy(*hops[ctx_count - 1 + d]).wait_recv()
        part = part + s_in[ctx_count - 1 + d]
    total_ref[...] = part
    for layer in (1, 0):
        from_owners(ctx_count, layer, [whole_ref], d_send.at[layer], d_recv)
    for where in range(ctx_count):
        for core in range(2):
            start = (where * 2 + core) * piece
            block = whole_ref[where, core].astype(f32)
            size = max(min(wide - start, piece), 0)
            if size:
                projections_ref[:, start : start + size] = block[:, :size]
            if size < piece:
                first = start + size - wide
                output_ref[:, first : first + piece - size] = block[:, size:]
    owners.end()
    handouts[1].relay()
    for handout in handouts:
        handout.end()
    down.sent()

    @pl.when(section == 0)
    def _():
        kept.wait()

    @pl.when(section == 1)
    def _():
        load.wait()

    for i in range(2):
        swap(i, 0).wait()
    steps.sent()
    for layer in (1, 0):
        for d in shards:
            c_copy(layer, d).wait_send()
        every_owner(
            ctx_count, layer, "wait", [d_out.at[layer]], [whole_ref], d_send.at[layer], d_recv
        )
    for hop in hops:
        s_copy(*hop).wait_send()


def attn_sum(low, high, small, down_one, acts, grads, down_grad, expand_part, expand_all, wide):
    ctx_count, fsdp_count = lax.axis_size(CTX), lax.axis_size(FSDP)
    width, both = low.shape
    rows = width // fsdp_count
    piece = both // (2 * ctx_count)
    hops = ctx_count + fsdp_count - 1
    return call(
        functools.partial(attn_sum_kernel, ctx_count, fsdp_count, wide),
        [
            ((rows, wide), f32),
            ((rows, both - wide), f32),
            (small.shape, f32),
            ((ctx_count,) + down_one.shape, bf16),
            ((2,) + acts[0].shape, bf16),
            ((2,) + grads[0].shape, f32),
            (expand_all.shape, bf16),
        ],
        [
            VMEM(grads[0].shape, f32),
            VMEM(down_one.shape, bf16),
            VMEM((2, width, piece), bf16),
            VMEM((2, fsdp_count, rows, piece), bf16),
            VMEM((2, rows, piece), bf16),
            VMEM((ctx_count, 2, rows, piece), bf16),
            VMEM((3,) + small.shape, f32),
            VMEM((hops,) + small.shape, f32),
            dma(2, fsdp_count), dma(2, fsdp_count),
            dma(2, 1, ctx_count), dma(1, 2, ctx_count),
            dma(hops), dma(hops),
        ]
        + square_scratch(ctx_count, low)
        + owner_sems(ctx_count)
        + [dma(2), dma(2), dma(2)]
        + line_scratch(fsdp_count, down_grad)
        + handout_sems(ctx_count) * 2,
        7,
        low, high, small, down_one, *acts, *grads, down_grad, expand_part, expand_all,
        far=(8, 10), far_outs=(3,),
    )


def spread_kernel(chunk, stride, shards, side_width, block_ref, out_ref):
    count = block_ref.shape[0]
    for where in range(count):
        sides = unpack_units(block_ref[where].astype(f32))
        for side, values in enumerate(sides):
            for shard in range(shards):
                start = side * side_width + (shard * count + where) * chunk
                out_ref[:, start : start + chunk] = values[:, shard * stride : shard * stride + chunk]


def finish(expand_all, ff_width, units):
    ctx_count, fsdp_count = lax.axis_size(CTX), lax.axis_size(FSDP)
    half, packed = expand_all.shape[2:]
    rows = 2 * half
    step = 32 if rows % 32 == 0 else 16
    stride = packed // 2 // fsdp_count
    return pl.pallas_call(
        functools.partial(spread_kernel, units, stride, fsdp_count, ff_width),
        grid=(rows // step,),
        out_shape=jax.ShapeDtypeStruct((rows, 2 * ff_width), f32),
        in_specs=[pl.BlockSpec((ctx_count, step, packed), lambda i: (0, i, 0))],
        out_specs=pl.BlockSpec((step, 2 * ff_width), lambda i: (i, 0)),
        compiler_params=pltpu.CompilerParams(vmem_limit_bytes=LIMIT),
    )(expand_all.reshape(ctx_count, rows, packed))


def per_device(
    inputs,
    attend_gain,
    projections,
    biases,
    output_weight,
    mixer_gain,
    expand_weight,
    down_weight,
    positions,
    cotangent,
):
    row_count, model_width = inputs.shape[2:]
    section = lax.axis_index(SECTION)
    is_first = section == 0
    ctx = lax.axis_index(CTX)
    fsdp = lax.axis_index(FSDP)
    ctx_count = lax.axis_size(CTX)
    fsdp_count = lax.axis_size(FSDP)
    shard_rows = projections.shape[1]
    wide = projections.shape[2]
    ff_width = expand_weight.shape[2] // 2
    shard_units = down_weight.shape[1]
    units = shard_units // ctx_count
    spare_units = -units % 16
    both = (FSDP, SECTION)

    def mine(array):
        return lax.dynamic_index_in_dim(array, section, 0, keepdims=False)

    source = mine(inputs)[0]
    upstream = mine(cotangent)[0]
    key_positions = mine(positions)[0]
    query_positions = lax.dynamic_slice_in_dim(key_positions, ctx * row_count, row_count)
    cosine, sine = tables(query_positions)
    by_distance = jnp.concatenate(
        [
            lax.dynamic_slice_in_dim(key_positions, (ctx ^ k) * row_count, row_count)
            for k in range(ctx_count)
        ]
    )
    place = (cosine, sine, by_distance[:, None], query_positions[None])

    bias_part = biases.shape[1]
    small_width = -(-bias_part // 128) * 128

    def padded(row):
        return jnp.pad(row, ((0, 0), (0, small_width - row.shape[1])))

    small_shard = jnp.concatenate(
        [padded(attend_gain), padded(biases), padded(mixer_gain), jnp.zeros((13, small_width), bf16)]
    )
    attn_shard = jnp.concatenate([projections[0], output_weight[0]], axis=1)

    def in_order(array):
        other = swap_sections(array)
        return jnp.where(is_first, array, other), jnp.where(is_first, other, array)

    def unit_columns(side):
        pieces = []
        for shard in range(fsdp_count):
            start = side * ff_width + shard * shard_units
            pieces.append(
                pick(
                    ctx,
                    [
                        expand_weight[0, :, start + k * units : start + (k + 1) * units]
                        for k in range(ctx_count)
                    ],
                )
            )
            if spare_units:
                pieces.append(jnp.zeros((shard_rows, spare_units), bf16))
        return jnp.concatenate(pieces, axis=1)

    expand_shard = pack_units(unit_columns(0), unit_columns(1))
    down_shard = lax.dynamic_slice_in_dim(down_weight[0], ctx * units, units)
    down_shard = jnp.pad(down_shard, ((0, spare_units), (0, 0)))

    def halves(array):
        size = array.shape[0] // 2
        low, high = array[:size], array[size:]
        own = jnp.where(is_first, low, high)
        other = swap_sections(jnp.where(is_first, high, low))
        return jnp.where(is_first, own, other), jnp.where(is_first, other, own)

    expand_pair = halves(expand_shard)
    down_first, down_next = in_order(down_shard)
    half_units = down_shard.shape[0] // 2
    down_halves = jnp.where(is_first, down_first[:half_units], down_first[half_units:])
    first_shard, second_shard = in_order(attn_shard)
    small_pair = jnp.concatenate(in_order(small_shard))

    def gather(piece):
        return lax.all_gather(piece, both, axis=0, tiled=True)

    down_w = gather(down_halves)
    expands = [gather(piece) for piece in expand_pair]
    first_shard, second_shard, small_pair = lax.optimization_barrier(
        (first_shard, second_shard, small_pair, expand_pair[0], down_halves)
    )[:3]
    sizes = (shard_rows, bias_part, shard_rows)
    *weights, vectors = collect(first_shard, second_shard, small_pair, sizes)

    layers = []
    hidden = source
    stored = []
    sent = []
    for layer in range(2):
        now = (layer, vectors, weights[layer])
        normed, queries, every_kv, lse, context, middle, second_normed, *fetched = attend(
            now, hidden, place, (down_next,) if layer else ()
        )
        if layer:
            (down_w,) = fetched
        now = now + (expands[layer], down_w)
        layers.append(now)
        kept = (hidden, normed, queries, every_kv, lse, context)
        hidden, blocks, kept_gate, kept_up = feed(now, second_normed, middle)
        sent.append(hidden)
        stored.append((middle, kept, blocks, kept_gate, kept_up))

    def scatter(array):
        return lax.psum_scatter(array, both, scatter_dimension=0, tiled=True)

    grad = upstream
    hidden_grads = [None, None]
    small_grads = [None, None]
    attn_grads = [None, None]
    for layer in (1, 0):
        middle, kept, blocks, kept_gate, kept_up = stored[layer]
        load = () if layer else (down_grad,)
        middle_grad, second_grad, expand_grad, down_grad, *summed = feed_back(
            layers[layer], middle, blocks, kept_gate, kept_up, grad, load
        )
        if layer:
            expand_one = scatter(expand_grad)
            load = ()
        else:
            expand_grad, expand_one = lax.optimization_barrier((expand_grad, expand_one))
            expand_zero = scatter(expand_grad)
            (down_one,) = summed
            load = (attn_grads[1], expand_one)
        hidden_grad, first_grad, offset_grad, attn_grads[layer], *summed = attend_back(
            layers[layer], kept, middle_grad, place, load
        )
        small_grads[layer] = jnp.concatenate([first_grad, offset_grad, second_grad], axis=1)[0]
        hidden_grads[layer] = hidden_grad
        grad = hidden_grad

    spare = -small_grads[0].shape[0] % model_width
    small_rows = [jnp.pad(vector, (0, spare)).reshape(-1, model_width) for vector in small_grads]
    small_count = small_rows[0].shape[0]
    rows_left = -2 * small_count % 8
    small_stack = jnp.pad(jnp.concatenate(small_rows), ((0, rows_left), (0, 0)))
    attn_one, expand_one = summed
    (
        grad_projections, grad_output, small_all, down_all, activations, input_grads, expand_all,
    ) = attn_sum(
        attn_grads[0], attn_one, small_stack, down_one, sent, hidden_grads,
        down_grad, expand_zero, expand_one, wide,
    )
    grad_expand = finish(expand_all, ff_width, units)
    grad_down = down_all[:, :units].astype(f32).reshape(shard_units, model_width)
    small_own = jnp.where(
        is_first, small_all[:small_count], small_all[small_count : 2 * small_count]
    ).reshape(-1)
    first_all, offset_all, second_all = (
        small_own[:model_width],
        small_own[model_width : model_width + wide],
        small_own[model_width + wide : 2 * model_width + wide],
    )
    pair_width = (wide - model_width) // 2

    def part(vector):
        size = vector.shape[0] // fsdp_count
        return lax.dynamic_slice_in_dim(vector, fsdp * size, size)[None]

    return (
        activations[None, :, None],
        input_grads[None, :, None],
        part(first_all),
        grad_projections[None],
        part(offset_all[: model_width + pair_width]),
        part(offset_all[model_width + pair_width :]),
        grad_output[None],
        part(second_all),
        grad_expand[None],
        grad_down[None],
    )


def solution(mesh):
    return jax.shard_map(
        per_device,
        mesh=mesh,
        in_specs=(
            P(None, FSDP, CTX, None),
            P(SECTION, FSDP),
            P(SECTION, FSDP, None),
            P(SECTION, FSDP),
            P(SECTION, FSDP, None),
            P(SECTION, FSDP),
            P(SECTION, FSDP, None),
            P(SECTION, FSDP, None),
            P(None, FSDP, None),
            P(None, FSDP, CTX, None),
        ),
        out_specs=(
            P(SECTION, None, FSDP, CTX, None),
            P(SECTION, None, FSDP, CTX, None),
            P(SECTION, FSDP),
            P(SECTION, FSDP, None),
            P(SECTION, FSDP),
            P(SECTION, FSDP),
            P(SECTION, FSDP, None),
            P(SECTION, FSDP),
            P(SECTION, FSDP, None),
            P(SECTION, FSDP, None),
        ),
        check_vma=False,
    )
```

```python
import functools

import jax
import jax.numpy as jnp
from jax import lax
from jax.experimental import pallas as pl
from jax.experimental.pallas import tpu as pltpu
from jax.sharding import PartitionSpec as P

HEAD_DIM = 64
SECTION, CTX, FSDP = "section", "ctx", "fsdp"

epsilon = 1e-06
theta_base = 1000000.0
masked_value = -1e30

bf16 = jnp.bfloat16
f32 = jnp.float32


def swap_sections(block):
    return lax.ppermute(block, SECTION, [(0, 1), (1, 0)])


def tables(positions_row):
    half_dim = HEAD_DIM // 2
    frequency = theta_base ** (-(jnp.arange(half_dim, dtype=f32) * 2.0) / HEAD_DIM)
    angles = positions_row.astype(f32)[:, None] * frequency[None, :]
    cosine, sine = jnp.cos(angles), jnp.sin(angles)
    return (
        jnp.concatenate([cosine] * 4, axis=-1),
        jnp.concatenate([-sine, sine, -sine, sine], axis=-1),
    )


def pick(index, options):
    chosen = options[0]
    for position in range(1, len(options)):
        chosen = jnp.where(index == position, options[position], chosen)
    return chosen


MESH = pl.DeviceIdType.MESH
VMEM = pltpu.VMEM
LIMIT = 56 * 1024 * 1024


def flip(index, distance):
    place = 1
    while place <= distance:
        if (distance // place) % 2:
            index = index + place - 2 * place * ((index // place) % 2)
        place *= 2
    return index


def place_of():
    return lax.axis_index(SECTION), lax.axis_index(CTX), lax.axis_index(FSDP)


def peer_of(distance):
    section, ctx, fsdp = place_of()
    return (section, flip(ctx, distance), fsdp)


def greet_all(devices):
    barrier = pltpu.get_barrier_semaphore()
    for device in devices:
        pl.semaphore_signal(barrier, inc=1, device_id=device, device_id_type=MESH)
    pl.semaphore_wait(barrier, len(devices))


def greet(count):
    greet_all([peer_of(k) for k in range(1, count)])


def send(source, target, send_sem, recv_sem, device):
    return pltpu.make_async_remote_copy(
        src_ref=source,
        dst_ref=target,
        send_sem=send_sem,
        recv_sem=recv_sem,
        device_id=device,
        device_id_type=MESH,
    )


def remote(source, target, send_sem, recv_sem, k):
    return send(source, target, send_sem.at[k], recv_sem.at[k], peer_of(k))


def matmul(left, right):
    return lax.dot_general(left, right, (((1,), (0,)), ((), ())), preferred_element_type=f32)


def matmul_nt(left, right):
    return lax.dot_general(left, right, (((1,), (1,)), ((), ())), preferred_element_type=f32)


def matmul_tn(left, right):
    return lax.dot_general(left, right, (((0,), (0,)), ((), ())), preferred_element_type=f32)


def tiles(size, step):
    return [(start, min(step, size - start)) for start in range(0, size, step)]


def row_scale(values):
    return lax.rsqrt(jnp.mean(values * values, axis=-1, keepdims=True) + epsilon)


def call(kernel, outs, scratch, cid, *args, far=(), far_outs=()):
    def spec(position, away):
        return pl.BlockSpec(memory_space=pl.ANY if position in away else VMEM)

    return pl.pallas_call(
        kernel,
        out_shape=[jax.ShapeDtypeStruct(shape, kind) for shape, kind in outs],
        in_specs=[spec(position, far) for position in range(len(args))],
        out_specs=[spec(position, far_outs) for position in range(len(outs))],
        scratch_shapes=scratch,
        compiler_params=pltpu.CompilerParams(
            collective_id=cid, has_side_effects=True, vmem_limit_bytes=LIMIT
        ),
    )(*args)


def dma(*shape):
    return pltpu.SemaphoreType.DMA(shape)


class Relay:
    def __init__(self, fsdp_count, source, spot, z_send, z_recv):
        self.count, self.source, self.spot = fsdp_count, source, spot
        self.z_send, self.z_recv = z_send, z_recv
        self.section, self.ctx, self.fsdp = place_of()
        self.hops = [(side, e) for e in range(1, fsdp_count) for side in (1, 0)]

    def device(self, side):
        step = 1 if side else self.count - 1
        return (self.section, self.ctx, lax.rem(self.fsdp + step, self.count))

    def goes_on(self, side):
        return self.fsdp < self.count - 1 if side else self.fsdp > 0

    def came(self, side, e):
        return self.fsdp >= e if side else self.fsdp < self.count - e

    def origin(self, side, e):
        return lax.rem(self.fsdp + (self.count - e if side else e), self.count)

    def copy(self, side, e):
        spot = self.spot(self.origin(side, e))
        source = spot if e else self.source
        return send(source, spot, self.z_send.at[side, e], self.z_recv.at[side, e + 1], self.device(side))

    def begin(self):
        for side in range(2):

            @pl.when(self.goes_on(side))
            def _():
                self.copy(side, 0).start()

    def each(self, step):
        for side, e in self.hops:
            pl.when(self.came(side, e))(functools.partial(step, side, e))

    def steps(self):
        return range(1, self.count)

    def take(self, side, e):
        spot = self.spot(self.origin(side, e))
        sems = self.z_send.at[side, e], self.z_recv.at[side, e]
        send(spot, spot, *sems, self.device(side)).wait_recv()
        if e < self.count - 1:

            @pl.when(self.goes_on(side))
            def _():
                self.copy(side, e).start()

    def sent(self):
        for side, e in [(0, 0), (1, 0)] + self.hops:
            if e < self.count - 1:

                @pl.when(jnp.logical_and(self.came(side, e), self.goes_on(side)))
                def _():
                    self.copy(side, e).wait_send()


class Collect:
    def __init__(self, ctx_count, fsdp_count, shard_ref, w_ref, sems):
        self.shard_ref, self.w_ref = shard_ref, w_ref
        z_send, z_recv, self.y_send, self.y_recv, self.v_send, self.v_recv, self.own_sem = sems
        self.places = range(1, ctx_count)
        self.square = ctx_count == 4
        self.early = ((1, 1), (2, 0)) if self.square else ()
        self.fsdp_count = fsdp_count
        self.section, self.ctx, self.fsdp = place_of()
        self.sister = (1 - self.section, self.ctx, self.fsdp)
        self.rows, width = shard_ref.shape
        self.piece = width // (2 * ctx_count)
        self.mine = pl.ds(pl.multiple_of(self.fsdp * self.rows, self.rows), self.rows)
        own = shard_ref.at[:, self.columns(self.ctx, self.section)]
        self.line = Relay(
            fsdp_count, own, lambda shard: self.spot(shard, self.ctx, self.section), z_send, z_recv
        )
        self.ahead = [
            (self.section, self.ctx, lax.rem(self.fsdp + d, fsdp_count)) for d in range(1, fsdp_count)
        ]
        self.friends = self.ahead + [peer_of(k) for k in self.places] + [self.sister]

    def columns(self, where, core):
        return pl.ds(pl.multiple_of((where * 2 + core) * self.piece, self.piece), self.piece)

    def spot(self, shard, where, core):
        rows = pl.ds(pl.multiple_of(shard * self.rows, self.rows), self.rows)
        return self.w_ref.at[rows, self.columns(where, core)]

    def block(self, side, e, where, core):
        return self.spot(self.line.origin(side, e), where, core)

    def kept(self):
        return pltpu.make_async_copy(self.shard_ref, self.w_ref.at[self.mine], self.own_sem.at[0])

    def half(self, side, e, where, core, h):
        size = self.rows // 2
        start = self.line.origin(side, e) * self.rows + h * size
        rows = pl.ds(pl.multiple_of(start, size), size)
        return self.w_ref.at[rows, self.columns(where, core)]

    def spread(self, side, e, k, h, came=0):
        source = self.half(side, e, flip(self.ctx, came), self.section, h)
        device = peer_of(k) if k else self.sister
        i, j = side * self.fsdp_count + e, 2 * (k ^ came) + h
        return send(source, source, self.y_send.at[i, j], self.y_recv.at[i, j], device)

    def arrival(self, side, e, k, h, core):
        came = self.half(side, e, flip(self.ctx, k), core, h)
        i, j = side * self.fsdp_count + e, 2 * k + h
        return send(came, came, self.y_send.at[i, j], self.y_recv.at[i, j], self.sister)

    def outgoing(self):
        if self.square:
            return [(1, 1), (2, 0), (0, 0), (0, 1), (1, 0), (2, 1)]
        return [(k, h) for k in (*self.places, 0) for h in range(2)]

    def passed(self, side, e, k):
        source = self.block(side, e, flip(self.ctx, k), self.section)
        i = side * self.fsdp_count + e
        return send(source, source, self.v_send.at[i, k], self.v_recv.at[i, k], self.sister)

    def begin(self):
        self.line.begin()
        self.kept().start()

    def relay(self, which):
        def step(side, e):
            if e == which:
                self.line.take(side, e)
                for k, h in self.outgoing():
                    self.spread(side, e, k, h).start()

        self.line.each(step)

    def corner(self):
        def step(side, e):
            for k, h in self.early:
                self.arrival(side, e, k, h, self.section).wait_recv()
                self.spread(side, e, 3 - k, h, k).start()

        if self.square:
            self.line.each(step)

    def hand(self):
        def step(side, e):
            for k in self.places:
                for h in range(2):
                    if (k, h) not in self.early:
                        self.arrival(side, e, k, h, self.section).wait_recv()
                self.passed(side, e, k).start()

        self.line.each(step)

    def finish(self):
        def arrivals(side, e):
            i = side * self.fsdp_count + e
            for h in range(2):
                self.arrival(side, e, 0, h, 1 - self.section).wait_recv()
            for k in self.places:
                came = self.block(side, e, flip(self.ctx, k), 1 - self.section)
                send(came, came, self.v_send.at[i, k], self.v_recv.at[i, k], self.sister).wait_recv()

        def sent(side, e):
            for k, h in self.outgoing():
                self.spread(side, e, k, h).wait_send()
            for k, h in self.early:
                self.spread(side, e, 3 - k, h, k).wait_send()
            for k in self.places:
                self.passed(side, e, k).wait_send()

        self.line.each(arrivals)
        self.line.each(sent)
        self.line.sent()
        self.kept().wait()


def collect_sems(ctx_count, fsdp_count):
    line = dma(2, fsdp_count)
    table = dma(2 * fsdp_count, ctx_count)
    halves = dma(2 * fsdp_count, 2 * ctx_count)
    return [line, line, halves, halves, table, table, dma(1)]


class Line:
    def __init__(self, fsdp_count, piece_ref, out_ref, sems):
        self.piece_ref, self.out_ref = piece_ref, out_ref
        z_send, z_recv, self.v_send, self.v_recv, self.own_sem = sems
        self.section, self.ctx, self.fsdp = place_of()
        self.count = fsdp_count
        self.rows = piece_ref.shape[0]
        cut = -(-self.rows // 32) * 16
        self.parts = ((0, cut), (cut, self.rows - cut))
        self.sister = (1 - self.section, self.ctx, self.fsdp)
        self.lines = [
            Relay(
                fsdp_count,
                piece_ref.at[pl.ds(start, size)],
                functools.partial(self.spot, core),
                z_send,
                z_recv,
            )
            for core, (start, size) in enumerate(self.parts)
        ]
        self.ahead = [
            (self.section, self.ctx, lax.rem(self.fsdp + d, fsdp_count)) for d in range(1, fsdp_count)
        ]

    def spot(self, core, shard):
        start, size = self.parts[core]
        return self.out_ref.at[pl.ds(pl.multiple_of(shard * self.rows + start, 16), size)]

    def passed(self, core, side, e):
        spot = self.spot(core, self.lines[core].origin(side, e))
        i = side * self.count + e
        return send(spot, spot, self.v_send.at[i], self.v_recv.at[i], self.sister)

    def kept(self):
        start = pl.multiple_of(self.fsdp * self.rows, 16)
        return pltpu.make_async_copy(
            self.piece_ref, self.out_ref.at[pl.ds(start, self.rows)], self.own_sem.at[0]
        )

    def each_core(self, step):
        for core in range(2):
            pl.when(self.section == core)(functools.partial(step, core))

    def begin(self):
        self.each_core(lambda core: self.lines[core].begin())
        self.kept().start()

    def relay(self, which):
        def step(core):
            def take(side, e):
                if e == which:
                    self.lines[core].take(side, e)
                    self.passed(core, side, e).start()

            self.lines[core].each(take)

        self.each_core(step)

    def end(self):
        def step(core):
            line = self.lines[core]
            line.each(lambda side, e: self.passed(1 - core, side, e).wait_recv())
            line.each(lambda side, e: self.passed(core, side, e).wait_send())
            line.sent()

        self.each_core(step)
        self.kept().wait()


def line_sems(fsdp_count):
    hops = dma(2 * fsdp_count)
    return [dma(2, fsdp_count), dma(2, fsdp_count), hops, hops, dma(1)]


def collect_kernel(
    ctx_count, fsdp_count, sizes, low_ref, high_ref, small_ref, low_w_ref, high_w_ref, vectors_ref,
    smalls_ref, s_send, s_recv, *sems
):
    half = len(sems) // 2
    steps = Collect(ctx_count, fsdp_count, low_ref, low_w_ref, sems[:half])
    later = Collect(ctx_count, fsdp_count, high_ref, high_w_ref, sems[half:])

    shards = range(1, fsdp_count)

    def small(d):
        target = smalls_ref.at[steps.fsdp]
        return send(small_ref, target, s_send.at[d], s_recv.at[d], steps.ahead[d - 1])

    greet_all(steps.friends)
    steps.begin()
    later.begin()
    for d in shards:
        small(d).start()
    smalls_ref[steps.fsdp] = small_ref[...]
    for e in steps.line.steps():
        steps.relay(e)
        later.relay(e)
    steps.corner()
    later.corner()
    steps.hand()
    later.hand()
    steps.finish()
    later.finish()
    for d in shards:
        came = smalls_ref.at[lax.rem(steps.fsdp + fsdp_count - d, fsdp_count)]
        send(came, came, s_send.at[d], s_recv.at[d], steps.sister).wait_recv()
    for shard in range(fsdp_count):
        rows = smalls_ref[shard].astype(f32)
        for layer in range(2):
            for i, size in enumerate(sizes):
                row = 4 * layer + i
                vectors_ref[row : row + 1, shard * size : (shard + 1) * size] = rows[
                    16 * layer + i : 16 * layer + i + 1, :size
                ]
    for d in shards:
        small(d).wait_send()


def collect(low, high, small, sizes):
    ctx_count, fsdp_count = lax.axis_size(CTX), lax.axis_size(FSDP)
    rows, width = low.shape
    whole = ((fsdp_count * rows, width), bf16)
    return call(
        functools.partial(collect_kernel, ctx_count, fsdp_count, sizes),
        [whole, whole, ((8, fsdp_count * max(sizes)), f32)],
        [VMEM((fsdp_count,) + small.shape, bf16), dma(fsdp_count), dma(fsdp_count)]
        + collect_sems(ctx_count, fsdp_count) * 2,
        5,
        low, high, small, far_outs=(0, 1),
    )


class SquareSum:
    def __init__(self, ctx_count, grad_ref, a_ref, b_out, b_in, sems):
        self.grad_ref, self.a_ref, self.b_out = grad_ref, a_ref, b_out
        self.a_send, self.a_recv, b_send, b_recv = sems
        self.parts = Parts(ctx_count, b_out, b_in, b_send, b_recv)
        self.order = (*range(ctx_count - 1, 0, -1), 0)
        self.section, self.ctx, fsdp = place_of()
        self.sister = (1 - self.section, self.ctx, fsdp)
        self.piece = grad_ref.shape[1] // (2 * ctx_count)

    def columns(self, k, core):
        start = (flip(self.ctx, k) * 2 + core) * self.piece
        return pl.ds(pl.multiple_of(start, self.piece), self.piece)

    def chip(self, k):
        source = self.grad_ref.at[:, self.columns(k, 1 - self.section)]
        return send(source, self.a_ref.at[k], self.a_send.at[k], self.a_recv.at[k], self.sister)

    def begin(self):
        for k in self.order:
            self.chip(k).start()

    def middle(self):
        for k in self.order:
            self.chip(k).wait_recv()
            own = self.grad_ref[:, self.columns(k, self.section)].astype(f32)
            total = own + self.a_ref[k].astype(f32)
            if k:
                self.parts.put(k, total)
            else:
                self.b_out[0] = total.astype(bf16)

    def merge(self):
        self.parts.merge()

    def end(self):
        return self.parts.total(self.b_out[0].astype(f32)).astype(bf16)

    def sent(self):
        for k in self.order:
            self.chip(k).wait_send()
        self.parts.sent()


def square_scratch(ctx_count, grad):
    width, both = grad.shape
    piece = VMEM((ctx_count, width, both // (2 * ctx_count)), bf16)
    sems = [dma(ctx_count), dma(ctx_count), dma(ctx_count, 2), dma(ctx_count, 2)]
    return [piece, piece, piece] + sems


def every_owner(ctx_count, layer, start_or_wait, sources, targets, send_sem, recv_sem):
    section, ctx, fsdp = place_of()
    for k in range(ctx_count):
        device = (layer, flip(ctx, k), fsdp)

        def go():
            for i, (source, target) in enumerate(zip(sources, targets)):
                copy = send(
                    source,
                    target.at[ctx, section],
                    send_sem.at[i, k],
                    recv_sem.at[i, section, k],
                    device,
                )
                copy.start() if start_or_wait == "start" else copy.wait_send()

        pl.when(section != layer)(go) if k == 0 else go()


def from_owners(ctx_count, layer, targets, send_sem, recv_sem):
    section, ctx, fsdp = place_of()
    for core in range(2):
        for k in range(ctx_count):
            if core == layer and k == 0:
                continue

            def go():
                for i, target in enumerate(targets):
                    came = target.at[flip(ctx, k), core]
                    send(
                        came, came, send_sem.at[i, k], recv_sem.at[i, core, k], (1 - section, ctx, fsdp)
                    ).wait_recv()

            pl.when(section == layer)(go)


class Owners:
    def __init__(self, ctx_count, layer, sources, targets, cuts, sems):
        self.layer, self.targets = layer, targets
        self.send_sem, self.recv_sem, self.onward_sem = sems
        self.section, self.ctx, self.fsdp = place_of()
        self.count, self.square = ctx_count, ctx_count == 4
        self.pieces = []
        for i, source in enumerate(sources):
            for h in range(2) if self.square else (0,):
                cut = cuts[i][h] if self.square else None
                self.pieces.append((source.at[cut] if self.square else source, i, cut, h))
        self.all = range(len(self.pieces))
        self.early = [(i, 2 - self.pieces[i][3]) for i in self.all if self.square]
        self.keeper = self.section == layer

    def spot(self, i, k, core):
        _, which, cut, _ = self.pieces[i]
        spot = self.targets[which].at[flip(self.ctx, k), core]
        return spot if cut is None else spot.at[cut]

    def peer(self, k):
        return (self.layer, flip(self.ctx, k), self.fsdp)

    def own(self, i, k):
        return send(
            self.pieces[i][0],
            self.spot(i, 0, self.section),
            self.send_sem.at[i, k],
            self.recv_sem.at[i, self.section, k],
            self.peer(k),
        )

    def onward(self, i, core):
        came = 2 - self.pieces[i][3]
        spot = self.spot(i, came, core)
        return send(
            spot, spot, self.onward_sem.at[i, core], self.recv_sem.at[i, core, 3], self.peer(3 - came)
        )

    def outgoing(self):
        if self.square:
            late = [(i, 3 - k) for i, k in self.early]
            return self.early + late
        return [(i, k) for k in range(1, self.count) for i in self.all]

    def begin(self):
        for i, k in self.outgoing():
            self.own(i, k).start()

        @pl.when(jnp.logical_not(self.keeper))
        def _():
            for i in self.all:
                self.own(i, 0).start()

    def arrival(self, i, core, k):
        spot = self.spot(i, k, core)
        recv = self.recv_sem.at[i, core, k]
        sister = (1 - self.section, self.ctx, self.fsdp)
        send(spot, spot, self.send_sem.at[i, k], recv, sister).wait_recv()

    def relay(self):
        if self.square:

            @pl.when(self.keeper)
            def _():
                for i, k in self.early:
                    for core in range(2):
                        self.arrival(i, core, k)
                        self.onward(i, core).start()

    def end(self):
        @pl.when(self.keeper)
        def _():
            for k in range(self.count):
                for core in range(2):
                    for i in self.all:
                        if (i, k) not in self.early and (k or core != self.layer):
                            self.arrival(i, core, k)
            if self.square:
                for i in self.all:
                    for core in range(2):
                        self.onward(i, core).wait_send()

        @pl.when(jnp.logical_not(self.keeper))
        def _():
            for i in self.all:
                self.own(i, 0).wait_send()

        for i, k in self.outgoing():
            self.own(i, k).wait_send()


def row_halves(rows):
    cut = rows // 2 // 16 * 16
    return (pl.ds(0, cut), pl.ds(cut, rows - cut))


def column_halves(width):
    cut = -(-width // 256) * 128
    return ((slice(None), pl.ds(0, cut)), (slice(None), pl.ds(cut, width - cut)))


def owner_sems(ctx_count):
    return [dma(4, ctx_count), dma(4, 2, ctx_count), dma(4, 2)]


class LineSum:
    def __init__(self, fsdp_count, grad_ref, done_ref, refs):
        self.own_ref, self.a_ref, self.sum_ref, self.in_ref, self.a_sem, self.z_send, self.z_recv = refs
        self.grad_ref, self.done_ref = grad_ref, done_ref
        self.section, self.ctx, self.fsdp = place_of()
        self.fsdp_count = fsdp_count
        self.group = fsdp_count // 2
        self.units = grad_ref.shape[0] // fsdp_count
        self.sister = (1 - self.section, self.ctx, self.fsdp)
        self.holds = self.fsdp // self.group == self.section

    def part(self, core):
        size = self.group * self.units
        return self.grad_ref.at[pl.ds(pl.multiple_of(core * size, size), size)]

    def load(self):
        return pltpu.make_async_copy(self.part(self.section), self.own_ref, self.a_sem.at[2])

    def chip(self):
        source = self.part(1 - self.section)
        return send(source, self.a_ref, self.a_sem.at[0], self.a_sem.at[1], self.sister)

    def line(self, j):
        device = (self.section, self.ctx, self.section * self.group + j)
        source = self.sum_ref.at[pl.ds(j * self.units, self.units)]
        return send(source, self.in_ref.at[self.fsdp], self.z_send.at[j], self.z_recv.at[self.fsdp], device)

    def elsewhere(self, j):
        return pl.when(self.section * self.group + j != self.fsdp)

    def begin(self):
        self.chip().start()
        self.load().start()

    def middle(self):
        self.load().wait()
        self.chip().wait_recv()
        self.sum_ref[...] = (self.own_ref[...].astype(f32) + self.a_ref[...].astype(f32)).astype(bf16)
        for j in range(self.group):

            @self.elsewhere(j)
            def _():
                self.line(j).start()

    def end(self):
        @pl.when(self.holds)
        def _():
            start = lax.rem(self.fsdp, self.group) * self.units
            total = self.sum_ref[pl.ds(pl.multiple_of(start, self.units), self.units)].astype(f32)
            for d in range(1, self.fsdp_count):
                came = lax.rem(self.fsdp + d, self.fsdp_count)
                spot = self.in_ref.at[came]
                send(spot, spot, self.z_send.at[0], self.z_recv.at[came], self.sister).wait_recv()
                total = total + self.in_ref[came].astype(f32)
            self.done_ref[...] = total.astype(bf16)

    def sent(self):
        self.chip().wait_send()
        for j in range(self.group):

            @self.elsewhere(j)
            def _():
                self.line(j).wait_send()


def line_scratch(fsdp_count, grad):
    units, width = grad.shape
    half = VMEM((units // 2, width), bf16)
    shards = VMEM((fsdp_count, units // fsdp_count, width), bf16)
    return [half, half, half, shards, dma(3), dma(fsdp_count), dma(fsdp_count)]


class Handout:
    def __init__(self, ctx_count, fsdp_count, layer, done_ref, all_ref, refs):
        self.own_sem, self.o_send, self.o_recv, self.n_send = refs
        self.layer, self.done_ref, self.all_ref = layer, done_ref, all_ref
        self.section, self.ctx, self.fsdp = place_of()
        self.count, self.square = ctx_count, ctx_count == 4
        self.halves = column_halves(done_ref.shape[1])
        self.holder = self.fsdp // (fsdp_count // 2)
        self.holds = self.section == self.holder
        self.keeps = self.section == layer
        self.away = jnp.logical_and(self.holds, jnp.logical_not(self.keeps))
        self.at_home = jnp.logical_and(self.holds, self.keeps)
        self.early = ((1, 1), (2, 0)) if self.square else ()
        late = ((1, 0), (2, 1)) if self.square else ()
        pairs = [(k, h) for k in range(1, ctx_count) for h in range(2)]
        self.sends = (*self.early, *late) if self.square else pairs

    def spot(self, k, h):
        return self.all_ref.at[flip(self.ctx, k)].at[self.halves[h]]

    def peer(self, k):
        return (self.layer, flip(self.ctx, k), self.fsdp)

    def out(self, k, h):
        source = self.done_ref.at[self.halves[h]]
        return send(source, self.spot(0, h), self.o_send.at[k, h], self.o_recv.at[k, h], self.peer(k))

    def onward(self, h):
        came = 1 if h else 2
        spot = self.spot(came, h)
        return send(spot, spot, self.n_send.at[h], self.o_recv.at[3, h], self.peer(3 - came))

    def arrival(self, k, h):
        spot = self.spot(k, h)
        sister = (1 - self.section, self.ctx, self.fsdp)
        send(spot, spot, self.o_send.at[k, h], self.o_recv.at[k, h], sister).wait_recv()

    def kept(self):
        return pltpu.make_async_copy(self.done_ref, self.all_ref.at[self.ctx], self.own_sem.at[0])

    def begin(self):
        @pl.when(self.holds)
        def _():
            for k, h in self.sends:
                self.out(k, h).start()

        @pl.when(self.away)
        def _():
            for h in range(2):
                self.out(0, h).start()

        @pl.when(self.at_home)
        def _():
            self.kept().start()

    def relay(self):
        @pl.when(self.keeps)
        def _():
            for k, h in self.early:
                self.arrival(k, h)
                self.onward(h).start()

    def end(self):
        @pl.when(self.keeps)
        def _():
            for k in range(1, self.count):
                for h in range(2):
                    if (k, h) not in self.early:
                        self.arrival(k, h)
            for _, h in self.early:
                self.onward(h).wait_send()

        @pl.when(jnp.logical_and(self.keeps, jnp.logical_not(self.holds)))
        def _():
            for h in range(2):
                self.arrival(0, h)

        @pl.when(self.holds)
        def _():
            for k, h in self.sends:
                self.out(k, h).wait_send()

        @pl.when(self.away)
        def _():
            for h in range(2):
                self.out(0, h).wait_send()

        @pl.when(self.at_home)
        def _():
            self.kept().wait()


def handout_sems(ctx_count):
    return [dma(1), dma(ctx_count, 2), dma(ctx_count, 2), dma(2)]


def chip_square(ctx_count):
    section, ctx, fsdp = place_of()
    return [
        (section if same else 1 - section, flip(ctx, k), fsdp)
        for k in range(ctx_count)
        for same in (True, False)
        if k or not same
    ]


def turn_tile(values):
    lane = lax.broadcasted_iota(jnp.int32, values.shape, 1)
    width = values.shape[1]
    half = HEAD_DIM // 2
    ahead = pltpu.roll(values, width - half, 1)
    behind = pltpu.roll(values, half, 1)
    return jnp.where(lane % HEAD_DIM < half, ahead, behind)


def head_in_group(tile, head, group):
    lane = lax.broadcasted_iota(jnp.int32, tile.shape, 1)
    values = tile.astype(f32)
    moved = values if head % 2 == group else pltpu.roll(values, HEAD_DIM, 1)
    return jnp.where(lane // HEAD_DIM == group, moved, 0.0).astype(bf16)


def attend_kernel(count, fsdp_count, layer, *refs):
    x_ref, vectors_ref, w_ref, cos_ref, sin_ref, kpos_ref, qpos_ref = refs[:7]
    refs = refs[7:]
    if layer:
        shard_ref, *refs = refs
    normed_ref, q_ref, kv_ref, lse_ref, ctx_ref, mid_ref, low2_ref = refs[:7]
    refs = refs[7:]
    if layer:
        next_ref, *refs = refs
    mask_ref, s_ref, p_ref, vt_ref, ctxf_ref, send_sem, recv_sem, *sems = refs
    rows, width = x_ref.shape
    pair = kv_ref.shape[2] // 2
    wide = width + 2 * pair
    heads = width // HEAD_DIM
    group_size = heads // (pair // HEAD_DIM)
    if layer:
        line = Line(fsdp_count, shard_ref, next_ref, sems)
        greet_all([peer_of(k) for k in range(1, count)] + [line.sister] + line.ahead)
        line.begin()
    else:
        greet(count)
    x = x_ref[...].astype(f32)
    gain1, bias, gain2 = (vectors_ref[4 * layer + i : 4 * layer + i + 1, :] for i in range(3))
    normed = (x * row_scale(x) * gain1[:, :width]).astype(bf16)
    normed_ref[...] = normed
    cos, sin = cos_ref[...], sin_ref[...]
    kv = matmul(normed, w_ref[:, width:wide]) + bias[:, width:wide]
    keys = kv[:, :pair]
    kv_ref[0, :, :pair] = (keys * cos + turn_tile(keys) * sin).astype(bf16)
    kv_ref[0, :, pair:] = kv[:, pair:].astype(bf16)
    for k in range(1, count):
        remote(kv_ref.at[0], kv_ref.at[k], send_sem, recv_sem, k).start()
    merged = matmul(normed, w_ref[:, :width]) + bias[:, :width]
    for start, size in tiles(width, 2 * HEAD_DIM):
        part = merged[:, start : start + size]
        turned_part = (part * cos + turn_tile(part) * sin) * HEAD_DIM ** (-0.5)
        q_ref[:, start : start + size] = turned_part.astype(bf16)
    for k in range(count):
        allowed = kpos_ref[k * rows : (k + 1) * rows, :] <= qpos_ref[...]
        mask_ref[k] = jnp.where(allowed, 0.0, masked_value)
    for k in range(count):
        if k:
            remote(kv_ref.at[0], kv_ref.at[k], send_sem, recv_sem, k).wait_recv()
        vt_ref[:, k * rows : (k + 1) * rows] = kv_ref[k, :, pair:].astype(f32).T.astype(bf16)

    for head in range(heads):
        group = head // group_size
        start = head // 2 * (2 * HEAD_DIM)
        query = head_in_group(q_ref[:, start : start + 2 * HEAD_DIM], head, group)
        top = None
        for k in range(count):
            scores = matmul_nt(kv_ref[k, :, :pair], query) + mask_ref[k]
            s_ref[k] = scores
            here = jnp.max(scores, axis=0, keepdims=True)
            top = here if top is None else jnp.maximum(top, here)
        total = None
        for k in range(count):
            weight = jnp.exp(s_ref[k] - top)
            here = jnp.sum(weight, axis=0, keepdims=True)
            total = here if total is None else total + here
            p_ref[k * rows : (k + 1) * rows, :] = weight.astype(bf16)
        value_rows = vt_ref[group * HEAD_DIM : (group + 1) * HEAD_DIM, :]
        context = matmul(value_rows, p_ref[...]) * (1.0 / total)
        ctxf_ref[head * HEAD_DIM : (head + 1) * HEAD_DIM, :] = context
        lse_ref[head : head + 1, :] = top + jnp.log(total)
        for e in range(1, fsdp_count - 1) if layer else ():
            if head == e * heads // fsdp_count + 1:
                line.relay(e)
    context = ctxf_ref[...]
    ctx_ref[...] = context.astype(bf16)
    middle = x + matmul(context.T.astype(bf16), w_ref[:, wide:])
    mid_ref[...] = middle
    low2_ref[...] = (middle * row_scale(middle) * gain2[:, :width]).astype(bf16)
    for k in range(1, count):
        remote(kv_ref.at[0], kv_ref.at[k], send_sem, recv_sem, k).wait_send()
    if layer:
        line.relay(fsdp_count - 1)
        line.end()


def attend(layer, hidden, place, piece=()):
    index, vectors, weights = layer[:3]
    cosine, sine, key_positions, query_positions = place
    rows, width = hidden.shape
    count = lax.axis_size(CTX)
    wide = weights.shape[1] - width
    pair = (wide - width) // 2
    keys = count * rows
    heads = width // HEAD_DIM
    fsdp_count = lax.axis_size(FSDP)
    args = (hidden, vectors, weights, cosine, sine, key_positions, query_positions)
    return call(
        functools.partial(attend_kernel, count, fsdp_count, index),
        [
            ((rows, width), bf16),
            ((rows, width), bf16),
            ((count, rows, 2 * pair), bf16),
            ((-(-heads // 8) * 8, rows), f32),
            ((width, rows), bf16),
            ((rows, width), f32),
            ((rows, width), bf16),
        ]
        + [((fsdp_count * array.shape[0], width), bf16) for array in piece],
        [
            VMEM((count, rows, rows), f32),
            VMEM((count, rows, rows), f32),
            VMEM((keys, rows), bf16),
            VMEM((pair, keys), bf16),
            VMEM((width, rows), f32),
            dma(count),
            dma(count),
        ]
        + line_sems(fsdp_count) * len(piece),
        1 if index else 10,
        *args, *piece,
        far_outs=(7,) * len(piece),
    )


def attend_back_kernel(count, layer, carried, *refs):
    (
        dmid_ref, x_ref, vectors_ref, w_ref, cos_ref, sin_ref, kpos_ref, qpos_ref,
        normed_ref, q_ref, kv_ref, lse_ref, ctx_ref,
    ) = refs[:13]
    refs = refs[13:]
    (load_ref, expand_ref), refs = (refs[:2], refs[2:]) if carried else ((None, None), refs)
    dh_ref, gain_ref, bias_ref, grad_ref = refs[:4]
    refs = refs[4:]
    (summed_ref, expand_all_ref), refs = (refs[:2], refs[2:]) if carried else ((None, None), refs)
    (
        mask_ref, p_ref, dp_ref, ds_ref, kt_ref, dctx_ref, dq_ref, dkv_ref, out_ref, in_ref,
        merged_ref, low_ref, send_sem, recv_sem, *scratch,
    ) = refs
    rows, width = x_ref.shape
    pair = kv_ref.shape[2] // 2
    wide = width + 2 * pair
    heads = width // HEAD_DIM
    group_size = heads // (pair // HEAD_DIM)
    if carried:
        section, ctx, _ = place_of()
        steps = SquareSum(count, load_ref, *scratch[:3], scratch[3:7])
        halves = [row_halves(expand_ref.shape[0])]
        owners = Owners(count, 1, [expand_ref], [expand_all_ref], halves, scratch[7:10])
        kept = pltpu.make_async_copy(expand_ref, expand_all_ref.at[ctx, section], scratch[10].at[0])
        greet_all(chip_square(count))
        steps.begin()
        owners.begin()

        @pl.when(owners.keeper)
        def _():
            kept.start()

    else:
        greet(count)
    low = dmid_ref[...].astype(bf16)
    low_ref[...] = low
    dctx = matmul_nt(low, w_ref[:, wide:]).astype(bf16)
    dctx_ref[...] = dctx
    for k in range(count):
        allowed = kpos_ref[k * rows : (k + 1) * rows, :] <= qpos_ref[...]
        mask_ref[k] = jnp.where(allowed, 0.0, masked_value)
        kt_ref[:, k * rows : (k + 1) * rows] = kv_ref[k, :, :pair].astype(f32).T.astype(bf16)
    dkv_ref[...] = jnp.zeros_like(dkv_ref)

    for head in range(heads):
        group = head // group_size
        start = head // 2 * (2 * HEAD_DIM)
        query = head_in_group(q_ref[:, start : start + 2 * HEAD_DIM], head, group)
        upstream = head_in_group(dctx_ref[:, start : start + 2 * HEAD_DIM], head, group)
        lse = lse_ref[head : head + 1, :]
        delta = None
        for k in range(count):
            scores = matmul_nt(kv_ref[k, :, :pair], query) + mask_ref[k]
            weight = jnp.exp(scores - lse)
            weight_grad = matmul_nt(kv_ref[k, :, pair:], upstream)
            p_ref[k] = weight
            dp_ref[k] = weight_grad
            dkv_ref[k, :, pair:] += matmul(weight.astype(bf16), upstream)
            here = jnp.sum(weight * weight_grad, axis=0, keepdims=True)
            delta = here if delta is None else delta + here
        for k in range(count):
            score_grad = (p_ref[k] * (dp_ref[k] - delta)).astype(bf16)
            ds_ref[k * rows : (k + 1) * rows, :] = score_grad
            dkv_ref[k, :, :pair] += matmul(score_grad, query)
        key_rows = kt_ref[group * HEAD_DIM : (group + 1) * HEAD_DIM, :]
        dq_ref[head * HEAD_DIM : (head + 1) * HEAD_DIM, :] = (
            matmul(key_rows, ds_ref[...]) * HEAD_DIM ** (-0.5)
        )
        if carried and head == heads // 5:
            steps.middle()
        if carried and head == heads // 3:
            owners.relay()
        if carried and head == heads * 2 // 3:
            steps.merge()
    for k in range(1, count):
        out_ref[k] = dkv_ref[k].astype(bf16)
        remote(out_ref.at[k], in_ref.at[k], send_sem, recv_sem, k).start()
    cos, sin = cos_ref[...], sin_ref[...]
    dq = dq_ref[...].T

    def unturn(part):
        return (part * cos - turn_tile(part) * sin).astype(bf16)

    for start, size in tiles(width, 2 * HEAD_DIM):
        merged_ref[:, start : start + size] = unturn(dq[:, start : start + size])
    grad_ref[:, wide:] = matmul(ctx_ref[...], low_ref[...]).astype(bf16)
    normed = normed_ref[...]

    def project_grad(first, last):
        for start, size in tiles(last - first, 512):
            cut = slice(first + start, first + start + size)
            grad_ref[:, cut] = matmul_tn(normed, merged_ref[:, cut]).astype(bf16)

    project_grad(0, width)
    normed_grad = matmul_nt(merged_ref[:, :width], w_ref[:, :width])
    total = dkv_ref[0]
    for k in range(1, count):
        remote(out_ref.at[k], in_ref.at[k], send_sem, recv_sem, k).wait_recv()
        total = total + in_ref[k].astype(f32)
    merged_ref[:, width : width + pair] = unturn(total[:, :pair])
    merged_ref[:, width + pair :] = total[:, pair:].astype(bf16)
    project_grad(width, wide)
    normed_grad = normed_grad + matmul_nt(merged_ref[:, width:], w_ref[:, width:wide])
    bias_ref[...] = jnp.sum(merged_ref[...].astype(f32), axis=0, keepdims=True)
    x = x_ref[...].astype(f32)
    scale = row_scale(x)
    gain_ref[...] = jnp.sum(normed_grad * x * scale, axis=0, keepdims=True)
    scaled = normed_grad * vectors_ref[4 * layer : 4 * layer + 1, :width]
    mean = jnp.mean(scaled * x, axis=-1, keepdims=True)
    hidden_grad = dmid_ref[...] + scale * scaled - x * (scale * scale * scale * mean)
    dh_ref[...] = hidden_grad.astype(dh_ref.dtype)
    for k in range(1, count):
        remote(out_ref.at[k], in_ref.at[k], send_sem, recv_sem, k).wait_send()
    if carried:
        summed_ref[...] = steps.end()
        steps.sent()
        owners.end()

        @pl.when(owners.keeper)
        def _():
            kept.wait()


def attend_back(layer, kept, middle_grad, place, load=()):
    index, vectors, weights = layer[:3]
    cosine, sine, key_positions, query_positions = place
    hidden, normed, queries, every_kv, lse, context = kept
    rows, width = hidden.shape
    count = lax.axis_size(CTX)
    wide = weights.shape[1] - width
    pair = (wide - width) // 2
    keys = count * rows
    carried = bool(load)
    args = (
        middle_grad, hidden, vectors, weights, cosine, sine, key_positions, query_positions,
        normed, queries, every_kv, lse, context,
    )
    return call(
        functools.partial(attend_back_kernel, count, index, carried),
        [
            ((rows, width), bf16 if index else f32),
            ((1, width), f32),
            ((1, wide), f32),
            ((width, wide + width), bf16),
        ]
        + (
            [((width, (wide + width) // (2 * count)), bf16), ((count, 2) + load[1].shape, bf16)]
            if carried
            else []
        ),
        [
            VMEM((count, rows, rows), f32),
            VMEM((count, rows, rows), f32),
            VMEM((count, rows, rows), f32),
            VMEM((keys, rows), bf16),
            VMEM((pair, keys), bf16),
            VMEM((rows, width), bf16),
            VMEM((width, rows), f32),
            VMEM((count, rows, 2 * pair), f32),
            VMEM((count, rows, 2 * pair), bf16),
            VMEM((count, rows, 2 * pair), bf16),
            VMEM((rows, wide), bf16),
            VMEM((rows, width), bf16),
            dma(count),
            dma(count),
        ]
        + (square_scratch(count, load[0]) + owner_sems(count) + [dma(1)] if carried else []),
        6 if carried else 2,
        *args, *load,
        far_outs=(5,) if carried else (),
    )


def unit_chunks(units):
    main = units // 128 * 128
    chunks = [(start, main + start, start, size) for start, size in tiles(main, 512)]
    if units > main:
        chunks.append((2 * main, main + units, main, units - main))
    return chunks


def pack_units(gate, up):
    main = gate.shape[1] // 128 * 128
    return jnp.concatenate([gate[:, :main], up[:, :main], gate[:, main:], up[:, main:]], axis=1)


def unpack_units(packed):
    units = packed.shape[-1] // 2
    main = units // 128 * 128
    if units == main:
        return packed[..., :main], packed[..., main:]
    gate = jnp.concatenate([packed[..., :main], packed[..., 2 * main : main + units]], axis=-1)
    up = jnp.concatenate([packed[..., main : 2 * main], packed[..., main + units :]], axis=-1)
    return gate, up


class Rows:
    def __init__(self, count, own_ref, slots_ref, send_sem, recv_sem):
        self.own_ref, self.slots_ref = own_ref, slots_ref
        self.send_sem, self.recv_sem = send_sem, recv_sem
        self.count, self.square = count, count == 4
        self.half = own_ref.shape[0] // 2

    def rows(self, h):
        return pl.ds(h * self.half, self.half)

    def copy(self, source, k, h, peer):
        target = self.slots_ref.at[k, self.rows(h)]
        return send(source, target, self.send_sem.at[k, h], self.recv_sem.at[k, h], peer_of(peer))

    def own(self, k, h):
        return self.copy(self.own_ref.at[self.rows(h)], k, h, k)

    def onward(self, h):
        came = 1 if h else 2
        return self.copy(self.slots_ref.at[came, self.rows(h)], 3, h, 3 - came)

    def order(self):
        if self.square:
            return [(1, 1), (2, 0), (1, 0), (2, 1)]
        return [(k, h) for k in range(1, self.count) for h in range(2)]

    def begin(self):
        for k, h in self.order():
            self.own(k, h).start()

    def relay(self):
        if self.square:
            for k, h in ((1, 1), (2, 0)):
                self.own(k, h).wait_recv()
                self.onward(h).start()

    def take(self, k):
        for h in range(2):
            if not (self.square and (k, h) in ((1, 1), (2, 0))):
                self.copy(self.own_ref.at[self.rows(h)], k, h, k).wait_recv()

    def sent(self):
        for k, h in self.order():
            self.own(k, h).wait_send()
        if self.square:
            for h in range(2):
                self.onward(h).wait_send()


class Parts:
    def __init__(self, count, parts_ref, got_ref, send_sem, recv_sem):
        self.parts_ref, self.got_ref = parts_ref, got_ref
        self.send_sem, self.recv_sem = send_sem, recv_sem
        self.count, self.square = count, count == 4
        self.half = parts_ref.shape[1] // 2

    def rows(self, h):
        return pl.ds(h * self.half, self.half)

    def copy(self, k, h):
        peer = 1 + h if self.square and k == 3 else k
        source, target = self.parts_ref.at[k, self.rows(h)], self.got_ref.at[k, self.rows(h)]
        return send(source, target, self.send_sem.at[k, h], self.recv_sem.at[k, h], peer_of(peer))

    def put(self, k, part):
        self.parts_ref[k] = part.astype(bf16)
        for h in range(2):
            if not (self.square and (k, h) in ((1, 1), (2, 0))):
                self.copy(k, h).start()

    def merge(self):
        if self.square:
            for k, h in ((2, 0), (1, 1)):
                self.copy(3, h).wait_recv()
                rows = slice(h * self.half, (h + 1) * self.half)
                total = self.parts_ref[k, rows].astype(f32) + self.got_ref[3, rows].astype(f32)
                self.parts_ref[k, rows] = total.astype(bf16)
                self.copy(k, h).start()

    def total(self, own):
        for k in range(1, 3 if self.square else self.count):
            for h in range(2):
                self.copy(k, h).wait_recv()
            own = own + self.got_ref[k].astype(f32)
        return own

    def sent(self):
        for k in range(1, self.count):
            for h in range(2):
                self.copy(k, h).wait_send()


class Loads:
    def __init__(self, sources, targets, sem):
        self.copies = [
            pltpu.make_async_copy(source, target, sem.at[i])
            for i, (source, target) in enumerate(zip(sources, targets))
        ]
        for copy in self.copies:
            copy.start()

    def take(self, *which):
        for i in which:
            self.copies[i].wait()


def gate_and_up(block, expand_ref, gate_start, up_start, size):
    if size % 128:
        both = matmul(block, expand_ref[:, gate_start : up_start + size])
        return both[:, :size], both[:, size:]
    gate = matmul(block, expand_ref[:, gate_start : gate_start + size])
    return gate, matmul(block, expand_ref[:, up_start : up_start + size])


def feed_kernel(
    count, low_ref, mid_ref, expand_any, down_any,
    out_ref, blocks_ref, kept_gate_ref, kept_up_ref,
    expand_ref, down_ref, act_ref, part_ref, sent_ref, got_ref,
    send_sem, recv_sem, send_sem2, recv_sem2, load_sem,
):
    units = down_ref.shape[0]
    loads = Loads((expand_any, down_any), (expand_ref, down_ref), load_sem)
    rows = Rows(count, low_ref, blocks_ref, send_sem, recv_sem)
    parts = Parts(count, sent_ref, got_ref, send_sem2, recv_sem2)
    greet(count)
    rows.begin()
    blocks_ref[0] = low_ref[...]
    loads.take(0, 1)
    for k in range(count):
        if k:
            rows.take(k)
        block = blocks_ref[k]
        for gate_start, up_start, start, size in unit_chunks(units):
            gate, up = gate_and_up(block, expand_ref, gate_start, up_start, size)
            kept_gate_ref[k, :, start : start + size] = gate.astype(bf16)
            kept_up_ref[k, :, start : start + size] = up.astype(bf16)
            act_ref[:, start : start + size] = (gate / (1.0 + jnp.exp(-gate)) * up).astype(bf16)
        part = matmul(act_ref[...], down_ref[...])
        if k:
            parts.put(k, part)
        else:
            part_ref[...] = part + mid_ref[...]
            rows.relay()
    parts.merge()
    out_ref[...] = parts.total(part_ref[...]).astype(bf16)
    rows.sent()
    parts.sent()


def feed(layer, second_normed, middle):
    expand_w, down_w = layer[3:]
    count = lax.axis_size(CTX)
    rows, width = second_normed.shape
    units = down_w.shape[0]
    return call(
        functools.partial(feed_kernel, count),
        [
            ((rows, width), bf16),
            ((count, rows, width), bf16),
            ((count, rows, units), bf16),
            ((count, rows, units), bf16),
        ],
        [
            VMEM(expand_w.shape, bf16),
            VMEM(down_w.shape, bf16),
            VMEM((rows, units), bf16),
            VMEM((rows, width), f32),
            VMEM((count, rows, width), bf16),
            VMEM((count, rows, width), bf16),
        ]
        + [dma(count, 2)] * 4
        + [dma(2)],
        3,
        second_normed, middle, expand_w, down_w, far=(2, 3),
    )


def feed_back_kernel(count, fsdp_count, layer, carried, *refs):
    (
        grad_ref, mid_ref, vectors_ref,
        blocks_any, kept_gate_any, kept_up_any, expand_any, down_any,
    ) = refs[:8]
    refs = refs[8:]
    line_ref, refs = (refs[0], refs[1:]) if carried else (None, refs)
    dmid_ref, gain_ref, dexpand_ref, ddown_ref = refs[:4]
    refs = refs[4:]
    done_ref, refs = (refs[0], refs[1:]) if carried else (None, refs)
    (
        blocks_ref, kept_gate_ref, kept_up_ref, expand_ref, down_ref,
        grads_ref, act_ref, dwide_ref, part_ref, sent_ref, got_ref,
        send_sem, recv_sem, send_sem2, recv_sem2, load_sem, *scratch,
    ) = refs
    rows, width = grad_ref.shape
    units = down_ref.shape[0]
    loads = Loads(
        (down_any, kept_gate_any, kept_up_any, expand_any, blocks_any),
        (down_ref, kept_gate_ref, kept_up_ref, expand_ref, blocks_ref),
        load_sem,
    )
    gather = Rows(count, grad_ref, grads_ref, send_sem, recv_sem)
    parts = Parts(count, sent_ref, got_ref, send_sem2, recv_sem2)
    if carried:
        line = LineSum(fsdp_count, line_ref, done_ref, scratch)
        section, ctx, fsdp = place_of()
        greet_all(
            [peer_of(k) for k in range(1, count)]
            + [line.sister]
            + [(section, ctx, lax.rem(fsdp + d, fsdp_count)) for d in range(1, fsdp_count)]
        )
        line.begin()
    else:
        greet(count)
    gather.begin()
    grads_ref[0] = grad_ref[...]
    loads.take(0, 1, 2)
    for k in range(count):
        if k:
            gather.take(k)
        block = grads_ref[k]
        for gate_start, up_start, start, size in unit_chunks(units):
            cut = slice(start, start + size)
            spread = matmul_nt(block, down_ref[cut, :])
            gate = kept_gate_ref[k, :, cut].astype(f32)
            up = kept_up_ref[k, :, cut].astype(f32)
            sig = 1.0 / (1.0 + jnp.exp(-gate))
            silu = gate * sig
            act_ref[k, :, cut] = (silu * up).astype(bf16)
            dgate = (spread * up * sig * (1.0 + gate * (1.0 - sig))).astype(bf16)
            dup = (spread * silu).astype(bf16)
            if size % 128:
                dwide_ref[k, :, gate_start : up_start + size] = jnp.concatenate([dgate, dup], axis=1)
            else:
                dwide_ref[k, :, gate_start : gate_start + size] = dgate
                dwide_ref[k, :, up_start : up_start + size] = dup
        if not k:
            loads.take(3)
        part = matmul_nt(dwide_ref[k], expand_ref[...])
        if k:
            parts.put(k, part)
        else:
            part_ref[...] = part
            gather.relay()
            if carried:
                line.middle()
    loads.take(4)
    tall = count * rows
    grads = grads_ref[...].reshape(tall, width)
    main = units // 128 * 128
    for start, size in tiles(main, 384) + [(main, units - main)] * (units > main):
        act = act_ref[:, :, start : start + size].reshape(tall, size)
        ddown_ref[start : start + size, :] = matmul_tn(act, grads).astype(bf16)
    parts.merge()
    blocks = blocks_ref[...].reshape(tall, width)
    for start, size in tiles(2 * units, 512):
        dwide = dwide_ref[:, :, start : start + size].reshape(tall, size)
        dexpand_ref[:, start : start + size] = matmul_tn(blocks, dwide).astype(bf16)
    if carried:
        line.end()
    total = parts.total(part_ref[...])
    middle = mid_ref[...]
    scale = row_scale(middle)
    gain_ref[...] = jnp.sum(total * middle * scale, axis=0, keepdims=True)
    scaled = total * vectors_ref[4 * layer + 2 : 4 * layer + 3, :width]
    mean = jnp.mean(scaled * middle, axis=-1, keepdims=True)
    dmid_ref[...] = (
        grad_ref[...].astype(f32) + scale * scaled - middle * (scale * scale * scale * mean)
    )
    gather.sent()
    parts.sent()
    if carried:
        line.sent()


def feed_back(layer, middle, blocks, kept_gate, kept_up, grad_out, load=()):
    index, vectors = layer[:2]
    expand_w, down_w = layer[3:]
    count = lax.axis_size(CTX)
    rows, width = grad_out.shape
    units = down_w.shape[0]
    fsdp_count = lax.axis_size(FSDP)
    brought = (blocks, kept_gate, kept_up, expand_w, down_w)
    return call(
        functools.partial(feed_back_kernel, count, fsdp_count, index, bool(load)),
        [
            ((rows, width), f32),
            ((1, width), f32),
            ((width, 2 * units), bf16),
            ((units, width), bf16),
        ]
        + [((units // fsdp_count, width), bf16)] * len(load),
        [VMEM(array.shape, bf16) for array in brought]
        + [
            VMEM((count, rows, width), bf16),
            VMEM((count, rows, units), bf16),
            VMEM((count, rows, 2 * units), bf16),
            VMEM((rows, width), f32),
            VMEM((count, rows, width), bf16),
            VMEM((count, rows, width), bf16),
        ]
        + [dma(count, 2)] * 4
        + [dma(5)]
        + (line_scratch(fsdp_count, load[0]) if load else []),
        4 + 7 * index,
        grad_out, middle, vectors, *brought, *load, far=(3, 4, 5, 6, 7, 8),
    )


def attn_sum_kernel(
    ctx_count, fsdp_count, wide, low_ref, high_ref, small_ref, down_ref,
    act_zero_ref, act_one_ref, grad_zero_ref, grad_one_ref, down_grad_ref, expand_ref, expand_all_ref,
    projections_ref, output_ref, total_ref, down_all_ref, act_ref, grad_ref, expand_out,
    wide_ref, done_ref,
    c_out, c_in, d_out, whole_ref, s_out, s_in,
    c_send, c_recv, d_send, d_recv, s_send, s_recv, *more,
):
    section, ctx, fsdp = place_of()
    sister = (1 - section, ctx, fsdp)
    width, piece = high_ref.shape
    rows = width // fsdp_count
    places = range(1, ctx_count)
    shards = range(1, fsdp_count)
    steps = SquareSum(ctx_count, low_ref, *more[:3], more[3:7])
    halves = [row_halves(expand_ref.shape[0])]
    owners = Owners(ctx_count, 0, [expand_ref], [expand_out], halves, more[7:10])
    own_sem, swap_send, swap_recv = more[10:13]
    kept = pltpu.make_async_copy(expand_ref, expand_out.at[ctx, section], own_sem.at[0])
    load = pltpu.make_async_copy(expand_all_ref, expand_out, own_sem.at[1])
    down = LineSum(fsdp_count, down_grad_ref, done_ref, more[13:20])
    handouts = [
        Handout(ctx_count, fsdp_count, 1, down_ref, down_all_ref, more[20:24]),
        Handout(ctx_count, fsdp_count, 0, done_ref, down_all_ref, more[24:28]),
    ]
    layers = ((act_zero_ref, grad_zero_ref), (act_one_ref, wide_ref))

    def swap(i, layer):
        target = (act_ref, grad_ref)[i].at[section]
        return send(layers[layer][i], target, swap_send.at[i], swap_recv.at[i], sister)

    def ahead(d):
        return (section, ctx, lax.rem(fsdp + d, fsdp_count))

    def c_copy(layer, d):
        target = lax.rem(fsdp + d, fsdp_count)
        source = c_out.at[layer, pl.ds(pl.multiple_of(target * rows, rows), rows)]
        return send(source, c_in.at[layer, d], c_send.at[layer, d], c_recv.at[layer, d], ahead(d))

    def s_copy(step, source, device):
        return send(s_out.at[source], s_in.at[step], s_send.at[step], s_recv.at[step], device)

    def line_sum(layer):
        total = c_out[layer, pl.ds(pl.multiple_of(fsdp * rows, rows), rows)].astype(f32)
        for d in shards:
            c_copy(layer, d).wait_recv()
            total = total + c_in[layer, d].astype(f32)
        d_out[layer] = total.astype(bf16)
        every_owner(
            ctx_count, layer, "start", [d_out.at[layer]], [whole_ref], d_send.at[layer], d_recv
        )

        @pl.when(section == layer)
        def _():
            whole_ref[ctx, section] = d_out[layer]

    hops = [(0, 0, sister)]
    hops += [(k, 1, peer_of(k)) for k in places]
    hops += [(ctx_count - 1 + d, 2, ahead(d)) for d in shards]

    greet_all(chip_square(ctx_count) + [ahead(d) for d in shards])
    steps.begin()
    down.begin()
    owners.begin()

    @pl.when(section == 0)
    def _():
        kept.start()

    @pl.when(section == 1)
    def _():
        load.start()

    wide_ref[...] = grad_one_ref[...].astype(f32)
    for layer in range(2):

        @pl.when(section != layer)
        def _():
            for i in range(2):
                swap(i, layer).start()

        @pl.when(section == layer)
        def _():
            for i, target in enumerate((act_ref, grad_ref)):
                target[section] = layers[layer][i][...]

    s_out[0] = small_ref[...]
    s_copy(*hops[0]).start()
    c_out[1] = high_ref[...]
    for d in shards:
        c_copy(1, d).start()

    steps.middle()
    down.middle()
    handouts[0].begin()
    owners.relay()
    s_copy(*hops[0]).wait_recv()
    s_out[1] = s_out[0] + s_in[0]
    for k in places:
        s_copy(*hops[k]).start()
    line_sum(1)
    steps.merge()
    c_out[0] = steps.end()
    for d in shards:
        c_copy(0, d).start()
    handouts[0].relay()
    down.end()
    handouts[1].begin()
    part = s_out[1]
    for k in places:
        s_copy(*hops[k]).wait_recv()
        part = part + s_in[k]
    s_out[2] = part
    for d in shards:
        s_copy(*hops[ctx_count - 1 + d]).start()
    line_sum(0)
    part = s_out[2]
    for d in shards:
        s_copy(*hops[ctx_count - 1 + d]).wait_recv()
        part = part + s_in[ctx_count - 1 + d]
    total_ref[...] = part
    for layer in (1, 0):
        from_owners(ctx_count, layer, [whole_ref], d_send.at[layer], d_recv)
    for where in range(ctx_count):
        for core in range(2):
            start = (where * 2 + core) * piece
            block = whole_ref[where, core].astype(f32)
            size = max(min(wide - start, piece), 0)
            if size:
                projections_ref[:, start : start + size] = block[:, :size]
            if size < piece:
                first = start + size - wide
                output_ref[:, first : first + piece - size] = block[:, size:]
    owners.end()
    handouts[1].relay()
    for handout in handouts:
        handout.end()
    down.sent()

    @pl.when(section == 0)
    def _():
        kept.wait()

    @pl.when(section == 1)
    def _():
        load.wait()

    for i in range(2):
        swap(i, 0).wait()
    steps.sent()
    for layer in (1, 0):
        for d in shards:
            c_copy(layer, d).wait_send()
        every_owner(
            ctx_count, layer, "wait", [d_out.at[layer]], [whole_ref], d_send.at[layer], d_recv
        )
    for hop in hops:
        s_copy(*hop).wait_send()


def attn_sum(low, high, small, down_one, acts, grads, down_grad, expand_part, expand_all, wide):
    ctx_count, fsdp_count = lax.axis_size(CTX), lax.axis_size(FSDP)
    width, both = low.shape
    rows = width // fsdp_count
    piece = both // (2 * ctx_count)
    hops = ctx_count + fsdp_count - 1
    return call(
        functools.partial(attn_sum_kernel, ctx_count, fsdp_count, wide),
        [
            ((rows, wide), f32),
            ((rows, both - wide), f32),
            (small.shape, f32),
            ((ctx_count,) + down_one.shape, bf16),
            ((2,) + acts[0].shape, bf16),
            ((2,) + grads[0].shape, f32),
            (expand_all.shape, bf16),
        ],
        [
            VMEM(grads[0].shape, f32),
            VMEM(down_one.shape, bf16),
            VMEM((2, width, piece), bf16),
            VMEM((2, fsdp_count, rows, piece), bf16),
            VMEM((2, rows, piece), bf16),
            VMEM((ctx_count, 2, rows, piece), bf16),
            VMEM((3,) + small.shape, f32),
            VMEM((hops,) + small.shape, f32),
            dma(2, fsdp_count), dma(2, fsdp_count),
            dma(2, 1, ctx_count), dma(1, 2, ctx_count),
            dma(hops), dma(hops),
        ]
        + square_scratch(ctx_count, low)
        + owner_sems(ctx_count)
        + [dma(2), dma(2), dma(2)]
        + line_scratch(fsdp_count, down_grad)
        + handout_sems(ctx_count) * 2,
        7,
        low, high, small, down_one, *acts, *grads, down_grad, expand_part, expand_all,
        far=(8, 10), far_outs=(3,),
    )


def spread_kernel(chunk, stride, shards, side_width, block_ref, out_ref):
    count = block_ref.shape[0]
    for where in range(count):
        sides = unpack_units(block_ref[where].astype(f32))
        for side, values in enumerate(sides):
            for shard in range(shards):
                start = side * side_width + (shard * count + where) * chunk
                out_ref[:, start : start + chunk] = values[:, shard * stride : shard * stride + chunk]


def finish(expand_all, ff_width, units):
    ctx_count, fsdp_count = lax.axis_size(CTX), lax.axis_size(FSDP)
    half, packed = expand_all.shape[2:]
    rows = 2 * half
    step = 32 if rows % 32 == 0 else 16
    stride = packed // 2 // fsdp_count
    return pl.pallas_call(
        functools.partial(spread_kernel, units, stride, fsdp_count, ff_width),
        grid=(rows // step,),
        out_shape=jax.ShapeDtypeStruct((rows, 2 * ff_width), f32),
        in_specs=[pl.BlockSpec((ctx_count, step, packed), lambda i: (0, i, 0))],
        out_specs=pl.BlockSpec((step, 2 * ff_width), lambda i: (i, 0)),
        compiler_params=pltpu.CompilerParams(vmem_limit_bytes=LIMIT),
    )(expand_all.reshape(ctx_count, rows, packed))


def per_device(
    inputs,
    attend_gain,
    projections,
    biases,
    output_weight,
    mixer_gain,
    expand_weight,
    down_weight,
    positions,
    cotangent,
):
    row_count, model_width = inputs.shape[2:]
    section = lax.axis_index(SECTION)
    is_first = section == 0
    ctx = lax.axis_index(CTX)
    fsdp = lax.axis_index(FSDP)
    ctx_count = lax.axis_size(CTX)
    fsdp_count = lax.axis_size(FSDP)
    shard_rows = projections.shape[1]
    wide = projections.shape[2]
    ff_width = expand_weight.shape[2] // 2
    shard_units = down_weight.shape[1]
    units = shard_units // ctx_count
    spare_units = -units % 16
    both = (FSDP, SECTION)

    def mine(array):
        return lax.dynamic_index_in_dim(array, section, 0, keepdims=False)

    source = mine(inputs)[0]
    upstream = mine(cotangent)[0]
    key_positions = mine(positions)[0]
    query_positions = lax.dynamic_slice_in_dim(key_positions, ctx * row_count, row_count)
    cosine, sine = tables(query_positions)
    by_distance = jnp.concatenate(
        [
            lax.dynamic_slice_in_dim(key_positions, (ctx ^ k) * row_count, row_count)
            for k in range(ctx_count)
        ]
    )
    place = (cosine, sine, by_distance[:, None], query_positions[None])

    bias_part = biases.shape[1]
    small_width = -(-bias_part // 128) * 128

    def padded(row):
        return jnp.pad(row, ((0, 0), (0, small_width - row.shape[1])))

    small_shard = jnp.concatenate(
        [padded(attend_gain), padded(biases), padded(mixer_gain), jnp.zeros((13, small_width), bf16)]
    )
    attn_shard = jnp.concatenate([projections[0], output_weight[0]], axis=1)

    def in_order(array):
        other = swap_sections(array)
        return jnp.where(is_first, array, other), jnp.where(is_first, other, array)

    def unit_columns(side):
        pieces = []
        for shard in range(fsdp_count):
            start = side * ff_width + shard * shard_units
            pieces.append(
                pick(
                    ctx,
                    [
                        expand_weight[0, :, start + k * units : start + (k + 1) * units]
                        for k in range(ctx_count)
                    ],
                )
            )
            if spare_units:
                pieces.append(jnp.zeros((shard_rows, spare_units), bf16))
        return jnp.concatenate(pieces, axis=1)

    expand_shard = pack_units(unit_columns(0), unit_columns(1))
    down_shard = lax.dynamic_slice_in_dim(down_weight[0], ctx * units, units)
    down_shard = jnp.pad(down_shard, ((0, spare_units), (0, 0)))

    def halves(array):
        size = array.shape[0] // 2
        low, high = array[:size], array[size:]
        own = jnp.where(is_first, low, high)
        other = swap_sections(jnp.where(is_first, high, low))
        return jnp.where(is_first, own, other), jnp.where(is_first, other, own)

    expand_pair = halves(expand_shard)
    down_first, down_next = in_order(down_shard)
    half_units = down_shard.shape[0] // 2
    down_halves = jnp.where(is_first, down_first[:half_units], down_first[half_units:])
    first_shard, second_shard = in_order(attn_shard)
    small_pair = jnp.concatenate(in_order(small_shard))

    def gather(piece):
        return lax.all_gather(piece, both, axis=0, tiled=True)

    down_w = gather(down_halves)
    expands = [gather(piece) for piece in expand_pair]
    first_shard, second_shard, small_pair = lax.optimization_barrier(
        (first_shard, second_shard, small_pair, expand_pair[0], down_halves)
    )[:3]
    sizes = (shard_rows, bias_part, shard_rows)
    *weights, vectors = collect(first_shard, second_shard, small_pair, sizes)

    layers = []
    hidden = source
    stored = []
    sent = []
    for layer in range(2):
        now = (layer, vectors, weights[layer])
        normed, queries, every_kv, lse, context, middle, second_normed, *fetched = attend(
            now, hidden, place, (down_next,) if layer else ()
        )
        if layer:
            (down_w,) = fetched
        now = now + (expands[layer], down_w)
        layers.append(now)
        kept = (hidden, normed, queries, every_kv, lse, context)
        hidden, blocks, kept_gate, kept_up = feed(now, second_normed, middle)
        sent.append(hidden)
        stored.append((middle, kept, blocks, kept_gate, kept_up))

    def scatter(array):
        return lax.psum_scatter(array, both, scatter_dimension=0, tiled=True)

    grad = upstream
    hidden_grads = [None, None]
    small_grads = [None, None]
    attn_grads = [None, None]
    for layer in (1, 0):
        middle, kept, blocks, kept_gate, kept_up = stored[layer]
        load = () if layer else (down_grad,)
        middle_grad, second_grad, expand_grad, down_grad, *summed = feed_back(
            layers[layer], middle, blocks, kept_gate, kept_up, grad, load
        )
        if layer:
            expand_one = scatter(expand_grad)
            load = ()
        else:
            expand_grad, expand_one = lax.optimization_barrier((expand_grad, expand_one))
            expand_zero = scatter(expand_grad)
            (down_one,) = summed
            load = (attn_grads[1], expand_one)
        hidden_grad, first_grad, offset_grad, attn_grads[layer], *summed = attend_back(
            layers[layer], kept, middle_grad, place, load
        )
        small_grads[layer] = jnp.concatenate([first_grad, offset_grad, second_grad], axis=1)[0]
        hidden_grads[layer] = hidden_grad
        grad = hidden_grad

    spare = -small_grads[0].shape[0] % model_width
    small_rows = [jnp.pad(vector, (0, spare)).reshape(-1, model_width) for vector in small_grads]
    small_count = small_rows[0].shape[0]
    rows_left = -2 * small_count % 8
    small_stack = jnp.pad(jnp.concatenate(small_rows), ((0, rows_left), (0, 0)))
    attn_one, expand_one = summed
    (
        grad_projections, grad_output, small_all, down_all, activations, input_grads, expand_all,
    ) = attn_sum(
        attn_grads[0], attn_one, small_stack, down_one, sent, hidden_grads,
        down_grad, expand_zero, expand_one, wide,
    )
    grad_expand = finish(expand_all, ff_width, units)
    grad_down = down_all[:, :units].astype(f32).reshape(shard_units, model_width)
    small_own = jnp.where(
        is_first, small_all[:small_count], small_all[small_count : 2 * small_count]
    ).reshape(-1)
    first_all, offset_all, second_all = (
        small_own[:model_width],
        small_own[model_width : model_width + wide],
        small_own[model_width + wide : 2 * model_width + wide],
    )
    pair_width = (wide - model_width) // 2

    def part(vector):
        size = vector.shape[0] // fsdp_count
        return lax.dynamic_slice_in_dim(vector, fsdp * size, size)[None]

    return (
        activations[None, :, None],
        input_grads[None, :, None],
        part(first_all),
        grad_projections[None],
        part(offset_all[: model_width + pair_width]),
        part(offset_all[model_width + pair_width :]),
        grad_output[None],
        part(second_all),
        grad_expand[None],
        grad_down[None],
    )


def solution(mesh):
    return jax.shard_map(
        per_device,
        mesh=mesh,
        in_specs=(
            P(None, FSDP, CTX, None),
            P(SECTION, FSDP),
            P(SECTION, FSDP, None),
            P(SECTION, FSDP),
            P(SECTION, FSDP, None),
            P(SECTION, FSDP),
            P(SECTION, FSDP, None),
            P(SECTION, FSDP, None),
            P(None, FSDP, None),
            P(None, FSDP, CTX, None),
        ),
        out_specs=(
            P(SECTION, None, FSDP, CTX, None),
            P(SECTION, None, FSDP, CTX, None),
            P(SECTION, FSDP),
            P(SECTION, FSDP, None),
            P(SECTION, FSDP),
            P(SECTION, FSDP),
            P(SECTION, FSDP, None),
            P(SECTION, FSDP),
            P(SECTION, FSDP, None),
            P(SECTION, FSDP, None),
        ),
        check_vma=False,
    )
```

```python
import functools

import jax
import jax.numpy as jnp
from jax import lax
from jax.experimental import pallas as pl
from jax.experimental.pallas import tpu as pltpu
from jax.sharding import PartitionSpec as P

HEAD_DIM = 64
SECTION, CTX, FSDP = "section", "ctx", "fsdp"

epsilon = 1e-06
theta_base = 1000000.0
masked_value = -1e30

bf16 = jnp.bfloat16
f32 = jnp.float32


def swap_sections(block):
    return lax.ppermute(block, SECTION, [(0, 1), (1, 0)])


def tables(positions_row):
    half_dim = HEAD_DIM // 2
    frequency = theta_base ** (-(jnp.arange(half_dim, dtype=f32) * 2.0) / HEAD_DIM)
    angles = positions_row.astype(f32)[:, None] * frequency[None, :]
    cosine, sine = jnp.cos(angles), jnp.sin(angles)
    return (
        jnp.concatenate([cosine] * 4, axis=-1),
        jnp.concatenate([-sine, sine, -sine, sine], axis=-1),
    )


def pick(index, options):
    chosen = options[0]
    for position in range(1, len(options)):
        chosen = jnp.where(index == position, options[position], chosen)
    return chosen


MESH = pl.DeviceIdType.MESH
VMEM = pltpu.VMEM
LIMIT = 56 * 1024 * 1024


def flip(index, distance):
    place = 1
    while place <= distance:
        if (distance // place) % 2:
            index = index + place - 2 * place * ((index // place) % 2)
        place *= 2
    return index


def place_of():
    return lax.axis_index(SECTION), lax.axis_index(CTX), lax.axis_index(FSDP)


def peer_of(distance):
    section, ctx, fsdp = place_of()
    return (section, flip(ctx, distance), fsdp)


def greet_all(devices):
    barrier = pltpu.get_barrier_semaphore()
    for device in devices:
        pl.semaphore_signal(barrier, inc=1, device_id=device, device_id_type=MESH)
    pl.semaphore_wait(barrier, len(devices))


def greet(count):
    greet_all([peer_of(k) for k in range(1, count)])


def send(source, target, send_sem, recv_sem, device):
    return pltpu.make_async_remote_copy(
        src_ref=source,
        dst_ref=target,
        send_sem=send_sem,
        recv_sem=recv_sem,
        device_id=device,
        device_id_type=MESH,
    )


def remote(source, target, send_sem, recv_sem, k):
    return send(source, target, send_sem.at[k], recv_sem.at[k], peer_of(k))


def matmul(left, right):
    return lax.dot_general(left, right, (((1,), (0,)), ((), ())), preferred_element_type=f32)


def matmul_nt(left, right):
    return lax.dot_general(left, right, (((1,), (1,)), ((), ())), preferred_element_type=f32)


def matmul_tn(left, right):
    return lax.dot_general(left, right, (((0,), (0,)), ((), ())), preferred_element_type=f32)


def tiles(size, step):
    return [(start, min(step, size - start)) for start in range(0, size, step)]


def row_scale(values):
    return lax.rsqrt(jnp.mean(values * values, axis=-1, keepdims=True) + epsilon)


def call(kernel, outs, scratch, cid, *args, far=(), far_outs=()):
    def spec(position, away):
        return pl.BlockSpec(memory_space=pl.ANY if position in away else VMEM)

    return pl.pallas_call(
        kernel,
        out_shape=[jax.ShapeDtypeStruct(shape, kind) for shape, kind in outs],
        in_specs=[spec(position, far) for position in range(len(args))],
        out_specs=[spec(position, far_outs) for position in range(len(outs))],
        scratch_shapes=scratch,
        compiler_params=pltpu.CompilerParams(
            collective_id=cid, has_side_effects=True, vmem_limit_bytes=LIMIT
        ),
    )(*args)


def dma(*shape):
    return pltpu.SemaphoreType.DMA(shape)


class Relay:
    def __init__(self, fsdp_count, source, spot, z_send, z_recv):
        self.count, self.source, self.spot = fsdp_count, source, spot
        self.z_send, self.z_recv = z_send, z_recv
        self.section, self.ctx, self.fsdp = place_of()
        self.hops = [(side, e) for e in range(1, fsdp_count) for side in (1, 0)]

    def device(self, side):
        step = 1 if side else self.count - 1
        return (self.section, self.ctx, lax.rem(self.fsdp + step, self.count))

    def goes_on(self, side):
        return self.fsdp < self.count - 1 if side else self.fsdp > 0

    def came(self, side, e):
        return self.fsdp >= e if side else self.fsdp < self.count - e

    def origin(self, side, e):
        return lax.rem(self.fsdp + (self.count - e if side else e), self.count)

    def copy(self, side, e):
        spot = self.spot(self.origin(side, e))
        source = spot if e else self.source
        return send(source, spot, self.z_send.at[side, e], self.z_recv.at[side, e + 1], self.device(side))

    def begin(self):
        for side in range(2):

            @pl.when(self.goes_on(side))
            def _():
                self.copy(side, 0).start()

    def each(self, step):
        for side, e in self.hops:
            pl.when(self.came(side, e))(functools.partial(step, side, e))

    def steps(self):
        return range(1, self.count)

    def take(self, side, e):
        spot = self.spot(self.origin(side, e))
        sems = self.z_send.at[side, e], self.z_recv.at[side, e]
        send(spot, spot, *sems, self.device(side)).wait_recv()
        if e < self.count - 1:

            @pl.when(self.goes_on(side))
            def _():
                self.copy(side, e).start()

    def sent(self):
        for side, e in [(0, 0), (1, 0)] + self.hops:
            if e < self.count - 1:

                @pl.when(jnp.logical_and(self.came(side, e), self.goes_on(side)))
                def _():
                    self.copy(side, e).wait_send()


class Collect:
    def __init__(self, ctx_count, fsdp_count, shard_ref, w_ref, sems):
        self.shard_ref, self.w_ref = shard_ref, w_ref
        z_send, z_recv, self.y_send, self.y_recv, self.v_send, self.v_recv, self.own_sem = sems
        self.places = range(1, ctx_count)
        self.square = ctx_count == 4
        self.early = ((1, 1), (2, 0)) if self.square else ()
        self.fsdp_count = fsdp_count
        self.section, self.ctx, self.fsdp = place_of()
        self.sister = (1 - self.section, self.ctx, self.fsdp)
        self.rows, width = shard_ref.shape
        self.piece = width // (2 * ctx_count)
        self.mine = pl.ds(pl.multiple_of(self.fsdp * self.rows, self.rows), self.rows)
        own = shard_ref.at[:, self.columns(self.ctx, self.section)]
        self.line = Relay(
            fsdp_count, own, lambda shard: self.spot(shard, self.ctx, self.section), z_send, z_recv
        )
        self.ahead = [
            (self.section, self.ctx, lax.rem(self.fsdp + d, fsdp_count)) for d in range(1, fsdp_count)
        ]
        self.friends = self.ahead + [peer_of(k) for k in self.places] + [self.sister]

    def columns(self, where, core):
        return pl.ds(pl.multiple_of((where * 2 + core) * self.piece, self.piece), self.piece)

    def spot(self, shard, where, core):
        rows = pl.ds(pl.multiple_of(shard * self.rows, self.rows), self.rows)
        return self.w_ref.at[rows, self.columns(where, core)]

    def block(self, side, e, where, core):
        return self.spot(self.line.origin(side, e), where, core)

    def kept(self):
        return pltpu.make_async_copy(self.shard_ref, self.w_ref.at[self.mine], self.own_sem.at[0])

    def half(self, side, e, where, core, h):
        size = self.rows // 2
        start = self.line.origin(side, e) * self.rows + h * size
        rows = pl.ds(pl.multiple_of(start, size), size)
        return self.w_ref.at[rows, self.columns(where, core)]

    def spread(self, side, e, k, h, came=0):
        source = self.half(side, e, flip(self.ctx, came), self.section, h)
        device = peer_of(k) if k else self.sister
        i, j = side * self.fsdp_count + e, 2 * (k ^ came) + h
        return send(source, source, self.y_send.at[i, j], self.y_recv.at[i, j], device)

    def arrival(self, side, e, k, h, core):
        came = self.half(side, e, flip(self.ctx, k), core, h)
        i, j = side * self.fsdp_count + e, 2 * k + h
        return send(came, came, self.y_send.at[i, j], self.y_recv.at[i, j], self.sister)

    def outgoing(self):
        if self.square:
            return [(1, 1), (2, 0), (0, 0), (0, 1), (1, 0), (2, 1)]
        return [(k, h) for k in (*self.places, 0) for h in range(2)]

    def passed(self, side, e, k):
        source = self.block(side, e, flip(self.ctx, k), self.section)
        i = side * self.fsdp_count + e
        return send(source, source, self.v_send.at[i, k], self.v_recv.at[i, k], self.sister)

    def begin(self):
        self.line.begin()
        self.kept().start()

    def relay(self, which):
        def step(side, e):
            if e == which:
                self.line.take(side, e)
                for k, h in self.outgoing():
                    self.spread(side, e, k, h).start()

        self.line.each(step)

    def corner(self):
        def step(side, e):
            for k, h in self.early:
                self.arrival(side, e, k, h, self.section).wait_recv()
                self.spread(side, e, 3 - k, h, k).start()

        if self.square:
            self.line.each(step)

    def hand(self):
        def step(side, e):
            for k in self.places:
                for h in range(2):
                    if (k, h) not in self.early:
                        self.arrival(side, e, k, h, self.section).wait_recv()
                self.passed(side, e, k).start()

        self.line.each(step)

    def finish(self):
        def arrivals(side, e):
            i = side * self.fsdp_count + e
            for h in range(2):
                self.arrival(side, e, 0, h, 1 - self.section).wait_recv()
            for k in self.places:
                came = self.block(side, e, flip(self.ctx, k), 1 - self.section)
                send(came, came, self.v_send.at[i, k], self.v_recv.at[i, k], self.sister).wait_recv()

        def sent(side, e):
            for k, h in self.outgoing():
                self.spread(side, e, k, h).wait_send()
            for k, h in self.early:
                self.spread(side, e, 3 - k, h, k).wait_send()
            for k in self.places:
                self.passed(side, e, k).wait_send()

        self.line.each(arrivals)
        self.line.each(sent)
        self.line.sent()
        self.kept().wait()


def collect_sems(ctx_count, fsdp_count):
    line = dma(2, fsdp_count)
    table = dma(2 * fsdp_count, ctx_count)
    halves = dma(2 * fsdp_count, 2 * ctx_count)
    return [line, line, halves, halves, table, table, dma(1)]


class Line:
    def __init__(self, fsdp_count, piece_ref, out_ref, sems):
        self.piece_ref, self.out_ref = piece_ref, out_ref
        z_send, z_recv, self.v_send, self.v_recv, self.own_sem = sems
        self.section, self.ctx, self.fsdp = place_of()
        self.count = fsdp_count
        self.rows = piece_ref.shape[0]
        cut = -(-self.rows // 32) * 16
        self.parts = ((0, cut), (cut, self.rows - cut))
        self.sister = (1 - self.section, self.ctx, self.fsdp)
        self.lines = [
            Relay(
                fsdp_count,
                piece_ref.at[pl.ds(start, size)],
                functools.partial(self.spot, core),
                z_send,
                z_recv,
            )
            for core, (start, size) in enumerate(self.parts)
        ]
        self.ahead = [
            (self.section, self.ctx, lax.rem(self.fsdp + d, fsdp_count)) for d in range(1, fsdp_count)
        ]

    def spot(self, core, shard):
        start, size = self.parts[core]
        return self.out_ref.at[pl.ds(pl.multiple_of(shard * self.rows + start, 16), size)]

    def passed(self, core, side, e):
        spot = self.spot(core, self.lines[core].origin(side, e))
        i = side * self.count + e
        return send(spot, spot, self.v_send.at[i], self.v_recv.at[i], self.sister)

    def kept(self):
        start = pl.multiple_of(self.fsdp * self.rows, 16)
        return pltpu.make_async_copy(
            self.piece_ref, self.out_ref.at[pl.ds(start, self.rows)], self.own_sem.at[0]
        )

    def each_core(self, step):
        for core in range(2):
            pl.when(self.section == core)(functools.partial(step, core))

    def begin(self):
        self.each_core(lambda core: self.lines[core].begin())
        self.kept().start()

    def relay(self, which):
        def step(core):
            def take(side, e):
                if e == which:
                    self.lines[core].take(side, e)
                    self.passed(core, side, e).start()

            self.lines[core].each(take)

        self.each_core(step)

    def end(self):
        def step(core):
            line = self.lines[core]
            line.each(lambda side, e: self.passed(1 - core, side, e).wait_recv())
            line.each(lambda side, e: self.passed(core, side, e).wait_send())
            line.sent()

        self.each_core(step)
        self.kept().wait()


def line_sems(fsdp_count):
    hops = dma(2 * fsdp_count)
    return [dma(2, fsdp_count), dma(2, fsdp_count), hops, hops, dma(1)]


def collect_kernel(
    ctx_count, fsdp_count, sizes, low_ref, high_ref, small_ref, low_w_ref, high_w_ref, vectors_ref,
    smalls_ref, s_send, s_recv, *sems
):
    half = len(sems) // 2
    steps = Collect(ctx_count, fsdp_count, low_ref, low_w_ref, sems[:half])
    later = Collect(ctx_count, fsdp_count, high_ref, high_w_ref, sems[half:])

    shards = range(1, fsdp_count)

    def small(d):
        target = smalls_ref.at[steps.fsdp]
        return send(small_ref, target, s_send.at[d], s_recv.at[d], steps.ahead[d - 1])

    greet_all(steps.friends)
    steps.begin()
    later.begin()
    for d in shards:
        small(d).start()
    smalls_ref[steps.fsdp] = small_ref[...]
    for e in steps.line.steps():
        steps.relay(e)
        later.relay(e)
    steps.corner()
    later.corner()
    steps.hand()
    later.hand()
    steps.finish()
    later.finish()
    for d in shards:
        came = smalls_ref.at[lax.rem(steps.fsdp + fsdp_count - d, fsdp_count)]
        send(came, came, s_send.at[d], s_recv.at[d], steps.sister).wait_recv()
    for shard in range(fsdp_count):
        rows = smalls_ref[shard].astype(f32)
        for layer in range(2):
            for i, size in enumerate(sizes):
                row = 4 * layer + i
                vectors_ref[row : row + 1, shard * size : (shard + 1) * size] = rows[
                    16 * layer + i : 16 * layer + i + 1, :size
                ]
    for d in shards:
        small(d).wait_send()


def collect(low, high, small, sizes):
    ctx_count, fsdp_count = lax.axis_size(CTX), lax.axis_size(FSDP)
    rows, width = low.shape
    whole = ((fsdp_count * rows, width), bf16)
    return call(
        functools.partial(collect_kernel, ctx_count, fsdp_count, sizes),
        [whole, whole, ((8, fsdp_count * max(sizes)), f32)],
        [VMEM((fsdp_count,) + small.shape, bf16), dma(fsdp_count), dma(fsdp_count)]
        + collect_sems(ctx_count, fsdp_count) * 2,
        5,
        low, high, small, far_outs=(0, 1),
    )


class SquareSum:
    def __init__(self, ctx_count, grad_ref, a_ref, b_out, b_in, sems):
        self.grad_ref, self.a_ref, self.b_out = grad_ref, a_ref, b_out
        self.a_send, self.a_recv, b_send, b_recv = sems
        self.parts = Parts(ctx_count, b_out, b_in, b_send, b_recv)
        self.order = (*range(ctx_count - 1, 0, -1), 0)
        self.section, self.ctx, fsdp = place_of()
        self.sister = (1 - self.section, self.ctx, fsdp)
        self.piece = grad_ref.shape[1] // (2 * ctx_count)

    def columns(self, k, core):
        start = (flip(self.ctx, k) * 2 + core) * self.piece
        return pl.ds(pl.multiple_of(start, self.piece), self.piece)

    def chip(self, k):
        source = self.grad_ref.at[:, self.columns(k, 1 - self.section)]
        return send(source, self.a_ref.at[k], self.a_send.at[k], self.a_recv.at[k], self.sister)

    def begin(self):
        for k in self.order:
            self.chip(k).start()

    def middle(self):
        for k in self.order:
            self.chip(k).wait_recv()
            own = self.grad_ref[:, self.columns(k, self.section)].astype(f32)
            total = own + self.a_ref[k].astype(f32)
            if k:
                self.parts.put(k, total)
            else:
                self.b_out[0] = total.astype(bf16)

    def merge(self):
        self.parts.merge()

    def end(self):
        return self.parts.total(self.b_out[0].astype(f32)).astype(bf16)

    def sent(self):
        for k in self.order:
            self.chip(k).wait_send()
        self.parts.sent()


def square_scratch(ctx_count, grad):
    width, both = grad.shape
    piece = VMEM((ctx_count, width, both // (2 * ctx_count)), bf16)
    sems = [dma(ctx_count), dma(ctx_count), dma(ctx_count, 2), dma(ctx_count, 2)]
    return [piece, piece, piece] + sems


def every_owner(ctx_count, layer, start_or_wait, sources, targets, send_sem, recv_sem):
    section, ctx, fsdp = place_of()
    for k in range(ctx_count):
        device = (layer, flip(ctx, k), fsdp)

        def go():
            for i, (source, target) in enumerate(zip(sources, targets)):
                copy = send(
                    source,
                    target.at[ctx, section],
                    send_sem.at[i, k],
                    recv_sem.at[i, section, k],
                    device,
                )
                copy.start() if start_or_wait == "start" else copy.wait_send()

        pl.when(section != layer)(go) if k == 0 else go()


def from_owners(ctx_count, layer, targets, send_sem, recv_sem):
    section, ctx, fsdp = place_of()
    for core in range(2):
        for k in range(ctx_count):
            if core == layer and k == 0:
                continue

            def go():
                for i, target in enumerate(targets):
                    came = target.at[flip(ctx, k), core]
                    send(
                        came, came, send_sem.at[i, k], recv_sem.at[i, core, k], (1 - section, ctx, fsdp)
                    ).wait_recv()

            pl.when(section == layer)(go)


class Owners:
    def __init__(self, ctx_count, layer, sources, targets, cuts, sems):
        self.layer, self.targets = layer, targets
        self.send_sem, self.recv_sem, self.onward_sem = sems
        self.section, self.ctx, self.fsdp = place_of()
        self.count, self.square = ctx_count, ctx_count == 4
        self.pieces = []
        for i, source in enumerate(sources):
            for h in range(2) if self.square else (0,):
                cut = cuts[i][h] if self.square else None
                self.pieces.append((source.at[cut] if self.square else source, i, cut, h))
        self.all = range(len(self.pieces))
        self.early = [(i, 2 - self.pieces[i][3]) for i in self.all if self.square]
        self.keeper = self.section == layer

    def spot(self, i, k, core):
        _, which, cut, _ = self.pieces[i]
        spot = self.targets[which].at[flip(self.ctx, k), core]
        return spot if cut is None else spot.at[cut]

    def peer(self, k):
        return (self.layer, flip(self.ctx, k), self.fsdp)

    def own(self, i, k):
        return send(
            self.pieces[i][0],
            self.spot(i, 0, self.section),
            self.send_sem.at[i, k],
            self.recv_sem.at[i, self.section, k],
            self.peer(k),
        )

    def onward(self, i, core):
        came = 2 - self.pieces[i][3]
        spot = self.spot(i, came, core)
        return send(
            spot, spot, self.onward_sem.at[i, core], self.recv_sem.at[i, core, 3], self.peer(3 - came)
        )

    def outgoing(self):
        if self.square:
            late = [(i, 3 - k) for i, k in self.early]
            return self.early + late
        return [(i, k) for k in range(1, self.count) for i in self.all]

    def begin(self):
        for i, k in self.outgoing():
            self.own(i, k).start()

        @pl.when(jnp.logical_not(self.keeper))
        def _():
            for i in self.all:
                self.own(i, 0).start()

    def arrival(self, i, core, k):
        spot = self.spot(i, k, core)
        recv = self.recv_sem.at[i, core, k]
        sister = (1 - self.section, self.ctx, self.fsdp)
        send(spot, spot, self.send_sem.at[i, k], recv, sister).wait_recv()

    def relay(self):
        if self.square:

            @pl.when(self.keeper)
            def _():
                for i, k in self.early:
                    for core in range(2):
                        self.arrival(i, core, k)
                        self.onward(i, core).start()

    def end(self):
        @pl.when(self.keeper)
        def _():
            for k in range(self.count):
                for core in range(2):
                    for i in self.all:
                        if (i, k) not in self.early and (k or core != self.layer):
                            self.arrival(i, core, k)
            if self.square:
                for i in self.all:
                    for core in range(2):
                        self.onward(i, core).wait_send()

        @pl.when(jnp.logical_not(self.keeper))
        def _():
            for i in self.all:
                self.own(i, 0).wait_send()

        for i, k in self.outgoing():
            self.own(i, k).wait_send()


def row_halves(rows):
    cut = rows // 2 // 16 * 16
    return (pl.ds(0, cut), pl.ds(cut, rows - cut))


def column_halves(width):
    cut = -(-width // 256) * 128
    return ((slice(None), pl.ds(0, cut)), (slice(None), pl.ds(cut, width - cut)))


def owner_sems(ctx_count):
    return [dma(4, ctx_count), dma(4, 2, ctx_count), dma(4, 2)]


class LineSum:
    def __init__(self, fsdp_count, grad_ref, done_ref, refs):
        self.own_ref, self.a_ref, self.sum_ref, self.in_ref, self.a_sem, self.z_send, self.z_recv = refs
        self.grad_ref, self.done_ref = grad_ref, done_ref
        self.section, self.ctx, self.fsdp = place_of()
        self.fsdp_count = fsdp_count
        self.group = fsdp_count // 2
        self.units = grad_ref.shape[0] // fsdp_count
        self.sister = (1 - self.section, self.ctx, self.fsdp)
        self.holds = self.fsdp // self.group == self.section

    def part(self, core):
        size = self.group * self.units
        return self.grad_ref.at[pl.ds(pl.multiple_of(core * size, size), size)]

    def load(self):
        return pltpu.make_async_copy(self.part(self.section), self.own_ref, self.a_sem.at[2])

    def chip(self):
        source = self.part(1 - self.section)
        return send(source, self.a_ref, self.a_sem.at[0], self.a_sem.at[1], self.sister)

    def line(self, j):
        device = (self.section, self.ctx, self.section * self.group + j)
        source = self.sum_ref.at[pl.ds(j * self.units, self.units)]
        return send(source, self.in_ref.at[self.fsdp], self.z_send.at[j], self.z_recv.at[self.fsdp], device)

    def elsewhere(self, j):
        return pl.when(self.section * self.group + j != self.fsdp)

    def begin(self):
        self.chip().start()
        self.load().start()

    def middle(self):
        self.load().wait()
        self.chip().wait_recv()
        self.sum_ref[...] = (self.own_ref[...].astype(f32) + self.a_ref[...].astype(f32)).astype(bf16)
        for j in range(self.group):

            @self.elsewhere(j)
            def _():
                self.line(j).start()

    def end(self):
        @pl.when(self.holds)
        def _():
            start = lax.rem(self.fsdp, self.group) * self.units
            total = self.sum_ref[pl.ds(pl.multiple_of(start, self.units), self.units)].astype(f32)
            for d in range(1, self.fsdp_count):
                came = lax.rem(self.fsdp + d, self.fsdp_count)
                spot = self.in_ref.at[came]
                send(spot, spot, self.z_send.at[0], self.z_recv.at[came], self.sister).wait_recv()
                total = total + self.in_ref[came].astype(f32)
            self.done_ref[...] = total.astype(bf16)

    def sent(self):
        self.chip().wait_send()
        for j in range(self.group):

            @self.elsewhere(j)
            def _():
                self.line(j).wait_send()


def line_scratch(fsdp_count, grad):
    units, width = grad.shape
    half = VMEM((units // 2, width), bf16)
    shards = VMEM((fsdp_count, units // fsdp_count, width), bf16)
    return [half, half, half, shards, dma(3), dma(fsdp_count), dma(fsdp_count)]


class Handout:
    def __init__(self, ctx_count, fsdp_count, layer, done_ref, all_ref, refs):
        self.own_sem, self.o_send, self.o_recv, self.n_send = refs
        self.layer, self.done_ref, self.all_ref = layer, done_ref, all_ref
        self.section, self.ctx, self.fsdp = place_of()
        self.count, self.square = ctx_count, ctx_count == 4
        self.halves = column_halves(done_ref.shape[1])
        self.holder = self.fsdp // (fsdp_count // 2)
        self.holds = self.section == self.holder
        self.keeps = self.section == layer
        self.away = jnp.logical_and(self.holds, jnp.logical_not(self.keeps))
        self.at_home = jnp.logical_and(self.holds, self.keeps)
        self.early = ((1, 1), (2, 0)) if self.square else ()
        late = ((1, 0), (2, 1)) if self.square else ()
        pairs = [(k, h) for k in range(1, ctx_count) for h in range(2)]
        self.sends = (*self.early, *late) if self.square else pairs

    def spot(self, k, h):
        return self.all_ref.at[flip(self.ctx, k)].at[self.halves[h]]

    def peer(self, k):
        return (self.layer, flip(self.ctx, k), self.fsdp)

    def out(self, k, h):
        source = self.done_ref.at[self.halves[h]]
        return send(source, self.spot(0, h), self.o_send.at[k, h], self.o_recv.at[k, h], self.peer(k))

    def onward(self, h):
        came = 1 if h else 2
        spot = self.spot(came, h)
        return send(spot, spot, self.n_send.at[h], self.o_recv.at[3, h], self.peer(3 - came))

    def arrival(self, k, h):
        spot = self.spot(k, h)
        sister = (1 - self.section, self.ctx, self.fsdp)
        send(spot, spot, self.o_send.at[k, h], self.o_recv.at[k, h], sister).wait_recv()

    def kept(self):
        return pltpu.make_async_copy(self.done_ref, self.all_ref.at[self.ctx], self.own_sem.at[0])

    def begin(self):
        @pl.when(self.holds)
        def _():
            for k, h in self.sends:
                self.out(k, h).start()

        @pl.when(self.away)
        def _():
            for h in range(2):
                self.out(0, h).start()

        @pl.when(self.at_home)
        def _():
            self.kept().start()

    def relay(self):
        @pl.when(self.keeps)
        def _():
            for k, h in self.early:
                self.arrival(k, h)
                self.onward(h).start()

    def end(self):
        @pl.when(self.keeps)
        def _():
            for k in range(1, self.count):
                for h in range(2):
                    if (k, h) not in self.early:
                        self.arrival(k, h)
            for _, h in self.early:
                self.onward(h).wait_send()

        @pl.when(jnp.logical_and(self.keeps, jnp.logical_not(self.holds)))
        def _():
            for h in range(2):
                self.arrival(0, h)

        @pl.when(self.holds)
        def _():
            for k, h in self.sends:
                self.out(k, h).wait_send()

        @pl.when(self.away)
        def _():
            for h in range(2):
                self.out(0, h).wait_send()

        @pl.when(self.at_home)
        def _():
            self.kept().wait()


def handout_sems(ctx_count):
    return [dma(1), dma(ctx_count, 2), dma(ctx_count, 2), dma(2)]


def chip_square(ctx_count):
    section, ctx, fsdp = place_of()
    return [
        (section if same else 1 - section, flip(ctx, k), fsdp)
        for k in range(ctx_count)
        for same in (True, False)
        if k or not same
    ]


def turn_tile(values):
    lane = lax.broadcasted_iota(jnp.int32, values.shape, 1)
    width = values.shape[1]
    half = HEAD_DIM // 2
    ahead = pltpu.roll(values, width - half, 1)
    behind = pltpu.roll(values, half, 1)
    return jnp.where(lane % HEAD_DIM < half, ahead, behind)


def head_in_group(tile, head, group):
    lane = lax.broadcasted_iota(jnp.int32, tile.shape, 1)
    values = tile.astype(f32)
    moved = values if head % 2 == group else pltpu.roll(values, HEAD_DIM, 1)
    return jnp.where(lane // HEAD_DIM == group, moved, 0.0).astype(bf16)


def attend_kernel(count, fsdp_count, layer, *refs):
    x_ref, vectors_ref, w_ref, cos_ref, sin_ref, kpos_ref, qpos_ref = refs[:7]
    refs = refs[7:]
    if layer:
        shard_ref, *refs = refs
    normed_ref, q_ref, kv_ref, lse_ref, ctx_ref, mid_ref, low2_ref = refs[:7]
    refs = refs[7:]
    if layer:
        next_ref, *refs = refs
    mask_ref, s_ref, p_ref, vt_ref, ctxf_ref, send_sem, recv_sem, *sems = refs
    rows, width = x_ref.shape
    pair = kv_ref.shape[2] // 2
    wide = width + 2 * pair
    heads = width // HEAD_DIM
    group_size = heads // (pair // HEAD_DIM)
    if layer:
        line = Line(fsdp_count, shard_ref, next_ref, sems)
        greet_all([peer_of(k) for k in range(1, count)] + [line.sister] + line.ahead)
        line.begin()
    else:
        greet(count)
    x = x_ref[...].astype(f32)
    gain1, bias, gain2 = (vectors_ref[4 * layer + i : 4 * layer + i + 1, :] for i in range(3))
    normed = (x * row_scale(x) * gain1[:, :width]).astype(bf16)
    normed_ref[...] = normed
    cos, sin = cos_ref[...], sin_ref[...]
    kv = matmul(normed, w_ref[:, width:wide]) + bias[:, width:wide]
    keys = kv[:, :pair]
    kv_ref[0, :, :pair] = (keys * cos + turn_tile(keys) * sin).astype(bf16)
    kv_ref[0, :, pair:] = kv[:, pair:].astype(bf16)
    for k in range(1, count):
        remote(kv_ref.at[0], kv_ref.at[k], send_sem, recv_sem, k).start()
    merged = matmul(normed, w_ref[:, :width]) + bias[:, :width]
    for start, size in tiles(width, 2 * HEAD_DIM):
        part = merged[:, start : start + size]
        turned_part = (part * cos + turn_tile(part) * sin) * HEAD_DIM ** (-0.5)
        q_ref[:, start : start + size] = turned_part.astype(bf16)
    for k in range(count):
        allowed = kpos_ref[k * rows : (k + 1) * rows, :] <= qpos_ref[...]
        mask_ref[k] = jnp.where(allowed, 0.0, masked_value)
    for k in range(count):
        if k:
            remote(kv_ref.at[0], kv_ref.at[k], send_sem, recv_sem, k).wait_recv()
        vt_ref[:, k * rows : (k + 1) * rows] = kv_ref[k, :, pair:].astype(f32).T.astype(bf16)

    for head in range(heads):
        group = head // group_size
        start = head // 2 * (2 * HEAD_DIM)
        query = head_in_group(q_ref[:, start : start + 2 * HEAD_DIM], head, group)
        top = None
        for k in range(count):
            scores = matmul_nt(kv_ref[k, :, :pair], query) + mask_ref[k]
            s_ref[k] = scores
            here = jnp.max(scores, axis=0, keepdims=True)
            top = here if top is None else jnp.maximum(top, here)
        total = None
        for k in range(count):
            weight = jnp.exp(s_ref[k] - top)
            here = jnp.sum(weight, axis=0, keepdims=True)
            total = here if total is None else total + here
            p_ref[k * rows : (k + 1) * rows, :] = weight.astype(bf16)
        value_rows = vt_ref[group * HEAD_DIM : (group + 1) * HEAD_DIM, :]
        context = matmul(value_rows, p_ref[...]) * (1.0 / total)
        ctxf_ref[head * HEAD_DIM : (head + 1) * HEAD_DIM, :] = context
        lse_ref[head : head + 1, :] = top + jnp.log(total)
        for e in range(1, fsdp_count - 1) if layer else ():
            if head == e * heads // fsdp_count + 1:
                line.relay(e)
    context = ctxf_ref[...]
    ctx_ref[...] = context.astype(bf16)
    middle = x + matmul(context.T.astype(bf16), w_ref[:, wide:])
    mid_ref[...] = middle
    low2_ref[...] = (middle * row_scale(middle) * gain2[:, :width]).astype(bf16)
    for k in range(1, count):
        remote(kv_ref.at[0], kv_ref.at[k], send_sem, recv_sem, k).wait_send()
    if layer:
        line.relay(fsdp_count - 1)
        line.end()


def attend(layer, hidden, place, piece=()):
    index, vectors, weights = layer[:3]
    cosine, sine, key_positions, query_positions = place
    rows, width = hidden.shape
    count = lax.axis_size(CTX)
    wide = weights.shape[1] - width
    pair = (wide - width) // 2
    keys = count * rows
    heads = width // HEAD_DIM
    fsdp_count = lax.axis_size(FSDP)
    args = (hidden, vectors, weights, cosine, sine, key_positions, query_positions)
    return call(
        functools.partial(attend_kernel, count, fsdp_count, index),
        [
            ((rows, width), bf16),
            ((rows, width), bf16),
            ((count, rows, 2 * pair), bf16),
            ((-(-heads // 8) * 8, rows), f32),
            ((width, rows), bf16),
            ((rows, width), f32),
            ((rows, width), bf16),
        ]
        + [((fsdp_count * array.shape[0], width), bf16) for array in piece],
        [
            VMEM((count, rows, rows), f32),
            VMEM((count, rows, rows), f32),
            VMEM((keys, rows), bf16),
            VMEM((pair, keys), bf16),
            VMEM((width, rows), f32),
            dma(count),
            dma(count),
        ]
        + line_sems(fsdp_count) * len(piece),
        1 if index else 10,
        *args, *piece,
        far_outs=(7,) * len(piece),
    )


def attend_back_kernel(count, layer, carried, *refs):
    (
        dmid_ref, x_ref, vectors_ref, w_ref, cos_ref, sin_ref, kpos_ref, qpos_ref,
        normed_ref, q_ref, kv_ref, lse_ref, ctx_ref,
    ) = refs[:13]
    refs = refs[13:]
    (load_ref, expand_ref), refs = (refs[:2], refs[2:]) if carried else ((None, None), refs)
    dh_ref, gain_ref, bias_ref, grad_ref = refs[:4]
    refs = refs[4:]
    (summed_ref, expand_all_ref), refs = (refs[:2], refs[2:]) if carried else ((None, None), refs)
    (
        mask_ref, p_ref, dp_ref, ds_ref, kt_ref, dctx_ref, dq_ref, dkv_ref, out_ref, in_ref,
        merged_ref, low_ref, send_sem, recv_sem, *scratch,
    ) = refs
    rows, width = x_ref.shape
    pair = kv_ref.shape[2] // 2
    wide = width + 2 * pair
    heads = width // HEAD_DIM
    group_size = heads // (pair // HEAD_DIM)
    if carried:
        section, ctx, _ = place_of()
        steps = SquareSum(count, load_ref, *scratch[:3], scratch[3:7])
        halves = [row_halves(expand_ref.shape[0])]
        owners = Owners(count, 1, [expand_ref], [expand_all_ref], halves, scratch[7:10])
        kept = pltpu.make_async_copy(expand_ref, expand_all_ref.at[ctx, section], scratch[10].at[0])
        greet_all(chip_square(count))
        steps.begin()
        owners.begin()

        @pl.when(owners.keeper)
        def _():
            kept.start()

    else:
        greet(count)
    low = dmid_ref[...].astype(bf16)
    low_ref[...] = low
    dctx = matmul_nt(low, w_ref[:, wide:]).astype(bf16)
    dctx_ref[...] = dctx
    for k in range(count):
        allowed = kpos_ref[k * rows : (k + 1) * rows, :] <= qpos_ref[...]
        mask_ref[k] = jnp.where(allowed, 0.0, masked_value)
        kt_ref[:, k * rows : (k + 1) * rows] = kv_ref[k, :, :pair].astype(f32).T.astype(bf16)
    dkv_ref[...] = jnp.zeros_like(dkv_ref)

    for head in range(heads):
        group = head // group_size
        start = head // 2 * (2 * HEAD_DIM)
        query = head_in_group(q_ref[:, start : start + 2 * HEAD_DIM], head, group)
        upstream = head_in_group(dctx_ref[:, start : start + 2 * HEAD_DIM], head, group)
        lse = lse_ref[head : head + 1, :]
        delta = None
        for k in range(count):
            scores = matmul_nt(kv_ref[k, :, :pair], query) + mask_ref[k]
            weight = jnp.exp(scores - lse)
            weight_grad = matmul_nt(kv_ref[k, :, pair:], upstream)
            p_ref[k] = weight
            dp_ref[k] = weight_grad
            dkv_ref[k, :, pair:] += matmul(weight.astype(bf16), upstream)
            here = jnp.sum(weight * weight_grad, axis=0, keepdims=True)
            delta = here if delta is None else delta + here
        for k in range(count):
            score_grad = (p_ref[k] * (dp_ref[k] - delta)).astype(bf16)
            ds_ref[k * rows : (k + 1) * rows, :] = score_grad
            dkv_ref[k, :, :pair] += matmul(score_grad, query)
        key_rows = kt_ref[group * HEAD_DIM : (group + 1) * HEAD_DIM, :]
        dq_ref[head * HEAD_DIM : (head + 1) * HEAD_DIM, :] = (
            matmul(key_rows, ds_ref[...]) * HEAD_DIM ** (-0.5)
        )
        if carried and head == heads // 5:
            steps.middle()
        if carried and head == heads // 3:
            owners.relay()
        if carried and head == heads * 2 // 3:
            steps.merge()
    for k in range(1, count):
        out_ref[k] = dkv_ref[k].astype(bf16)
        remote(out_ref.at[k], in_ref.at[k], send_sem, recv_sem, k).start()
    cos, sin = cos_ref[...], sin_ref[...]
    dq = dq_ref[...].T

    def unturn(part):
        return (part * cos - turn_tile(part) * sin).astype(bf16)

    for start, size in tiles(width, 2 * HEAD_DIM):
        merged_ref[:, start : start + size] = unturn(dq[:, start : start + size])
    grad_ref[:, wide:] = matmul(ctx_ref[...], low_ref[...]).astype(bf16)
    normed = normed_ref[...]

    def project_grad(first, last):
        for start, size in tiles(last - first, 512):
            cut = slice(first + start, first + start + size)
            grad_ref[:, cut] = matmul_tn(normed, merged_ref[:, cut]).astype(bf16)

    project_grad(0, width)
    normed_grad = matmul_nt(merged_ref[:, :width], w_ref[:, :width])
    total = dkv_ref[0]
    for k in range(1, count):
        remote(out_ref.at[k], in_ref.at[k], send_sem, recv_sem, k).wait_recv()
        total = total + in_ref[k].astype(f32)
    merged_ref[:, width : width + pair] = unturn(total[:, :pair])
    merged_ref[:, width + pair :] = total[:, pair:].astype(bf16)
    project_grad(width, wide)
    normed_grad = normed_grad + matmul_nt(merged_ref[:, width:], w_ref[:, width:wide])
    bias_ref[...] = jnp.sum(merged_ref[...].astype(f32), axis=0, keepdims=True)
    x = x_ref[...].astype(f32)
    scale = row_scale(x)
    gain_ref[...] = jnp.sum(normed_grad * x * scale, axis=0, keepdims=True)
    scaled = normed_grad * vectors_ref[4 * layer : 4 * layer + 1, :width]
    mean = jnp.mean(scaled * x, axis=-1, keepdims=True)
    hidden_grad = dmid_ref[...] + scale * scaled - x * (scale * scale * scale * mean)
    dh_ref[...] = hidden_grad.astype(dh_ref.dtype)
    for k in range(1, count):
        remote(out_ref.at[k], in_ref.at[k], send_sem, recv_sem, k).wait_send()
    if carried:
        summed_ref[...] = steps.end()
        steps.sent()
        owners.end()

        @pl.when(owners.keeper)
        def _():
            kept.wait()


def attend_back(layer, kept, middle_grad, place, load=()):
    index, vectors, weights = layer[:3]
    cosine, sine, key_positions, query_positions = place
    hidden, normed, queries, every_kv, lse, context = kept
    rows, width = hidden.shape
    count = lax.axis_size(CTX)
    wide = weights.shape[1] - width
    pair = (wide - width) // 2
    keys = count * rows
    carried = bool(load)
    args = (
        middle_grad, hidden, vectors, weights, cosine, sine, key_positions, query_positions,
        normed, queries, every_kv, lse, context,
    )
    return call(
        functools.partial(attend_back_kernel, count, index, carried),
        [
            ((rows, width), bf16 if index else f32),
            ((1, width), f32),
            ((1, wide), f32),
            ((width, wide + width), bf16),
        ]
        + (
            [((width, (wide + width) // (2 * count)), bf16), ((count, 2) + load[1].shape, bf16)]
            if carried
            else []
        ),
        [
            VMEM((count, rows, rows), f32),
            VMEM((count, rows, rows), f32),
            VMEM((count, rows, rows), f32),
            VMEM((keys, rows), bf16),
            VMEM((pair, keys), bf16),
            VMEM((rows, width), bf16),
            VMEM((width, rows), f32),
            VMEM((count, rows, 2 * pair), f32),
            VMEM((count, rows, 2 * pair), bf16),
            VMEM((count, rows, 2 * pair), bf16),
            VMEM((rows, wide), bf16),
            VMEM((rows, width), bf16),
            dma(count),
            dma(count),
        ]
        + (square_scratch(count, load[0]) + owner_sems(count) + [dma(1)] if carried else []),
        6 if carried else 2,
        *args, *load,
        far_outs=(5,) if carried else (),
    )


def unit_chunks(units):
    main = units // 128 * 128
    chunks = [(start, main + start, start, size) for start, size in tiles(main, 512)]
    if units > main:
        chunks.append((2 * main, main + units, main, units - main))
    return chunks


def pack_units(gate, up):
    main = gate.shape[1] // 128 * 128
    return jnp.concatenate([gate[:, :main], up[:, :main], gate[:, main:], up[:, main:]], axis=1)


def unpack_units(packed):
    units = packed.shape[-1] // 2
    main = units // 128 * 128
    if units == main:
        return packed[..., :main], packed[..., main:]
    gate = jnp.concatenate([packed[..., :main], packed[..., 2 * main : main + units]], axis=-1)
    up = jnp.concatenate([packed[..., main : 2 * main], packed[..., main + units :]], axis=-1)
    return gate, up


class Rows:
    def __init__(self, count, own_ref, slots_ref, send_sem, recv_sem):
        self.own_ref, self.slots_ref = own_ref, slots_ref
        self.send_sem, self.recv_sem = send_sem, recv_sem
        self.count, self.square = count, count == 4
        self.half = own_ref.shape[0] // 2

    def rows(self, h):
        return pl.ds(h * self.half, self.half)

    def copy(self, source, k, h, peer):
        target = self.slots_ref.at[k, self.rows(h)]
        return send(source, target, self.send_sem.at[k, h], self.recv_sem.at[k, h], peer_of(peer))

    def own(self, k, h):
        return self.copy(self.own_ref.at[self.rows(h)], k, h, k)

    def onward(self, h):
        came = 1 if h else 2
        return self.copy(self.slots_ref.at[came, self.rows(h)], 3, h, 3 - came)

    def order(self):
        if self.square:
            return [(1, 1), (2, 0), (1, 0), (2, 1)]
        return [(k, h) for k in range(1, self.count) for h in range(2)]

    def begin(self):
        for k, h in self.order():
            self.own(k, h).start()

    def relay(self):
        if self.square:
            for k, h in ((1, 1), (2, 0)):
                self.own(k, h).wait_recv()
                self.onward(h).start()

    def take(self, k):
        for h in range(2):
            if not (self.square and (k, h) in ((1, 1), (2, 0))):
                self.copy(self.own_ref.at[self.rows(h)], k, h, k).wait_recv()

    def sent(self):
        for k, h in self.order():
            self.own(k, h).wait_send()
        if self.square:
            for h in range(2):
                self.onward(h).wait_send()


class Parts:
    def __init__(self, count, parts_ref, got_ref, send_sem, recv_sem):
        self.parts_ref, self.got_ref = parts_ref, got_ref
        self.send_sem, self.recv_sem = send_sem, recv_sem
        self.count, self.square = count, count == 4
        self.half = parts_ref.shape[1] // 2

    def rows(self, h):
        return pl.ds(h * self.half, self.half)

    def copy(self, k, h):
        peer = 1 + h if self.square and k == 3 else k
        source, target = self.parts_ref.at[k, self.rows(h)], self.got_ref.at[k, self.rows(h)]
        return send(source, target, self.send_sem.at[k, h], self.recv_sem.at[k, h], peer_of(peer))

    def put(self, k, part):
        self.parts_ref[k] = part.astype(bf16)
        for h in range(2):
            if not (self.square and (k, h) in ((1, 1), (2, 0))):
                self.copy(k, h).start()

    def merge(self):
        if self.square:
            for k, h in ((2, 0), (1, 1)):
                self.copy(3, h).wait_recv()
                rows = slice(h * self.half, (h + 1) * self.half)
                total = self.parts_ref[k, rows].astype(f32) + self.got_ref[3, rows].astype(f32)
                self.parts_ref[k, rows] = total.astype(bf16)
                self.copy(k, h).start()

    def total(self, own):
        for k in range(1, 3 if self.square else self.count):
            for h in range(2):
                self.copy(k, h).wait_recv()
            own = own + self.got_ref[k].astype(f32)
        return own

    def sent(self):
        for k in range(1, self.count):
            for h in range(2):
                self.copy(k, h).wait_send()


class Loads:
    def __init__(self, sources, targets, sem):
        self.copies = [
            pltpu.make_async_copy(source, target, sem.at[i])
            for i, (source, target) in enumerate(zip(sources, targets))
        ]
        for copy in self.copies:
            copy.start()

    def take(self, *which):
        for i in which:
            self.copies[i].wait()


def units_kernel(ctx_count, fsdp_count, units, stride, expand_ref, out_ref):
    ff_width = expand_ref.shape[1] // 2
    rows = expand_ref.shape[0]
    main = fsdp_count * stride // 128 * 128
    size = fsdp_count * stride
    for where in range(ctx_count):

        @pl.when(lax.axis_index(CTX) == where)
        def _():
            sides = []
            for side in range(2):
                pieces = []
                for shard in range(fsdp_count):
                    start = side * ff_width + (shard * ctx_count + where) * units
                    pieces.append(expand_ref[:, start : start + units])
                    if stride > units:
                        pieces.append(jnp.zeros((rows, stride - units), bf16))
                sides.append(jnp.concatenate(pieces, axis=1))
            out_ref[:, :main] = sides[0][:, :main]
            out_ref[:, main : 2 * main] = sides[1][:, :main]
            if size > main:
                out_ref[:, 2 * main :] = jnp.concatenate([side[:, main:] for side in sides], axis=1)


def gate_and_up(block, expand_ref, gate_start, up_start, size):
    if size % 128:
        both = matmul(block, expand_ref[:, gate_start : up_start + size])
        return both[:, :size], both[:, size:]
    gate = matmul(block, expand_ref[:, gate_start : gate_start + size])
    return gate, matmul(block, expand_ref[:, up_start : up_start + size])


def feed_kernel(
    count, low_ref, mid_ref, expand_any, down_any,
    out_ref, blocks_ref, kept_gate_ref, kept_up_ref,
    expand_ref, down_ref, act_ref, part_ref, sent_ref, got_ref,
    send_sem, recv_sem, send_sem2, recv_sem2, load_sem,
):
    units = down_ref.shape[0]
    loads = Loads((expand_any, down_any), (expand_ref, down_ref), load_sem)
    rows = Rows(count, low_ref, blocks_ref, send_sem, recv_sem)
    parts = Parts(count, sent_ref, got_ref, send_sem2, recv_sem2)
    greet(count)
    rows.begin()
    blocks_ref[0] = low_ref[...]
    loads.take(0, 1)
    for k in range(count):
        if k:
            rows.take(k)
        block = blocks_ref[k]
        for gate_start, up_start, start, size in unit_chunks(units):
            gate, up = gate_and_up(block, expand_ref, gate_start, up_start, size)
            kept_gate_ref[k, :, start : start + size] = gate.astype(bf16)
            kept_up_ref[k, :, start : start + size] = up.astype(bf16)
            act_ref[:, start : start + size] = (gate / (1.0 + jnp.exp(-gate)) * up).astype(bf16)
        part = matmul(act_ref[...], down_ref[...])
        if k:
            parts.put(k, part)
        else:
            part_ref[...] = part + mid_ref[...]
            rows.relay()
    parts.merge()
    out_ref[...] = parts.total(part_ref[...]).astype(bf16)
    rows.sent()
    parts.sent()


def feed(layer, second_normed, middle):
    expand_w, down_w = layer[3:]
    count = lax.axis_size(CTX)
    rows, width = second_normed.shape
    units = down_w.shape[0]
    return call(
        functools.partial(feed_kernel, count),
        [
            ((rows, width), bf16),
            ((count, rows, width), bf16),
            ((count, rows, units), bf16),
            ((count, rows, units), bf16),
        ],
        [
            VMEM(expand_w.shape, bf16),
            VMEM(down_w.shape, bf16),
            VMEM((rows, units), bf16),
            VMEM((rows, width), f32),
            VMEM((count, rows, width), bf16),
            VMEM((count, rows, width), bf16),
        ]
        + [dma(count, 2)] * 4
        + [dma(2)],
        3,
        second_normed, middle, expand_w, down_w, far=(2, 3),
    )


def feed_back_kernel(count, fsdp_count, layer, carried, *refs):
    (
        grad_ref, mid_ref, vectors_ref,
        blocks_any, kept_gate_any, kept_up_any, expand_any, down_any,
    ) = refs[:8]
    refs = refs[8:]
    line_ref, refs = (refs[0], refs[1:]) if carried else (None, refs)
    dmid_ref, gain_ref, dexpand_ref, ddown_ref = refs[:4]
    refs = refs[4:]
    done_ref, refs = (refs[0], refs[1:]) if carried else (None, refs)
    (
        blocks_ref, kept_gate_ref, kept_up_ref, expand_ref, down_ref,
        grads_ref, act_ref, dwide_ref, part_ref, sent_ref, got_ref,
        send_sem, recv_sem, send_sem2, recv_sem2, load_sem, *scratch,
    ) = refs
    rows, width = grad_ref.shape
    units = down_ref.shape[0]
    loads = Loads(
        (down_any, kept_gate_any, kept_up_any, expand_any, blocks_any),
        (down_ref, kept_gate_ref, kept_up_ref, expand_ref, blocks_ref),
        load_sem,
    )
    gather = Rows(count, grad_ref, grads_ref, send_sem, recv_sem)
    parts = Parts(count, sent_ref, got_ref, send_sem2, recv_sem2)
    if carried:
        line = LineSum(fsdp_count, line_ref, done_ref, scratch)
        section, ctx, fsdp = place_of()
        greet_all(
            [peer_of(k) for k in range(1, count)]
            + [line.sister]
            + [(section, ctx, lax.rem(fsdp + d, fsdp_count)) for d in range(1, fsdp_count)]
        )
        line.begin()
    else:
        greet(count)
    gather.begin()
    grads_ref[0] = grad_ref[...]
    loads.take(0, 1, 2)
    for k in range(count):
        if k:
            gather.take(k)
        block = grads_ref[k]
        for gate_start, up_start, start, size in unit_chunks(units):
            cut = slice(start, start + size)
            spread = matmul_nt(block, down_ref[cut, :])
            gate = kept_gate_ref[k, :, cut].astype(f32)
            up = kept_up_ref[k, :, cut].astype(f32)
            sig = 1.0 / (1.0 + jnp.exp(-gate))
            silu = gate * sig
            act_ref[k, :, cut] = (silu * up).astype(bf16)
            dgate = (spread * up * sig * (1.0 + gate * (1.0 - sig))).astype(bf16)
            dup = (spread * silu).astype(bf16)
            if size % 128:
                dwide_ref[k, :, gate_start : up_start + size] = jnp.concatenate([dgate, dup], axis=1)
            else:
                dwide_ref[k, :, gate_start : gate_start + size] = dgate
                dwide_ref[k, :, up_start : up_start + size] = dup
        if not k:
            loads.take(3)
        part = matmul_nt(dwide_ref[k], expand_ref[...])
        if k:
            parts.put(k, part)
        else:
            part_ref[...] = part
            gather.relay()
            if carried:
                line.middle()
    loads.take(4)
    tall = count * rows
    grads = grads_ref[...].reshape(tall, width)
    main = units // 128 * 128
    for start, size in tiles(main, 384) + [(main, units - main)] * (units > main):
        act = act_ref[:, :, start : start + size].reshape(tall, size)
        ddown_ref[start : start + size, :] = matmul_tn(act, grads).astype(bf16)
    parts.merge()
    blocks = blocks_ref[...].reshape(tall, width)
    for start, size in tiles(2 * units, 512):
        dwide = dwide_ref[:, :, start : start + size].reshape(tall, size)
        dexpand_ref[:, start : start + size] = matmul_tn(blocks, dwide).astype(bf16)
    if carried:
        line.end()
    total = parts.total(part_ref[...])
    middle = mid_ref[...]
    scale = row_scale(middle)
    gain_ref[...] = jnp.sum(total * middle * scale, axis=0, keepdims=True)
    scaled = total * vectors_ref[4 * layer + 2 : 4 * layer + 3, :width]
    mean = jnp.mean(scaled * middle, axis=-1, keepdims=True)
    dmid_ref[...] = (
        grad_ref[...].astype(f32) + scale * scaled - middle * (scale * scale * scale * mean)
    )
    gather.sent()
    parts.sent()
    if carried:
        line.sent()


def feed_back(layer, middle, blocks, kept_gate, kept_up, grad_out, load=()):
    index, vectors = layer[:2]
    expand_w, down_w = layer[3:]
    count = lax.axis_size(CTX)
    rows, width = grad_out.shape
    units = down_w.shape[0]
    fsdp_count = lax.axis_size(FSDP)
    brought = (blocks, kept_gate, kept_up, expand_w, down_w)
    return call(
        functools.partial(feed_back_kernel, count, fsdp_count, index, bool(load)),
        [
            ((rows, width), f32),
            ((1, width), f32),
            ((width, 2 * units), bf16),
            ((units, width), bf16),
        ]
        + [((units // fsdp_count, width), bf16)] * len(load),
        [VMEM(array.shape, bf16) for array in brought]
        + [
            VMEM((count, rows, width), bf16),
            VMEM((count, rows, units), bf16),
            VMEM((count, rows, 2 * units), bf16),
            VMEM((rows, width), f32),
            VMEM((count, rows, width), bf16),
            VMEM((count, rows, width), bf16),
        ]
        + [dma(count, 2)] * 4
        + [dma(5)]
        + (line_scratch(fsdp_count, load[0]) if load else []),
        4 + 7 * index,
        grad_out, middle, vectors, *brought, *load, far=(3, 4, 5, 6, 7, 8),
    )


def attn_sum_kernel(
    ctx_count, fsdp_count, wide, low_ref, high_ref, small_ref, down_ref,
    act_zero_ref, act_one_ref, grad_zero_ref, grad_one_ref, down_grad_ref, expand_ref, expand_all_ref,
    projections_ref, output_ref, total_ref, down_all_ref, act_ref, grad_ref, expand_out,
    wide_ref, done_ref,
    c_out, c_in, d_out, whole_ref, s_out, s_in,
    c_send, c_recv, d_send, d_recv, s_send, s_recv, *more,
):
    section, ctx, fsdp = place_of()
    sister = (1 - section, ctx, fsdp)
    width, piece = high_ref.shape
    rows = width // fsdp_count
    places = range(1, ctx_count)
    shards = range(1, fsdp_count)
    steps = SquareSum(ctx_count, low_ref, *more[:3], more[3:7])
    halves = [row_halves(expand_ref.shape[0])]
    owners = Owners(ctx_count, 0, [expand_ref], [expand_out], halves, more[7:10])
    own_sem, swap_send, swap_recv = more[10:13]
    kept = pltpu.make_async_copy(expand_ref, expand_out.at[ctx, section], own_sem.at[0])
    load = pltpu.make_async_copy(expand_all_ref, expand_out, own_sem.at[1])
    down = LineSum(fsdp_count, down_grad_ref, done_ref, more[13:20])
    handouts = [
        Handout(ctx_count, fsdp_count, 1, down_ref, down_all_ref, more[20:24]),
        Handout(ctx_count, fsdp_count, 0, done_ref, down_all_ref, more[24:28]),
    ]
    layers = ((act_zero_ref, grad_zero_ref), (act_one_ref, wide_ref))

    def swap(i, layer):
        target = (act_ref, grad_ref)[i].at[section]
        return send(layers[layer][i], target, swap_send.at[i], swap_recv.at[i], sister)

    def ahead(d):
        return (section, ctx, lax.rem(fsdp + d, fsdp_count))

    def c_copy(layer, d):
        target = lax.rem(fsdp + d, fsdp_count)
        source = c_out.at[layer, pl.ds(pl.multiple_of(target * rows, rows), rows)]
        return send(source, c_in.at[layer, d], c_send.at[layer, d], c_recv.at[layer, d], ahead(d))

    def s_copy(step, source, device):
        return send(s_out.at[source], s_in.at[step], s_send.at[step], s_recv.at[step], device)

    def line_sum(layer):
        total = c_out[layer, pl.ds(pl.multiple_of(fsdp * rows, rows), rows)].astype(f32)
        for d in shards:
            c_copy(layer, d).wait_recv()
            total = total + c_in[layer, d].astype(f32)
        d_out[layer] = total.astype(bf16)
        every_owner(
            ctx_count, layer, "start", [d_out.at[layer]], [whole_ref], d_send.at[layer], d_recv
        )

        @pl.when(section == layer)
        def _():
            whole_ref[ctx, section] = d_out[layer]

    hops = [(0, 0, sister)]
    hops += [(k, 1, peer_of(k)) for k in places]
    hops += [(ctx_count - 1 + d, 2, ahead(d)) for d in shards]

    greet_all(chip_square(ctx_count) + [ahead(d) for d in shards])
    steps.begin()
    down.begin()
    owners.begin()

    @pl.when(section == 0)
    def _():
        kept.start()

    @pl.when(section == 1)
    def _():
        load.start()

    wide_ref[...] = grad_one_ref[...].astype(f32)
    for layer in range(2):

        @pl.when(section != layer)
        def _():
            for i in range(2):
                swap(i, layer).start()

        @pl.when(section == layer)
        def _():
            for i, target in enumerate((act_ref, grad_ref)):
                target[section] = layers[layer][i][...]

    s_out[0] = small_ref[...]
    s_copy(*hops[0]).start()
    c_out[1] = high_ref[...]
    for d in shards:
        c_copy(1, d).start()

    steps.middle()
    down.middle()
    handouts[0].begin()
    owners.relay()
    s_copy(*hops[0]).wait_recv()
    s_out[1] = s_out[0] + s_in[0]
    for k in places:
        s_copy(*hops[k]).start()
    line_sum(1)
    steps.merge()
    c_out[0] = steps.end()
    for d in shards:
        c_copy(0, d).start()
    handouts[0].relay()
    down.end()
    handouts[1].begin()
    part = s_out[1]
    for k in places:
        s_copy(*hops[k]).wait_recv()
        part = part + s_in[k]
    s_out[2] = part
    for d in shards:
        s_copy(*hops[ctx_count - 1 + d]).start()
    line_sum(0)
    part = s_out[2]
    for d in shards:
        s_copy(*hops[ctx_count - 1 + d]).wait_recv()
        part = part + s_in[ctx_count - 1 + d]
    total_ref[...] = part
    for layer in (1, 0):
        from_owners(ctx_count, layer, [whole_ref], d_send.at[layer], d_recv)
    for where in range(ctx_count):
        for core in range(2):
            start = (where * 2 + core) * piece
            block = whole_ref[where, core].astype(f32)
            size = max(min(wide - start, piece), 0)
            if size:
                projections_ref[:, start : start + size] = block[:, :size]
            if size < piece:
                first = start + size - wide
                output_ref[:, first : first + piece - size] = block[:, size:]
    owners.end()
    handouts[1].relay()
    for handout in handouts:
        handout.end()
    down.sent()

    @pl.when(section == 0)
    def _():
        kept.wait()

    @pl.when(section == 1)
    def _():
        load.wait()

    for i in range(2):
        swap(i, 0).wait()
    steps.sent()
    for layer in (1, 0):
        for d in shards:
            c_copy(layer, d).wait_send()
        every_owner(
            ctx_count, layer, "wait", [d_out.at[layer]], [whole_ref], d_send.at[layer], d_recv
        )
    for hop in hops:
        s_copy(*hop).wait_send()


def attn_sum(low, high, small, down_one, acts, grads, down_grad, expand_part, expand_all, wide):
    ctx_count, fsdp_count = lax.axis_size(CTX), lax.axis_size(FSDP)
    width, both = low.shape
    rows = width // fsdp_count
    piece = both // (2 * ctx_count)
    hops = ctx_count + fsdp_count - 1
    return call(
        functools.partial(attn_sum_kernel, ctx_count, fsdp_count, wide),
        [
            ((rows, wide), f32),
            ((rows, both - wide), f32),
            (small.shape, f32),
            ((ctx_count,) + down_one.shape, bf16),
            ((2,) + acts[0].shape, bf16),
            ((2,) + grads[0].shape, f32),
            (expand_all.shape, bf16),
        ],
        [
            VMEM(grads[0].shape, f32),
            VMEM(down_one.shape, bf16),
            VMEM((2, width, piece), bf16),
            VMEM((2, fsdp_count, rows, piece), bf16),
            VMEM((2, rows, piece), bf16),
            VMEM((ctx_count, 2, rows, piece), bf16),
            VMEM((3,) + small.shape, f32),
            VMEM((hops,) + small.shape, f32),
            dma(2, fsdp_count), dma(2, fsdp_count),
            dma(2, 1, ctx_count), dma(1, 2, ctx_count),
            dma(hops), dma(hops),
        ]
        + square_scratch(ctx_count, low)
        + owner_sems(ctx_count)
        + [dma(2), dma(2), dma(2)]
        + line_scratch(fsdp_count, down_grad)
        + handout_sems(ctx_count) * 2,
        7,
        low, high, small, down_one, *acts, *grads, down_grad, expand_part, expand_all,
        far=(8, 10), far_outs=(3,),
    )


def spread_kernel(chunk, stride, shards, side_width, block_ref, out_ref):
    count = block_ref.shape[0]
    for where in range(count):
        sides = unpack_units(block_ref[where].astype(f32))
        for side, values in enumerate(sides):
            for shard in range(shards):
                start = side * side_width + (shard * count + where) * chunk
                out_ref[:, start : start + chunk] = values[:, shard * stride : shard * stride + chunk]


def finish(expand_all, ff_width, units):
    ctx_count, fsdp_count = lax.axis_size(CTX), lax.axis_size(FSDP)
    half, packed = expand_all.shape[2:]
    rows = 2 * half
    step = 32 if rows % 32 == 0 else 16
    stride = packed // 2 // fsdp_count
    return pl.pallas_call(
        functools.partial(spread_kernel, units, stride, fsdp_count, ff_width),
        grid=(rows // step,),
        out_shape=jax.ShapeDtypeStruct((rows, 2 * ff_width), f32),
        in_specs=[pl.BlockSpec((ctx_count, step, packed), lambda i: (0, i, 0))],
        out_specs=pl.BlockSpec((step, 2 * ff_width), lambda i: (i, 0)),
        compiler_params=pltpu.CompilerParams(vmem_limit_bytes=LIMIT),
    )(expand_all.reshape(ctx_count, rows, packed))


def per_device(
    inputs,
    attend_gain,
    projections,
    biases,
    output_weight,
    mixer_gain,
    expand_weight,
    down_weight,
    positions,
    cotangent,
):
    row_count, model_width = inputs.shape[2:]
    section = lax.axis_index(SECTION)
    is_first = section == 0
    ctx = lax.axis_index(CTX)
    fsdp = lax.axis_index(FSDP)
    ctx_count = lax.axis_size(CTX)
    fsdp_count = lax.axis_size(FSDP)
    shard_rows = projections.shape[1]
    wide = projections.shape[2]
    ff_width = expand_weight.shape[2] // 2
    shard_units = down_weight.shape[1]
    units = shard_units // ctx_count
    spare_units = -units % 16
    both = (FSDP, SECTION)

    def mine(array):
        return lax.dynamic_index_in_dim(array, section, 0, keepdims=False)

    source = mine(inputs)[0]
    upstream = mine(cotangent)[0]
    key_positions = mine(positions)[0]
    query_positions = lax.dynamic_slice_in_dim(key_positions, ctx * row_count, row_count)
    cosine, sine = tables(query_positions)
    by_distance = jnp.concatenate(
        [
            lax.dynamic_slice_in_dim(key_positions, (ctx ^ k) * row_count, row_count)
            for k in range(ctx_count)
        ]
    )
    place = (cosine, sine, by_distance[:, None], query_positions[None])

    bias_part = biases.shape[1]
    small_width = -(-bias_part // 128) * 128

    def padded(row):
        return jnp.pad(row, ((0, 0), (0, small_width - row.shape[1])))

    small_shard = jnp.concatenate(
        [padded(attend_gain), padded(biases), padded(mixer_gain), jnp.zeros((13, small_width), bf16)]
    )
    attn_shard = jnp.concatenate([projections[0], output_weight[0]], axis=1)

    def in_order(array):
        other = swap_sections(array)
        return jnp.where(is_first, array, other), jnp.where(is_first, other, array)

    stride = units + spare_units
    expand_shard = pl.pallas_call(
        functools.partial(units_kernel, ctx_count, fsdp_count, units, stride),
        out_shape=jax.ShapeDtypeStruct((shard_rows, 2 * fsdp_count * stride), bf16),
        in_specs=[pl.BlockSpec(memory_space=VMEM)],
        out_specs=pl.BlockSpec(memory_space=VMEM),
        compiler_params=pltpu.CompilerParams(vmem_limit_bytes=LIMIT),
    )(expand_weight[0])
    down_shard = lax.dynamic_slice_in_dim(down_weight[0], ctx * units, units)
    down_shard = jnp.pad(down_shard, ((0, spare_units), (0, 0)))

    def halves(array):
        size = array.shape[0] // 2
        low, high = array[:size], array[size:]
        own = jnp.where(is_first, low, high)
        other = swap_sections(jnp.where(is_first, high, low))
        return jnp.where(is_first, own, other), jnp.where(is_first, other, own)

    expand_pair = halves(expand_shard)
    down_first, down_next = in_order(down_shard)
    half_units = down_shard.shape[0] // 2
    down_halves = jnp.where(is_first, down_first[:half_units], down_first[half_units:])
    first_shard, second_shard = in_order(attn_shard)
    small_pair = jnp.concatenate(in_order(small_shard))

    def gather(piece):
        return lax.all_gather(piece, both, axis=0, tiled=True)

    down_w = gather(down_halves)
    expands = [gather(piece) for piece in expand_pair]
    first_shard, second_shard, small_pair = lax.optimization_barrier(
        (first_shard, second_shard, small_pair, expand_pair[0], down_halves)
    )[:3]
    sizes = (shard_rows, bias_part, shard_rows)
    *weights, vectors = collect(first_shard, second_shard, small_pair, sizes)

    layers = []
    hidden = source
    stored = []
    sent = []
    for layer in range(2):
        now = (layer, vectors, weights[layer])
        normed, queries, every_kv, lse, context, middle, second_normed, *fetched = attend(
            now, hidden, place, (down_next,) if layer else ()
        )
        if layer:
            (down_w,) = fetched
        now = now + (expands[layer], down_w)
        layers.append(now)
        kept = (hidden, normed, queries, every_kv, lse, context)
        hidden, blocks, kept_gate, kept_up = feed(now, second_normed, middle)
        sent.append(hidden)
        stored.append((middle, kept, blocks, kept_gate, kept_up))

    def scatter(array):
        return lax.psum_scatter(array, both, scatter_dimension=0, tiled=True)

    grad = upstream
    hidden_grads = [None, None]
    small_grads = [None, None]
    attn_grads = [None, None]
    for layer in (1, 0):
        middle, kept, blocks, kept_gate, kept_up = stored[layer]
        load = () if layer else (down_grad,)
        middle_grad, second_grad, expand_grad, down_grad, *summed = feed_back(
            layers[layer], middle, blocks, kept_gate, kept_up, grad, load
        )
        if layer:
            expand_one = scatter(expand_grad)
            load = ()
        else:
            expand_grad, expand_one = lax.optimization_barrier((expand_grad, expand_one))
            expand_zero = scatter(expand_grad)
            (down_one,) = summed
            load = (attn_grads[1], expand_one)
        hidden_grad, first_grad, offset_grad, attn_grads[layer], *summed = attend_back(
            layers[layer], kept, middle_grad, place, load
        )
        small_grads[layer] = jnp.concatenate([first_grad, offset_grad, second_grad], axis=1)[0]
        hidden_grads[layer] = hidden_grad
        grad = hidden_grad

    spare = -small_grads[0].shape[0] % model_width
    small_rows = [jnp.pad(vector, (0, spare)).reshape(-1, model_width) for vector in small_grads]
    small_count = small_rows[0].shape[0]
    rows_left = -2 * small_count % 8
    small_stack = jnp.pad(jnp.concatenate(small_rows), ((0, rows_left), (0, 0)))
    attn_one, expand_one = summed
    (
        grad_projections, grad_output, small_all, down_all, activations, input_grads, expand_all,
    ) = attn_sum(
        attn_grads[0], attn_one, small_stack, down_one, sent, hidden_grads,
        down_grad, expand_zero, expand_one, wide,
    )
    grad_expand = finish(expand_all, ff_width, units)
    grad_down = down_all[:, :units].astype(f32).reshape(shard_units, model_width)
    small_own = jnp.where(
        is_first, small_all[:small_count], small_all[small_count : 2 * small_count]
    ).reshape(-1)
    first_all, offset_all, second_all = (
        small_own[:model_width],
        small_own[model_width : model_width + wide],
        small_own[model_width + wide : 2 * model_width + wide],
    )
    pair_width = (wide - model_width) // 2

    def part(vector):
        size = vector.shape[0] // fsdp_count
        return lax.dynamic_slice_in_dim(vector, fsdp * size, size)[None]

    return (
        activations[None, :, None],
        input_grads[None, :, None],
        part(first_all),
        grad_projections[None],
        part(offset_all[: model_width + pair_width]),
        part(offset_all[model_width + pair_width :]),
        grad_output[None],
        part(second_all),
        grad_expand[None],
        grad_down[None],
    )


def solution(mesh):
    return jax.shard_map(
        per_device,
        mesh=mesh,
        in_specs=(
            P(None, FSDP, CTX, None),
            P(SECTION, FSDP),
            P(SECTION, FSDP, None),
            P(SECTION, FSDP),
            P(SECTION, FSDP, None),
            P(SECTION, FSDP),
            P(SECTION, FSDP, None),
            P(SECTION, FSDP, None),
            P(None, FSDP, None),
            P(None, FSDP, CTX, None),
        ),
        out_specs=(
            P(SECTION, None, FSDP, CTX, None),
            P(SECTION, None, FSDP, CTX, None),
            P(SECTION, FSDP),
            P(SECTION, FSDP, None),
            P(SECTION, FSDP),
            P(SECTION, FSDP),
            P(SECTION, FSDP, None),
            P(SECTION, FSDP),
            P(SECTION, FSDP, None),
            P(SECTION, FSDP, None),
        ),
        check_vma=False,
    )
```
